32 devices in a mesh: groups: 2 (over y), tensor: 4 (over z), inner: 4 (over x, core).
Axes of the slice: x: 2, y: 2, z: 4, core: 2. Of those that a mesh axis runs over, the one named last changes fastest.
Arguments:
- states: bfloat16 [16, 8192], P(('groups', 'tensor'), 'inner'), parts along dimension 0, may hold values from -6 to 6
- attn_gain: bfloat16 [8192], P('inner'), may hold values from 0.5 to 1.5
- ffn_gain: bfloat16 [8192], P('inner'), may hold values from 0.5 to 1.5
- w_query: bfloat16 [8192, 4096], P('inner', 'tensor'), may hold values from -3 to 3
- w_kv: bfloat16 [8192, 1024], P('inner', 'tensor'), may hold values from -0.0625 to 0.0625
- w_out: bfloat16 [4096, 8192], P('tensor', 'inner'), may hold values from -0.1875 to 0.1875
- w_gate: bfloat16 [8192, 14336], P('inner', 'tensor'), may hold values from -0.0625 to 0.0625
- w_up: bfloat16 [8192, 14336], P('inner', 'tensor'), may hold values from -0.0625 to 0.0625
- w_down: bfloat16 [14336, 8192], P('tensor', 'inner'), may hold values from -0.046875 to 0.046875
- key_cache: bfloat16 [16, 4096, 4, 128], P(('groups', 'tensor'), 'inner'), parts along dimension 0, may hold values from -12 to 12
- value_cache: bfloat16 [16, 4096, 4, 128], P(('groups', 'tensor'), 'inner'), parts along dimension 0, may hold values from -6 to 6
- lengths: int32 [16], P('groups'), parts along dimension 0, may hold values from 1 to 4096, as said below
Outputs:
- result: bfloat16 [16, 8192], P(('groups', 'tensor'), 'inner'), parts along dimension 0
The draws below stay inside these ranges and needn't reach their ends.
There are 2 independent parts, one for each index of `groups`. The reference program is written for one: setup_inputs(seed, part) draws one part's arguments, and reference() takes and returns one part's arrays. A program takes and returns all parts, laid end to end along the dimension named above; an argument that names none is the same for every part. Nothing has to cross between parts.
Inputs may be any that keep to these rules, and one draw needn't show every extreme that they name: `lengths`: some row has exactly 4096 and some row exactly 1.
All inputs are finite; a program needn't handle non-finite values.
Results may differ from the reference program's by a relative error of at most 0.02.
Values may be sent and summed in bfloat16 or wider, within the bound.
No kernel may reach another device: no remote copies, remote signals or barrier semaphores. Data moves between devices by JAX's collectives and lax.ppermute only.
A program may use at most 128 MiB of HBM per device.

```python
import math
import jax
import jax.numpy as jnp
from jax import lax

D = 8192
FF = 14336
HEADS = 32
KV_HEADS = 4
HEAD_DIM = 128
CACHE = 4096
ROWS = 8
N_TENSOR = 4


def row_plan(key):
    plan_key = jax.random.fold_in(key, 7)
    key_lengths, key_ranking = jax.random.split(plan_key, 2)
    lengths = jax.random.randint(key_lengths, (ROWS,), 1, CACHE + 1)
    ranking = jax.random.permutation(key_ranking, ROWS)
    lengths = lengths.at[ranking[0]].set(CACHE)
    lengths = lengths.at[ranking[1]].set(1)
    return lengths.astype(jnp.int32)


def draw_lengths(key, part):
    lengths = row_plan(key)
    return lengths


def draw_states(key, part):
    key = jax.random.fold_in(key, 11)
    along = jnp.arange(D).astype(jnp.float32) / float(D - 1)
    column_scale = 0.4 * 5.0 ** along
    values = jax.random.truncated_normal(key, -2.9, 2.9, (ROWS, D), jnp.float32) * column_scale[None, :]
    return values.astype(jnp.bfloat16)


def draw_w_query(key, part):
    key = jax.random.fold_in(key, 17)
    values = jax.random.truncated_normal(key, -6.0, 6.0, (D, HEADS * HEAD_DIM), jnp.float32) * D ** (-0.5)
    return values.astype(jnp.bfloat16)


def draw_key_cache(key, part):
    key = jax.random.fold_in(key, 13)
    values = 2.0 * jax.random.truncated_normal(key, -6.0, 6.0, (ROWS, CACHE, KV_HEADS, HEAD_DIM), jnp.float32)
    return values.astype(jnp.bfloat16)


def level_of(rng, extent, cuts, low, top_value):
    factor_of = 1.0
    for dim, parts in cuts:
        draws = jax.random.uniform(jax.random.fold_in(jax.random.fold_in(rng, 6), dim), (parts,), jnp.float32, low / len(cuts), top_value / len(cuts))
        factor_of = factor_of * jnp.repeat(jnp.exp(draws), extent[dim] // parts).reshape((-1,) + (1,) * (len(extent) - 1 - dim))
    return factor_of


def centred(own_key, dims, width, most, cuts=(), kind=jnp.bfloat16):
    level = level_of(own_key, dims, cuts, -0.22, 0.18) if cuts else 1.0
    array = jax.random.normal(own_key, dims, jnp.float32) * width * level
    return jnp.minimum(jnp.maximum(array, -most), most).astype(kind)


def setup_inputs(seed: int = 0, part: int = 0) -> dict:
    streams_of = jax.random.split(jax.random.key(seed), 13)
    part_keys = jax.random.split(jax.random.fold_in(streams_of[12], part), 13)
    states = draw_states(jax.random.fold_in(jax.random.fold_in(streams_of[12], part), 71), part)
    attn_gain = jnp.clip(1.0 + 0.1 * jax.random.normal(streams_of[1], (D,), jnp.float32), 0.5, 1.5).astype(jnp.bfloat16)
    ffn_gain = jnp.clip(1.0 + 0.1 * jax.random.normal(streams_of[2], (D,), jnp.float32), 0.5, 1.5).astype(jnp.bfloat16)
    w_query = draw_w_query(jax.random.fold_in(streams_of[12], 71), part)
    w_kv = centred(streams_of[4], (D, 2 * KV_HEADS * HEAD_DIM), D ** -0.5, 0.0625, ((0, 4), (1, 4)))
    w_out = centred(streams_of[5], (HEADS * HEAD_DIM, D), (HEAD_DIM * 8) ** -0.5, 0.1875, ((0, 4), (1, 4)))
    w_gate = centred(streams_of[6], (D, FF), D ** -0.5, 0.0625, ((0, 4), (1, 4)))
    w_up = centred(streams_of[7], (D, FF), D ** -0.5, 0.0625, ((0, 4), (1, 4)))
    w_down = centred(streams_of[8], (FF, D), FF ** -0.5, 0.046875, ((0, 4), (1, 4)))
    key_cache = draw_key_cache(jax.random.fold_in(jax.random.fold_in(streams_of[12], part), 71), part)
    value_cache = centred(part_keys[10], (ROWS, CACHE, KV_HEADS, HEAD_DIM), 1.0, 6.0, ((0, 4), (1, 4)))
    lengths = draw_lengths(jax.random.fold_in(jax.random.fold_in(streams_of[12], part), 71), part)
    return dict(states=states, attn_gain=attn_gain, ffn_gain=ffn_gain, w_query=w_query, w_kv=w_kv, w_out=w_out, w_gate=w_gate, w_up=w_up, w_down=w_down, key_cache=key_cache, value_cache=value_cache, lengths=lengths)


epsilon = 1e-05
rope_base = 500000.0

def rms_scale(values, gain):
    widened = values.astype(jnp.float32)
    square_mean = lax.optimization_barrier(jnp.mean(widened * widened, axis=1, keepdims=True))
    return (widened * lax.rsqrt(square_mean + epsilon) * gain.astype(jnp.float32)[None, :]).astype(jnp.bfloat16)

def rotate(values, positions, pair_index):
    row_total = values.shape[0]
    paired = values.reshape(row_total, -1, 2)
    inverse = jnp.exp(pair_index.astype(jnp.float32) * (-2.0 / HEAD_DIM) * math.log(rope_base))
    angles = positions[:, None] * inverse[None, :]
    cosine = jnp.cos(angles)
    sines = jnp.sin(angles)
    lead_part = paired[:, :, 0]
    tail_part = paired[:, :, 1]
    turned = jnp.stack([lead_part * cosine - tail_part * sines, lead_part * sines + tail_part * cosine], axis=-1)
    return turned.reshape(row_total, -1)

def grouped_sum(left, right):
    pieces = left.reshape(left.shape[0], N_TENSOR, -1).astype(jnp.float32)
    blocks = right.reshape(N_TENSOR, -1, right.shape[1]).astype(jnp.float32)
    products = jnp.einsum('rtk,tkd->trd', pieces, blocks)
    rounded = lax.optimization_barrier(products.astype(jnp.bfloat16)).astype(jnp.float32)
    return lax.optimization_barrier(jnp.sum(rounded, axis=0))

def reference(states, attn_gain, ffn_gain, w_query, w_kv, w_out, w_gate, w_up, w_down, key_cache, value_cache, lengths):
    positions = lengths.astype(jnp.float32)
    half_dim = HEAD_DIM // 2
    group_size = HEADS // KV_HEADS
    normed = rms_scale(states, attn_gain)
    query_lin = jnp.dot(normed, w_query, preferred_element_type=jnp.float32)
    kv_lin = jnp.dot(normed, w_kv, preferred_element_type=jnp.float32)
    queries = rotate(query_lin, positions, jnp.arange(HEADS * half_dim) % half_dim).astype(jnp.bfloat16)
    queries = queries.reshape(ROWS, KV_HEADS, group_size, HEAD_DIM)
    new_keys = rotate(kv_lin[:, :KV_HEADS * HEAD_DIM], positions, jnp.arange(KV_HEADS * half_dim) % half_dim)
    new_keys = new_keys.astype(jnp.bfloat16).reshape(ROWS, KV_HEADS, HEAD_DIM)
    new_values = kv_lin[:, KV_HEADS * HEAD_DIM:].astype(jnp.bfloat16).reshape(ROWS, KV_HEADS, HEAD_DIM)
    score_scale = HEAD_DIM ** (-0.5)
    query_wide = queries.astype(jnp.float32)
    scores = jnp.einsum('rgjd,rsgd->rgjs', query_wide, key_cache.astype(jnp.float32)) * score_scale
    usable = jnp.arange(CACHE)[None, :] < lengths[:, None]
    masked = jnp.where(usable[:, None, None, :], scores, -1e+30)
    new_score = jnp.einsum('rgjd,rgd->rgj', query_wide, new_keys.astype(jnp.float32)) * score_scale
    row_peak = jnp.maximum(lax.optimization_barrier(jnp.max(masked, axis=3)), new_score)
    weights = jnp.exp(masked - row_peak[..., None])
    new_weight = jnp.exp(new_score - row_peak)
    totals = lax.optimization_barrier(jnp.sum(weights, axis=3)) + new_weight
    mixture = jnp.einsum('rgjs,rsgd->rgjd', weights.astype(jnp.bfloat16).astype(jnp.float32), value_cache.astype(jnp.float32))
    mixture = mixture + new_weight.astype(jnp.bfloat16).astype(jnp.float32)[..., None] * new_values.astype(jnp.float32)[:, :, None, :]
    attended = (mixture / totals[..., None]).reshape(ROWS, HEADS * HEAD_DIM).astype(jnp.bfloat16)
    attn_sum = grouped_sum(attended, w_out)
    updated = (states.astype(jnp.float32) + attn_sum).astype(jnp.bfloat16)
    normed_two = rms_scale(updated, ffn_gain)
    gate = jnp.dot(normed_two, w_gate, preferred_element_type=jnp.float32)
    upward = jnp.dot(normed_two, w_up, preferred_element_type=jnp.float32)
    hidden = (jax.nn.silu(gate) * upward).astype(jnp.bfloat16)
    down_sum = grouped_sum(hidden, w_down)
    return (updated.astype(jnp.float32) + down_sum).astype(jnp.bfloat16)
```

```python
import math

import jax
import jax.numpy as jnp
from jax import lax
from jax.sharding import PartitionSpec as P

D = 8192
HEADS = 32
KV_HEADS = 4
HEAD_DIM = 128

epsilon = 1e-05
rope_base = 500000.0


def swap_with(value, axis, step):
    count = lax.axis_size(axis)
    return lax.ppermute(value, axis, [(i, i ^ step) for i in range(count)])


def exchange(value, axis):
    return [value] + [swap_with(value, axis, k) for k in range(1, lax.axis_size(axis))]


def scatter_slots(pieces, axis):
    return [pieces[0]] + [swap_with(pieces[k], axis, k) for k in range(1, len(pieces))]


def unslot(stacked, index):
    count = stacked.shape[0]
    bit = 1
    while bit < count:
        shape = (count // (2 * bit), 2, bit) + stacked.shape[1:]
        turned = stacked.reshape(shape)[:, ::-1].reshape(stacked.shape)
        stacked = jnp.where((index & bit) != 0, turned, stacked)
        bit *= 2
    return stacked


def rotate(values, positions):
    inverse = jnp.exp(
        jnp.arange(HEAD_DIM // 2).astype(jnp.float32) * (-2.0 / HEAD_DIM) * math.log(rope_base)
    )
    angles = positions[:, None] * inverse[None, :]
    cosine = jnp.repeat(jnp.cos(angles), 2, axis=1)[:, None, :]
    sines = jnp.repeat(jnp.sin(angles), 2, axis=1)[:, None, :]
    even = (jnp.arange(HEAD_DIM) % 2 == 0)[None, None, :]
    other = jnp.where(even, -jnp.roll(values, -1, axis=-1), jnp.roll(values, 1, axis=-1))
    return values * cosine + other * sines


def local(
    states,
    attn_gain,
    ffn_gain,
    w_query,
    w_kv,
    w_out,
    w_gate,
    w_up,
    w_down,
    key_cache,
    value_cache,
    lengths,
):
    tensor_index = lax.axis_index("tensor")
    tensor_count = lax.axis_size("tensor")
    inner_index = lax.axis_index("inner")
    own_rows = states.shape[0]
    all_rows = own_rows * tensor_count
    group_size = HEADS // KV_HEADS
    query_cols = w_query.shape[1]

    own = states.astype(jnp.float32)
    squares = exchange(jnp.sum(own * own, axis=1), "inner")
    rows = jnp.concatenate(exchange(states, "tensor"), axis=0)
    scaled = (rows.astype(jnp.float32) * attn_gain.astype(jnp.float32)[None, :]).astype(jnp.bfloat16)
    joined = jnp.concatenate(
        [
            jnp.dot(scaled, w_query, preferred_element_type=jnp.float32),
            jnp.dot(scaled, w_kv, preferred_element_type=jnp.float32),
        ],
        axis=1,
    ).astype(jnp.bfloat16)
    joined = joined.reshape(tensor_count, own_rows, -1)
    got = scatter_slots([joined[k] for k in range(tensor_count)], "tensor")
    partial = exchange(jnp.stack(got), "inner")
    total = sum(p.astype(jnp.float32) for p in partial)
    scale = lax.rsqrt(sum(squares) / D + epsilon)
    total = unslot(total, tensor_index) * scale[None, :, None]
    total = total.transpose(1, 0, 2)
    my_lengths = lax.dynamic_slice_in_dim(lengths, tensor_index * own_rows, own_rows, 0)
    positions = my_lengths.astype(jnp.float32)
    queries = rotate(total[:, :, :query_cols].reshape(own_rows, HEADS, HEAD_DIM), positions)
    queries = queries.astype(jnp.bfloat16).reshape(own_rows, KV_HEADS, group_size, HEAD_DIM)
    kv_whole = total[:, :, query_cols:].reshape(own_rows, 2 * KV_HEADS, HEAD_DIM)
    new_keys = rotate(kv_whole[:, :KV_HEADS], positions).astype(jnp.bfloat16)
    new_values = kv_whole[:, KV_HEADS:].astype(jnp.bfloat16)

    score_scale = HEAD_DIM ** (-0.5)
    slot_count = key_cache.shape[1]
    slot_places = inner_index * slot_count + jnp.arange(slot_count)
    usable = slot_places[None, :] < my_lengths[:, None]
    scores = (
        jnp.einsum("rgjd,rsgd->rgjs", queries, key_cache, preferred_element_type=jnp.float32)
        * score_scale
    )
    masked = jnp.where(usable[:, None, None, :], scores, -1e30)
    new_score = (
        jnp.einsum("rgjd,rgd->rgj", queries, new_keys, preferred_element_type=jnp.float32)
        * score_scale
    )
    new_score = jnp.where(inner_index == 0, new_score, -1e30)
    peak = jnp.maximum(jnp.max(masked, axis=3), new_score)
    weights = jnp.exp(masked - peak[..., None])
    new_weight = jnp.exp(new_score - peak)
    totals = jnp.sum(weights, axis=3) + new_weight
    mixture = jnp.einsum(
        "rgjs,rsgd->rgjd",
        weights.astype(jnp.bfloat16),
        value_cache,
        preferred_element_type=jnp.float32,
    )
    mixture = mixture + (
        new_weight.astype(jnp.bfloat16).astype(jnp.float32)[..., None]
        * new_values.astype(jnp.float32)[:, :, None, :]
    )
    peak = peak.reshape(own_rows, HEADS, 1)
    totals = totals.reshape(own_rows, HEADS, 1)
    mixture = mixture.reshape(own_rows, HEADS, HEAD_DIM)
    wide = jnp.concatenate(
        [
            mixture,
            jnp.broadcast_to(totals, (own_rows, HEADS, HEAD_DIM // 2)),
            jnp.broadcast_to(peak, (own_rows, HEADS, HEAD_DIM // 2)),
        ],
        axis=2,
    )
    shards = exchange(wide, "inner")
    peaks = [s[:, :, HEAD_DIM + HEAD_DIM // 2 :][:, :, :1] for s in shards]
    top = peaks[0]
    for p in peaks[1:]:
        top = jnp.maximum(top, p)
    factors = [jnp.exp(p - top) for p in peaks]
    mixed = sum(s[:, :, :HEAD_DIM] * f for s, f in zip(shards, factors))
    denominator = sum(s[:, :, HEAD_DIM : HEAD_DIM + 1] * f for s, f in zip(shards, factors))
    attended = (mixed / denominator).astype(jnp.bfloat16)
    attended = attended.reshape(own_rows, tensor_count, -1).transpose(1, 0, 2)
    attended = unslot(attended, tensor_index)
    picked = scatter_slots([attended[k] for k in range(tensor_count)], "tensor")
    picked = jnp.concatenate(picked, axis=0)

    part = jnp.dot(picked, w_out, preferred_element_type=jnp.float32).astype(jnp.bfloat16)
    parts = exchange(part.reshape(tensor_count, own_rows, -1), "tensor")
    attn_sum = jnp.stack(
        [
            sum(parts[k][s ^ k].astype(jnp.float32) for k in range(tensor_count))
            for s in range(tensor_count)
        ]
    ).reshape(all_rows, -1)
    updated = (rows.astype(jnp.float32) + attn_sum).astype(jnp.bfloat16)
    wide_updated = updated.astype(jnp.float32)
    squares = exchange(jnp.sum(wide_updated * wide_updated, axis=1), "inner")
    scaled = (wide_updated * ffn_gain.astype(jnp.float32)[None, :]).astype(jnp.bfloat16)
    gates = exchange(
        jnp.dot(scaled, w_gate, preferred_element_type=jnp.float32).astype(jnp.bfloat16), "inner"
    )
    ups = exchange(
        jnp.dot(scaled, w_up, preferred_element_type=jnp.float32).astype(jnp.bfloat16), "inner"
    )
    scale = lax.rsqrt(sum(squares) / D + epsilon)[:, None]
    gate = sum(g.astype(jnp.float32) for g in gates) * scale
    upward = sum(u.astype(jnp.float32) for u in ups) * scale
    hidden = (jax.nn.silu(gate) * upward).astype(jnp.bfloat16)
    part = jnp.dot(hidden, w_down, preferred_element_type=jnp.float32).astype(jnp.bfloat16)
    part = part.reshape(tensor_count, own_rows, -1)
    parts = scatter_slots([part[k] for k in range(tensor_count)], "tensor")
    down_sum = sum(p.astype(jnp.float32) for p in parts)
    return (wide_updated[:own_rows] + down_sum).astype(jnp.bfloat16)


def solution(mesh):
    in_specs = (
        P(("groups", "tensor"), "inner"),
        P("inner"),
        P("inner"),
        P("inner", "tensor"),
        P("inner", "tensor"),
        P("tensor", "inner"),
        P("inner", "tensor"),
        P("inner", "tensor"),
        P("tensor", "inner"),
        P(("groups", "tensor"), "inner", None, None),
        P(("groups", "tensor"), "inner", None, None),
        P("groups"),
    )
    out_specs = P(("groups", "tensor"), "inner")
    return jax.shard_map(local, mesh=mesh, in_specs=in_specs, out_specs=out_specs, check_vma=False)
```

```python
import functools
import math

import jax
import jax.numpy as jnp
from jax import lax
from jax.experimental import pallas as pl
from jax.experimental.pallas import tpu as pltpu
from jax.sharding import PartitionSpec as P

D = 8192
HEADS = 32
KV_HEADS = 4
HEAD_DIM = 128
GROUP = HEADS // KV_HEADS
LANES = 128
MIB = 2**20

epsilon = 1e-05
rope_base = 500000.0

in_vmem = pl.BlockSpec(memory_space=pltpu.VMEM)
in_smem = pl.BlockSpec(memory_space=pltpu.SMEM)
in_place = pl.BlockSpec(memory_space=pl.ANY)


def swap_with(value, axis, step):
    count = lax.axis_size(axis)
    return lax.ppermute(value, axis, [(i, i ^ step) for i in range(count)])


def exchange(value, axis):
    count = lax.axis_size(axis)
    got = {k: swap_with(value, axis, k) for k in reversed(range(1, count))}
    return [value] + [got[k] for k in range(1, count)]


def scatter_slots(pieces, axis):
    got = {k: swap_with(pieces[k], axis, k) for k in reversed(range(1, len(pieces)))}
    return [pieces[0]] + [got[k] for k in range(1, len(pieces))]


def pair_sums(value, axis):
    count = lax.axis_size(axis)
    step = 1
    while 2 * step < count:
        other = swap_with(value, axis, step)
        value = (value.astype(jnp.float32) + other.astype(jnp.float32)).astype(value.dtype)
        step *= 2
    return value, swap_with(value, axis, step)


def params(mib):
    return pltpu.CompilerParams(vmem_limit_bytes=mib * MIB)


def resident(weight):
    return pltpu.with_memory_space_constraint(weight, pltpu.VMEM)


def tile_of(columns):
    for tile in (512, 256, 128):
        if columns % tile == 0:
            return tile
    return columns


def product_tiles(left, weight_ref, store):
    columns = weight_ref.shape[1]
    tile = tile_of(columns)

    @pl.loop(0, columns // tile)
    def _(step):
        start = pl.multiple_of(step * tile, tile)
        store(
            start,
            tile,
            jnp.dot(left, weight_ref[:, pl.ds(start, tile)], preferred_element_type=jnp.float32),
        )


def three_parts(value):
    high = value.astype(jnp.bfloat16).astype(jnp.float32)
    rest = value - high
    middle = rest.astype(jnp.bfloat16).astype(jnp.float32)
    return high, middle, rest - middle


def spread(parts, lanes, first):
    out = 0.0
    for n, part in enumerate(parts):
        out = out + jnp.where(lanes == first + n, part, 0.0)
    return out


def squares_block(total, place):
    lanes = lax.broadcasted_iota(jnp.int32, (total.shape[0], LANES), 1)
    return spread(three_parts(total), lanes, place * 4).astype(jnp.bfloat16)


def load_kernel(count, *refs):
    sems = refs[-1]
    outs = refs[-1 - count : -1]
    copies = [pltpu.make_async_copy(refs[n], outs[n], sems.at[n]) for n in range(count)]
    for copy in copies:
        copy.start()
    for copy in copies:
        copy.wait()


def load(*weights, after):
    return pl.pallas_call(
        functools.partial(load_kernel, len(weights)),
        out_shape=tuple(pltpu.VMEM(w.shape, w.dtype) for w in weights),
        in_specs=[in_place] * (len(weights) + 1),
        out_specs=tuple(in_vmem for _ in weights),
        cost_estimate=pl.CostEstimate(
            flops=0, bytes_accessed=2 * sum(w.size for w in weights), transcendentals=0
        ),
        scratch_shapes=[pltpu.SemaphoreType.DMA((len(weights),))],
        compiler_params=params(1),
        name="load",
    )(*[pltpu.with_memory_space_constraint(w, pltpu.HBM) for w in weights], after)


def qkv_kernel(meta_ref, rows_ref, gain_ref, wq_ref, wkv_ref, out_ref):
    wide = rows_ref[...].astype(jnp.float32)
    total = jnp.sum(wide * wide, axis=1, keepdims=True)
    scaled = (wide * gain_ref[...].astype(jnp.float32)).astype(jnp.bfloat16)
    query_cols = wq_ref.shape[1]
    kv_cols = wkv_ref.shape[1]

    def store_query(start, size, value):
        out_ref[:, pl.ds(start, size)] = value.astype(jnp.bfloat16)

    product_tiles(scaled, wq_ref, store_query)
    out_ref[:, query_cols : query_cols + kv_cols] = jnp.dot(
        scaled, wkv_ref[...], preferred_element_type=jnp.float32
    ).astype(jnp.bfloat16)
    out_ref[:, query_cols + kv_cols :] = squares_block(total, meta_ref[1])


def project_qkv(meta, rows, gain, w_query, w_kv):
    columns = w_query.shape[1] + w_kv.shape[1] + LANES
    return pl.pallas_call(
        qkv_kernel,
        out_shape=jax.ShapeDtypeStruct((rows.shape[0], columns), jnp.bfloat16),
        in_specs=[in_smem] + [in_vmem] * 4,
        out_specs=in_vmem,
        compiler_params=params(2),
        name="project_qkv",
    )(meta, rows, gain, resident(w_query), resident(w_kv))


def attend_kernel(
    slots,
    meta_ref,
    cosine_ref,
    sine_ref,
    near_ref,
    far_ref,
    key_ref,
    value_ref,
    out_ref,
    query_s,
    kv_s,
    kv_wide_s,
    mixed_s,
    stats_s,
):
    all_rows = near_ref.shape[0]
    own_rows = all_rows // slots
    here = HEADS // slots
    query_cols = here * HEAD_DIM
    kv_cols = 2 * KV_HEADS * HEAD_DIM // slots
    columns = query_cols + kv_cols
    tensor_index = meta_ref[0]
    inner_index = meta_ref[1]
    positions = key_ref.shape[1] // KV_HEADS

    joined = near_ref[...].astype(jnp.float32) + far_ref[...].astype(jnp.float32)
    squares = jnp.sum(joined[:, columns:], axis=1, keepdims=True)
    joined = joined[:, :columns] * lax.rsqrt(squares / D + epsilon)
    cosine = cosine_ref[...]
    sine = sine_ref[...]

    def rotate(block):
        count = block.shape[0]
        even = lax.broadcasted_iota(jnp.int32, block.shape, 1) % 2 == 0
        other = jnp.where(
            even, pltpu.roll(block, HEAD_DIM - 1, axis=1), pltpu.roll(block, 1, axis=1)
        )
        return block * cosine[:count] + other * sine[:count]

    for j in range(here):
        block = rotate(joined[:, j * HEAD_DIM : (j + 1) * HEAD_DIM])
        query_s[j * all_rows : (j + 1) * all_rows, :] = block
    for s in range(slots):
        kv_s[s] = joined[s * own_rows : (s + 1) * own_rows, query_cols:]
    for d in range(slots):
        kv_wide_s[:, d * kv_cols : (d + 1) * kv_cols] = kv_s[d ^ tensor_index]
    new_keys = []
    new_values = []
    for g in range(KV_HEADS):
        block = kv_wide_s[:, g * HEAD_DIM : (g + 1) * HEAD_DIM]
        new_keys.append(rotate(block).astype(jnp.bfloat16).astype(jnp.float32))
        block = kv_wide_s[:, (KV_HEADS + g) * HEAD_DIM : (KV_HEADS + g + 1) * HEAD_DIM]
        new_values.append(block.astype(jnp.bfloat16).astype(jnp.float32))

    score_scale = HEAD_DIM ** (-0.5)
    row = lax.broadcasted_iota(jnp.int32, (HEADS, 1), 0)
    head = ((row % slots) ^ tensor_index) * here + row // slots
    kv_head = head // GROUP
    column = lax.broadcasted_iota(jnp.int32, (1, positions * KV_HEADS), 1)
    place = column // KV_HEADS + inner_index * positions
    column_head = column % KV_HEADS
    lanes = lax.broadcasted_iota(jnp.int32, (HEADS, LANES), 1)
    for r in range(own_rows):
        queries = query_s[pl.ds(r, HEADS, stride=own_rows), :].astype(jnp.bfloat16)
        scores = (
            lax.dot_general(
                queries,
                key_ref[r],
                (((1,), (1,)), ((), ())),
                preferred_element_type=jnp.float32,
            )
            * score_scale
        )
        used = jnp.where(place < meta_ref[2 + r], column_head, -1)
        masked = jnp.where(used == kv_head, scores, -1e30)
        key_rows = 0.0
        value_rows = 0.0
        for g in range(KV_HEADS):
            key_rows = key_rows + jnp.where(kv_head == g, new_keys[g][r : r + 1], 0.0)
            value_rows = value_rows + jnp.where(kv_head == g, new_values[g][r : r + 1], 0.0)
        new_score = (
            jnp.sum(queries.astype(jnp.float32) * key_rows, axis=1, keepdims=True) * score_scale
        )
        new_score = jnp.where(inner_index == 0, new_score, -1e30)
        peak = jnp.maximum(jnp.max(masked, axis=1, keepdims=True), new_score)
        weights = jnp.exp(masked - peak)
        new_weight = jnp.exp(new_score - peak)
        totals = jnp.sum(weights, axis=1, keepdims=True) + new_weight
        mixture = jnp.dot(
            weights.astype(jnp.bfloat16), value_ref[r], preferred_element_type=jnp.float32
        )
        mixture = mixture + new_weight.astype(jnp.bfloat16).astype(jnp.float32) * value_rows
        mixed_s[pl.ds(r, HEADS, stride=own_rows), :] = mixture
        stats_s[pl.ds(r, HEADS, stride=own_rows), :] = spread(
            three_parts(peak), lanes, 0
        ) + spread(three_parts(totals), lanes, 4)
    out_ref[:, :HEAD_DIM] = mixed_s[...].astype(jnp.bfloat16)
    out_ref[:, HEAD_DIM:] = stats_s[...].astype(jnp.bfloat16)


def attend(meta, cosine, sine, near, far, keys, values, slots):
    own_rows = near.shape[0] // slots
    kv_cols = 2 * KV_HEADS * HEAD_DIM // slots
    return pl.pallas_call(
        functools.partial(attend_kernel, slots),
        out_shape=jax.ShapeDtypeStruct((own_rows * HEADS, HEAD_DIM + LANES), jnp.bfloat16),
        in_specs=[in_smem] + [in_vmem] * 6,
        out_specs=in_vmem,
        scratch_shapes=[
            pltpu.VMEM((own_rows * HEADS, HEAD_DIM), jnp.float32),
            pltpu.VMEM((slots, own_rows, kv_cols), jnp.float32),
            pltpu.VMEM((own_rows, slots * kv_cols), jnp.float32),
            pltpu.VMEM((own_rows * HEADS, HEAD_DIM), jnp.float32),
            pltpu.VMEM((own_rows * HEADS, LANES), jnp.float32),
        ],
        compiler_params=params(6),
        name="attend",
    )(meta, cosine, sine, near, far, resident(keys), resident(values))


def combine_kernel(shards, all_rows, *refs):
    ins = refs[:shards]
    out_ref = refs[-1]
    peaks = []
    totals = []
    for ref in ins:
        stats = ref[:, HEAD_DIM:].astype(jnp.float32)
        peaks.append(stats[:, 0:1] + stats[:, 1:2] + stats[:, 2:3])
        totals.append(stats[:, 4:5] + stats[:, 5:6] + stats[:, 6:7])
    top = functools.reduce(jnp.maximum, peaks)
    mixed = 0.0
    denominator = 0.0
    for ref, peak, total in zip(ins, peaks, totals):
        factor = jnp.exp(peak - top)
        mixed = mixed + factor * ref[:, :HEAD_DIM].astype(jnp.float32)
        denominator = denominator + factor * total
    attended = mixed / denominator
    for j in range(attended.shape[0] // all_rows):
        out_ref[:, j * HEAD_DIM : (j + 1) * HEAD_DIM] = attended[
            j * all_rows : (j + 1) * all_rows
        ].astype(jnp.bfloat16)


def combine(parts, later, all_rows):
    count = len(parts)
    columns = parts[0].shape[0] // all_rows * HEAD_DIM
    return pl.pallas_call(
        functools.partial(combine_kernel, count, all_rows),
        out_shape=jax.ShapeDtypeStruct((all_rows, columns), jnp.bfloat16),
        in_specs=[in_vmem] * count + [in_place] * len(later),
        out_specs=in_vmem,
        compiler_params=params(2),
        name="combine",
    )(*parts, *[resident(w) for w in later])


def out_kernel(left_ref, weight_ref, later_ref, *outs):
    del later_ref
    left = left_ref[...]
    rows = outs[0].shape[0]

    def store(start, size, value):
        for k, ref in enumerate(outs):
            ref[:, pl.ds(start, size)] = value[k * rows : (k + 1) * rows].astype(jnp.bfloat16)

    product_tiles(left, weight_ref, store)


def project_out(left, weight, later, slots):
    rows = left.shape[0] // slots
    columns = weight.shape[1]
    return pl.pallas_call(
        out_kernel,
        out_shape=tuple([jax.ShapeDtypeStruct((rows, columns), jnp.bfloat16)] * slots),
        in_specs=[in_vmem, in_vmem, in_place],
        out_specs=tuple([in_vmem] * slots),
        compiler_params=params(2),
        name="project_out",
    )(left, resident(weight), resident(later))


def gate_up_kernel(slots, meta_ref, rows_ref, gain_ref, *refs):
    parts = refs[:slots]
    gate_ref, up_ref, out_ref, updated_ref = refs[slots:]
    own_rows = updated_ref.shape[0]
    total = parts[0][...].astype(jnp.float32)
    for ref in parts[1:]:
        total = total + ref[...].astype(jnp.float32)
    updated = (rows_ref[...].astype(jnp.float32) + total).astype(jnp.bfloat16)
    wide = updated.astype(jnp.float32)
    updated_ref[...] = wide[:own_rows]
    squares = jnp.sum(wide * wide, axis=1, keepdims=True)
    scaled = (wide * gain_ref[...].astype(jnp.float32)).astype(jnp.bfloat16)
    hidden = gate_ref.shape[1]

    def store_gate(start, size, value):
        out_ref[:, pl.ds(start, size)] = value.astype(jnp.bfloat16)

    def store_up(start, size, value):
        place = pl.multiple_of(start + hidden, math.gcd(hidden, size))
        out_ref[:, pl.ds(place, size)] = value.astype(jnp.bfloat16)

    product_tiles(scaled, gate_ref, store_gate)
    product_tiles(scaled, up_ref, store_up)
    out_ref[:, 2 * hidden :] = squares_block(squares, meta_ref[1])


def gate_up(meta, rows, gain, parts, w_gate, w_up, own_rows):
    hidden = w_gate.shape[1]
    slots = len(parts)
    return pl.pallas_call(
        functools.partial(gate_up_kernel, slots),
        out_shape=(
            jax.ShapeDtypeStruct((rows.shape[0], 2 * hidden + LANES), jnp.bfloat16),
            jax.ShapeDtypeStruct((own_rows, rows.shape[1]), jnp.float32),
        ),
        in_specs=[in_smem] + [in_vmem] * (4 + slots),
        out_specs=(in_vmem, in_vmem),
        compiler_params=params(3),
        name="gate_up",
    )(meta, rows, gain, *parts, resident(w_gate), resident(w_up))


def down_kernel(near_ref, far_ref, weight_ref, out_ref, hidden_s):
    hidden = weight_ref.shape[0]
    squares = jnp.sum(
        near_ref[:, 2 * hidden :].astype(jnp.float32) + far_ref[:, 2 * hidden :].astype(jnp.float32),
        axis=1,
        keepdims=True,
    )
    scale = lax.rsqrt(squares / D + epsilon)
    gate = near_ref[:, :hidden].astype(jnp.float32) + far_ref[:, :hidden].astype(jnp.float32)
    up = (
        near_ref[:, hidden : 2 * hidden].astype(jnp.float32)
        + far_ref[:, hidden : 2 * hidden].astype(jnp.float32)
    )
    gate = gate * scale
    hidden_s[...] = (gate / (1.0 + jnp.exp(-gate)) * (up * scale)).astype(jnp.bfloat16)

    def store(start, size, value):
        out_ref[:, pl.ds(start, size)] = value.astype(jnp.bfloat16)

    product_tiles(hidden_s[...], weight_ref, store)


def project_down(near, far, weight):
    rows = near.shape[0]
    return pl.pallas_call(
        down_kernel,
        out_shape=jax.ShapeDtypeStruct((rows, weight.shape[1]), jnp.bfloat16),
        in_specs=[in_vmem] * 3,
        out_specs=in_vmem,
        scratch_shapes=[pltpu.VMEM((rows, weight.shape[0]), jnp.bfloat16)],
        compiler_params=params(3),
        name="project_down",
    )(near, far, resident(weight))


def rotation_tables(positions, repeats):
    inverse = jnp.exp(
        (jnp.arange(HEAD_DIM) // 2).astype(jnp.float32) * (-2.0 / HEAD_DIM) * math.log(rope_base)
    )
    angles = positions[:, None] * inverse[None, :]
    sign = jnp.where(jnp.arange(HEAD_DIM) % 2 == 0, -1.0, 1.0)
    return (
        jnp.tile(jnp.cos(angles), (repeats, 1)),
        jnp.tile(jnp.sin(angles) * sign[None, :], (repeats, 1)),
    )


def local(
    states,
    attn_gain,
    ffn_gain,
    w_query,
    w_kv,
    w_out,
    w_gate,
    w_up,
    w_down,
    key_cache,
    value_cache,
    lengths,
):
    tensor_index = lax.axis_index("tensor")
    slots = lax.axis_size("tensor")
    inner_index = lax.axis_index("inner")
    own_rows = states.shape[0]
    all_rows = own_rows * slots

    rows = jnp.concatenate(exchange(states, "tensor"), axis=0)
    w_query, w_kv = load(w_query, w_kv, after=states)
    my_lengths = lax.dynamic_slice_in_dim(lengths, tensor_index * own_rows, own_rows, 0)
    meta = jnp.concatenate([jnp.stack([tensor_index, inner_index]).astype(jnp.int32), my_lengths])
    cosine, sine = rotation_tables(my_lengths.astype(jnp.float32), slots)

    flat = (own_rows, key_cache.shape[1] * KV_HEADS, HEAD_DIM)
    keys = key_cache.reshape(flat)
    values = value_cache.reshape(flat)
    joined = project_qkv(meta, rows, attn_gain[None, :], w_query, w_kv)
    keys, values = load(keys, values, after=joined)
    pieces = [joined[k * own_rows : (k + 1) * own_rows] for k in range(slots)]
    joined = jnp.concatenate(scatter_slots(pieces, "tensor"), axis=0)
    joined, keys, values = lax.optimization_barrier((joined, keys, values))
    near, far = pair_sums(joined, "inner")
    shard = attend(meta, cosine, sine, near, far, keys, values, slots)
    (w_out,) = load(w_out, after=shard)
    attended = combine(exchange(shard, "inner"), [w_out], all_rows)
    (w_up,) = load(w_up, after=attended)

    pieces = [attended[k * own_rows : (k + 1) * own_rows] for k in range(slots)]
    picked = scatter_slots(pieces, "tensor")
    left = jnp.concatenate([picked[s ^ k] for k in range(slots) for s in range(slots)], axis=0)
    parts = project_out(left, w_out, w_up, slots)
    (w_gate,) = load(w_gate, after=parts[0])
    parts = scatter_slots(parts, "tensor")
    joined, updated = gate_up(meta, rows, ffn_gain[None, :], parts, w_gate, w_up, own_rows)
    (w_down,) = load(w_down, after=joined)

    near, far = pair_sums(joined, "inner")
    part = project_down(near, far, w_down)
    pieces = [part[k * own_rows : (k + 1) * own_rows] for k in range(slots)]
    parts = scatter_slots(pieces, "tensor")
    down_sum = sum(p.astype(jnp.float32) for p in parts)
    return (updated + down_sum).astype(jnp.bfloat16)


def solution(mesh):
    in_specs = (
        P(("groups", "tensor"), "inner"),
        P("inner"),
        P("inner"),
        P("inner", "tensor"),
        P("inner", "tensor"),
        P("tensor", "inner"),
        P("inner", "tensor"),
        P("inner", "tensor"),
        P("tensor", "inner"),
        P(("groups", "tensor"), "inner", None, None),
        P(("groups", "tensor"), "inner", None, None),
        P("groups"),
    )
    out_specs = P(("groups", "tensor"), "inner")
    return jax.shard_map(local, mesh=mesh, in_specs=in_specs, out_specs=out_specs, check_vma=False)
```

```python
import functools
import math

import jax
import jax.numpy as jnp
from jax import lax
from jax.experimental import pallas as pl
from jax.experimental.pallas import tpu as pltpu
from jax.sharding import PartitionSpec as P

D = 8192
HEADS = 32
KV_HEADS = 4
HEAD_DIM = 128
GROUP = HEADS // KV_HEADS
LANES = 128
MIB = 2**20

epsilon = 1e-05
rope_base = 500000.0

in_vmem = pl.BlockSpec(memory_space=pltpu.VMEM)
in_smem = pl.BlockSpec(memory_space=pltpu.SMEM)
in_place = pl.BlockSpec(memory_space=pl.ANY)


def swap_with(value, axis, step):
    count = lax.axis_size(axis)
    return lax.ppermute(value, axis, [(i, i ^ step) for i in range(count)])


def exchange(value, axis):
    count = lax.axis_size(axis)
    got = {k: swap_with(value, axis, k) for k in reversed(range(1, count))}
    return [value] + [got[k] for k in range(1, count)]


def scatter_slots(pieces, axis):
    got = {k: swap_with(pieces[k], axis, k) for k in reversed(range(1, len(pieces)))}
    return [pieces[0]] + [got[k] for k in range(1, len(pieces))]


def pair_sums(value, axis):
    count = lax.axis_size(axis)
    step = 1
    while 2 * step < count:
        other = swap_with(value, axis, step)
        value = (value.astype(jnp.float32) + other.astype(jnp.float32)).astype(value.dtype)
        step *= 2
    return value, swap_with(value, axis, step)


def params(mib):
    return pltpu.CompilerParams(vmem_limit_bytes=mib * MIB)


def resident(weight):
    return pltpu.with_memory_space_constraint(weight, pltpu.VMEM)


def tile_of(columns):
    for tile in (512, 256, 128):
        if columns % tile == 0:
            return tile
    return columns


def product_tiles(left, weight_ref, store):
    columns = weight_ref.shape[1]
    tile = tile_of(columns)

    @pl.loop(0, columns // tile)
    def _(step):
        start = pl.multiple_of(step * tile, tile)
        store(
            start,
            tile,
            jnp.dot(left, weight_ref[:, pl.ds(start, tile)], preferred_element_type=jnp.float32),
        )


def three_parts(value):
    high = value.astype(jnp.bfloat16).astype(jnp.float32)
    rest = value - high
    middle = rest.astype(jnp.bfloat16).astype(jnp.float32)
    return high, middle, rest - middle


def spread(parts, lanes, first):
    out = 0.0
    for n, part in enumerate(parts):
        out = out + jnp.where(lanes == first + n, part, 0.0)
    return out


def squares_block(total, place):
    lanes = lax.broadcasted_iota(jnp.int32, (total.shape[0], LANES), 1)
    return spread(three_parts(total), lanes, place * 4).astype(jnp.bfloat16)


def load_kernel(count, *refs):
    sems = refs[-1]
    outs = refs[-1 - count : -1]
    copies = [pltpu.make_async_copy(refs[n], outs[n], sems.at[n]) for n in range(count)]
    for copy in copies:
        copy.start()
    for copy in copies:
        copy.wait()


def load(*weights, after):
    return pl.pallas_call(
        functools.partial(load_kernel, len(weights)),
        out_shape=tuple(pltpu.VMEM(w.shape, w.dtype) for w in weights),
        in_specs=[in_place] * (len(weights) + 1),
        out_specs=tuple(in_vmem for _ in weights),
        cost_estimate=pl.CostEstimate(
            flops=0, bytes_accessed=2 * sum(w.size for w in weights), transcendentals=0
        ),
        scratch_shapes=[pltpu.SemaphoreType.DMA((len(weights),))],
        compiler_params=params(1),
        name="load",
    )(*[pltpu.with_memory_space_constraint(w, pltpu.HBM) for w in weights], after)


def qkv_kernel(meta_ref, rows_ref, gain_ref, wq_ref, wkv_ref, out_ref):
    wide = rows_ref[...].astype(jnp.float32)
    total = jnp.sum(wide * wide, axis=1, keepdims=True)
    scaled = (wide * gain_ref[...].astype(jnp.float32)).astype(jnp.bfloat16)
    query_cols = wq_ref.shape[1]
    kv_cols = wkv_ref.shape[1]

    def store_query(start, size, value):
        out_ref[:, pl.ds(start, size)] = value.astype(jnp.bfloat16)

    product_tiles(scaled, wq_ref, store_query)
    out_ref[:, query_cols : query_cols + kv_cols] = jnp.dot(
        scaled, wkv_ref[...], preferred_element_type=jnp.float32
    ).astype(jnp.bfloat16)
    out_ref[:, query_cols + kv_cols :] = squares_block(total, meta_ref[1])


def project_qkv(meta, rows, gain, w_query, w_kv):
    columns = w_query.shape[1] + w_kv.shape[1] + LANES
    return pl.pallas_call(
        qkv_kernel,
        out_shape=jax.ShapeDtypeStruct((rows.shape[0], columns), jnp.bfloat16),
        in_specs=[in_smem] + [in_vmem] * 4,
        out_specs=in_vmem,
        compiler_params=params(2),
        name="project_qkv",
    )(meta, rows, gain, resident(w_query), resident(w_kv))


def attend_kernel(
    slots,
    meta_ref,
    cosine_ref,
    sine_ref,
    near_ref,
    far_ref,
    key_ref,
    value_ref,
    out_ref,
    query_s,
    kv_s,
    kv_wide_s,
    mixed_s,
    stats_s,
):
    all_rows = near_ref.shape[0]
    own_rows = all_rows // slots
    here = HEADS // slots
    query_cols = here * HEAD_DIM
    kv_cols = 2 * KV_HEADS * HEAD_DIM // slots
    columns = query_cols + kv_cols
    tensor_index = meta_ref[0]
    inner_index = meta_ref[1]
    positions = key_ref.shape[1] // KV_HEADS

    joined = near_ref[...].astype(jnp.float32) + far_ref[...].astype(jnp.float32)
    squares = jnp.sum(joined[:, columns:], axis=1, keepdims=True)
    joined = joined[:, :columns] * lax.rsqrt(squares / D + epsilon)
    cosine = cosine_ref[...]
    sine = sine_ref[...]

    def rotate(block):
        count = block.shape[0]
        even = lax.broadcasted_iota(jnp.int32, block.shape, 1) % 2 == 0
        other = jnp.where(
            even, pltpu.roll(block, HEAD_DIM - 1, axis=1), pltpu.roll(block, 1, axis=1)
        )
        return block * cosine[:count] + other * sine[:count]

    for j in range(here):
        block = rotate(joined[:, j * HEAD_DIM : (j + 1) * HEAD_DIM])
        query_s[j * all_rows : (j + 1) * all_rows, :] = block
    for s in range(slots):
        kv_s[s] = joined[s * own_rows : (s + 1) * own_rows, query_cols:]
    for d in range(slots):
        kv_wide_s[:, d * kv_cols : (d + 1) * kv_cols] = kv_s[d ^ tensor_index]
    new_keys = []
    new_values = []
    for g in range(KV_HEADS):
        block = kv_wide_s[:, g * HEAD_DIM : (g + 1) * HEAD_DIM]
        new_keys.append(rotate(block).astype(jnp.bfloat16).astype(jnp.float32))
        block = kv_wide_s[:, (KV_HEADS + g) * HEAD_DIM : (KV_HEADS + g + 1) * HEAD_DIM]
        new_values.append(block.astype(jnp.bfloat16).astype(jnp.float32))

    score_scale = HEAD_DIM ** (-0.5)
    row = lax.broadcasted_iota(jnp.int32, (HEADS, 1), 0)
    head = ((row % slots) ^ tensor_index) * here + row // slots
    kv_head = head // GROUP
    column = lax.broadcasted_iota(jnp.int32, (1, positions * KV_HEADS), 1)
    place = column // KV_HEADS + inner_index * positions
    column_head = column % KV_HEADS
    lanes = lax.broadcasted_iota(jnp.int32, (HEADS, LANES), 1)
    for r in range(own_rows):
        queries = query_s[pl.ds(r, HEADS, stride=own_rows), :].astype(jnp.bfloat16)
        scores = (
            lax.dot_general(
                queries,
                key_ref[r],
                (((1,), (1,)), ((), ())),
                preferred_element_type=jnp.float32,
            )
            * score_scale
        )
        used = jnp.where(place < meta_ref[2 + r], column_head, -1)
        masked = jnp.where(used == kv_head, scores, -1e30)
        key_rows = 0.0
        value_rows = 0.0
        for g in range(KV_HEADS):
            key_rows = key_rows + jnp.where(kv_head == g, new_keys[g][r : r + 1], 0.0)
            value_rows = value_rows + jnp.where(kv_head == g, new_values[g][r : r + 1], 0.0)
        new_score = (
            jnp.sum(queries.astype(jnp.float32) * key_rows, axis=1, keepdims=True) * score_scale
        )
        new_score = jnp.where(inner_index == 0, new_score, -1e30)
        peak = jnp.maximum(jnp.max(masked, axis=1, keepdims=True), new_score)
        weights = jnp.exp(masked - peak)
        new_weight = jnp.exp(new_score - peak)
        totals = jnp.sum(weights, axis=1, keepdims=True) + new_weight
        mixture = jnp.dot(
            weights.astype(jnp.bfloat16), value_ref[r], preferred_element_type=jnp.float32
        )
        mixture = mixture + new_weight.astype(jnp.bfloat16).astype(jnp.float32) * value_rows
        mixed_s[pl.ds(r, HEADS, stride=own_rows), :] = mixture
        stats_s[pl.ds(r, HEADS, stride=own_rows), :] = spread(
            three_parts(peak), lanes, 0
        ) + spread(three_parts(totals), lanes, 4)
    out_ref[:, :HEAD_DIM] = mixed_s[...].astype(jnp.bfloat16)
    out_ref[:, HEAD_DIM:] = stats_s[...].astype(jnp.bfloat16)


def attend(meta, cosine, sine, near, far, keys, values, slots):
    own_rows = near.shape[0] // slots
    kv_cols = 2 * KV_HEADS * HEAD_DIM // slots
    return pl.pallas_call(
        functools.partial(attend_kernel, slots),
        out_shape=jax.ShapeDtypeStruct((own_rows * HEADS, HEAD_DIM + LANES), jnp.bfloat16),
        in_specs=[in_smem] + [in_vmem] * 6,
        out_specs=in_vmem,
        scratch_shapes=[
            pltpu.VMEM((own_rows * HEADS, HEAD_DIM), jnp.float32),
            pltpu.VMEM((slots, own_rows, kv_cols), jnp.float32),
            pltpu.VMEM((own_rows, slots * kv_cols), jnp.float32),
            pltpu.VMEM((own_rows * HEADS, HEAD_DIM), jnp.float32),
            pltpu.VMEM((own_rows * HEADS, LANES), jnp.float32),
        ],
        compiler_params=params(6),
        name="attend",
    )(meta, cosine, sine, near, far, resident(keys), resident(values))


def combine_kernel(shards, all_rows, *refs):
    ins = refs[:shards]
    out_ref = refs[-1]
    peaks = []
    totals = []
    for ref in ins:
        stats = ref[:, HEAD_DIM:].astype(jnp.float32)
        peaks.append(stats[:, 0:1] + stats[:, 1:2] + stats[:, 2:3])
        totals.append(stats[:, 4:5] + stats[:, 5:6] + stats[:, 6:7])
    top = functools.reduce(jnp.maximum, peaks)
    mixed = 0.0
    denominator = 0.0
    for ref, peak, total in zip(ins, peaks, totals):
        factor = jnp.exp(peak - top)
        mixed = mixed + factor * ref[:, :HEAD_DIM].astype(jnp.float32)
        denominator = denominator + factor * total
    attended = mixed / denominator
    for j in range(attended.shape[0] // all_rows):
        out_ref[:, j * HEAD_DIM : (j + 1) * HEAD_DIM] = attended[
            j * all_rows : (j + 1) * all_rows
        ].astype(jnp.bfloat16)


def combine(parts, later, all_rows):
    count = len(parts)
    columns = parts[0].shape[0] // all_rows * HEAD_DIM
    return pl.pallas_call(
        functools.partial(combine_kernel, count, all_rows),
        out_shape=jax.ShapeDtypeStruct((all_rows, columns), jnp.bfloat16),
        in_specs=[in_vmem] * count + [in_place] * len(later),
        out_specs=in_vmem,
        compiler_params=params(2),
        name="combine",
    )(*parts, *[resident(w) for w in later])


def out_kernel(slots, weight_ref, later_ref, *refs):
    del later_ref
    picked = refs[:slots]
    outs = refs[slots : 2 * slots]
    left_s = refs[2 * slots]
    rows = outs[0].shape[0]
    own_rows = picked[0].shape[0]
    values = [ref[...].astype(jnp.float32) for ref in picked]
    for k in range(slots):
        for s in range(slots):
            place = (k * slots + s) * own_rows
            left_s[place : place + own_rows, :] = values[s ^ k]
    left = left_s[...].astype(jnp.bfloat16)

    def store(start, size, value):
        for k, ref in enumerate(outs):
            ref[:, pl.ds(start, size)] = value[k * rows : (k + 1) * rows].astype(jnp.bfloat16)

    product_tiles(left, weight_ref, store)


def project_out(picked, weight, later):
    slots = len(picked)
    own_rows, depth = picked[0].shape
    rows = own_rows * slots
    columns = weight.shape[1]
    return pl.pallas_call(
        functools.partial(out_kernel, slots),
        out_shape=tuple([jax.ShapeDtypeStruct((rows, columns), jnp.bfloat16)] * slots),
        in_specs=[in_vmem, in_place] + [in_vmem] * slots,
        out_specs=tuple([in_vmem] * slots),
        scratch_shapes=[pltpu.VMEM((slots * rows, depth), jnp.float32)],
        compiler_params=params(3),
        name="project_out",
    )(resident(weight), resident(later), *picked)


def gate_up_kernel(slots, meta_ref, rows_ref, gain_ref, *refs):
    parts = refs[:slots]
    gate_ref, up_ref, out_ref, updated_ref = refs[slots:]
    own_rows = updated_ref.shape[0]
    total = parts[0][...].astype(jnp.float32)
    for ref in parts[1:]:
        total = total + ref[...].astype(jnp.float32)
    updated = (rows_ref[...].astype(jnp.float32) + total).astype(jnp.bfloat16)
    wide = updated.astype(jnp.float32)
    updated_ref[...] = wide[:own_rows]
    squares = jnp.sum(wide * wide, axis=1, keepdims=True)
    scaled = (wide * gain_ref[...].astype(jnp.float32)).astype(jnp.bfloat16)
    hidden = gate_ref.shape[1]

    def store_gate(start, size, value):
        out_ref[:, pl.ds(start, size)] = value.astype(jnp.bfloat16)

    def store_up(start, size, value):
        place = pl.multiple_of(start + hidden, math.gcd(hidden, size))
        out_ref[:, pl.ds(place, size)] = value.astype(jnp.bfloat16)

    product_tiles(scaled, gate_ref, store_gate)
    product_tiles(scaled, up_ref, store_up)
    out_ref[:, 2 * hidden :] = squares_block(squares, meta_ref[1])


def gate_up(meta, rows, gain, parts, w_gate, w_up, own_rows):
    hidden = w_gate.shape[1]
    slots = len(parts)
    return pl.pallas_call(
        functools.partial(gate_up_kernel, slots),
        out_shape=(
            jax.ShapeDtypeStruct((rows.shape[0], 2 * hidden + LANES), jnp.bfloat16),
            jax.ShapeDtypeStruct((own_rows, rows.shape[1]), jnp.float32),
        ),
        in_specs=[in_smem] + [in_vmem] * (4 + slots),
        out_specs=(in_vmem, in_vmem),
        compiler_params=params(3),
        name="gate_up",
    )(meta, rows, gain, *parts, resident(w_gate), resident(w_up))


def down_kernel(near_ref, far_ref, weight_ref, out_ref, hidden_s):
    hidden = weight_ref.shape[0]
    squares = jnp.sum(
        near_ref[:, 2 * hidden :].astype(jnp.float32) + far_ref[:, 2 * hidden :].astype(jnp.float32),
        axis=1,
        keepdims=True,
    )
    scale = lax.rsqrt(squares / D + epsilon)
    gate = near_ref[:, :hidden].astype(jnp.float32) + far_ref[:, :hidden].astype(jnp.float32)
    up = (
        near_ref[:, hidden : 2 * hidden].astype(jnp.float32)
        + far_ref[:, hidden : 2 * hidden].astype(jnp.float32)
    )
    gate = gate * scale
    hidden_s[...] = (gate / (1.0 + jnp.exp(-gate)) * (up * scale)).astype(jnp.bfloat16)

    def store(start, size, value):
        out_ref[:, pl.ds(start, size)] = value.astype(jnp.bfloat16)

    product_tiles(hidden_s[...], weight_ref, store)


def project_down(near, far, weight):
    rows = near.shape[0]
    return pl.pallas_call(
        down_kernel,
        out_shape=jax.ShapeDtypeStruct((rows, weight.shape[1]), jnp.bfloat16),
        in_specs=[in_vmem] * 3,
        out_specs=in_vmem,
        scratch_shapes=[pltpu.VMEM((rows, weight.shape[0]), jnp.bfloat16)],
        compiler_params=params(3),
        name="project_down",
    )(near, far, resident(weight))


def rotation_tables(positions, repeats):
    inverse = jnp.exp(
        (jnp.arange(HEAD_DIM) // 2).astype(jnp.float32) * (-2.0 / HEAD_DIM) * math.log(rope_base)
    )
    angles = positions[:, None] * inverse[None, :]
    sign = jnp.where(jnp.arange(HEAD_DIM) % 2 == 0, -1.0, 1.0)
    return (
        jnp.tile(jnp.cos(angles), (repeats, 1)),
        jnp.tile(jnp.sin(angles) * sign[None, :], (repeats, 1)),
    )


def local(
    states,
    attn_gain,
    ffn_gain,
    w_query,
    w_kv,
    w_out,
    w_gate,
    w_up,
    w_down,
    key_cache,
    value_cache,
    lengths,
):
    tensor_index = lax.axis_index("tensor")
    slots = lax.axis_size("tensor")
    inner_index = lax.axis_index("inner")
    own_rows = states.shape[0]
    all_rows = own_rows * slots

    rows = jnp.concatenate(exchange(states, "tensor"), axis=0)
    w_query, w_kv = load(w_query, w_kv, after=states)
    my_lengths = lax.dynamic_slice_in_dim(lengths, tensor_index * own_rows, own_rows, 0)
    meta = jnp.concatenate([jnp.stack([tensor_index, inner_index]).astype(jnp.int32), my_lengths])
    cosine, sine = rotation_tables(my_lengths.astype(jnp.float32), slots)

    flat = (own_rows, key_cache.shape[1] * KV_HEADS, HEAD_DIM)
    keys = key_cache.reshape(flat)
    values = value_cache.reshape(flat)
    joined = project_qkv(meta, rows, attn_gain[None, :], w_query, w_kv)
    keys, values = load(keys, values, after=joined)
    pieces = [joined[k * own_rows : (k + 1) * own_rows] for k in range(slots)]
    joined = jnp.concatenate(scatter_slots(pieces, "tensor"), axis=0)
    joined, keys, values = lax.optimization_barrier((joined, keys, values))
    near, far = pair_sums(joined, "inner")
    shard = attend(meta, cosine, sine, near, far, keys, values, slots)
    (w_out,) = load(w_out, after=shard)
    attended = combine(exchange(shard, "inner"), [w_out, w_gate], all_rows)

    pieces = [attended[k * own_rows : (k + 1) * own_rows] for k in range(slots)]
    picked = scatter_slots(pieces, "tensor")
    parts = project_out(picked, w_out, w_up)
    parts = scatter_slots(parts, "tensor")
    joined, updated = gate_up(meta, rows, ffn_gain[None, :], parts, w_gate, w_up, own_rows)
    (w_down,) = load(w_down, after=joined)

    near, far = pair_sums(joined, "inner")
    part = project_down(near, far, w_down)
    pieces = [part[k * own_rows : (k + 1) * own_rows] for k in range(slots)]
    parts = scatter_slots(pieces, "tensor")
    down_sum = sum(p.astype(jnp.float32) for p in parts)
    return (updated + down_sum).astype(jnp.bfloat16)


def solution(mesh):
    in_specs = (
        P(("groups", "tensor"), "inner"),
        P("inner"),
        P("inner"),
        P("inner", "tensor"),
        P("inner", "tensor"),
        P("tensor", "inner"),
        P("inner", "tensor"),
        P("inner", "tensor"),
        P("tensor", "inner"),
        P(("groups", "tensor"), "inner", None, None),
        P(("groups", "tensor"), "inner", None, None),
        P("groups"),
    )
    out_specs = P(("groups", "tensor"), "inner")
    return jax.shard_map(local, mesh=mesh, in_specs=in_specs, out_specs=out_specs, check_vma=False)
```

```python
import functools
import math

import jax
import jax.numpy as jnp
from jax import lax
from jax.experimental import pallas as pl
from jax.experimental.pallas import tpu as pltpu
from jax.sharding import PartitionSpec as P

D = 8192
HEADS = 32
KV_HEADS = 4
HEAD_DIM = 128
GROUP = HEADS // KV_HEADS
LANES = 128
MIB = 2**20
COPIES = 4

epsilon = 1e-05
rope_base = 500000.0

in_vmem = pl.BlockSpec(memory_space=pltpu.VMEM)
in_smem = pl.BlockSpec(memory_space=pltpu.SMEM)
in_place = pl.BlockSpec(memory_space=pl.ANY)


def swap_with(value, axis, step):
    count = lax.axis_size(axis)
    return lax.ppermute(value, axis, [(i, i ^ step) for i in range(count)])


def exchange(value, axis):
    count = lax.axis_size(axis)
    got = {k: swap_with(value, axis, k) for k in reversed(range(1, count))}
    return [value] + [got[k] for k in range(1, count)]


def steps_up(count):
    return [1 << n for n in range(count.bit_length() - 1)]


def gather_rows(value, axis, beside):
    for step in steps_up(lax.axis_size(axis)):
        other = swap_with(value, axis, step)
        value = beside(step, value)
        value = jnp.concatenate([value, other], axis=0)
    return value


def scatter_rows(near, far, axis, beside):
    count = lax.axis_size(axis)
    rows = (near.shape[0] + far.shape[0]) // count
    cut = lambda array, n: array[n * rows : (n + 1) * rows]
    half = count // 2
    held = [[cut(near, n)] for n in range(half)] + [[cut(far, n)] for n in range(half)]
    order = [0]
    step = half
    while step:
        if step == half:
            sent = far
        else:
            sent = jnp.concatenate([p for n in range(step, 2 * step) for p in held[n]], axis=0)
        got = swap_with(sent, axis, step)
        got = beside(step, got)
        each = len(held[0])
        for n in range(step):
            held[n] = held[n] + [cut(got, n * each + m) for m in range(each)]
        held = held[:step]
        order = order + [n ^ step for n in order]
        step //= 2
    return [held[0][order.index(n)] for n in range(count)]


def params(mib):
    return pltpu.CompilerParams(vmem_limit_bytes=mib * MIB)


def resident(weight):
    return pltpu.with_memory_space_constraint(weight, pltpu.VMEM)


def tile_of(columns):
    for tile in (1792, 1024, 896, 512, 256, 128):
        if columns % tile == 0:
            return tile
    return columns


def product_tiles(left, weight_ref, store):
    columns = weight_ref.shape[1]
    tile = tile_of(columns)

    @pl.loop(0, columns // tile)
    def _(step):
        start = pl.multiple_of(step * tile, tile)
        store(
            start,
            tile,
            jnp.dot(left, weight_ref[:, pl.ds(start, tile)], preferred_element_type=jnp.float32),
        )


def three_parts(value):
    high = value.astype(jnp.bfloat16).astype(jnp.float32)
    rest = value - high
    middle = rest.astype(jnp.bfloat16).astype(jnp.float32)
    return high, middle, rest - middle


def spread(parts, lanes, first):
    out = 0.0
    for n, part in enumerate(parts):
        out = out + jnp.where(lanes == first + n, part, 0.0)
    return out


def squares_block(total):
    lanes = lax.broadcasted_iota(jnp.int32, (total.shape[0], LANES), 1)
    return spread(three_parts(total), lanes, lax.axis_index("inner") * 4)


def load_kernel(spans, *refs):
    count = len(spans)
    outs = refs[count + 1 : 2 * count + 1]
    sems = refs[-1]
    copies = []
    for n, (start, size) in enumerate(spans):
        cuts = COPIES if len(refs[n].shape) > 1 and size % (16 * COPIES) == 0 else 1
        each = size // cuts
        for m in range(cuts):
            copies.append(
                pltpu.make_async_copy(
                    refs[n].at[pl.ds(start + m * each, each)],
                    outs[n].at[pl.ds(m * each, each)],
                    sems.at[n, m],
                )
            )
    for copy in copies:
        copy.start()
    for copy in copies:
        copy.wait()


def load(*arrays, after, spans=None):
    spans = spans or [(0, a.shape[0]) for a in arrays]
    shapes = [(size,) + a.shape[1:] for a, (_, size) in zip(arrays, spans)]
    return pl.pallas_call(
        functools.partial(load_kernel, spans),
        out_shape=tuple(pltpu.VMEM(shape, a.dtype) for shape, a in zip(shapes, arrays)),
        in_specs=[in_place] * (len(arrays) + 1),
        out_specs=tuple(in_vmem for _ in arrays),
        cost_estimate=pl.CostEstimate(
            flops=0, bytes_accessed=2 * sum(math.prod(shape) for shape in shapes), transcendentals=0
        ),
        scratch_shapes=[pltpu.SemaphoreType.DMA((len(arrays), COPIES))],
        compiler_params=params(1),
        name="load",
    )(*[pltpu.with_memory_space_constraint(a, pltpu.HBM) for a in arrays], after)


def qkv_kernel(rows_ref, gain_ref, wq_ref, wkv_ref, near_ref, far_ref, out_s):
    wide = rows_ref[...].astype(jnp.float32)
    total = jnp.sum(wide * wide, axis=1, keepdims=True)
    gain = gain_ref[...].astype(jnp.float32)[None, :]
    scaled = (wide * gain).astype(jnp.bfloat16)
    query_cols = wq_ref.shape[1]
    kv_cols = wkv_ref.shape[1]

    def store_query(start, size, value):
        out_s[:, pl.ds(start, size)] = value

    product_tiles(scaled, wq_ref, store_query)
    out_s[:, query_cols : query_cols + kv_cols] = jnp.dot(
        scaled, wkv_ref[...], preferred_element_type=jnp.float32
    )
    out_s[:, query_cols + kv_cols :] = squares_block(total)
    half = near_ref.shape[0]
    near_ref[...] = out_s[:half, :].astype(jnp.bfloat16)
    far_ref[...] = out_s[half:, :].astype(jnp.bfloat16)


def project_qkv(rows, gain, w_query, w_kv):
    count = rows.shape[0]
    columns = w_query.shape[1] + w_kv.shape[1] + LANES
    return pl.pallas_call(
        qkv_kernel,
        out_shape=(jax.ShapeDtypeStruct((count // 2, columns), jnp.bfloat16),) * 2,
        in_specs=[in_vmem] * 4,
        out_specs=(in_vmem,) * 2,
        scratch_shapes=[pltpu.VMEM((count, columns), jnp.float32)],
        compiler_params=params(2),
        name="project_qkv",
    )(rows, gain, resident(w_query), resident(w_kv))


def attend_kernel(
    slots,
    shards,
    lengths_ref,
    cosine_ref,
    sine_ref,
    key_ref,
    value_ref,
    *refs,
):
    parts = refs[:shards]
    out_ref, query_s, kv_s, kv_wide_s, mixed_s, stats_s = refs[shards:]
    all_rows = parts[0].shape[0]
    own_rows = all_rows // slots
    here = HEADS // slots
    query_cols = here * HEAD_DIM
    kv_cols = 2 * KV_HEADS * HEAD_DIM // slots
    columns = query_cols + kv_cols
    tensor_index = lax.axis_index("tensor")
    inner_index = lax.axis_index("inner")
    positions = key_ref.shape[1] // KV_HEADS

    joined = functools.reduce(jnp.add, [ref[...].astype(jnp.float32) for ref in parts])
    squares = jnp.sum(joined[:, columns:], axis=1, keepdims=True)
    joined = joined[:, :columns] * lax.rsqrt(squares / D + epsilon)
    cosine = cosine_ref[...]
    sine = sine_ref[...]

    def rotate(block):
        count = block.shape[0]
        even = lax.broadcasted_iota(jnp.int32, block.shape, 1) % 2 == 0
        other = jnp.where(
            even, pltpu.roll(block, HEAD_DIM - 1, axis=1), pltpu.roll(block, 1, axis=1)
        )
        return block * cosine[:count] + other * sine[:count]

    for j in range(here):
        block = rotate(joined[:, j * HEAD_DIM : (j + 1) * HEAD_DIM])
        query_s[j * all_rows : (j + 1) * all_rows, :] = block
    for s in range(slots):
        kv_s[s] = joined[s * own_rows : (s + 1) * own_rows, query_cols:]
    for d in range(slots):
        kv_wide_s[:, d * kv_cols : (d + 1) * kv_cols] = kv_s[d ^ tensor_index]
    new_keys = []
    new_values = []
    for g in range(KV_HEADS):
        block = kv_wide_s[:, g * HEAD_DIM : (g + 1) * HEAD_DIM]
        new_keys.append(rotate(block).astype(jnp.bfloat16).astype(jnp.float32))
        block = kv_wide_s[:, (KV_HEADS + g) * HEAD_DIM : (KV_HEADS + g + 1) * HEAD_DIM]
        new_values.append(block.astype(jnp.bfloat16).astype(jnp.float32))

    score_scale = HEAD_DIM ** (-0.5)
    row = lax.broadcasted_iota(jnp.int32, (HEADS, 1), 0)
    head = ((row % slots) ^ tensor_index) * here + row // slots
    kv_head = head // GROUP
    column = lax.broadcasted_iota(jnp.int32, (1, positions * KV_HEADS), 1)
    place = column // KV_HEADS + inner_index * positions
    column_head = column % KV_HEADS
    lanes = lax.broadcasted_iota(jnp.int32, (HEADS, LANES), 1)
    for r in range(own_rows):
        queries = query_s[pl.ds(r, HEADS, stride=own_rows), :].astype(jnp.bfloat16)
        scores = (
            lax.dot_general(
                queries,
                key_ref[r],
                (((1,), (1,)), ((), ())),
                preferred_element_type=jnp.float32,
            )
            * score_scale
        )
        used = jnp.where(place < lengths_ref[r : r + 1, 0:1], column_head, -1)
        masked = jnp.where(used == kv_head, scores, -1e30)
        key_rows = 0.0
        value_rows = 0.0
        for g in range(KV_HEADS):
            key_rows = key_rows + jnp.where(kv_head == g, new_keys[g][r : r + 1], 0.0)
            value_rows = value_rows + jnp.where(kv_head == g, new_values[g][r : r + 1], 0.0)
        new_score = (
            jnp.sum(queries.astype(jnp.float32) * key_rows, axis=1, keepdims=True) * score_scale
        )
        new_score = jnp.where(inner_index == 0, new_score, -1e30)
        peak = jnp.maximum(jnp.max(masked, axis=1, keepdims=True), new_score)
        weights = jnp.exp(masked - peak)
        new_weight = jnp.exp(new_score - peak)
        totals = jnp.sum(weights, axis=1, keepdims=True) + new_weight
        mixture = jnp.dot(
            weights.astype(jnp.bfloat16), value_ref[r], preferred_element_type=jnp.float32
        )
        mixture = mixture + new_weight.astype(jnp.bfloat16).astype(jnp.float32) * value_rows
        mixed_s[pl.ds(r, HEADS, stride=own_rows), :] = mixture
        stats_s[pl.ds(r, HEADS, stride=own_rows), :] = spread(
            three_parts(peak), lanes, 0
        ) + spread(three_parts(totals), lanes, 4)
    out_ref[:, :HEAD_DIM] = mixed_s[...].astype(jnp.bfloat16)
    out_ref[:, HEAD_DIM:] = stats_s[...].astype(jnp.bfloat16)


def attend(lengths, cosine, sine, parts, keys, values, slots):
    own_rows = parts[0].shape[0] // slots
    kv_cols = 2 * KV_HEADS * HEAD_DIM // slots
    return pl.pallas_call(
        functools.partial(attend_kernel, slots, len(parts)),
        out_shape=jax.ShapeDtypeStruct((own_rows * HEADS, HEAD_DIM + LANES), jnp.bfloat16),
        in_specs=[in_vmem] * (5 + len(parts)),
        out_specs=in_vmem,
        scratch_shapes=[
            pltpu.VMEM((own_rows * HEADS, HEAD_DIM), jnp.float32),
            pltpu.VMEM((slots, own_rows, kv_cols), jnp.float32),
            pltpu.VMEM((own_rows, slots * kv_cols), jnp.float32),
            pltpu.VMEM((own_rows * HEADS, HEAD_DIM), jnp.float32),
            pltpu.VMEM((own_rows * HEADS, LANES), jnp.float32),
        ],
        compiler_params=params(6),
        name="attend",
    )(lengths, cosine, sine, resident(keys), resident(values), *parts)


def combine_kernel(shards, all_rows, *refs):
    ins = refs[:shards]
    near_ref, far_ref = refs[-2:]
    half = all_rows // 2
    peaks = []
    totals = []
    for ref in ins:
        stats = ref[:, HEAD_DIM:].astype(jnp.float32)
        peaks.append(stats[:, 0:1] + stats[:, 1:2] + stats[:, 2:3])
        totals.append(stats[:, 4:5] + stats[:, 5:6] + stats[:, 6:7])
    top = functools.reduce(jnp.maximum, peaks)
    mixed = 0.0
    denominator = 0.0
    for ref, peak, total in zip(ins, peaks, totals):
        factor = jnp.exp(peak - top)
        mixed = mixed + factor * ref[:, :HEAD_DIM].astype(jnp.float32)
        denominator = denominator + factor * total
    attended = mixed / denominator
    for j in range(attended.shape[0] // all_rows):
        block = attended[j * all_rows : (j + 1) * all_rows]
        near_ref[:, j * HEAD_DIM : (j + 1) * HEAD_DIM] = block[:half].astype(jnp.bfloat16)
        far_ref[:, j * HEAD_DIM : (j + 1) * HEAD_DIM] = block[half:].astype(jnp.bfloat16)


def combine(parts, later, all_rows):
    count = len(parts)
    columns = parts[0].shape[0] // all_rows * HEAD_DIM
    return pl.pallas_call(
        functools.partial(combine_kernel, count, all_rows),
        out_shape=(jax.ShapeDtypeStruct((all_rows // 2, columns), jnp.bfloat16),) * 2,
        in_specs=[in_vmem] * count + [in_place] * len(later),
        out_specs=(in_vmem,) * 2,
        compiler_params=params(2),
        name="combine",
    )(*parts, *[resident(w) for w in later])


def turned(block, step, own_rows):
    count = block.shape[0]
    span = step * own_rows
    row = lax.broadcasted_iota(jnp.int32, (count, 1), 0)
    return jnp.where(
        (row // span) % 2 == 0,
        pltpu.roll(block, count - span, axis=0),
        pltpu.roll(block, span, axis=0),
    )


def out_kernel(own_rows, left_ref, weight_ref, later_ref, part_ref, sent_ref):
    del later_ref
    rows = left_ref.shape[0]
    left = left_ref[...].astype(jnp.float32)
    left = jnp.concatenate([left, turned(left, 1, own_rows)], axis=0).astype(jnp.bfloat16)

    def store(start, size, value):
        part_ref[:, pl.ds(start, size)] = value[:rows].astype(jnp.bfloat16)
        sent_ref[:, pl.ds(start, size)] = value[rows:].astype(jnp.bfloat16)

    product_tiles(left, weight_ref, store)


def project_out(left, weight, later, own_rows):
    shape = jax.ShapeDtypeStruct((left.shape[0], weight.shape[1]), jnp.bfloat16)
    return pl.pallas_call(
        functools.partial(out_kernel, own_rows),
        out_shape=(shape, shape),
        in_specs=[in_vmem, in_vmem, in_place],
        out_specs=(in_vmem, in_vmem),
        compiler_params=params(3),
        name="project_out",
    )(left, resident(weight), resident(later))


def pair_kernel(step, own_rows, first_ref, second_ref, *refs):
    total = first_ref[...].astype(jnp.float32) + second_ref[...].astype(jnp.float32)
    if step is None:
        refs[-1][...] = total.astype(jnp.bfloat16)
    else:
        refs[-2][...] = total.astype(jnp.bfloat16)
        refs[-1][...] = turned(total, step, own_rows).astype(jnp.bfloat16)


def pair_sum(first, second, step=None, own_rows=None, later=()):
    shape = jax.ShapeDtypeStruct(first.shape, first.dtype)
    return pl.pallas_call(
        functools.partial(pair_kernel, step, own_rows),
        out_shape=shape if step is None else (shape, shape),
        in_specs=[in_vmem] * 2 + [in_place] * len(later),
        out_specs=in_vmem if step is None else (in_vmem, in_vmem),
        compiler_params=params(2),
        name="pair_sum",
    )(first, second, *[resident(w) for w in later])


def gate_up_kernel(
    rows_ref, gain_ref, first_ref, second_ref, gate_ref, up_ref, out_ref, updated_ref
):
    own_rows = updated_ref.shape[0]
    total = first_ref[...].astype(jnp.float32) + second_ref[...].astype(jnp.float32)
    updated = (rows_ref[...].astype(jnp.float32) + total).astype(jnp.bfloat16)
    wide = updated.astype(jnp.float32)
    updated_ref[...] = wide[:own_rows]
    squares = jnp.sum(wide * wide, axis=1, keepdims=True)
    scaled = (wide * gain_ref[...].astype(jnp.float32)[None, :]).astype(jnp.bfloat16)
    hidden = gate_ref.shape[1]

    def store_gate(start, size, value):
        out_ref[:, pl.ds(start, size)] = value.astype(jnp.bfloat16)

    def store_up(start, size, value):
        place = pl.multiple_of(start + hidden, math.gcd(hidden, size))
        out_ref[:, pl.ds(place, size)] = value.astype(jnp.bfloat16)

    product_tiles(scaled, gate_ref, store_gate)
    product_tiles(scaled, up_ref, store_up)
    out_ref[:, 2 * hidden :] = squares_block(squares).astype(jnp.bfloat16)


def gate_up(rows, gain, first, second, w_gate, w_up, own_rows):
    hidden = w_gate.shape[1]
    return pl.pallas_call(
        gate_up_kernel,
        out_shape=(
            jax.ShapeDtypeStruct((rows.shape[0], 2 * hidden + LANES), jnp.bfloat16),
            jax.ShapeDtypeStruct((own_rows, rows.shape[1]), jnp.float32),
        ),
        in_specs=[in_vmem] * 6,
        out_specs=(in_vmem, in_vmem),
        compiler_params=params(3),
        name="gate_up",
    )(rows, gain, first, second, resident(w_gate), resident(w_up))


def down_kernel(near_ref, far_ref, upper_ref, lower_ref, low_ref, high_ref, hidden_s, out_s):
    hidden = hidden_s.shape[1]
    cut = upper_ref.shape[0]
    squares = jnp.sum(
        near_ref[:, 2 * hidden :].astype(jnp.float32) + far_ref[:, 2 * hidden :].astype(jnp.float32),
        axis=1,
        keepdims=True,
    )
    scale = lax.rsqrt(squares / D + epsilon)
    gate = near_ref[:, :hidden].astype(jnp.float32) + far_ref[:, :hidden].astype(jnp.float32)
    up = (
        near_ref[:, hidden : 2 * hidden].astype(jnp.float32)
        + far_ref[:, hidden : 2 * hidden].astype(jnp.float32)
    )
    gate = gate * scale
    hidden_s[...] = (gate / (1.0 + jnp.exp(-gate)) * (up * scale)).astype(jnp.bfloat16)
    columns = upper_ref.shape[1]
    tile = tile_of(columns)

    @pl.loop(0, columns // tile)
    def _(step):
        span = pl.ds(pl.multiple_of(step * tile, tile), tile)
        out_s[:, span] = jnp.dot(
            hidden_s[:, :cut], upper_ref[:, span], preferred_element_type=jnp.float32
        ) + jnp.dot(hidden_s[:, cut:], lower_ref[:, span], preferred_element_type=jnp.float32)

    half = low_ref.shape[0]
    low_ref[...] = out_s[:half, :].astype(jnp.bfloat16)
    high_ref[...] = out_s[half:, :].astype(jnp.bfloat16)


def project_down(near, far, upper, lower):
    rows = near.shape[0]
    columns = upper.shape[1]
    return pl.pallas_call(
        down_kernel,
        out_shape=(jax.ShapeDtypeStruct((rows // 2, columns), jnp.bfloat16),) * 2,
        in_specs=[in_vmem] * 4,
        out_specs=(in_vmem,) * 2,
        scratch_shapes=[
            pltpu.VMEM((rows, upper.shape[0] + lower.shape[0]), jnp.bfloat16),
            pltpu.VMEM((rows, columns), jnp.float32),
        ],
        compiler_params=params(3),
        name="project_down",
    )(near, far, resident(upper), resident(lower))


def rotation_tables(positions, repeats):
    inverse = jnp.exp(
        (jnp.arange(HEAD_DIM) // 2).astype(jnp.float32) * (-2.0 / HEAD_DIM) * math.log(rope_base)
    )
    angles = positions[:, None] * inverse[None, :]
    sign = jnp.where(jnp.arange(HEAD_DIM) % 2 == 0, -1.0, 1.0)
    return (
        jnp.tile(jnp.cos(angles), (repeats, 1)),
        jnp.tile(jnp.sin(angles) * sign[None, :], (repeats, 1)),
    )


def local(
    states,
    attn_gain,
    ffn_gain,
    w_query,
    w_kv,
    w_out,
    w_gate,
    w_up,
    w_down,
    key_cache,
    value_cache,
    lengths,
):
    tensor_index = lax.axis_index("tensor")
    slots = lax.axis_size("tensor")
    own_rows = states.shape[0]
    all_rows = own_rows * slots

    loaded = {}

    def during_gather(step, value):
        if step == 1:
            value, loaded["attn_gain"], loaded["ffn_gain"], loaded["w_kv"] = load(
                value, attn_gain, ffn_gain, w_kv, after=value
            )
        if step == slots // 2:
            (loaded["w_query"],) = load(w_query, after=value)
        return value

    rows = gather_rows(states, "tensor", during_gather)
    near, far = project_qkv(rows, loaded["attn_gain"], loaded["w_query"], loaded["w_kv"])
    near, lengths = lax.optimization_barrier((near, lengths))
    my_lengths = lax.dynamic_slice_in_dim(lengths, tensor_index * own_rows, own_rows, 0)
    cosine, sine = rotation_tables(my_lengths.astype(jnp.float32), slots)
    my_lengths = jnp.broadcast_to(my_lengths[:, None], (own_rows, LANES))
    flat = (own_rows, key_cache.shape[1] * KV_HEADS, HEAD_DIM)

    def during_scatter(step, got):
        if step == slots // 2:
            (keys,) = load(key_cache.reshape(flat), after=near)
            got, loaded["keys"] = lax.optimization_barrier((got, keys))
        if step == 1:
            (values,) = load(value_cache.reshape(flat), after=loaded["keys"])
            got, loaded["values"] = lax.optimization_barrier((got, values))
        return got

    joined = jnp.concatenate(scatter_rows(near, far, "tensor", during_scatter), axis=0)
    shard = attend(
        my_lengths,
        cosine,
        sine,
        exchange(joined, "inner"),
        loaded["keys"],
        loaded["values"],
        slots,
    )
    (w_out,) = load(w_out, after=shard)
    near, far = combine(exchange(shard, "inner"), [w_out, w_gate], all_rows)

    alone = lambda step, value: value
    picked = jnp.concatenate(scatter_rows(near, far, "tensor", alone), axis=0)
    part, sent = project_out(picked, w_out, w_up, own_rows)
    steps = steps_up(slots)
    for step, following in zip(steps, steps[1:] + [None]):
        other = swap_with(sent, "tensor", step)
        if following:
            part, sent = pair_sum(part, other, following, own_rows)
    joined, updated = gate_up(rows, loaded["ffn_gain"], part, other, w_gate, w_up, own_rows)

    steps = steps_up(lax.axis_size("inner"))
    cut = w_down.shape[0] // 64 * 16
    (upper,) = load(w_down, after=joined, spans=[(0, cut)])
    for step in steps[:-1]:
        joined = pair_sum(joined, swap_with(joined, "inner", step), later=[upper])
    (lower,) = load(w_down, after=joined, spans=[(cut, w_down.shape[0] - cut)])
    other = swap_with(joined, "inner", steps[-1])
    near, far = project_down(joined, other, upper, lower)
    parts = scatter_rows(near, far, "tensor", alone)
    down_sum = sum(p.astype(jnp.float32) for p in parts)
    return (updated + down_sum).astype(jnp.bfloat16)


def solution(mesh):
    in_specs = (
        P(("groups", "tensor"), "inner"),
        P("inner"),
        P("inner"),
        P("inner", "tensor"),
        P("inner", "tensor"),
        P("tensor", "inner"),
        P("inner", "tensor"),
        P("inner", "tensor"),
        P("tensor", "inner"),
        P(("groups", "tensor"), "inner", None, None),
        P(("groups", "tensor"), "inner", None, None),
        P("groups"),
    )
    out_specs = P(("groups", "tensor"), "inner")
    return jax.shard_map(local, mesh=mesh, in_specs=in_specs, out_specs=out_specs, check_vma=False)
```

```python
import functools
import math

import jax
import jax.numpy as jnp
from jax import lax
from jax.experimental import pallas as pl
from jax.experimental.pallas import tpu as pltpu
from jax.sharding import PartitionSpec as P

D = 8192
HEADS = 32
KV_HEADS = 4
HEAD_DIM = 128
GROUP = HEADS // KV_HEADS
LANES = 128
MIB = 2**20
COPIES = 4

epsilon = 1e-05
rope_base = 500000.0

in_vmem = pl.BlockSpec(memory_space=pltpu.VMEM)
in_smem = pl.BlockSpec(memory_space=pltpu.SMEM)
in_place = pl.BlockSpec(memory_space=pl.ANY)


def swap_with(value, axis, step):
    count = lax.axis_size(axis)
    return lax.ppermute(value, axis, [(i, i ^ step) for i in range(count)])


def exchange(value, axis):
    count = lax.axis_size(axis)
    got = {k: swap_with(value, axis, k) for k in reversed(range(1, count))}
    return [value] + [got[k] for k in range(1, count)]


def scatter_slots(pieces, cross):
    count = lax.axis_size("tensor")
    width = lax.axis_size("inner")
    got = [pieces[0]]
    for k in range(1, count):
        pairs = [
            (t * width + i, (t ^ k) * width + (i ^ cross))
            for t in range(count)
            for i in range(width)
        ]
        got.append(lax.ppermute(pieces[k], ("tensor", "inner"), pairs))
    return got


def steps_up(count):
    return [1 << n for n in range(count.bit_length() - 1)]


def params(mib):
    return pltpu.CompilerParams(vmem_limit_bytes=mib * MIB)


def resident(weight):
    return pltpu.with_memory_space_constraint(weight, pltpu.VMEM)


def in_hbm(weight):
    return pltpu.with_memory_space_constraint(weight, pltpu.HBM)


def tile_of(columns):
    for tile in (1792, 1024, 896, 512, 256, 128):
        if columns % tile == 0:
            return tile
    return columns


def product_tiles(left, weight_ref, store):
    columns = weight_ref.shape[1]
    tile = tile_of(columns)

    @pl.loop(0, columns // tile)
    def _(step):
        start = pl.multiple_of(step * tile, tile)
        store(
            start,
            tile,
            jnp.dot(left, weight_ref[:, pl.ds(start, tile)], preferred_element_type=jnp.float32),
        )


def three_parts(value):
    high = value.astype(jnp.bfloat16).astype(jnp.float32)
    rest = value - high
    middle = rest.astype(jnp.bfloat16).astype(jnp.float32)
    return high, middle, rest - middle


def spread(parts, lanes, first):
    out = 0.0
    for n, part in enumerate(parts):
        out = out + jnp.where(lanes == first + n, part, 0.0)
    return out


def squares_block(total):
    lanes = lax.broadcasted_iota(jnp.int32, (total.shape[0], LANES), 1)
    return spread(three_parts(total), lanes, lax.axis_index("inner") * 4)


def copies_of(source, start, target, sems):
    size = target.shape[0]
    cuts = COPIES if len(target.shape) > 1 and size % (16 * COPIES) == 0 else 1
    each = size // cuts
    return [
        pltpu.make_async_copy(
            source.at[pl.ds(start + m * each, each)], target.at[pl.ds(m * each, each)], sems.at[m]
        )
        for m in range(cuts)
    ]


def load_kernel(spans, *refs):
    count = len(spans)
    outs = refs[count + 1 : 2 * count + 1]
    sems = refs[-1]
    copies = []
    for n, (start, _) in enumerate(spans):
        copies += copies_of(refs[n], start, outs[n], sems.at[n])
    for copy in copies:
        copy.start()
    for copy in copies:
        copy.wait()


def load(*arrays, after, spans=None):
    spans = spans or [(0, a.shape[0]) for a in arrays]
    shapes = [(size,) + a.shape[1:] for a, (_, size) in zip(arrays, spans)]
    return pl.pallas_call(
        functools.partial(load_kernel, spans),
        out_shape=tuple(pltpu.VMEM(shape, a.dtype) for shape, a in zip(shapes, arrays)),
        in_specs=[in_place] * (len(arrays) + 1),
        out_specs=tuple(in_vmem for _ in arrays),
        cost_estimate=pl.CostEstimate(
            flops=0, bytes_accessed=2 * sum(math.prod(shape) for shape in shapes), transcendentals=0
        ),
        scratch_shapes=[pltpu.SemaphoreType.DMA((len(arrays), COPIES))],
        compiler_params=params(1),
        name="load",
    )(*[in_hbm(a) for a in arrays], after)


def qkv_kernel(rows_ref, gain_ref, wq_ref, wkv_ref, out_ref):
    wide = rows_ref[...].astype(jnp.float32)
    total = jnp.sum(wide * wide, axis=1, keepdims=True)
    gain = gain_ref[...].astype(jnp.float32)[None, :]
    scaled = (wide * gain).astype(jnp.bfloat16)
    query_cols = wq_ref.shape[1]
    kv_cols = wkv_ref.shape[1]

    def store_query(start, size, value):
        out_ref[:, pl.ds(start, size)] = value.astype(jnp.bfloat16)

    product_tiles(scaled, wq_ref, store_query)
    out_ref[:, query_cols : query_cols + kv_cols] = jnp.dot(
        scaled, wkv_ref[...], preferred_element_type=jnp.float32
    ).astype(jnp.bfloat16)
    out_ref[:, query_cols + kv_cols :] = squares_block(total).astype(jnp.bfloat16)


def project_qkv(rows, gain, w_query, w_kv):
    count = rows.shape[0]
    columns = w_query.shape[1] + w_kv.shape[1] + LANES
    return pl.pallas_call(
        qkv_kernel,
        out_shape=jax.ShapeDtypeStruct((count, columns), jnp.bfloat16),
        in_specs=[in_vmem] * 4,
        out_specs=in_vmem,
        compiler_params=params(2),
        name="project_qkv",
    )(rows, gain, resident(w_query), resident(w_kv))


def attend_kernel(
    slots,
    shards,
    lengths_ref,
    cosine_ref,
    sine_ref,
    key_ref,
    value_ref,
    later_ref,
    *refs,
):
    parts = refs[:shards]
    out_ref, loaded_ref, query_s, kv_s, kv_wide_s, mixed_s, stats_s, sems = refs[shards:]
    copies = copies_of(later_ref, 0, loaded_ref, sems)
    for copy in copies:
        copy.start()
    all_rows = parts[0].shape[0]
    own_rows = all_rows // slots
    here = HEADS // slots
    query_cols = here * HEAD_DIM
    kv_cols = 2 * KV_HEADS * HEAD_DIM // slots
    columns = query_cols + kv_cols
    tensor_index = lax.axis_index("tensor")
    inner_index = lax.axis_index("inner")
    positions = key_ref.shape[1] // KV_HEADS

    joined = functools.reduce(jnp.add, [ref[...].astype(jnp.float32) for ref in parts])
    squares = jnp.sum(joined[:, columns:], axis=1, keepdims=True)
    joined = joined[:, :columns] * lax.rsqrt(squares / D + epsilon)
    cosine = cosine_ref[...]
    sine = sine_ref[...]

    def rotate(block):
        count = block.shape[0]
        even = lax.broadcasted_iota(jnp.int32, block.shape, 1) % 2 == 0
        other = jnp.where(
            even, pltpu.roll(block, HEAD_DIM - 1, axis=1), pltpu.roll(block, 1, axis=1)
        )
        return block * cosine[:count] + other * sine[:count]

    for j in range(here):
        block = rotate(joined[:, j * HEAD_DIM : (j + 1) * HEAD_DIM])
        query_s[j * all_rows : (j + 1) * all_rows, :] = block
    for s in range(slots):
        kv_s[s] = joined[s * own_rows : (s + 1) * own_rows, query_cols:]
    for d in range(slots):
        kv_wide_s[:, d * kv_cols : (d + 1) * kv_cols] = kv_s[d ^ tensor_index]
    new_keys = []
    new_values = []
    for g in range(KV_HEADS):
        block = kv_wide_s[:, g * HEAD_DIM : (g + 1) * HEAD_DIM]
        new_keys.append(rotate(block).astype(jnp.bfloat16).astype(jnp.float32))
        block = kv_wide_s[:, (KV_HEADS + g) * HEAD_DIM : (KV_HEADS + g + 1) * HEAD_DIM]
        new_values.append(block.astype(jnp.bfloat16).astype(jnp.float32))

    score_scale = HEAD_DIM ** (-0.5)
    row = lax.broadcasted_iota(jnp.int32, (HEADS, 1), 0)
    head = ((row % slots) ^ tensor_index) * here + row // slots
    kv_head = head // GROUP
    column = lax.broadcasted_iota(jnp.int32, (1, positions * KV_HEADS), 1)
    place = column // KV_HEADS + inner_index * positions
    column_head = column % KV_HEADS
    lanes = lax.broadcasted_iota(jnp.int32, (HEADS, LANES), 1)
    for r in range(own_rows):
        queries = query_s[pl.ds(r, HEADS, stride=own_rows), :].astype(jnp.bfloat16)
        scores = (
            lax.dot_general(
                queries,
                key_ref[r],
                (((1,), (1,)), ((), ())),
                preferred_element_type=jnp.float32,
            )
            * score_scale
        )
        used = jnp.where(place < lengths_ref[r : r + 1, 0:1], column_head, -1)
        masked = jnp.where(used == kv_head, scores, -1e30)
        key_rows = 0.0
        value_rows = 0.0
        for g in range(KV_HEADS):
            key_rows = key_rows + jnp.where(kv_head == g, new_keys[g][r : r + 1], 0.0)
            value_rows = value_rows + jnp.where(kv_head == g, new_values[g][r : r + 1], 0.0)
        new_score = (
            jnp.sum(queries.astype(jnp.float32) * key_rows, axis=1, keepdims=True) * score_scale
        )
        new_score = jnp.where(inner_index == 0, new_score, -1e30)
        peak = jnp.maximum(jnp.max(masked, axis=1, keepdims=True), new_score)
        weights = jnp.exp(masked - peak)
        new_weight = jnp.exp(new_score - peak)
        totals = jnp.sum(weights, axis=1, keepdims=True) + new_weight
        mixture = jnp.dot(
            weights.astype(jnp.bfloat16), value_ref[r], preferred_element_type=jnp.float32
        )
        mixture = mixture + new_weight.astype(jnp.bfloat16).astype(jnp.float32) * value_rows
        mixed_s[pl.ds(r, HEADS, stride=own_rows), :] = mixture
        stats_s[pl.ds(r, HEADS, stride=own_rows), :] = spread(
            three_parts(peak), lanes, 0
        ) + spread(three_parts(totals), lanes, 4)
    out_ref[:, :HEAD_DIM] = mixed_s[...].astype(jnp.bfloat16)
    out_ref[:, HEAD_DIM:] = stats_s[...].astype(jnp.bfloat16)
    for copy in copies:
        copy.wait()


def attend(lengths, cosine, sine, parts, keys, values, later, slots):
    own_rows = parts[0].shape[0] // slots
    kv_cols = 2 * KV_HEADS * HEAD_DIM // slots
    return pl.pallas_call(
        functools.partial(attend_kernel, slots, len(parts)),
        out_shape=(
            jax.ShapeDtypeStruct((own_rows * HEADS, HEAD_DIM + LANES), jnp.bfloat16),
            pltpu.VMEM(later.shape, later.dtype),
        ),
        in_specs=[in_vmem] * 5 + [in_place] + [in_vmem] * len(parts),
        out_specs=(in_vmem, in_vmem),
        scratch_shapes=[
            pltpu.VMEM((own_rows * HEADS, HEAD_DIM), jnp.float32),
            pltpu.VMEM((slots, own_rows, kv_cols), jnp.float32),
            pltpu.VMEM((own_rows, slots * kv_cols), jnp.float32),
            pltpu.VMEM((own_rows * HEADS, HEAD_DIM), jnp.float32),
            pltpu.VMEM((own_rows * HEADS, LANES), jnp.float32),
            pltpu.SemaphoreType.DMA((COPIES,)),
        ],
        compiler_params=params(6),
        name="attend",
    )(lengths, cosine, sine, resident(keys), resident(values), in_hbm(later), *parts)


def combine_kernel(shards, all_rows, *refs):
    ins = refs[:shards]
    out_ref = refs[-1]
    peaks = []
    totals = []
    for ref in ins:
        stats = ref[:, HEAD_DIM:].astype(jnp.float32)
        peaks.append(stats[:, 0:1] + stats[:, 1:2] + stats[:, 2:3])
        totals.append(stats[:, 4:5] + stats[:, 5:6] + stats[:, 6:7])
    top = functools.reduce(jnp.maximum, peaks)
    mixed = 0.0
    denominator = 0.0
    for ref, peak, total in zip(ins, peaks, totals):
        factor = jnp.exp(peak - top)
        mixed = mixed + factor * ref[:, :HEAD_DIM].astype(jnp.float32)
        denominator = denominator + factor * total
    attended = mixed / denominator
    for j in range(attended.shape[0] // all_rows):
        block = attended[j * all_rows : (j + 1) * all_rows]
        out_ref[:, j * HEAD_DIM : (j + 1) * HEAD_DIM] = block.astype(jnp.bfloat16)


def combine(parts, later, all_rows):
    count = len(parts)
    columns = parts[0].shape[0] // all_rows * HEAD_DIM
    return pl.pallas_call(
        functools.partial(combine_kernel, count, all_rows),
        out_shape=jax.ShapeDtypeStruct((all_rows, columns), jnp.bfloat16),
        in_specs=[in_vmem] * count + [in_place] * len(later),
        out_specs=in_vmem,
        compiler_params=params(2),
        name="combine",
    )(*parts, *[resident(w) for w in later])


def turned(block, step, own_rows):
    count = block.shape[0]
    span = step * own_rows
    row = lax.broadcasted_iota(jnp.int32, (count, 1), 0)
    return jnp.where(
        (row // span) % 2 == 0,
        pltpu.roll(block, count - span, axis=0),
        pltpu.roll(block, span, axis=0),
    )


def out_kernel(own_rows, left_ref, weight_ref, later_ref, *outs):
    del later_ref
    rows = left_ref.shape[0]
    lefts = [left_ref[...].astype(jnp.float32)]
    for k in range(1, len(outs)):
        low = k & -k
        lefts.append(turned(lefts[k ^ low], low, own_rows))
    left = jnp.concatenate(lefts, axis=0).astype(jnp.bfloat16)

    def store(start, size, value):
        for k, ref in enumerate(outs):
            ref[:, pl.ds(start, size)] = value[k * rows : (k + 1) * rows].astype(jnp.bfloat16)

    product_tiles(left, weight_ref, store)


def project_out(left, weight, later, own_rows):
    rows = left.shape[0]
    count = rows // own_rows
    shape = jax.ShapeDtypeStruct((rows, weight.shape[1]), jnp.bfloat16)
    return pl.pallas_call(
        functools.partial(out_kernel, own_rows),
        out_shape=(shape,) * count,
        in_specs=[in_vmem, in_vmem, in_place],
        out_specs=(in_vmem,) * count,
        compiler_params=params(3),
        name="project_out",
    )(left, resident(weight), resident(later))


def pair_kernel(first_ref, second_ref, out_ref):
    total = first_ref[...].astype(jnp.float32) + second_ref[...].astype(jnp.float32)
    out_ref[...] = total.astype(jnp.bfloat16)


def pair_sum(first, second):
    return pl.pallas_call(
        pair_kernel,
        out_shape=jax.ShapeDtypeStruct(first.shape, first.dtype),
        in_specs=[in_vmem] * 2,
        out_specs=in_vmem,
        compiler_params=params(2),
        name="pair_sum",
    )(first, second)


def gate_up_kernel(slots, rows_ref, gain_ref, gate_ref, up_ref, later_ref, *refs):
    parts = refs[:slots]
    out_ref, updated_ref, loaded_ref, sems = refs[slots:]
    copies = copies_of(later_ref, 0, loaded_ref, sems)
    for copy in copies:
        copy.start()
    own_rows = updated_ref.shape[0]
    total = functools.reduce(jnp.add, [ref[...].astype(jnp.float32) for ref in parts])
    updated = (rows_ref[...].astype(jnp.float32) + total).astype(jnp.bfloat16)
    wide = updated.astype(jnp.float32)
    updated_ref[...] = wide[:own_rows]
    squares = jnp.sum(wide * wide, axis=1, keepdims=True)
    scaled = (wide * gain_ref[...].astype(jnp.float32)[None, :]).astype(jnp.bfloat16)
    hidden = gate_ref.shape[1]

    def store_gate(start, size, value):
        out_ref[:, pl.ds(start, size)] = value.astype(jnp.bfloat16)

    def store_up(start, size, value):
        place = pl.multiple_of(start + hidden, math.gcd(hidden, size))
        out_ref[:, pl.ds(place, size)] = value.astype(jnp.bfloat16)

    product_tiles(scaled, gate_ref, store_gate)
    product_tiles(scaled, up_ref, store_up)
    out_ref[:, 2 * hidden :] = squares_block(squares).astype(jnp.bfloat16)
    for copy in copies:
        copy.wait()


def gate_up(rows, gain, parts, w_gate, w_up, later, cut, own_rows):
    hidden = w_gate.shape[1]
    slots = len(parts)
    return pl.pallas_call(
        functools.partial(gate_up_kernel, slots),
        out_shape=(
            jax.ShapeDtypeStruct((rows.shape[0], 2 * hidden + LANES), jnp.bfloat16),
            jax.ShapeDtypeStruct((own_rows, rows.shape[1]), jnp.float32),
            pltpu.VMEM((cut, later.shape[1]), later.dtype),
        ),
        in_specs=[in_vmem] * 4 + [in_place] + [in_vmem] * slots,
        out_specs=(in_vmem,) * 3,
        scratch_shapes=[pltpu.SemaphoreType.DMA((COPIES,))],
        compiler_params=params(3),
        name="gate_up",
    )(rows, gain, resident(w_gate), resident(w_up), in_hbm(later), *parts)


def down_kernel(near_ref, far_ref, upper_ref, lower_ref, out_ref, hidden_s):
    hidden = hidden_s.shape[1]
    cut = upper_ref.shape[0]
    squares = jnp.sum(
        near_ref[:, 2 * hidden :].astype(jnp.float32) + far_ref[:, 2 * hidden :].astype(jnp.float32),
        axis=1,
        keepdims=True,
    )
    scale = lax.rsqrt(squares / D + epsilon)
    gate = near_ref[:, :hidden].astype(jnp.float32) + far_ref[:, :hidden].astype(jnp.float32)
    up = (
        near_ref[:, hidden : 2 * hidden].astype(jnp.float32)
        + far_ref[:, hidden : 2 * hidden].astype(jnp.float32)
    )
    gate = gate * scale
    hidden_s[...] = (gate / (1.0 + jnp.exp(-gate)) * (up * scale)).astype(jnp.bfloat16)
    columns = upper_ref.shape[1]
    tile = tile_of(columns)

    @pl.loop(0, columns // tile)
    def _(step):
        span = pl.ds(pl.multiple_of(step * tile, tile), tile)
        total = jnp.dot(
            hidden_s[:, :cut], upper_ref[:, span], preferred_element_type=jnp.float32
        ) + jnp.dot(hidden_s[:, cut:], lower_ref[:, span], preferred_element_type=jnp.float32)
        out_ref[:, span] = total.astype(jnp.bfloat16)


def project_down(near, far, upper, lower):
    rows = near.shape[0]
    columns = upper.shape[1]
    return pl.pallas_call(
        down_kernel,
        out_shape=jax.ShapeDtypeStruct((rows, columns), jnp.bfloat16),
        in_specs=[in_vmem] * 4,
        out_specs=in_vmem,
        scratch_shapes=[
            pltpu.VMEM((rows, upper.shape[0] + lower.shape[0]), jnp.bfloat16),
        ],
        compiler_params=params(3),
        name="project_down",
    )(near, far, resident(upper), resident(lower))


def rotation_tables(positions, repeats):
    inverse = jnp.exp(
        (jnp.arange(HEAD_DIM) // 2).astype(jnp.float32) * (-2.0 / HEAD_DIM) * math.log(rope_base)
    )
    angles = positions[:, None] * inverse[None, :]
    sign = jnp.where(jnp.arange(HEAD_DIM) % 2 == 0, -1.0, 1.0)
    return (
        jnp.tile(jnp.cos(angles), (repeats, 1)),
        jnp.tile(jnp.sin(angles) * sign[None, :], (repeats, 1)),
    )


def local(
    states,
    attn_gain,
    ffn_gain,
    w_query,
    w_kv,
    w_out,
    w_gate,
    w_up,
    w_down,
    key_cache,
    value_cache,
    lengths,
):
    tensor_index = lax.axis_index("tensor")
    slots = lax.axis_size("tensor")
    own_rows = states.shape[0]
    all_rows = own_rows * slots

    cut = lambda array: [array[k * own_rows : (k + 1) * own_rows] for k in range(slots)]

    got = exchange(states, "tensor")
    own, attn_gain, ffn_gain, w_kv, w_query = load(
        states, attn_gain, ffn_gain, w_kv, w_query, after=states
    )
    rows = jnp.concatenate([own] + got[1:], axis=0)
    joined = project_qkv(rows, attn_gain, w_query, w_kv)

    joined, lengths = lax.optimization_barrier((joined, lengths))
    my_lengths = lax.dynamic_slice_in_dim(lengths, tensor_index * own_rows, own_rows, 0)
    cosine, sine = rotation_tables(my_lengths.astype(jnp.float32), slots)
    my_lengths = jnp.broadcast_to(my_lengths[:, None], (own_rows, LANES))
    flat = (own_rows, key_cache.shape[1] * KV_HEADS, HEAD_DIM)
    keys, values = load(key_cache.reshape(flat), value_cache.reshape(flat), after=joined)
    joined = jnp.concatenate(scatter_slots(cut(joined), 1), axis=0)
    joined, keys, values = lax.optimization_barrier((joined, keys, values))
    shard, w_out = attend(
        my_lengths, cosine, sine, exchange(joined, "inner"), keys, values, w_out, slots
    )
    attended = combine(exchange(shard, "inner"), [w_gate], all_rows)
    picked = jnp.concatenate(scatter_slots(cut(attended), 1), axis=0)
    parts = project_out(picked, w_out, w_up, own_rows)
    parts = scatter_slots(parts, 0)
    first = w_down.shape[0] // 128 * 96
    joined, updated, upper = gate_up(
        rows, ffn_gain, parts, w_gate, w_up, w_down, first, own_rows
    )

    steps = steps_up(lax.axis_size("inner"))
    for step in steps[:-1]:
        joined = pair_sum(joined, swap_with(joined, "inner", step))
    (lower,) = load(w_down, after=joined, spans=[(first, w_down.shape[0] - first)])
    other = swap_with(joined, "inner", steps[-1])
    part = project_down(joined, other, upper, lower)
    parts = scatter_slots(cut(part), 0)
    down_sum = sum(p.astype(jnp.float32) for p in parts)
    return (updated + down_sum).astype(jnp.bfloat16)


def solution(mesh):
    in_specs = (
        P(("groups", "tensor"), "inner"),
        P("inner"),
        P("inner"),
        P("inner", "tensor"),
        P("inner", "tensor"),
        P("tensor", "inner"),
        P("inner", "tensor"),
        P("inner", "tensor"),
        P("tensor", "inner"),
        P(("groups", "tensor"), "inner", None, None),
        P(("groups", "tensor"), "inner", None, None),
        P("groups"),
    )
    out_specs = P(("groups", "tensor"), "inner")
    return jax.shard_map(local, mesh=mesh, in_specs=in_specs, out_specs=out_specs, check_vma=False)
```

```python
import functools
import math

import jax
import jax.numpy as jnp
from jax import lax
from jax.experimental import pallas as pl
from jax.experimental.pallas import tpu as pltpu
from jax.sharding import PartitionSpec as P

D = 8192
HEADS = 32
KV_HEADS = 4
HEAD_DIM = 128
GROUP = HEADS // KV_HEADS
LANES = 128
MIB = 2**20
COPIES = 4

epsilon = 1e-05
rope_base = 500000.0

in_vmem = pl.BlockSpec(memory_space=pltpu.VMEM)
in_smem = pl.BlockSpec(memory_space=pltpu.SMEM)
in_place = pl.BlockSpec(memory_space=pl.ANY)


def swap_with(value, axis, step):
    count = lax.axis_size(axis)
    return lax.ppermute(value, axis, [(i, i ^ step) for i in range(count)])


def exchange(value, axis):
    count = lax.axis_size(axis)
    got = {k: swap_with(value, axis, k) for k in reversed(range(1, count))}
    return [value] + [got[k] for k in range(1, count)]


def scatter_slots(pieces, cross):
    count = lax.axis_size("tensor")
    width = lax.axis_size("inner")
    got = [pieces[0]]
    for k in range(1, count):
        pairs = [
            (t * width + i, (t ^ k) * width + (i ^ cross))
            for t in range(count)
            for i in range(width)
        ]
        got.append(lax.ppermute(pieces[k], ("tensor", "inner"), pairs))
    return got


def steps_up(count):
    return [1 << n for n in range(count.bit_length() - 1)]


def params(mib):
    return pltpu.CompilerParams(vmem_limit_bytes=mib * MIB)


def resident(weight):
    return pltpu.with_memory_space_constraint(weight, pltpu.VMEM)


def in_hbm(weight):
    return pltpu.with_memory_space_constraint(weight, pltpu.HBM)


def product_cost(depth, columns):
    return pl.CostEstimate(
        flops=16 * depth * columns, bytes_accessed=2 * depth * columns, transcendentals=0
    )


def tile_of(columns):
    for tile in (1792, 1024, 896, 512, 256, 128):
        if columns % tile == 0:
            return tile
    return columns


def product_tiles(left, weight_ref, store, first=0, columns=None):
    columns = columns or weight_ref.shape[1]
    tile = tile_of(columns)

    @pl.loop(0, columns // tile)
    def _(step):
        start = pl.multiple_of(step * tile, tile)
        span = pl.ds(pl.multiple_of(first + start, math.gcd(first, tile)), tile)
        store(
            start,
            tile,
            jnp.dot(left, weight_ref[:, span], preferred_element_type=jnp.float32),
        )


def three_parts(value):
    high = value.astype(jnp.bfloat16).astype(jnp.float32)
    rest = value - high
    middle = rest.astype(jnp.bfloat16).astype(jnp.float32)
    return high, middle, rest - middle


def spread(parts, lanes, first):
    out = 0.0
    for n, part in enumerate(parts):
        out = out + jnp.where(lanes == first + n, part, 0.0)
    return out


def squares_block(total):
    lanes = lax.broadcasted_iota(jnp.int32, (total.shape[0], LANES), 1)
    return spread(three_parts(total), lanes, lax.axis_index("inner") * 4)


def copies_of(source, start, target, sems):
    size = target.shape[0]
    cuts = COPIES if len(target.shape) > 1 and size % (16 * COPIES) == 0 else 1
    each = size // cuts
    return [
        pltpu.make_async_copy(
            source.at[pl.ds(start + m * each, each)], target.at[pl.ds(m * each, each)], sems.at[m]
        )
        for m in range(cuts)
    ]


def load_kernel(spans, *refs):
    count = len(spans)
    outs = refs[count + 1 : 2 * count + 1]
    sems = refs[-1]
    copies = []
    for n, (start, _) in enumerate(spans):
        copies += copies_of(refs[n], start, outs[n], sems.at[n])
    for copy in copies:
        copy.start()
    for copy in copies:
        copy.wait()


def load(*arrays, after, spans=None):
    spans = spans or [(0, a.shape[0]) for a in arrays]
    shapes = [(size,) + a.shape[1:] for a, (_, size) in zip(arrays, spans)]
    return pl.pallas_call(
        functools.partial(load_kernel, spans),
        out_shape=tuple(pltpu.VMEM(shape, a.dtype) for shape, a in zip(shapes, arrays)),
        in_specs=[in_place] * (len(arrays) + 1),
        out_specs=tuple(in_vmem for _ in arrays),
        cost_estimate=pl.CostEstimate(
            flops=0, bytes_accessed=2 * sum(math.prod(shape) for shape in shapes), transcendentals=0
        ),
        scratch_shapes=[pltpu.SemaphoreType.DMA((len(arrays), COPIES))],
        compiler_params=params(1),
        name="load",
    )(*[in_hbm(a) for a in arrays], after)


def qkv_kernel(rows_ref, gain_ref, wq_ref, wkv_ref, out_ref):
    wide = rows_ref[...].astype(jnp.float32)
    total = jnp.sum(wide * wide, axis=1, keepdims=True)
    gain = gain_ref[...].astype(jnp.float32)[None, :]
    scaled = (wide * gain).astype(jnp.bfloat16)
    query_cols = wq_ref.shape[1]
    kv_cols = wkv_ref.shape[1]

    def store_query(start, size, value):
        out_ref[:, pl.ds(start, size)] = value.astype(jnp.bfloat16)

    product_tiles(scaled, wq_ref, store_query)
    out_ref[:, query_cols : query_cols + kv_cols] = jnp.dot(
        scaled, wkv_ref[...], preferred_element_type=jnp.float32
    ).astype(jnp.bfloat16)
    out_ref[:, query_cols + kv_cols :] = squares_block(total).astype(jnp.bfloat16)


def project_qkv(rows, gain, w_query, w_kv):
    count = rows.shape[0]
    columns = w_query.shape[1] + w_kv.shape[1] + LANES
    return pl.pallas_call(
        qkv_kernel,
        out_shape=jax.ShapeDtypeStruct((count, columns), jnp.bfloat16),
        in_specs=[in_vmem] * 4,
        out_specs=in_vmem,
        compiler_params=params(2),
        name="project_qkv",
    )(rows, gain, resident(w_query), resident(w_kv))


def attend_kernel(
    slots,
    shards,
    lengths_ref,
    cosine_ref,
    sine_ref,
    key_ref,
    value_ref,
    *refs,
):
    parts = refs[:shards]
    out_ref, query_s, kv_s, kv_wide_s, mixed_s, stats_s = refs[shards:]
    all_rows = parts[0].shape[0]
    own_rows = all_rows // slots
    here = HEADS // slots
    query_cols = here * HEAD_DIM
    kv_cols = 2 * KV_HEADS * HEAD_DIM // slots
    columns = query_cols + kv_cols
    tensor_index = lax.axis_index("tensor")
    inner_index = lax.axis_index("inner")
    positions = key_ref.shape[1] // KV_HEADS

    joined = functools.reduce(jnp.add, [ref[...].astype(jnp.float32) for ref in parts])
    squares = jnp.sum(joined[:, columns:], axis=1, keepdims=True)
    joined = joined[:, :columns] * lax.rsqrt(squares / D + epsilon)
    cosine = cosine_ref[...]
    sine = sine_ref[...]

    def rotate(block):
        count = block.shape[0]
        even = lax.broadcasted_iota(jnp.int32, block.shape, 1) % 2 == 0
        other = jnp.where(
            even, pltpu.roll(block, HEAD_DIM - 1, axis=1), pltpu.roll(block, 1, axis=1)
        )
        return block * cosine[:count] + other * sine[:count]

    for j in range(here):
        block = rotate(joined[:, j * HEAD_DIM : (j + 1) * HEAD_DIM])
        query_s[j * all_rows : (j + 1) * all_rows, :] = block
    for s in range(slots):
        kv_s[s] = joined[s * own_rows : (s + 1) * own_rows, query_cols:]
    for d in range(slots):
        kv_wide_s[:, d * kv_cols : (d + 1) * kv_cols] = kv_s[d ^ tensor_index]
    new_keys = []
    new_values = []
    for g in range(KV_HEADS):
        block = kv_wide_s[:, g * HEAD_DIM : (g + 1) * HEAD_DIM]
        new_keys.append(rotate(block).astype(jnp.bfloat16).astype(jnp.float32))
        block = kv_wide_s[:, (KV_HEADS + g) * HEAD_DIM : (KV_HEADS + g + 1) * HEAD_DIM]
        new_values.append(block.astype(jnp.bfloat16).astype(jnp.float32))

    score_scale = HEAD_DIM ** (-0.5)
    row = lax.broadcasted_iota(jnp.int32, (HEADS, 1), 0)
    head = ((row % slots) ^ tensor_index) * here + row // slots
    kv_head = head // GROUP
    column = lax.broadcasted_iota(jnp.int32, (1, positions * KV_HEADS), 1)
    place = column // KV_HEADS + inner_index * positions
    column_head = column % KV_HEADS
    lanes = lax.broadcasted_iota(jnp.int32, (HEADS, LANES), 1)
    for r in range(own_rows):
        queries = query_s[pl.ds(r, HEADS, stride=own_rows), :].astype(jnp.bfloat16)
        scores = (
            lax.dot_general(
                queries,
                key_ref[r],
                (((1,), (1,)), ((), ())),
                preferred_element_type=jnp.float32,
            )
            * score_scale
        )
        used = jnp.where(place < lengths_ref[r : r + 1, 0:1], column_head, -1)
        masked = jnp.where(used == kv_head, scores, -1e30)
        key_rows = 0.0
        value_rows = 0.0
        for g in range(KV_HEADS):
            key_rows = key_rows + jnp.where(kv_head == g, new_keys[g][r : r + 1], 0.0)
            value_rows = value_rows + jnp.where(kv_head == g, new_values[g][r : r + 1], 0.0)
        new_score = (
            jnp.sum(queries.astype(jnp.float32) * key_rows, axis=1, keepdims=True) * score_scale
        )
        new_score = jnp.where(inner_index == 0, new_score, -1e30)
        peak = jnp.maximum(jnp.max(masked, axis=1, keepdims=True), new_score)
        weights = jnp.exp(masked - peak)
        new_weight = jnp.exp(new_score - peak)
        totals = jnp.sum(weights, axis=1, keepdims=True) + new_weight
        mixture = jnp.dot(
            weights.astype(jnp.bfloat16), value_ref[r], preferred_element_type=jnp.float32
        )
        mixture = mixture + new_weight.astype(jnp.bfloat16).astype(jnp.float32) * value_rows
        mixed_s[pl.ds(r, HEADS, stride=own_rows), :] = mixture
        stats_s[pl.ds(r, HEADS, stride=own_rows), :] = spread(
            three_parts(peak), lanes, 0
        ) + spread(three_parts(totals), lanes, 4)
    out_ref[:, :HEAD_DIM] = mixed_s[...].astype(jnp.bfloat16)
    out_ref[:, HEAD_DIM:] = stats_s[...].astype(jnp.bfloat16)


def attend(lengths, cosine, sine, parts, keys, values, slots):
    own_rows = parts[0].shape[0] // slots
    kv_cols = 2 * KV_HEADS * HEAD_DIM // slots
    return pl.pallas_call(
        functools.partial(attend_kernel, slots, len(parts)),
        out_shape=jax.ShapeDtypeStruct((own_rows * HEADS, HEAD_DIM + LANES), jnp.bfloat16),
        in_specs=[in_vmem] * (5 + len(parts)),
        out_specs=in_vmem,
        scratch_shapes=[
            pltpu.VMEM((own_rows * HEADS, HEAD_DIM), jnp.float32),
            pltpu.VMEM((slots, own_rows, kv_cols), jnp.float32),
            pltpu.VMEM((own_rows, slots * kv_cols), jnp.float32),
            pltpu.VMEM((own_rows * HEADS, HEAD_DIM), jnp.float32),
            pltpu.VMEM((own_rows * HEADS, LANES), jnp.float32),
        ],
        compiler_params=params(6),
        name="attend",
    )(lengths, cosine, sine, resident(keys), resident(values), *parts)


def combine_kernel(shards, all_rows, *refs):
    ins = refs[:shards]
    out_ref = refs[-1]
    peaks = []
    totals = []
    for ref in ins:
        stats = ref[:, HEAD_DIM:].astype(jnp.float32)
        peaks.append(stats[:, 0:1] + stats[:, 1:2] + stats[:, 2:3])
        totals.append(stats[:, 4:5] + stats[:, 5:6] + stats[:, 6:7])
    top = functools.reduce(jnp.maximum, peaks)
    mixed = 0.0
    denominator = 0.0
    for ref, peak, total in zip(ins, peaks, totals):
        factor = jnp.exp(peak - top)
        mixed = mixed + factor * ref[:, :HEAD_DIM].astype(jnp.float32)
        denominator = denominator + factor * total
    attended = mixed / denominator
    for j in range(attended.shape[0] // all_rows):
        block = attended[j * all_rows : (j + 1) * all_rows]
        out_ref[:, j * HEAD_DIM : (j + 1) * HEAD_DIM] = block.astype(jnp.bfloat16)


def combine(parts, later, all_rows):
    count = len(parts)
    columns = parts[0].shape[0] // all_rows * HEAD_DIM
    return pl.pallas_call(
        functools.partial(combine_kernel, count, all_rows),
        out_shape=jax.ShapeDtypeStruct((all_rows, columns), jnp.bfloat16),
        in_specs=[in_vmem] * count + [in_place] * len(later),
        out_specs=in_vmem,
        compiler_params=params(2),
        name="combine",
    )(*parts, *[resident(w) for w in later])


def turned(block, step, own_rows):
    count = block.shape[0]
    span = step * own_rows
    row = lax.broadcasted_iota(jnp.int32, (count, 1), 0)
    return jnp.where(
        (row // span) % 2 == 0,
        pltpu.roll(block, count - span, axis=0),
        pltpu.roll(block, span, axis=0),
    )


def out_kernel(own_rows, left_ref, weight_ref, later_ref, *outs):
    del later_ref
    rows = left_ref.shape[0]
    lefts = [left_ref[...].astype(jnp.float32)]
    for k in range(1, len(outs)):
        low = k & -k
        lefts.append(turned(lefts[k ^ low], low, own_rows))
    left = jnp.concatenate(lefts, axis=0).astype(jnp.bfloat16)

    def store(start, size, value):
        for k, ref in enumerate(outs):
            ref[:, pl.ds(start, size)] = value[k * rows : (k + 1) * rows].astype(jnp.bfloat16)

    product_tiles(left, weight_ref, store)


def project_out(left, weight, later, own_rows):
    rows = left.shape[0]
    count = rows // own_rows
    shape = jax.ShapeDtypeStruct((rows, weight.shape[1]), jnp.bfloat16)
    return pl.pallas_call(
        functools.partial(out_kernel, own_rows),
        out_shape=(shape,) * count,
        in_specs=[in_vmem, in_vmem, in_place],
        out_specs=(in_vmem,) * count,
        compiler_params=params(3),
        name="project_out",
    )(left, resident(weight), resident(later))


def pair_kernel(first_ref, second_ref, out_ref):
    total = first_ref[...].astype(jnp.float32) + second_ref[...].astype(jnp.float32)
    out_ref[...] = total.astype(jnp.bfloat16)


def pair_sum(first, second):
    return pl.pallas_call(
        pair_kernel,
        out_shape=jax.ShapeDtypeStruct(first.shape, first.dtype),
        in_specs=[in_vmem] * 2,
        out_specs=in_vmem,
        compiler_params=params(2),
        name="pair_sum",
    )(first, second)


def gate_up_tiles(scaled, gate_ref, up_ref, out_ref, first, count):
    def store(offset):
        def place(start, size, value):
            start = pl.multiple_of(offset + start, math.gcd(offset, size))
            out_ref[:, pl.ds(start, size)] = value.astype(jnp.bfloat16)

        return place

    product_tiles(scaled, gate_ref, store(0), first, count)
    product_tiles(scaled, up_ref, store(count), first, count)


def first_gate_up_kernel(slots, count, rows_ref, gain_ref, gate_ref, up_ref, later_ref, *refs):
    parts = refs[:slots]
    out_ref, updated_ref, scaled_ref, loaded_ref, sems = refs[slots:]
    copies = copies_of(later_ref, 0, loaded_ref, sems)
    for copy in copies:
        copy.start()
    own_rows = updated_ref.shape[0]
    total = functools.reduce(jnp.add, [ref[...].astype(jnp.float32) for ref in parts])
    updated = (rows_ref[...].astype(jnp.float32) + total).astype(jnp.bfloat16)
    wide = updated.astype(jnp.float32)
    updated_ref[...] = wide[:own_rows]
    squares = jnp.sum(wide * wide, axis=1, keepdims=True)
    out_ref[:, 2 * count :] = squares_block(squares).astype(jnp.bfloat16)
    scaled = (wide * gain_ref[...].astype(jnp.float32)[None, :]).astype(jnp.bfloat16)
    scaled_ref[...] = scaled
    gate_up_tiles(scaled, gate_ref, up_ref, out_ref, 0, count)
    for copy in copies:
        copy.wait()


def first_gate_up(rows, gain, parts, w_gate, w_up, w_down, count, own_rows):
    slots = len(parts)
    return pl.pallas_call(
        functools.partial(first_gate_up_kernel, slots, count),
        out_shape=(
            jax.ShapeDtypeStruct((rows.shape[0], 2 * count + LANES), jnp.bfloat16),
            jax.ShapeDtypeStruct((own_rows, rows.shape[1]), jnp.float32),
            jax.ShapeDtypeStruct(rows.shape, jnp.bfloat16),
            pltpu.VMEM((count, w_down.shape[1]), w_down.dtype),
        ),
        in_specs=[in_vmem] * 4 + [in_place] + [in_vmem] * slots,
        out_specs=(in_vmem,) * 4,
        scratch_shapes=[pltpu.SemaphoreType.DMA((COPIES,))],
        compiler_params=params(3),
        cost_estimate=product_cost(w_gate.shape[0], 2 * count),
        name="first_gate_up",
    )(rows, gain, resident(w_gate), resident(w_up), in_hbm(w_down), *parts)


def second_gate_up_kernel(
    first, scaled_ref, gate_ref, up_ref, later_ref, out_ref, loaded_ref, sems
):
    copies = copies_of(later_ref, first, loaded_ref, sems)
    for copy in copies:
        copy.start()
    count = loaded_ref.shape[0]
    gate_up_tiles(scaled_ref[...], gate_ref, up_ref, out_ref, first, count)
    for copy in copies:
        copy.wait()


def second_gate_up(scaled, w_gate, w_up, w_down, first):
    count = w_down.shape[0] - first
    return pl.pallas_call(
        functools.partial(second_gate_up_kernel, first),
        out_shape=(
            jax.ShapeDtypeStruct((scaled.shape[0], 2 * count), jnp.bfloat16),
            pltpu.VMEM((count, w_down.shape[1]), w_down.dtype),
        ),
        in_specs=[in_vmem] * 3 + [in_place],
        out_specs=(in_vmem,) * 2,
        scratch_shapes=[pltpu.SemaphoreType.DMA((COPIES,))],
        compiler_params=params(3),
        cost_estimate=product_cost(w_gate.shape[0], 2 * count),
        name="second_gate_up",
    )(scaled, resident(w_gate), resident(w_up), in_hbm(w_down))


def hidden_of(near_ref, far_ref, scale, count):
    def total(start):
        span = slice(start, start + count)
        return (near_ref[:, span].astype(jnp.float32) + far_ref[:, span].astype(jnp.float32)) * scale

    gate = total(0)
    return (gate / (1.0 + jnp.exp(-gate)) * total(count)).astype(jnp.bfloat16)


def first_down_kernel(near_ref, far_ref, weight_ref, out_ref, scale_ref):
    count = weight_ref.shape[0]
    squares = jnp.sum(
        near_ref[:, 2 * count :].astype(jnp.float32) + far_ref[:, 2 * count :].astype(jnp.float32),
        axis=1,
        keepdims=True,
    )
    scale = lax.rsqrt(squares / D + epsilon)
    scale_ref[...] = jnp.broadcast_to(scale, scale_ref.shape)

    def store(start, size, value):
        out_ref[:, pl.ds(start, size)] = value

    product_tiles(hidden_of(near_ref, far_ref, scale, count), weight_ref, store)


def first_down(near, far, weight):
    rows = near.shape[0]
    return pl.pallas_call(
        first_down_kernel,
        out_shape=(
            jax.ShapeDtypeStruct((rows, weight.shape[1]), jnp.float32),
            jax.ShapeDtypeStruct((rows, LANES), jnp.float32),
        ),
        in_specs=[in_vmem] * 3,
        out_specs=(in_vmem,) * 2,
        compiler_params=params(3),
        cost_estimate=product_cost(*weight.shape),
        name="first_down",
    )(near, far, resident(weight))


def second_down_kernel(near_ref, far_ref, weight_ref, part_ref, scale_ref, out_ref):
    count = weight_ref.shape[0]

    def store(start, size, value):
        span = pl.ds(start, size)
        out_ref[:, span] = (part_ref[:, span] + value).astype(jnp.bfloat16)

    product_tiles(hidden_of(near_ref, far_ref, scale_ref[:, 0:1], count), weight_ref, store)


def second_down(near, far, weight, part, scale):
    return pl.pallas_call(
        second_down_kernel,
        out_shape=jax.ShapeDtypeStruct(part.shape, jnp.bfloat16),
        in_specs=[in_vmem] * 5,
        out_specs=in_vmem,
        compiler_params=params(3),
        name="second_down",
    )(near, far, resident(weight), part, scale)


def rotation_tables(positions, repeats):
    inverse = jnp.exp(
        (jnp.arange(HEAD_DIM) // 2).astype(jnp.float32) * (-2.0 / HEAD_DIM) * math.log(rope_base)
    )
    angles = positions[:, None] * inverse[None, :]
    sign = jnp.where(jnp.arange(HEAD_DIM) % 2 == 0, -1.0, 1.0)
    return (
        jnp.tile(jnp.cos(angles), (repeats, 1)),
        jnp.tile(jnp.sin(angles) * sign[None, :], (repeats, 1)),
    )


def local(
    states,
    attn_gain,
    ffn_gain,
    w_query,
    w_kv,
    w_out,
    w_gate,
    w_up,
    w_down,
    key_cache,
    value_cache,
    lengths,
):
    tensor_index = lax.axis_index("tensor")
    slots = lax.axis_size("tensor")
    own_rows = states.shape[0]
    all_rows = own_rows * slots

    cut = lambda array: [array[k * own_rows : (k + 1) * own_rows] for k in range(slots)]

    got = exchange(states, "tensor")
    own, attn_gain, ffn_gain, w_kv, w_query = load(
        states, attn_gain, ffn_gain, w_kv, w_query, after=states
    )
    rows = jnp.concatenate([own] + got[1:], axis=0)
    joined = project_qkv(rows, attn_gain, w_query, w_kv)

    joined, lengths = lax.optimization_barrier((joined, lengths))
    my_lengths = lax.dynamic_slice_in_dim(lengths, tensor_index * own_rows, own_rows, 0)
    cosine, sine = rotation_tables(my_lengths.astype(jnp.float32), slots)
    my_lengths = jnp.broadcast_to(my_lengths[:, None], (own_rows, LANES))
    flat = (own_rows, key_cache.shape[1] * KV_HEADS, HEAD_DIM)
    keys, values = load(key_cache.reshape(flat), value_cache.reshape(flat), after=joined)
    joined = jnp.concatenate(scatter_slots(cut(joined), 1), axis=0)
    joined, keys, values, w_gate = lax.optimization_barrier((joined, keys, values, w_gate))
    (w_out,) = load(w_out, after=joined)
    parts, w_out = lax.optimization_barrier((exchange(joined, "inner"), w_out))
    shard = attend(my_lengths, cosine, sine, parts, keys, values, slots)

    attended = combine(exchange(shard, "inner"), [w_gate], all_rows)
    picked = jnp.concatenate(scatter_slots(cut(attended), 1), axis=0)
    parts = scatter_slots(project_out(picked, w_out, w_up, own_rows), 0)

    tiles = w_gate.shape[1] // LANES
    first = (tiles + 1) // 2 * LANES
    one, updated, scaled, upper = first_gate_up(
        rows, ffn_gain, parts, w_gate, w_up, w_down, first, own_rows
    )
    two, lower = second_gate_up(scaled, w_gate, w_up, w_down, first)
    steps = steps_up(lax.axis_size("inner"))
    for step in steps[:-1]:
        one = pair_sum(one, swap_with(one, "inner", step))
        two = pair_sum(two, swap_with(two, "inner", step))
    part, scale = first_down(one, swap_with(one, "inner", steps[-1]), upper)
    part = second_down(two, swap_with(two, "inner", steps[-1]), lower, part, scale)
    parts = scatter_slots(cut(part), 0)
    down_sum = sum(p.astype(jnp.float32) for p in parts)
    return (updated + down_sum).astype(jnp.bfloat16)


def solution(mesh):
    in_specs = (
        P(("groups", "tensor"), "inner"),
        P("inner"),
        P("inner"),
        P("inner", "tensor"),
        P("inner", "tensor"),
        P("tensor", "inner"),
        P("inner", "tensor"),
        P("inner", "tensor"),
        P("tensor", "inner"),
        P(("groups", "tensor"), "inner", None, None),
        P(("groups", "tensor"), "inner", None, None),
        P("groups"),
    )
    out_specs = P(("groups", "tensor"), "inner")
    return jax.shard_map(local, mesh=mesh, in_specs=in_specs, out_specs=out_specs, check_vma=False)
```

```python
import functools
import math

import jax
import jax.numpy as jnp
from jax import lax
from jax.experimental import pallas as pl
from jax.experimental.pallas import tpu as pltpu
from jax.sharding import PartitionSpec as P

D = 8192
HEADS = 32
KV_HEADS = 4
HEAD_DIM = 128
GROUP = HEADS // KV_HEADS
LANES = 128
MIB = 2**20
COPIES = 4

epsilon = 1e-05
rope_base = 500000.0

in_vmem = pl.BlockSpec(memory_space=pltpu.VMEM)
in_smem = pl.BlockSpec(memory_space=pltpu.SMEM)
in_place = pl.BlockSpec(memory_space=pl.ANY)


def swap_with(value, axis, step):
    count = lax.axis_size(axis)
    return lax.ppermute(value, axis, [(i, i ^ step) for i in range(count)])


def exchange(value, axis):
    count = lax.axis_size(axis)
    got = {k: swap_with(value, axis, k) for k in reversed(range(1, count))}
    return [value] + [got[k] for k in range(1, count)]


def scatter_slots(pieces, cross):
    count = lax.axis_size("tensor")
    width = lax.axis_size("inner")
    got = [pieces[0]]
    for k in range(1, count):
        pairs = [
            (t * width + i, (t ^ k) * width + (i ^ cross))
            for t in range(count)
            for i in range(width)
        ]
        got.append(lax.ppermute(pieces[k], ("tensor", "inner"), pairs))
    return got


def steps_up(count):
    return [1 << n for n in range(count.bit_length() - 1)]


def params(mib):
    return pltpu.CompilerParams(vmem_limit_bytes=mib * MIB)


def resident(weight):
    return pltpu.with_memory_space_constraint(weight, pltpu.VMEM)


def in_hbm(weight):
    return pltpu.with_memory_space_constraint(weight, pltpu.HBM)


def product_cost(depth, columns):
    return pl.CostEstimate(
        flops=16 * depth * columns, bytes_accessed=2 * depth * columns, transcendentals=0
    )


def tile_of(columns):
    for tile in (1792, 1024, 896, 512, 256, 128):
        if columns % tile == 0:
            return tile
    return columns


def product_tiles(left, weight_ref, store, first=0, columns=None):
    columns = columns or weight_ref.shape[1]
    tile = tile_of(columns)

    @pl.loop(0, columns // tile)
    def _(step):
        start = pl.multiple_of(step * tile, tile)
        span = pl.ds(pl.multiple_of(first + start, math.gcd(first, tile)), tile)
        store(
            start,
            tile,
            jnp.dot(left, weight_ref[:, span], preferred_element_type=jnp.float32),
        )


def three_parts(value):
    high = value.astype(jnp.bfloat16).astype(jnp.float32)
    rest = value - high
    middle = rest.astype(jnp.bfloat16).astype(jnp.float32)
    return high, middle, rest - middle


def spread(parts, lanes, first):
    out = 0.0
    for n, part in enumerate(parts):
        out = out + jnp.where(lanes == first + n, part, 0.0)
    return out


def squares_block(total):
    lanes = lax.broadcasted_iota(jnp.int32, (total.shape[0], LANES), 1)
    return spread(three_parts(total), lanes, lax.axis_index("inner") * 4)


def copies_of(source, start, target, sems):
    size = target.shape[0]
    cuts = COPIES if len(target.shape) > 1 and size % (16 * COPIES) == 0 else 1
    each = size // cuts
    return [
        pltpu.make_async_copy(
            source.at[pl.ds(start + m * each, each)], target.at[pl.ds(m * each, each)], sems.at[m]
        )
        for m in range(cuts)
    ]


def load_kernel(spans, *refs):
    count = len(spans)
    outs = refs[count + 1 : 2 * count + 1]
    sems = refs[-1]
    copies = []
    for n, (start, _) in enumerate(spans):
        copies += copies_of(refs[n], start, outs[n], sems.at[n])
    for copy in copies:
        copy.start()
    for copy in copies:
        copy.wait()


def load(*arrays, after, spans=None):
    spans = spans or [(0, a.shape[0]) for a in arrays]
    shapes = [(size,) + a.shape[1:] for a, (_, size) in zip(arrays, spans)]
    return pl.pallas_call(
        functools.partial(load_kernel, spans),
        out_shape=tuple(pltpu.VMEM(shape, a.dtype) for shape, a in zip(shapes, arrays)),
        in_specs=[in_place] * (len(arrays) + 1),
        out_specs=tuple(in_vmem for _ in arrays),
        cost_estimate=pl.CostEstimate(
            flops=0, bytes_accessed=2 * sum(math.prod(shape) for shape in shapes), transcendentals=0
        ),
        scratch_shapes=[pltpu.SemaphoreType.DMA((len(arrays), COPIES))],
        compiler_params=params(1),
        name="load",
    )(*[in_hbm(a) for a in arrays], after)


def join_rows(refs, target):
    rows = refs[0].shape[0]
    for n, ref in enumerate(refs):
        target[n * rows : (n + 1) * rows, :] = ref[...].astype(jnp.float32)
    return target[...]


def part_rows(source, refs):
    rows = refs[0].shape[0]
    for n, ref in enumerate(refs):
        ref[...] = source[n * rows : (n + 1) * rows, :].astype(ref.dtype)


def qkv_kernel(slots, gain_ref, wq_ref, wkv_ref, *refs):
    rows_ref = refs[slots]
    out_s, rows_s = refs[-2:]
    wide = join_rows(refs[:slots], rows_s)
    rows_ref[...] = wide
    total = jnp.sum(wide * wide, axis=1, keepdims=True)
    gain = gain_ref[...].astype(jnp.float32)[None, :]
    scaled = (wide * gain).astype(jnp.bfloat16)
    query_cols = wq_ref.shape[1]
    kv_cols = wkv_ref.shape[1]

    def store_query(start, size, value):
        out_s[:, pl.ds(start, size)] = value

    product_tiles(scaled, wq_ref, store_query)
    out_s[:, query_cols : query_cols + kv_cols] = jnp.dot(
        scaled, wkv_ref[...], preferred_element_type=jnp.float32
    )
    out_s[:, query_cols + kv_cols :] = squares_block(total)
    part_rows(out_s, refs[slots + 1 : 2 * slots + 1])


def project_qkv(rows, gain, w_query, w_kv):
    slots = len(rows)
    own_rows, depth = rows[0].shape
    columns = w_query.shape[1] + w_kv.shape[1] + LANES
    return pl.pallas_call(
        functools.partial(qkv_kernel, slots),
        out_shape=(
            jax.ShapeDtypeStruct((own_rows * slots, depth), jnp.float32),
            *[jax.ShapeDtypeStruct((own_rows, columns), jnp.bfloat16)] * slots,
        ),
        in_specs=[in_vmem] * (3 + slots),
        out_specs=(in_vmem,) * (1 + slots),
        scratch_shapes=[
            pltpu.VMEM((own_rows * slots, columns), jnp.float32),
            pltpu.VMEM((own_rows * slots, depth), jnp.float32),
        ],
        compiler_params=params(2),
        name="project_qkv",
    )(gain, resident(w_query), resident(w_kv), *rows)


def stack_kernel(*refs):
    refs[-2][...] = join_rows(refs[:-2], refs[-1]).astype(refs[-2].dtype)


def stack(pieces):
    shape = (len(pieces) * pieces[0].shape[0], pieces[0].shape[1])
    return pl.pallas_call(
        stack_kernel,
        out_shape=jax.ShapeDtypeStruct(shape, pieces[0].dtype),
        in_specs=[in_vmem] * len(pieces),
        out_specs=in_vmem,
        scratch_shapes=[pltpu.VMEM(shape, jnp.float32)],
        compiler_params=params(1),
        name="stack",
    )(*pieces)


def attend_kernel(
    slots,
    shards,
    lengths_ref,
    cosine_ref,
    sine_ref,
    key_ref,
    value_ref,
    *refs,
):
    parts = refs[:shards]
    out_ref, query_s, kv_s, kv_wide_s, mixed_s, stats_s = refs[shards:]
    all_rows = parts[0].shape[0]
    own_rows = all_rows // slots
    here = HEADS // slots
    query_cols = here * HEAD_DIM
    kv_cols = 2 * KV_HEADS * HEAD_DIM // slots
    columns = query_cols + kv_cols
    tensor_index = lax.axis_index("tensor")
    inner_index = lax.axis_index("inner")
    positions = key_ref.shape[1] // KV_HEADS

    joined = functools.reduce(jnp.add, [ref[...].astype(jnp.float32) for ref in parts])
    squares = jnp.sum(joined[:, columns:], axis=1, keepdims=True)
    joined = joined[:, :columns] * lax.rsqrt(squares / D + epsilon)
    cosine = cosine_ref[...]
    sine = sine_ref[...]

    def rotate(block):
        count = block.shape[0]
        even = lax.broadcasted_iota(jnp.int32, block.shape, 1) % 2 == 0
        other = jnp.where(
            even, pltpu.roll(block, HEAD_DIM - 1, axis=1), pltpu.roll(block, 1, axis=1)
        )
        return block * cosine[:count] + other * sine[:count]

    for j in range(here):
        block = rotate(joined[:, j * HEAD_DIM : (j + 1) * HEAD_DIM])
        query_s[j * all_rows : (j + 1) * all_rows, :] = block
    for s in range(slots):
        kv_s[s] = joined[s * own_rows : (s + 1) * own_rows, query_cols:]
    for d in range(slots):
        kv_wide_s[:, d * kv_cols : (d + 1) * kv_cols] = kv_s[d ^ tensor_index]
    new_keys = []
    new_values = []
    for g in range(KV_HEADS):
        block = kv_wide_s[:, g * HEAD_DIM : (g + 1) * HEAD_DIM]
        new_keys.append(rotate(block).astype(jnp.bfloat16).astype(jnp.float32))
        block = kv_wide_s[:, (KV_HEADS + g) * HEAD_DIM : (KV_HEADS + g + 1) * HEAD_DIM]
        new_values.append(block.astype(jnp.bfloat16).astype(jnp.float32))

    score_scale = HEAD_DIM ** (-0.5)
    row = lax.broadcasted_iota(jnp.int32, (HEADS, 1), 0)
    head = ((row % slots) ^ tensor_index) * here + row // slots
    kv_head = head // GROUP
    column = lax.broadcasted_iota(jnp.int32, (1, positions * KV_HEADS), 1)
    place = column // KV_HEADS + inner_index * positions
    column_head = column % KV_HEADS
    lanes = lax.broadcasted_iota(jnp.int32, (HEADS, LANES), 1)
    for r in range(own_rows):
        queries = query_s[pl.ds(r, HEADS, stride=own_rows), :].astype(jnp.bfloat16)
        scores = (
            lax.dot_general(
                queries,
                key_ref[r],
                (((1,), (1,)), ((), ())),
                preferred_element_type=jnp.float32,
            )
            * score_scale
        )
        used = jnp.where(place < lengths_ref[r : r + 1, 0:1], column_head, -1)
        masked = jnp.where(used == kv_head, scores, -1e30)
        key_rows = 0.0
        value_rows = 0.0
        for g in range(KV_HEADS):
            key_rows = key_rows + jnp.where(kv_head == g, new_keys[g][r : r + 1], 0.0)
            value_rows = value_rows + jnp.where(kv_head == g, new_values[g][r : r + 1], 0.0)
        new_score = (
            jnp.sum(queries.astype(jnp.float32) * key_rows, axis=1, keepdims=True) * score_scale
        )
        new_score = jnp.where(inner_index == 0, new_score, -1e30)
        peak = jnp.maximum(jnp.max(masked, axis=1, keepdims=True), new_score)
        weights = jnp.exp(masked - peak)
        new_weight = jnp.exp(new_score - peak)
        totals = jnp.sum(weights, axis=1, keepdims=True) + new_weight
        mixture = jnp.dot(
            weights.astype(jnp.bfloat16), value_ref[r], preferred_element_type=jnp.float32
        )
        mixture = mixture + new_weight.astype(jnp.bfloat16).astype(jnp.float32) * value_rows
        mixed_s[pl.ds(r, HEADS, stride=own_rows), :] = mixture
        stats_s[pl.ds(r, HEADS, stride=own_rows), :] = spread(
            three_parts(peak), lanes, 0
        ) + spread(three_parts(totals), lanes, 4)
    out_ref[:, :HEAD_DIM] = mixed_s[...].astype(jnp.bfloat16)
    out_ref[:, HEAD_DIM:] = stats_s[...].astype(jnp.bfloat16)


def attend(lengths, cosine, sine, parts, keys, values, slots):
    own_rows = parts[0].shape[0] // slots
    kv_cols = 2 * KV_HEADS * HEAD_DIM // slots
    return pl.pallas_call(
        functools.partial(attend_kernel, slots, len(parts)),
        out_shape=jax.ShapeDtypeStruct((own_rows * HEADS, HEAD_DIM + LANES), jnp.bfloat16),
        in_specs=[in_vmem] * (5 + len(parts)),
        out_specs=in_vmem,
        scratch_shapes=[
            pltpu.VMEM((own_rows * HEADS, HEAD_DIM), jnp.float32),
            pltpu.VMEM((slots, own_rows, kv_cols), jnp.float32),
            pltpu.VMEM((own_rows, slots * kv_cols), jnp.float32),
            pltpu.VMEM((own_rows * HEADS, HEAD_DIM), jnp.float32),
            pltpu.VMEM((own_rows * HEADS, LANES), jnp.float32),
        ],
        compiler_params=params(6),
        name="attend",
    )(lengths, cosine, sine, resident(keys), resident(values), *parts)


def combine_kernel(shards, slots, *refs):
    ins = refs[:shards]
    out_s = refs[-1]
    all_rows = out_s.shape[0]
    peaks = []
    totals = []
    for ref in ins:
        stats = ref[:, HEAD_DIM:].astype(jnp.float32)
        peaks.append(stats[:, 0:1] + stats[:, 1:2] + stats[:, 2:3])
        totals.append(stats[:, 4:5] + stats[:, 5:6] + stats[:, 6:7])
    top = functools.reduce(jnp.maximum, peaks)
    mixed = 0.0
    denominator = 0.0
    for ref, peak, total in zip(ins, peaks, totals):
        factor = jnp.exp(peak - top)
        mixed = mixed + factor * ref[:, :HEAD_DIM].astype(jnp.float32)
        denominator = denominator + factor * total
    attended = mixed / denominator
    for j in range(attended.shape[0] // all_rows):
        block = attended[j * all_rows : (j + 1) * all_rows]
        out_s[:, j * HEAD_DIM : (j + 1) * HEAD_DIM] = block
    part_rows(out_s, refs[-1 - slots : -1])


def combine(parts, later, all_rows, slots):
    count = len(parts)
    columns = parts[0].shape[0] // all_rows * HEAD_DIM
    return pl.pallas_call(
        functools.partial(combine_kernel, count, slots),
        out_shape=(jax.ShapeDtypeStruct((all_rows // slots, columns), jnp.bfloat16),) * slots,
        in_specs=[in_vmem] * count + [in_place] * len(later),
        out_specs=(in_vmem,) * slots,
        scratch_shapes=[pltpu.VMEM((all_rows, columns), jnp.float32)],
        compiler_params=params(2),
        name="combine",
    )(*parts, *[resident(w) for w in later])


def turned(block, step, own_rows):
    count = block.shape[0]
    span = step * own_rows
    row = lax.broadcasted_iota(jnp.int32, (count, 1), 0)
    return jnp.where(
        (row // span) % 2 == 0,
        pltpu.roll(block, count - span, axis=0),
        pltpu.roll(block, span, axis=0),
    )


def out_kernel(slots, later, weight_ref, *refs):
    pieces = refs[:slots]
    outs = refs[slots + later : 2 * slots + later]
    left_s = refs[-1]
    own_rows = pieces[0].shape[0]
    rows = left_s.shape[0]
    lefts = [join_rows(pieces, left_s)]
    for k in range(1, slots):
        low = k & -k
        lefts.append(turned(lefts[k ^ low], low, own_rows))
    left = jnp.concatenate(lefts, axis=0).astype(jnp.bfloat16)

    def store(start, size, value):
        for k, ref in enumerate(outs):
            ref[:, pl.ds(start, size)] = value[k * rows : (k + 1) * rows].astype(jnp.bfloat16)

    product_tiles(left, weight_ref, store)


def project_out(pieces, weight, later):
    slots = len(pieces)
    own_rows, depth = pieces[0].shape
    shape = jax.ShapeDtypeStruct((own_rows * slots, weight.shape[1]), jnp.bfloat16)
    return pl.pallas_call(
        functools.partial(out_kernel, slots, len(later)),
        out_shape=(shape,) * slots,
        in_specs=[in_vmem] * (1 + slots) + [in_place] * len(later),
        out_specs=(in_vmem,) * slots,
        scratch_shapes=[pltpu.VMEM((own_rows * slots, depth), jnp.float32)],
        compiler_params=params(3),
        name="project_out",
    )(resident(weight), *pieces, *[resident(w) for w in later])


def pair_kernel(first_ref, second_ref, out_ref):
    total = first_ref[...].astype(jnp.float32) + second_ref[...].astype(jnp.float32)
    out_ref[...] = total.astype(jnp.bfloat16)


def pair_sum(first, second):
    return pl.pallas_call(
        pair_kernel,
        out_shape=jax.ShapeDtypeStruct(first.shape, first.dtype),
        in_specs=[in_vmem] * 2,
        out_specs=in_vmem,
        compiler_params=params(2),
        name="pair_sum",
    )(first, second)


def gate_up_tiles(scaled, gate_ref, up_ref, out_ref, first, count):
    def store(offset):
        def place(start, size, value):
            start = pl.multiple_of(offset + start, math.gcd(offset, size))
            out_ref[:, pl.ds(start, size)] = value.astype(jnp.bfloat16)

        return place

    product_tiles(scaled, gate_ref, store(0), first, count)
    product_tiles(scaled, up_ref, store(count), first, count)


def first_gate_up_kernel(
    slots, count, start, rows_ref, gain_ref, gate_ref, up_ref, down_ref, *refs
):
    parts = refs[:slots]
    out_ref, updated_ref, scaled_ref, loaded_ref, sems = refs[-5:]
    copies = copies_of(down_ref, start, loaded_ref, sems)
    for copy in copies:
        copy.start()
    own_rows = updated_ref.shape[0]
    total = functools.reduce(jnp.add, [ref[...].astype(jnp.float32) for ref in parts])
    updated = (rows_ref[...] + total).astype(jnp.bfloat16)
    wide = updated.astype(jnp.float32)
    updated_ref[...] = wide[:own_rows]
    squares = jnp.sum(wide * wide, axis=1, keepdims=True)
    out_ref[:, 2 * count :] = squares_block(squares).astype(jnp.bfloat16)
    scaled = (wide * gain_ref[...].astype(jnp.float32)[None, :]).astype(jnp.bfloat16)
    scaled_ref[...] = scaled
    gate_up_tiles(scaled, gate_ref, up_ref, out_ref, 0, count)
    for copy in copies:
        copy.wait()


def first_gate_up(rows, gain, parts, w_gate, w_up, w_down, span, later, count, own_rows):
    slots = len(parts)
    start, size = span
    return pl.pallas_call(
        functools.partial(first_gate_up_kernel, slots, count, start),
        out_shape=(
            jax.ShapeDtypeStruct((rows.shape[0], 2 * count + LANES), jnp.bfloat16),
            jax.ShapeDtypeStruct((own_rows, rows.shape[1]), jnp.float32),
            jax.ShapeDtypeStruct(rows.shape, jnp.bfloat16),
            pltpu.VMEM((size, w_down.shape[1]), w_down.dtype),
        ),
        in_specs=[in_vmem] * 4 + [in_place] + [in_vmem] * slots + [in_place] * len(later),
        out_specs=(in_vmem,) * 4,
        scratch_shapes=[pltpu.SemaphoreType.DMA((COPIES,))],
        compiler_params=params(3),
        cost_estimate=product_cost(w_gate.shape[0], 2 * count),
        name="first_gate_up",
    )(
        rows,
        gain,
        resident(w_gate),
        resident(w_up),
        in_hbm(w_down),
        *parts,
        *[resident(w) for w in later],
    )


def second_gate_up_kernel(
    first, count, start, scaled_ref, gate_ref, up_ref, down_ref, out_ref, loaded_ref, sems
):
    copies = copies_of(down_ref, start, loaded_ref, sems)
    for copy in copies:
        copy.start()
    gate_up_tiles(scaled_ref[...], gate_ref, up_ref, out_ref, first, count)
    for copy in copies:
        copy.wait()


def second_gate_up(scaled, w_gate, w_up, w_down, span, first):
    count = w_gate.shape[1] - first
    start, size = span
    return pl.pallas_call(
        functools.partial(second_gate_up_kernel, first, count, start),
        out_shape=(
            jax.ShapeDtypeStruct((scaled.shape[0], 2 * count), jnp.bfloat16),
            pltpu.VMEM((size, w_down.shape[1]), w_down.dtype),
        ),
        in_specs=[in_vmem] * 3 + [in_place],
        out_specs=(in_vmem,) * 2,
        scratch_shapes=[pltpu.SemaphoreType.DMA((COPIES,))],
        compiler_params=params(3),
        cost_estimate=product_cost(w_gate.shape[0], 2 * count),
        name="second_gate_up",
    )(scaled, resident(w_gate), resident(w_up), in_hbm(w_down))


def hidden_of(near_ref, far_ref, scale, count):
    def total(start):
        span = slice(start, start + count)
        return (near_ref[:, span].astype(jnp.float32) + far_ref[:, span].astype(jnp.float32)) * scale

    gate = total(0)
    return (gate / (1.0 + jnp.exp(-gate)) * total(count)).astype(jnp.bfloat16)


def first_down_kernel(near_ref, far_ref, one_ref, two_ref, later_ref, out_ref, scale_ref):
    del later_ref
    cut = one_ref.shape[0]
    count = (near_ref.shape[1] - LANES) // 2
    squares = jnp.sum(
        near_ref[:, 2 * count :].astype(jnp.float32) + far_ref[:, 2 * count :].astype(jnp.float32),
        axis=1,
        keepdims=True,
    )
    scale = lax.rsqrt(squares / D + epsilon)
    scale_ref[...] = jnp.broadcast_to(scale, scale_ref.shape)
    hidden = hidden_of(near_ref, far_ref, scale, count)
    lower_ref = two_ref.at[: count - cut]

    def store(start, size, value):
        span = pl.ds(start, size)
        out_ref[:, span] = value + jnp.dot(
            hidden[:, cut:], lower_ref[:, span], preferred_element_type=jnp.float32
        )

    product_tiles(hidden[:, :cut], one_ref, store)


def first_down(near, far, one, two, later):
    rows = near.shape[0]
    columns = one.shape[1]
    return pl.pallas_call(
        first_down_kernel,
        out_shape=(
            jax.ShapeDtypeStruct((rows, columns), jnp.float32),
            jax.ShapeDtypeStruct((rows, LANES), jnp.float32),
        ),
        in_specs=[in_vmem] * 4 + [in_place],
        out_specs=(in_vmem,) * 2,
        compiler_params=params(3),
        cost_estimate=product_cost((near.shape[1] - LANES) // 2, columns),
        name="first_down",
    )(near, far, resident(one), resident(two), resident(later))


def second_down_kernel(near_ref, far_ref, two_ref, three_ref, part_ref, scale_ref, *refs):
    out_s = refs[-1]
    count = near_ref.shape[1] // 2
    cut = count - three_ref.shape[0]
    hidden = hidden_of(near_ref, far_ref, scale_ref[:, 0:1], count)
    upper_ref = two_ref.at[two_ref.shape[0] - cut :]

    def store(start, size, value):
        span = pl.ds(start, size)
        out_s[:, span] = part_ref[:, span] + (
            value
            + jnp.dot(hidden[:, :cut], upper_ref[:, span], preferred_element_type=jnp.float32)
        )

    product_tiles(hidden[:, cut:], three_ref, store)
    part_rows(out_s, refs[:-1])


def second_down(near, far, two, three, part, scale, slots):
    rows, columns = part.shape
    return pl.pallas_call(
        second_down_kernel,
        out_shape=(jax.ShapeDtypeStruct((rows // slots, columns), jnp.bfloat16),) * slots,
        in_specs=[in_vmem] * 6,
        out_specs=(in_vmem,) * slots,
        scratch_shapes=[pltpu.VMEM(part.shape, jnp.float32)],
        compiler_params=params(3),
        name="second_down",
    )(near, far, resident(two), resident(three), part, scale)


def rotation_tables(positions, repeats):
    inverse = jnp.exp(
        (jnp.arange(HEAD_DIM) // 2).astype(jnp.float32) * (-2.0 / HEAD_DIM) * math.log(rope_base)
    )
    angles = positions[:, None] * inverse[None, :]
    sign = jnp.where(jnp.arange(HEAD_DIM) % 2 == 0, -1.0, 1.0)
    return (
        jnp.tile(jnp.cos(angles), (repeats, 1)),
        jnp.tile(jnp.sin(angles) * sign[None, :], (repeats, 1)),
    )


def local(
    states,
    attn_gain,
    ffn_gain,
    w_query,
    w_kv,
    w_out,
    w_gate,
    w_up,
    w_down,
    key_cache,
    value_cache,
    lengths,
):
    tensor_index = lax.axis_index("tensor")
    slots = lax.axis_size("tensor")
    own_rows = states.shape[0]
    all_rows = own_rows * slots

    got = exchange(states, "tensor")
    own, attn_gain, ffn_gain, w_kv, w_query = load(
        states, attn_gain, ffn_gain, w_kv, w_query, after=states
    )
    rows, *pieces = project_qkv([own] + got[1:], attn_gain, w_query, w_kv)

    rows, lengths = lax.optimization_barrier((rows, lengths))
    my_lengths = lax.dynamic_slice_in_dim(lengths, tensor_index * own_rows, own_rows, 0)
    cosine, sine = rotation_tables(my_lengths.astype(jnp.float32), slots)
    my_lengths = jnp.broadcast_to(my_lengths[:, None], (own_rows, LANES))
    flat = (own_rows, key_cache.shape[1] * KV_HEADS, HEAD_DIM)
    keys, values = load(key_cache.reshape(flat), value_cache.reshape(flat), after=rows)
    joined = stack(scatter_slots(pieces, 1))
    joined, keys, values = lax.optimization_barrier((joined, keys, values))
    (w_out,) = load(w_out, after=joined)
    parts, w_out = lax.optimization_barrier((exchange(joined, "inner"), w_out))
    shard = attend(my_lengths, cosine, sine, parts, keys, values, slots)

    pieces = combine(exchange(shard, "inner"), [], all_rows, slots)
    parts = scatter_slots(project_out(scatter_slots(pieces, 1), w_out, [w_up]), 0)

    tiles = w_gate.shape[1] // LANES
    half = (tiles + 1) // 2
    span = tiles * 9 // 28
    first = half * LANES
    starts = [0, span * LANES, (span + max(span, half - span + 1)) * LANES, tiles * LANES]
    spans = [(a, b - a) for a, b in zip(starts, starts[1:])]
    one, updated, scaled, down_one = first_gate_up(
        rows, ffn_gain, parts, w_gate, w_up, w_down, spans[0], [], first, own_rows
    )
    two, down_two = second_gate_up(scaled, w_gate, w_up, w_down, spans[1], first)
    steps = steps_up(lax.axis_size("inner"))
    for step in steps[:-1]:
        one = pair_sum(one, swap_with(one, "inner", step))
        two = pair_sum(two, swap_with(two, "inner", step))
    (down_three,) = load(w_down, after=two, spans=[spans[2]])
    part, scale = first_down(
        one, swap_with(one, "inner", steps[-1]), down_one, down_two, down_three
    )
    pieces = second_down(
        two, swap_with(two, "inner", steps[-1]), down_two, down_three, part, scale, slots
    )
    parts = scatter_slots(pieces, 0)
    down_sum = sum(p.astype(jnp.float32) for p in parts)
    return (updated + down_sum).astype(jnp.bfloat16)


def solution(mesh):
    in_specs = (
        P(("groups", "tensor"), "inner"),
        P("inner"),
        P("inner"),
        P("inner", "tensor"),
        P("inner", "tensor"),
        P("tensor", "inner"),
        P("inner", "tensor"),
        P("inner", "tensor"),
        P("tensor", "inner"),
        P(("groups", "tensor"), "inner", None, None),
        P(("groups", "tensor"), "inner", None, None),
        P("groups"),
    )
    out_specs = P(("groups", "tensor"), "inner")
    return jax.shard_map(local, mesh=mesh, in_specs=in_specs, out_specs=out_specs, check_vma=False)
```

```python
import functools
import math

import jax
import jax.numpy as jnp
from jax import lax
from jax.experimental import pallas as pl
from jax.experimental.pallas import tpu as pltpu
from jax.sharding import PartitionSpec as P

D = 8192
HEADS = 32
KV_HEADS = 4
HEAD_DIM = 128
GROUP = HEADS // KV_HEADS
LANES = 128
MIB = 2**20
COPIES = 4

epsilon = 1e-05
rope_base = 500000.0

in_vmem = pl.BlockSpec(memory_space=pltpu.VMEM)
in_smem = pl.BlockSpec(memory_space=pltpu.SMEM)
in_place = pl.BlockSpec(memory_space=pl.ANY)


def swap_with(value, axis, step):
    count = lax.axis_size(axis)
    return lax.ppermute(value, axis, [(i, i ^ step) for i in range(count)])


def exchange(value, axis):
    count = lax.axis_size(axis)
    got = {k: swap_with(value, axis, k) for k in reversed(range(1, count))}
    return [value] + [got[k] for k in range(1, count)]


def scatter_slots(pieces, cross):
    count = lax.axis_size("tensor")
    width = lax.axis_size("inner")
    got = [pieces[0]]
    for k in range(1, count):
        pairs = [
            (t * width + i, (t ^ k) * width + (i ^ cross))
            for t in range(count)
            for i in range(width)
        ]
        got.append(lax.ppermute(pieces[k], ("tensor", "inner"), pairs))
    return got


def steps_up(count):
    return [1 << n for n in range(count.bit_length() - 1)]


def params(mib):
    return pltpu.CompilerParams(vmem_limit_bytes=mib * MIB)


def resident(weight):
    return pltpu.with_memory_space_constraint(weight, pltpu.VMEM)


def in_hbm(weight):
    return pltpu.with_memory_space_constraint(weight, pltpu.HBM)


def product_cost(depth, columns):
    return pl.CostEstimate(
        flops=16 * depth * columns, bytes_accessed=2 * depth * columns, transcendentals=0
    )


def tile_of(columns):
    for tile in (1792, 1024, 896, 512, 256, 128):
        if columns % tile == 0:
            return tile
    return columns


def product_tiles(left, weight_ref, store, first=0, columns=None):
    columns = columns or weight_ref.shape[1]
    tile = tile_of(columns)

    @pl.loop(0, columns // tile)
    def _(step):
        start = pl.multiple_of(step * tile, tile)
        span = pl.ds(pl.multiple_of(first + start, math.gcd(first, tile)), tile)
        store(
            start,
            tile,
            jnp.dot(left, weight_ref[:, span], preferred_element_type=jnp.float32),
        )


def three_parts(value):
    high = value.astype(jnp.bfloat16).astype(jnp.float32)
    rest = value - high
    middle = rest.astype(jnp.bfloat16).astype(jnp.float32)
    return high, middle, rest - middle


def spread(parts, lanes, first):
    out = 0.0
    for n, part in enumerate(parts):
        out = out + jnp.where(lanes == first + n, part, 0.0)
    return out


def squares_block(total):
    lanes = lax.broadcasted_iota(jnp.int32, (total.shape[0], LANES), 1)
    return spread(three_parts(total), lanes, lax.axis_index("inner") * 4)


def copies_of(source, start, target, sems):
    size = target.shape[0]
    cuts = COPIES if len(target.shape) > 1 and size % (16 * COPIES) == 0 else 1
    each = size // cuts
    return [
        pltpu.make_async_copy(
            source.at[pl.ds(start + m * each, each)], target.at[pl.ds(m * each, each)], sems.at[m]
        )
        for m in range(cuts)
    ]


def load_kernel(spans, *refs):
    count = len(spans)
    outs = refs[count + 1 : 2 * count + 1]
    sems = refs[-1]
    copies = []
    for n, (start, _) in enumerate(spans):
        copies += copies_of(refs[n], start, outs[n], sems.at[n])
    for copy in copies:
        copy.start()
    for copy in copies:
        copy.wait()


def load(*arrays, after, spans=None):
    spans = spans or [(0, a.shape[0]) for a in arrays]
    shapes = [(size,) + a.shape[1:] for a, (_, size) in zip(arrays, spans)]
    return pl.pallas_call(
        functools.partial(load_kernel, spans),
        out_shape=tuple(pltpu.VMEM(shape, a.dtype) for shape, a in zip(shapes, arrays)),
        in_specs=[in_place] * (len(arrays) + 1),
        out_specs=tuple(in_vmem for _ in arrays),
        cost_estimate=pl.CostEstimate(
            flops=0, bytes_accessed=2 * sum(math.prod(shape) for shape in shapes), transcendentals=0
        ),
        scratch_shapes=[pltpu.SemaphoreType.DMA((len(arrays), COPIES))],
        compiler_params=params(1),
        name="load",
    )(*[in_hbm(a) for a in arrays], after)


def join_rows(refs, target):
    rows = refs[0].shape[0]
    for n, ref in enumerate(refs):
        target[n * rows : (n + 1) * rows, :] = ref[...].astype(jnp.float32)
    return target[...]


def part_rows(source, refs):
    rows = refs[0].shape[0]
    for n, ref in enumerate(refs):
        ref[...] = source[n * rows : (n + 1) * rows, :].astype(ref.dtype)


def qkv_kernel(slots, gain_ref, wq_ref, wkv_ref, *refs):
    rows_ref = refs[slots]
    out_s, rows_s = refs[-2:]
    wide = join_rows(refs[:slots][::-1], rows_s)
    rows_ref[...] = wide
    total = jnp.sum(wide * wide, axis=1, keepdims=True)
    scaled = (wide * gain_ref[...].astype(jnp.float32)).astype(jnp.bfloat16)
    query_cols = wq_ref.shape[1]
    kv_cols = wkv_ref.shape[1]

    def store_query(start, size, value):
        out_s[:, pl.ds(start, size)] = value

    product_tiles(scaled, wq_ref, store_query)
    out_s[:, query_cols : query_cols + kv_cols] = jnp.dot(
        scaled, wkv_ref[...], preferred_element_type=jnp.float32
    )
    out_s[:, query_cols + kv_cols :] = squares_block(total)
    part_rows(out_s, refs[slots + 1 : 2 * slots + 1])


def project_qkv(rows, gain, w_query, w_kv):
    slots = len(rows)
    own_rows, depth = rows[0].shape
    columns = w_query.shape[1] + w_kv.shape[1] + LANES
    return pl.pallas_call(
        functools.partial(qkv_kernel, slots),
        out_shape=(
            jax.ShapeDtypeStruct((own_rows * slots, depth), jnp.float32),
            *[jax.ShapeDtypeStruct((own_rows, columns), jnp.bfloat16)] * slots,
        ),
        in_specs=[in_vmem] * (3 + slots),
        out_specs=(in_vmem,) * (1 + slots),
        scratch_shapes=[
            pltpu.VMEM((own_rows * slots, columns), jnp.float32),
            pltpu.VMEM((own_rows * slots, depth), jnp.float32),
        ],
        compiler_params=params(2),
        name="project_qkv",
    )(gain, resident(w_query), resident(w_kv), *rows[::-1])


def stack_kernel(*refs):
    refs[-2][...] = join_rows(refs[:-2][::-1], refs[-1]).astype(refs[-2].dtype)


def stack(pieces):
    shape = (len(pieces) * pieces[0].shape[0], pieces[0].shape[1])
    return pl.pallas_call(
        stack_kernel,
        out_shape=jax.ShapeDtypeStruct(shape, pieces[0].dtype),
        in_specs=[in_vmem] * len(pieces),
        out_specs=in_vmem,
        scratch_shapes=[pltpu.VMEM(shape, jnp.float32)],
        compiler_params=params(1),
        name="stack",
    )(*pieces[::-1])


def attend_kernel(
    slots,
    shards,
    lengths_ref,
    cosine_ref,
    sine_ref,
    key_ref,
    value_ref,
    *refs,
):
    parts = refs[:shards]
    out_ref, query_s, kv_s, kv_wide_s, mixed_s, stats_s = refs[shards:]
    all_rows = parts[0].shape[0]
    own_rows = all_rows // slots
    here = HEADS // slots
    query_cols = here * HEAD_DIM
    kv_cols = 2 * KV_HEADS * HEAD_DIM // slots
    columns = query_cols + kv_cols
    tensor_index = lax.axis_index("tensor")
    inner_index = lax.axis_index("inner")
    positions = key_ref.shape[1] // KV_HEADS

    joined = functools.reduce(jnp.add, [ref[...].astype(jnp.float32) for ref in parts])
    squares = jnp.sum(joined[:, columns:], axis=1, keepdims=True)
    joined = joined[:, :columns] * lax.rsqrt(squares / D + epsilon)
    cosine = cosine_ref[...]
    sine = sine_ref[...]

    def rotate(block):
        count = block.shape[0]
        even = lax.broadcasted_iota(jnp.int32, block.shape, 1) % 2 == 0
        other = jnp.where(
            even, pltpu.roll(block, HEAD_DIM - 1, axis=1), pltpu.roll(block, 1, axis=1)
        )
        return block * cosine[:count] + other * sine[:count]

    for j in range(here):
        block = rotate(joined[:, j * HEAD_DIM : (j + 1) * HEAD_DIM])
        query_s[j * all_rows : (j + 1) * all_rows, :] = block
    for s in range(slots):
        kv_s[s] = joined[s * own_rows : (s + 1) * own_rows, query_cols:]
    for d in range(slots):
        kv_wide_s[:, d * kv_cols : (d + 1) * kv_cols] = kv_s[d ^ tensor_index]
    new_keys = []
    new_values = []
    for g in range(KV_HEADS):
        block = kv_wide_s[:, g * HEAD_DIM : (g + 1) * HEAD_DIM]
        new_keys.append(rotate(block).astype(jnp.bfloat16).astype(jnp.float32))
        block = kv_wide_s[:, (KV_HEADS + g) * HEAD_DIM : (KV_HEADS + g + 1) * HEAD_DIM]
        new_values.append(block.astype(jnp.bfloat16).astype(jnp.float32))

    score_scale = HEAD_DIM ** (-0.5)
    row = lax.broadcasted_iota(jnp.int32, (HEADS, 1), 0)
    head = ((row % slots) ^ tensor_index) * here + row // slots
    kv_head = head // GROUP
    column = lax.broadcasted_iota(jnp.int32, (1, positions * KV_HEADS), 1)
    place = column // KV_HEADS + inner_index * positions
    column_head = column % KV_HEADS
    lanes = lax.broadcasted_iota(jnp.int32, (HEADS, LANES), 1)
    for r in range(own_rows):
        queries = query_s[pl.ds(r, HEADS, stride=own_rows), :].astype(jnp.bfloat16)
        scores = (
            lax.dot_general(
                queries,
                key_ref[r],
                (((1,), (1,)), ((), ())),
                preferred_element_type=jnp.float32,
            )
            * score_scale
        )
        used = jnp.where(place < lengths_ref[r : r + 1, 0:1], column_head, -1)
        masked = jnp.where(used == kv_head, scores, -1e30)
        key_rows = 0.0
        value_rows = 0.0
        for g in range(KV_HEADS):
            key_rows = key_rows + jnp.where(kv_head == g, new_keys[g][r : r + 1], 0.0)
            value_rows = value_rows + jnp.where(kv_head == g, new_values[g][r : r + 1], 0.0)
        new_score = (
            jnp.sum(queries.astype(jnp.float32) * key_rows, axis=1, keepdims=True) * score_scale
        )
        new_score = jnp.where(inner_index == 0, new_score, -1e30)
        peak = jnp.maximum(jnp.max(masked, axis=1, keepdims=True), new_score)
        weights = jnp.exp(masked - peak)
        new_weight = jnp.exp(new_score - peak)
        totals = jnp.sum(weights, axis=1, keepdims=True) + new_weight
        mixture = jnp.dot(
            weights.astype(jnp.bfloat16), value_ref[r], preferred_element_type=jnp.float32
        )
        mixture = mixture + new_weight.astype(jnp.bfloat16).astype(jnp.float32) * value_rows
        mixed_s[pl.ds(r, HEADS, stride=own_rows), :] = mixture
        stats_s[pl.ds(r, HEADS, stride=own_rows), :] = spread(
            three_parts(peak), lanes, 0
        ) + spread(three_parts(totals), lanes, 4)
    out_ref[:, :HEAD_DIM] = mixed_s[...].astype(jnp.bfloat16)
    out_ref[:, HEAD_DIM:] = stats_s[...].astype(jnp.bfloat16)


def attend(lengths, cosine, sine, parts, keys, values, slots):
    own_rows = parts[0].shape[0] // slots
    kv_cols = 2 * KV_HEADS * HEAD_DIM // slots
    return pl.pallas_call(
        functools.partial(attend_kernel, slots, len(parts)),
        out_shape=jax.ShapeDtypeStruct((own_rows * HEADS, HEAD_DIM + LANES), jnp.bfloat16),
        in_specs=[in_vmem] * (5 + len(parts)),
        out_specs=in_vmem,
        scratch_shapes=[
            pltpu.VMEM((own_rows * HEADS, HEAD_DIM), jnp.float32),
            pltpu.VMEM((slots, own_rows, kv_cols), jnp.float32),
            pltpu.VMEM((own_rows, slots * kv_cols), jnp.float32),
            pltpu.VMEM((own_rows * HEADS, HEAD_DIM), jnp.float32),
            pltpu.VMEM((own_rows * HEADS, LANES), jnp.float32),
        ],
        compiler_params=params(6),
        name="attend",
    )(lengths, cosine, sine, resident(keys), resident(values), *parts[::-1])


def combine_kernel(shards, slots, *refs):
    ins = refs[:shards]
    out_s = refs[-1]
    all_rows = out_s.shape[0]
    peaks = []
    totals = []
    for ref in ins:
        stats = ref[:, HEAD_DIM:].astype(jnp.float32)
        peaks.append(stats[:, 0:1] + stats[:, 1:2] + stats[:, 2:3])
        totals.append(stats[:, 4:5] + stats[:, 5:6] + stats[:, 6:7])
    top = functools.reduce(jnp.maximum, peaks)
    mixed = 0.0
    denominator = 0.0
    for ref, peak, total in zip(ins, peaks, totals):
        factor = jnp.exp(peak - top)
        mixed = mixed + factor * ref[:, :HEAD_DIM].astype(jnp.float32)
        denominator = denominator + factor * total
    attended = mixed / denominator
    for j in range(attended.shape[0] // all_rows):
        block = attended[j * all_rows : (j + 1) * all_rows]
        out_s[:, j * HEAD_DIM : (j + 1) * HEAD_DIM] = block
    part_rows(out_s, refs[-1 - slots : -1])


def combine(parts, later, all_rows, slots):
    count = len(parts)
    columns = parts[0].shape[0] // all_rows * HEAD_DIM
    return pl.pallas_call(
        functools.partial(combine_kernel, count, slots),
        out_shape=(jax.ShapeDtypeStruct((all_rows // slots, columns), jnp.bfloat16),) * slots,
        in_specs=[in_vmem] * count + [in_place] * len(later),
        out_specs=(in_vmem,) * slots,
        scratch_shapes=[pltpu.VMEM((all_rows, columns), jnp.float32)],
        compiler_params=params(2),
        name="combine",
    )(*parts[::-1], *[resident(w) for w in later])


def turned(block, step, own_rows):
    count = block.shape[0]
    span = step * own_rows
    row = lax.broadcasted_iota(jnp.int32, (count, 1), 0)
    return jnp.where(
        (row // span) % 2 == 0,
        pltpu.roll(block, count - span, axis=0),
        pltpu.roll(block, span, axis=0),
    )


def out_kernel(slots, later, weight_ref, *refs):
    pieces = refs[:slots][::-1]
    outs = refs[slots + later : 2 * slots + later]
    left_s = refs[-1]
    own_rows = pieces[0].shape[0]
    rows = left_s.shape[0]
    lefts = [join_rows(pieces, left_s)]
    for k in range(1, slots):
        low = k & -k
        lefts.append(turned(lefts[k ^ low], low, own_rows))
    left = jnp.concatenate(lefts, axis=0).astype(jnp.bfloat16)

    def store(start, size, value):
        for k, ref in enumerate(outs):
            ref[:, pl.ds(start, size)] = value[k * rows : (k + 1) * rows].astype(jnp.bfloat16)

    product_tiles(left, weight_ref, store)


def project_out(pieces, weight, later):
    slots = len(pieces)
    own_rows, depth = pieces[0].shape
    shape = jax.ShapeDtypeStruct((own_rows * slots, weight.shape[1]), jnp.bfloat16)
    return pl.pallas_call(
        functools.partial(out_kernel, slots, len(later)),
        out_shape=(shape,) * slots,
        in_specs=[in_vmem] * (1 + slots) + [in_place] * len(later),
        out_specs=(in_vmem,) * slots,
        scratch_shapes=[pltpu.VMEM((own_rows * slots, depth), jnp.float32)],
        compiler_params=params(3),
        name="project_out",
    )(resident(weight), *pieces[::-1], *[resident(w) for w in later])


def pair_kernel(first_ref, second_ref, out_ref):
    total = first_ref[...].astype(jnp.float32) + second_ref[...].astype(jnp.float32)
    out_ref[...] = total.astype(jnp.bfloat16)


def pair_sum(first, second):
    return pl.pallas_call(
        pair_kernel,
        out_shape=jax.ShapeDtypeStruct(first.shape, first.dtype),
        in_specs=[in_vmem] * 2,
        out_specs=in_vmem,
        compiler_params=params(2),
        name="pair_sum",
    )(first, second)


def gate_up_tiles(scaled, gate_ref, up_ref, out_ref, first, count):
    def store(offset):
        def place(start, size, value):
            start = pl.multiple_of(offset + start, math.gcd(offset, size))
            out_ref[:, pl.ds(start, size)] = value.astype(jnp.bfloat16)

        return place

    product_tiles(scaled, gate_ref, store(0), first, count)
    product_tiles(scaled, up_ref, store(count), first, count)


def first_gate_up_kernel(
    slots, count, start, rows_ref, gain_ref, gate_ref, up_ref, down_ref, *refs
):
    parts = refs[:slots]
    out_ref, updated_ref, scaled_ref, loaded_ref, sems = refs[-5:]
    copies = copies_of(down_ref, start, loaded_ref, sems)
    for copy in copies:
        copy.start()
    own_rows = updated_ref.shape[0]
    total = functools.reduce(jnp.add, [ref[...].astype(jnp.float32) for ref in parts])
    updated = (rows_ref[...] + total).astype(jnp.bfloat16)
    wide = updated.astype(jnp.float32)
    updated_ref[...] = wide[:own_rows]
    squares = jnp.sum(wide * wide, axis=1, keepdims=True)
    out_ref[:, 2 * count :] = squares_block(squares).astype(jnp.bfloat16)
    scaled = (wide * gain_ref[...].astype(jnp.float32)).astype(jnp.bfloat16)
    scaled_ref[...] = scaled
    gate_up_tiles(scaled, gate_ref, up_ref, out_ref, 0, count)
    for copy in copies:
        copy.wait()


def first_gate_up(rows, gain, parts, w_gate, w_up, w_down, span, later, count, own_rows):
    slots = len(parts)
    start, size = span
    return pl.pallas_call(
        functools.partial(first_gate_up_kernel, slots, count, start),
        out_shape=(
            jax.ShapeDtypeStruct((rows.shape[0], 2 * count + LANES), jnp.bfloat16),
            jax.ShapeDtypeStruct((own_rows, rows.shape[1]), jnp.float32),
            jax.ShapeDtypeStruct(rows.shape, jnp.bfloat16),
            pltpu.VMEM((size, w_down.shape[1]), w_down.dtype),
        ),
        in_specs=[in_vmem] * 4 + [in_place] + [in_vmem] * slots + [in_place] * len(later),
        out_specs=(in_vmem,) * 4,
        scratch_shapes=[pltpu.SemaphoreType.DMA((COPIES,))],
        compiler_params=params(3),
        cost_estimate=product_cost(w_gate.shape[0], 2 * count),
        name="first_gate_up",
    )(
        rows,
        gain,
        resident(w_gate),
        resident(w_up),
        in_hbm(w_down),
        *parts[::-1],
        *[resident(w) for w in later],
    )


def second_gate_up_kernel(
    first, count, start, scaled_ref, gate_ref, up_ref, down_ref, out_ref, loaded_ref, sems
):
    copies = copies_of(down_ref, start, loaded_ref, sems)
    for copy in copies:
        copy.start()
    gate_up_tiles(scaled_ref[...], gate_ref, up_ref, out_ref, first, count)
    for copy in copies:
        copy.wait()


def second_gate_up(scaled, w_gate, w_up, w_down, span, first):
    count = w_gate.shape[1] - first
    start, size = span
    return pl.pallas_call(
        functools.partial(second_gate_up_kernel, first, count, start),
        out_shape=(
            jax.ShapeDtypeStruct((scaled.shape[0], 2 * count), jnp.bfloat16),
            pltpu.VMEM((size, w_down.shape[1]), w_down.dtype),
        ),
        in_specs=[in_vmem] * 3 + [in_place],
        out_specs=(in_vmem,) * 2,
        scratch_shapes=[pltpu.SemaphoreType.DMA((COPIES,))],
        compiler_params=params(3),
        cost_estimate=product_cost(w_gate.shape[0], 2 * count),
        name="second_gate_up",
    )(scaled, resident(w_gate), resident(w_up), in_hbm(w_down))


def hidden_of(near_ref, far_ref, scale, count):
    def total(start):
        span = slice(start, start + count)
        return (near_ref[:, span].astype(jnp.float32) + far_ref[:, span].astype(jnp.float32)) * scale

    gate = total(0)
    return (gate / (1.0 + jnp.exp(-gate)) * total(count)).astype(jnp.bfloat16)


def first_down_kernel(near_ref, far_ref, one_ref, two_ref, later_ref, out_ref, scale_ref):
    del later_ref
    cut = one_ref.shape[0]
    count = (near_ref.shape[1] - LANES) // 2
    squares = jnp.sum(
        near_ref[:, 2 * count :].astype(jnp.float32) + far_ref[:, 2 * count :].astype(jnp.float32),
        axis=1,
        keepdims=True,
    )
    scale = lax.rsqrt(squares / D + epsilon)
    scale_ref[...] = jnp.broadcast_to(scale, scale_ref.shape)
    hidden = hidden_of(near_ref, far_ref, scale, count)
    lower_ref = two_ref.at[: count - cut]

    def store(start, size, value):
        span = pl.ds(start, size)
        out_ref[:, span] = value + jnp.dot(
            hidden[:, cut:], lower_ref[:, span], preferred_element_type=jnp.float32
        )

    product_tiles(hidden[:, :cut], one_ref, store)


def first_down(near, far, one, two, later):
    rows = near.shape[0]
    columns = one.shape[1]
    return pl.pallas_call(
        first_down_kernel,
        out_shape=(
            jax.ShapeDtypeStruct((rows, columns), jnp.float32),
            jax.ShapeDtypeStruct((rows, LANES), jnp.float32),
        ),
        in_specs=[in_vmem] * 4 + [in_place],
        out_specs=(in_vmem,) * 2,
        compiler_params=params(3),
        cost_estimate=product_cost((near.shape[1] - LANES) // 2, columns),
        name="first_down",
    )(near, far, resident(one), resident(two), resident(later))


def second_down_kernel(near_ref, far_ref, two_ref, three_ref, part_ref, scale_ref, *refs):
    out_s = refs[-1]
    count = near_ref.shape[1] // 2
    cut = count - three_ref.shape[0]
    hidden = hidden_of(near_ref, far_ref, scale_ref[:, 0:1], count)
    upper_ref = two_ref.at[two_ref.shape[0] - cut :]

    def store(start, size, value):
        span = pl.ds(start, size)
        out_s[:, span] = part_ref[:, span] + (
            value
            + jnp.dot(hidden[:, :cut], upper_ref[:, span], preferred_element_type=jnp.float32)
        )

    product_tiles(hidden[:, cut:], three_ref, store)
    part_rows(out_s, refs[:-1])


def second_down(near, far, two, three, part, scale, slots):
    rows, columns = part.shape
    return pl.pallas_call(
        second_down_kernel,
        out_shape=(jax.ShapeDtypeStruct((rows // slots, columns), jnp.bfloat16),) * slots,
        in_specs=[in_vmem] * 6,
        out_specs=(in_vmem,) * slots,
        scratch_shapes=[pltpu.VMEM(part.shape, jnp.float32)],
        compiler_params=params(3),
        name="second_down",
    )(near, far, resident(two), resident(three), part, scale)


def rotation_tables(positions, repeats):
    inverse = jnp.exp(
        (jnp.arange(HEAD_DIM) // 2).astype(jnp.float32) * (-2.0 / HEAD_DIM) * math.log(rope_base)
    )
    angles = positions[:, None] * inverse[None, :]
    sign = jnp.where(jnp.arange(HEAD_DIM) % 2 == 0, -1.0, 1.0)
    return (
        jnp.tile(jnp.cos(angles), (repeats, 1)),
        jnp.tile(jnp.sin(angles) * sign[None, :], (repeats, 1)),
    )


def local(
    states,
    attn_gain,
    ffn_gain,
    w_query,
    w_kv,
    w_out,
    w_gate,
    w_up,
    w_down,
    key_cache,
    value_cache,
    lengths,
):
    tensor_index = lax.axis_index("tensor")
    slots = lax.axis_size("tensor")
    own_rows = states.shape[0]
    all_rows = own_rows * slots

    got = exchange(states, "tensor")
    own, attn_gain, ffn_gain, w_kv, w_query = load(
        states, attn_gain, ffn_gain, w_kv, w_query, after=states
    )
    rows, *pieces = project_qkv([own] + got[1:], attn_gain[None, :], w_query, w_kv)

    rows, lengths = lax.optimization_barrier((rows, lengths))
    my_lengths = lax.dynamic_slice_in_dim(lengths, tensor_index * own_rows, own_rows, 0)
    cosine, sine = rotation_tables(my_lengths.astype(jnp.float32), slots)
    my_lengths = jnp.broadcast_to(my_lengths[:, None], (own_rows, LANES))
    flat = (own_rows, key_cache.shape[1] * KV_HEADS, HEAD_DIM)
    keys, values = load(key_cache.reshape(flat), value_cache.reshape(flat), after=rows)
    joined = stack(scatter_slots(pieces, 1))
    joined, keys, values = lax.optimization_barrier((joined, keys, values))
    (w_out,) = load(w_out, after=joined)
    parts, w_out = lax.optimization_barrier((exchange(joined, "inner")[::-1], w_out))
    shard = attend(my_lengths, cosine, sine, parts, keys, values, slots)

    pieces = combine(exchange(shard, "inner"), [], all_rows, slots)
    parts = scatter_slots(project_out(scatter_slots(pieces, 1), w_out, [w_up]), 0)

    tiles = w_gate.shape[1] // LANES
    half = (tiles + 1) // 2
    first = half * LANES
    span = tiles // 4
    starts = [0, span * LANES, (span + max(tiles * 9 // 28, half - span + 1)) * LANES, tiles * LANES]
    spans = [(a, b - a) for a, b in zip(starts, starts[1:])]
    one, updated, scaled, down_one = first_gate_up(
        rows, ffn_gain[None, :], parts, w_gate, w_up, w_down, spans[0], [], first, own_rows
    )
    two, down_two = second_gate_up(scaled, w_gate, w_up, w_down, spans[1], first)
    steps = steps_up(lax.axis_size("inner"))
    for step in steps[:-1]:
        one = pair_sum(one, swap_with(one, "inner", step))
        two = pair_sum(two, swap_with(two, "inner", step))
    (down_three,) = load(w_down, after=two, spans=[spans[2]])
    part, scale = first_down(
        one, swap_with(one, "inner", steps[-1]), down_one, down_two, down_three
    )
    pieces = second_down(
        two, swap_with(two, "inner", steps[-1]), down_two, down_three, part, scale, slots
    )
    parts = scatter_slots(pieces, 0)
    down_sum = sum(p.astype(jnp.float32) for p in parts[::-1])
    return (updated + down_sum).astype(jnp.bfloat16)


def solution(mesh):
    in_specs = (
        P(("groups", "tensor"), "inner"),
        P("inner"),
        P("inner"),
        P("inner", "tensor"),
        P("inner", "tensor"),
        P("tensor", "inner"),
        P("inner", "tensor"),
        P("inner", "tensor"),
        P("tensor", "inner"),
        P(("groups", "tensor"), "inner", None, None),
        P(("groups", "tensor"), "inner", None, None),
        P("groups"),
    )
    out_specs = P(("groups", "tensor"), "inner")
    return jax.shard_map(local, mesh=mesh, in_specs=in_specs, out_specs=out_specs, check_vma=False)
```

```python
import functools
import math

import jax
import jax.numpy as jnp
from jax import lax
from jax.experimental import pallas as pl
from jax.experimental.pallas import tpu as pltpu
from jax.sharding import PartitionSpec as P

D = 8192
HEADS = 32
KV_HEADS = 4
HEAD_DIM = 128
GROUP = HEADS // KV_HEADS
LANES = 128
MIB = 2**20
COPIES = 4

epsilon = 1e-05
rope_base = 500000.0

in_vmem = pl.BlockSpec(memory_space=pltpu.VMEM)
in_smem = pl.BlockSpec(memory_space=pltpu.SMEM)
in_place = pl.BlockSpec(memory_space=pl.ANY)


def swap_with(value, axis, step):
    count = lax.axis_size(axis)
    return lax.ppermute(value, axis, [(i, i ^ step) for i in range(count)])


def exchange(value, axis):
    count = lax.axis_size(axis)
    got = {k: swap_with(value, axis, k) for k in reversed(range(1, count))}
    return [value] + [got[k] for k in range(1, count)]


def scatter_slots(pieces, cross):
    count = lax.axis_size("tensor")
    width = lax.axis_size("inner")
    got = [pieces[0]]
    for k in range(1, count):
        pairs = [
            (t * width + i, (t ^ k) * width + (i ^ cross))
            for t in range(count)
            for i in range(width)
        ]
        got.append(lax.ppermute(pieces[k], ("tensor", "inner"), pairs))
    return got


def steps_up(count):
    return [1 << n for n in range(count.bit_length() - 1)]


def params(mib):
    return pltpu.CompilerParams(vmem_limit_bytes=mib * MIB)


def resident(weight):
    return pltpu.with_memory_space_constraint(weight, pltpu.VMEM)


def in_hbm(weight):
    return pltpu.with_memory_space_constraint(weight, pltpu.HBM)


def product_cost(depth, columns):
    return pl.CostEstimate(
        flops=16 * depth * columns, bytes_accessed=2 * depth * columns, transcendentals=0
    )


def tile_of(columns):
    for tile in (1792, 1024, 896, 512, 256, 128):
        if columns % tile == 0:
            return tile
    return columns


def product_tiles(left, weight_ref, store, first=0, columns=None):
    columns = columns or weight_ref.shape[1]
    tile = tile_of(columns)

    @pl.loop(0, columns // tile)
    def _(step):
        start = pl.multiple_of(step * tile, tile)
        span = pl.ds(pl.multiple_of(first + start, math.gcd(first, tile)), tile)
        store(
            start,
            tile,
            jnp.dot(left, weight_ref[:, span], preferred_element_type=jnp.float32),
        )


def three_parts(value):
    high = value.astype(jnp.bfloat16).astype(jnp.float32)
    rest = value - high
    middle = rest.astype(jnp.bfloat16).astype(jnp.float32)
    return high, middle, rest - middle


def spread(parts, lanes, first):
    out = 0.0
    for n, part in enumerate(parts):
        out = out + jnp.where(lanes == first + n, part, 0.0)
    return out


def squares_block(total):
    lanes = lax.broadcasted_iota(jnp.int32, (total.shape[0], LANES), 1)
    return spread(three_parts(total), lanes, lax.axis_index("inner") * 4)


def copies_of(source, start, target, sems):
    size = target.shape[0]
    cuts = COPIES if len(target.shape) > 1 and size % (16 * COPIES) == 0 else 1
    each = size // cuts
    return [
        pltpu.make_async_copy(
            source.at[pl.ds(start + m * each, each)], target.at[pl.ds(m * each, each)], sems.at[m]
        )
        for m in range(cuts)
    ]


def load_kernel(spans, *refs):
    count = len(spans)
    outs = refs[count + 1 : 2 * count + 1]
    sems = refs[-1]
    copies = []
    for n, (start, _) in enumerate(spans):
        copies += copies_of(refs[n], start, outs[n], sems.at[n])
    for copy in copies:
        copy.start()
    for copy in copies:
        copy.wait()


def load(*arrays, after, spans=None):
    spans = spans or [(0, a.shape[0]) for a in arrays]
    shapes = [(size,) + a.shape[1:] for a, (_, size) in zip(arrays, spans)]
    return pl.pallas_call(
        functools.partial(load_kernel, spans),
        out_shape=tuple(pltpu.VMEM(shape, a.dtype) for shape, a in zip(shapes, arrays)),
        in_specs=[in_place] * (len(arrays) + 1),
        out_specs=tuple(in_vmem for _ in arrays),
        cost_estimate=pl.CostEstimate(
            flops=0, bytes_accessed=2 * sum(math.prod(shape) for shape in shapes), transcendentals=0
        ),
        scratch_shapes=[pltpu.SemaphoreType.DMA((len(arrays), COPIES))],
        compiler_params=params(1),
        name="load",
    )(*[in_hbm(a) for a in arrays], after)


def join_rows(refs, target):
    rows = refs[0].shape[0]
    for n, ref in enumerate(refs):
        target[n * rows : (n + 1) * rows, :] = ref[...].astype(jnp.float32)
    return target[...]


def part_rows(source, refs):
    rows = refs[0].shape[0]
    for n, ref in enumerate(refs):
        ref[...] = source[n * rows : (n + 1) * rows, :].astype(ref.dtype)


def qkv_kernel(slots, gain_ref, wq_ref, wkv_ref, *refs):
    rows_ref = refs[slots]
    out_s, rows_s = refs[-2:]
    wide = join_rows(refs[:slots][::-1], rows_s)
    rows_ref[...] = wide
    total = jnp.sum(wide * wide, axis=1, keepdims=True)
    scaled = (wide * gain_ref[...].astype(jnp.float32)[None, :]).astype(jnp.bfloat16)
    query_cols = wq_ref.shape[1]
    kv_cols = wkv_ref.shape[1]

    def store_query(start, size, value):
        out_s[:, pl.ds(start, size)] = value

    product_tiles(scaled, wq_ref, store_query)
    out_s[:, query_cols : query_cols + kv_cols] = jnp.dot(
        scaled, wkv_ref[...], preferred_element_type=jnp.float32
    )
    out_s[:, query_cols + kv_cols :] = squares_block(total)
    part_rows(out_s, refs[slots + 1 : 2 * slots + 1])


def project_qkv(rows, gain, w_query, w_kv):
    slots = len(rows)
    own_rows, depth = rows[0].shape
    columns = w_query.shape[1] + w_kv.shape[1] + LANES
    return pl.pallas_call(
        functools.partial(qkv_kernel, slots),
        out_shape=(
            jax.ShapeDtypeStruct((own_rows * slots, depth), jnp.float32),
            *[jax.ShapeDtypeStruct((own_rows, columns), jnp.bfloat16)] * slots,
        ),
        in_specs=[in_vmem] * (3 + slots),
        out_specs=(in_vmem,) * (1 + slots),
        scratch_shapes=[
            pltpu.VMEM((own_rows * slots, columns), jnp.float32),
            pltpu.VMEM((own_rows * slots, depth), jnp.float32),
        ],
        compiler_params=params(2),
        name="project_qkv",
    )(gain, resident(w_query), resident(w_kv), *rows[::-1])


def stack_kernel(*refs):
    refs[-2][...] = join_rows(refs[:-2][::-1], refs[-1]).astype(refs[-2].dtype)


def stack(pieces):
    shape = (len(pieces) * pieces[0].shape[0], pieces[0].shape[1])
    return pl.pallas_call(
        stack_kernel,
        out_shape=jax.ShapeDtypeStruct(shape, pieces[0].dtype),
        in_specs=[in_vmem] * len(pieces),
        out_specs=in_vmem,
        scratch_shapes=[pltpu.VMEM(shape, jnp.float32)],
        compiler_params=params(1),
        name="stack",
    )(*pieces[::-1])


def attend_kernel(
    slots,
    shards,
    lengths_ref,
    cosine_ref,
    sine_ref,
    key_ref,
    value_ref,
    *refs,
):
    parts = refs[:shards]
    out_ref, query_s, kv_s, kv_wide_s, mixed_s, stats_s = refs[shards:]
    all_rows = parts[0].shape[0]
    own_rows = all_rows // slots
    here = HEADS // slots
    query_cols = here * HEAD_DIM
    kv_cols = 2 * KV_HEADS * HEAD_DIM // slots
    columns = query_cols + kv_cols
    tensor_index = lax.axis_index("tensor")
    inner_index = lax.axis_index("inner")
    positions = key_ref.shape[1] // KV_HEADS

    joined = functools.reduce(jnp.add, [ref[...].astype(jnp.float32) for ref in parts])
    squares = jnp.sum(joined[:, columns:], axis=1, keepdims=True)
    joined = joined[:, :columns] * lax.rsqrt(squares / D + epsilon)
    cosine = cosine_ref[...]
    sine = sine_ref[...]

    def rotate(block):
        count = block.shape[0]
        even = lax.broadcasted_iota(jnp.int32, block.shape, 1) % 2 == 0
        other = jnp.where(
            even, pltpu.roll(block, HEAD_DIM - 1, axis=1), pltpu.roll(block, 1, axis=1)
        )
        return block * cosine[:count] + other * sine[:count]

    for j in range(here):
        block = rotate(joined[:, j * HEAD_DIM : (j + 1) * HEAD_DIM])
        query_s[j * all_rows : (j + 1) * all_rows, :] = block
    for s in range(slots):
        kv_s[s] = joined[s * own_rows : (s + 1) * own_rows, query_cols:]
    for d in range(slots):
        kv_wide_s[:, d * kv_cols : (d + 1) * kv_cols] = kv_s[d ^ tensor_index]
    new_keys = []
    new_values = []
    for g in range(KV_HEADS):
        block = kv_wide_s[:, g * HEAD_DIM : (g + 1) * HEAD_DIM]
        new_keys.append(rotate(block).astype(jnp.bfloat16).astype(jnp.float32))
        block = kv_wide_s[:, (KV_HEADS + g) * HEAD_DIM : (KV_HEADS + g + 1) * HEAD_DIM]
        new_values.append(block.astype(jnp.bfloat16).astype(jnp.float32))

    score_scale = HEAD_DIM ** (-0.5)
    row = lax.broadcasted_iota(jnp.int32, (HEADS, 1), 0)
    head = ((row % slots) ^ tensor_index) * here + row // slots
    kv_head = head // GROUP
    column = lax.broadcasted_iota(jnp.int32, (1, positions * KV_HEADS), 1)
    place = column // KV_HEADS + inner_index * positions
    column_head = column % KV_HEADS
    lanes = lax.broadcasted_iota(jnp.int32, (HEADS, LANES), 1)
    for r in range(own_rows):
        queries = query_s[pl.ds(r, HEADS, stride=own_rows), :].astype(jnp.bfloat16)
        scores = (
            lax.dot_general(
                queries,
                key_ref[r],
                (((1,), (1,)), ((), ())),
                preferred_element_type=jnp.float32,
            )
            * score_scale
        )
        used = jnp.where(place < lengths_ref[r : r + 1, 0:1], column_head, -1)
        masked = jnp.where(used == kv_head, scores, -1e30)
        key_rows = 0.0
        value_rows = 0.0
        for g in range(KV_HEADS):
            key_rows = key_rows + jnp.where(kv_head == g, new_keys[g][r : r + 1], 0.0)
            value_rows = value_rows + jnp.where(kv_head == g, new_values[g][r : r + 1], 0.0)
        new_score = (
            jnp.sum(queries.astype(jnp.float32) * key_rows, axis=1, keepdims=True) * score_scale
        )
        new_score = jnp.where(inner_index == 0, new_score, -1e30)
        peak = jnp.maximum(jnp.max(masked, axis=1, keepdims=True), new_score)
        weights = jnp.exp(masked - peak)
        new_weight = jnp.exp(new_score - peak)
        totals = jnp.sum(weights, axis=1, keepdims=True) + new_weight
        mixture = jnp.dot(
            weights.astype(jnp.bfloat16), value_ref[r], preferred_element_type=jnp.float32
        )
        mixture = mixture + new_weight.astype(jnp.bfloat16).astype(jnp.float32) * value_rows
        mixed_s[pl.ds(r, HEADS, stride=own_rows), :] = mixture
        stats_s[pl.ds(r, HEADS, stride=own_rows), :] = spread(
            three_parts(peak), lanes, 0
        ) + spread(three_parts(totals), lanes, 4)
    out_ref[:, :HEAD_DIM] = mixed_s[...].astype(jnp.bfloat16)
    out_ref[:, HEAD_DIM:] = stats_s[...].astype(jnp.bfloat16)


def attend(lengths, cosine, sine, parts, keys, values, slots):
    own_rows = parts[0].shape[0] // slots
    kv_cols = 2 * KV_HEADS * HEAD_DIM // slots
    return pl.pallas_call(
        functools.partial(attend_kernel, slots, len(parts)),
        out_shape=jax.ShapeDtypeStruct((own_rows * HEADS, HEAD_DIM + LANES), jnp.bfloat16),
        in_specs=[in_vmem] * (5 + len(parts)),
        out_specs=in_vmem,
        scratch_shapes=[
            pltpu.VMEM((own_rows * HEADS, HEAD_DIM), jnp.float32),
            pltpu.VMEM((slots, own_rows, kv_cols), jnp.float32),
            pltpu.VMEM((own_rows, slots * kv_cols), jnp.float32),
            pltpu.VMEM((own_rows * HEADS, HEAD_DIM), jnp.float32),
            pltpu.VMEM((own_rows * HEADS, LANES), jnp.float32),
        ],
        compiler_params=params(6),
        name="attend",
    )(lengths, cosine, sine, resident(keys), resident(values), *parts[::-1])


def combine_kernel(shards, slots, *refs):
    ins = refs[:shards]
    out_s = refs[-1]
    all_rows = out_s.shape[0]
    peaks = []
    totals = []
    for ref in ins:
        stats = ref[:, HEAD_DIM:].astype(jnp.float32)
        peaks.append(stats[:, 0:1] + stats[:, 1:2] + stats[:, 2:3])
        totals.append(stats[:, 4:5] + stats[:, 5:6] + stats[:, 6:7])
    top = functools.reduce(jnp.maximum, peaks)
    mixed = 0.0
    denominator = 0.0
    for ref, peak, total in zip(ins, peaks, totals):
        factor = jnp.exp(peak - top)
        mixed = mixed + factor * ref[:, :HEAD_DIM].astype(jnp.float32)
        denominator = denominator + factor * total
    attended = mixed / denominator
    for j in range(attended.shape[0] // all_rows):
        block = attended[j * all_rows : (j + 1) * all_rows]
        out_s[:, j * HEAD_DIM : (j + 1) * HEAD_DIM] = block
    part_rows(out_s, refs[-1 - slots : -1])


def combine(parts, later, all_rows, slots):
    count = len(parts)
    columns = parts[0].shape[0] // all_rows * HEAD_DIM
    return pl.pallas_call(
        functools.partial(combine_kernel, count, slots),
        out_shape=(jax.ShapeDtypeStruct((all_rows // slots, columns), jnp.bfloat16),) * slots,
        in_specs=[in_vmem] * count + [in_place] * len(later),
        out_specs=(in_vmem,) * slots,
        scratch_shapes=[pltpu.VMEM((all_rows, columns), jnp.float32)],
        compiler_params=params(2),
        name="combine",
    )(*parts[::-1], *[resident(w) for w in later])


def turned(block, step, own_rows):
    count = block.shape[0]
    span = step * own_rows
    row = lax.broadcasted_iota(jnp.int32, (count, 1), 0)
    return jnp.where(
        (row // span) % 2 == 0,
        pltpu.roll(block, count - span, axis=0),
        pltpu.roll(block, span, axis=0),
    )


def out_kernel(slots, later, weight_ref, *refs):
    pieces = refs[:slots][::-1]
    outs = refs[slots + later : 2 * slots + later]
    left_s = refs[-1]
    own_rows = pieces[0].shape[0]
    rows = left_s.shape[0]
    lefts = [join_rows(pieces, left_s)]
    for k in range(1, slots):
        low = k & -k
        lefts.append(turned(lefts[k ^ low], low, own_rows))
    left = jnp.concatenate(lefts, axis=0).astype(jnp.bfloat16)

    def store(start, size, value):
        for k, ref in enumerate(outs):
            ref[:, pl.ds(start, size)] = value[k * rows : (k + 1) * rows].astype(jnp.bfloat16)

    product_tiles(left, weight_ref, store)


def project_out(pieces, weight, later):
    slots = len(pieces)
    own_rows, depth = pieces[0].shape
    shape = jax.ShapeDtypeStruct((own_rows * slots, weight.shape[1]), jnp.bfloat16)
    return pl.pallas_call(
        functools.partial(out_kernel, slots, len(later)),
        out_shape=(shape,) * slots,
        in_specs=[in_vmem] * (1 + slots) + [in_place] * len(later),
        out_specs=(in_vmem,) * slots,
        scratch_shapes=[pltpu.VMEM((own_rows * slots, depth), jnp.float32)],
        compiler_params=params(3),
        name="project_out",
    )(resident(weight), *pieces[::-1], *[resident(w) for w in later])


def pair_kernel(first_ref, second_ref, out_ref):
    total = first_ref[...].astype(jnp.float32) + second_ref[...].astype(jnp.float32)
    out_ref[...] = total.astype(jnp.bfloat16)


def pair_sum(first, second):
    return pl.pallas_call(
        pair_kernel,
        out_shape=jax.ShapeDtypeStruct(first.shape, first.dtype),
        in_specs=[in_vmem] * 2,
        out_specs=in_vmem,
        compiler_params=params(2),
        name="pair_sum",
    )(first, second)


def gate_up_tiles(scaled, gate_ref, up_ref, out_ref, first, count):
    def store(offset):
        def place(start, size, value):
            start = pl.multiple_of(offset + start, math.gcd(offset, size))
            out_ref[:, pl.ds(start, size)] = value.astype(jnp.bfloat16)

        return place

    product_tiles(scaled, gate_ref, store(0), first, count)
    product_tiles(scaled, up_ref, store(count), first, count)


def first_gate_up_kernel(
    slots, count, start, rows_ref, gain_ref, gate_ref, up_ref, down_ref, *refs
):
    parts = refs[:slots]
    out_ref, updated_ref, scaled_ref, loaded_ref, sems = refs[-5:]
    copies = copies_of(down_ref, start, loaded_ref, sems)
    for copy in copies:
        copy.start()
    own_rows = updated_ref.shape[0]
    total = functools.reduce(jnp.add, [ref[...].astype(jnp.float32) for ref in parts])
    updated = (rows_ref[...] + total).astype(jnp.bfloat16)
    wide = updated.astype(jnp.float32)
    updated_ref[...] = wide[:own_rows]
    squares = jnp.sum(wide * wide, axis=1, keepdims=True)
    out_ref[:, 2 * count :] = squares_block(squares).astype(jnp.bfloat16)
    scaled = (wide * gain_ref[...].astype(jnp.float32)[None, :]).astype(jnp.bfloat16)
    scaled_ref[...] = scaled
    gate_up_tiles(scaled, gate_ref, up_ref, out_ref, 0, count)
    for copy in copies:
        copy.wait()


def first_gate_up(rows, gain, parts, w_gate, w_up, w_down, span, later, count, own_rows):
    slots = len(parts)
    start, size = span
    return pl.pallas_call(
        functools.partial(first_gate_up_kernel, slots, count, start),
        out_shape=(
            jax.ShapeDtypeStruct((rows.shape[0], 2 * count + LANES), jnp.bfloat16),
            jax.ShapeDtypeStruct((own_rows, rows.shape[1]), jnp.float32),
            jax.ShapeDtypeStruct(rows.shape, jnp.bfloat16),
            pltpu.VMEM((size, w_down.shape[1]), w_down.dtype),
        ),
        in_specs=[in_vmem] * 4 + [in_place] + [in_vmem] * slots + [in_place] * len(later),
        out_specs=(in_vmem,) * 4,
        scratch_shapes=[pltpu.SemaphoreType.DMA((COPIES,))],
        compiler_params=params(3),
        cost_estimate=product_cost(w_gate.shape[0], 2 * count),
        name="first_gate_up",
    )(
        rows,
        gain,
        resident(w_gate),
        resident(w_up),
        in_hbm(w_down),
        *parts[::-1],
        *[resident(w) for w in later],
    )


def second_gate_up_kernel(
    first, count, start, scaled_ref, gate_ref, up_ref, down_ref, out_ref, loaded_ref, sems
):
    copies = copies_of(down_ref, start, loaded_ref, sems)
    for copy in copies:
        copy.start()
    gate_up_tiles(scaled_ref[...], gate_ref, up_ref, out_ref, first, count)
    for copy in copies:
        copy.wait()


def second_gate_up(scaled, w_gate, w_up, w_down, span, first):
    count = w_gate.shape[1] - first
    start, size = span
    return pl.pallas_call(
        functools.partial(second_gate_up_kernel, first, count, start),
        out_shape=(
            jax.ShapeDtypeStruct((scaled.shape[0], 2 * count), jnp.bfloat16),
            pltpu.VMEM((size, w_down.shape[1]), w_down.dtype),
        ),
        in_specs=[in_vmem] * 3 + [in_place],
        out_specs=(in_vmem,) * 2,
        scratch_shapes=[pltpu.SemaphoreType.DMA((COPIES,))],
        compiler_params=params(3),
        cost_estimate=product_cost(w_gate.shape[0], 2 * count),
        name="second_gate_up",
    )(scaled, resident(w_gate), resident(w_up), in_hbm(w_down))


def hidden_of(near_ref, far_ref, scale, count):
    def total(start):
        span = slice(start, start + count)
        return (near_ref[:, span].astype(jnp.float32) + far_ref[:, span].astype(jnp.float32)) * scale

    gate = total(0)
    return (gate / (1.0 + jnp.exp(-gate)) * total(count)).astype(jnp.bfloat16)


def first_down_kernel(near_ref, far_ref, one_ref, two_ref, later_ref, out_ref, scale_ref):
    del later_ref
    cut = one_ref.shape[0]
    count = (near_ref.shape[1] - LANES) // 2
    squares = jnp.sum(
        near_ref[:, 2 * count :].astype(jnp.float32) + far_ref[:, 2 * count :].astype(jnp.float32),
        axis=1,
        keepdims=True,
    )
    scale = lax.rsqrt(squares / D + epsilon)
    scale_ref[...] = jnp.broadcast_to(scale, scale_ref.shape)
    hidden = hidden_of(near_ref, far_ref, scale, count)
    lower_ref = two_ref.at[: count - cut]

    def store(start, size, value):
        span = pl.ds(start, size)
        out_ref[:, span] = value + jnp.dot(
            hidden[:, cut:], lower_ref[:, span], preferred_element_type=jnp.float32
        )

    product_tiles(hidden[:, :cut], one_ref, store)


def first_down(near, far, one, two, later):
    rows = near.shape[0]
    columns = one.shape[1]
    return pl.pallas_call(
        first_down_kernel,
        out_shape=(
            jax.ShapeDtypeStruct((rows, columns), jnp.float32),
            jax.ShapeDtypeStruct((rows, LANES), jnp.float32),
        ),
        in_specs=[in_vmem] * 4 + [in_place],
        out_specs=(in_vmem,) * 2,
        compiler_params=params(3),
        cost_estimate=product_cost((near.shape[1] - LANES) // 2, columns),
        name="first_down",
    )(near, far, resident(one), resident(two), resident(later))


def second_down_kernel(near_ref, far_ref, two_ref, three_ref, part_ref, scale_ref, *refs):
    out_s = refs[-1]
    count = near_ref.shape[1] // 2
    cut = count - three_ref.shape[0]
    hidden = hidden_of(near_ref, far_ref, scale_ref[:, 0:1], count)
    upper_ref = two_ref.at[two_ref.shape[0] - cut :]

    def store(start, size, value):
        span = pl.ds(start, size)
        out_s[:, span] = part_ref[:, span] + (
            value
            + jnp.dot(hidden[:, :cut], upper_ref[:, span], preferred_element_type=jnp.float32)
        )

    product_tiles(hidden[:, cut:], three_ref, store)
    part_rows(out_s, refs[:-1])


def second_down(near, far, two, three, part, scale, slots):
    rows, columns = part.shape
    return pl.pallas_call(
        second_down_kernel,
        out_shape=(jax.ShapeDtypeStruct((rows // slots, columns), jnp.bfloat16),) * slots,
        in_specs=[in_vmem] * 6,
        out_specs=(in_vmem,) * slots,
        scratch_shapes=[pltpu.VMEM(part.shape, jnp.float32)],
        compiler_params=params(3),
        name="second_down",
    )(near, far, resident(two), resident(three), part, scale)


def rotation_tables(positions, repeats):
    inverse = jnp.exp(
        (jnp.arange(HEAD_DIM) // 2).astype(jnp.float32) * (-2.0 / HEAD_DIM) * math.log(rope_base)
    )
    angles = positions[:, None] * inverse[None, :]
    sign = jnp.where(jnp.arange(HEAD_DIM) % 2 == 0, -1.0, 1.0)
    return (
        jnp.tile(jnp.cos(angles), (repeats, 1)),
        jnp.tile(jnp.sin(angles) * sign[None, :], (repeats, 1)),
    )


def local(
    states,
    attn_gain,
    ffn_gain,
    w_query,
    w_kv,
    w_out,
    w_gate,
    w_up,
    w_down,
    key_cache,
    value_cache,
    lengths,
):
    tensor_index = lax.axis_index("tensor")
    slots = lax.axis_size("tensor")
    own_rows = states.shape[0]
    all_rows = own_rows * slots

    got = exchange(states, "tensor")
    own, attn_gain, ffn_gain, w_kv, w_query = load(
        states, attn_gain, ffn_gain, w_kv, w_query, after=states
    )
    rows, *pieces = project_qkv([own] + got[1:], attn_gain, w_query, w_kv)

    rows, lengths = lax.optimization_barrier((rows, lengths))
    my_lengths = lax.dynamic_slice_in_dim(lengths, tensor_index * own_rows, own_rows, 0)
    cosine, sine = rotation_tables(my_lengths.astype(jnp.float32), slots)
    my_lengths = jnp.broadcast_to(my_lengths[:, None], (own_rows, LANES))
    flat = (own_rows, key_cache.shape[1] * KV_HEADS, HEAD_DIM)
    keys, values = load(key_cache.reshape(flat), value_cache.reshape(flat), after=rows)
    joined = stack(scatter_slots(pieces, 1))
    joined, keys, values = lax.optimization_barrier((joined, keys, values))
    (w_out,) = load(w_out, after=joined)
    parts, w_out = lax.optimization_barrier((exchange(joined, "inner")[::-1], w_out))
    shard = attend(my_lengths, cosine, sine, parts, keys, values, slots)

    pieces = combine(exchange(shard, "inner"), [], all_rows, slots)
    parts = scatter_slots(project_out(scatter_slots(pieces, 1), w_out, [w_up]), 0)

    tiles = w_gate.shape[1] // LANES
    half = (tiles + 1) // 2
    first = half * LANES
    span = tiles // 4
    starts = [0, span * LANES, (span + max(tiles * 9 // 28, half - span + 1)) * LANES, tiles * LANES]
    spans = [(a, b - a) for a, b in zip(starts, starts[1:])]
    one, updated, scaled, down_one = first_gate_up(
        rows, ffn_gain, parts, w_gate, w_up, w_down, spans[0], [], first, own_rows
    )
    two, down_two = second_gate_up(scaled, w_gate, w_up, w_down, spans[1], first)
    steps = steps_up(lax.axis_size("inner"))
    for step in steps[:-1]:
        one = pair_sum(one, swap_with(one, "inner", step))
        two = pair_sum(two, swap_with(two, "inner", step))
    (down_three,) = load(w_down, after=two, spans=[spans[2]])
    part, scale = first_down(
        one, swap_with(one, "inner", steps[-1]), down_one, down_two, down_three
    )
    pieces = second_down(
        two, swap_with(two, "inner", steps[-1]), down_two, down_three, part, scale, slots
    )
    parts = scatter_slots(pieces, 0)
    down_sum = sum(p.astype(jnp.float32) for p in parts[::-1])
    return (updated + down_sum).astype(jnp.bfloat16)


def solution(mesh):
    in_specs = (
        P(("groups", "tensor"), "inner"),
        P("inner"),
        P("inner"),
        P("inner", "tensor"),
        P("inner", "tensor"),
        P("tensor", "inner"),
        P("inner", "tensor"),
        P("inner", "tensor"),
        P("tensor", "inner"),
        P(("groups", "tensor"), "inner", None, None),
        P(("groups", "tensor"), "inner", None, None),
        P("groups"),
    )
    out_specs = P(("groups", "tensor"), "inner")
    return jax.shard_map(local, mesh=mesh, in_specs=in_specs, out_specs=out_specs, check_vma=False)
```

```python
import functools
import math

import jax
import jax.numpy as jnp
from jax import lax
from jax.experimental import pallas as pl
from jax.experimental.pallas import tpu as pltpu
from jax.sharding import PartitionSpec as P

D = 8192
HEADS = 32
KV_HEADS = 4
HEAD_DIM = 128
GROUP = HEADS // KV_HEADS
LANES = 128
MIB = 2**20
COPIES = 4

epsilon = 1e-05
rope_base = 500000.0

in_vmem = pl.BlockSpec(memory_space=pltpu.VMEM)
in_smem = pl.BlockSpec(memory_space=pltpu.SMEM)
in_place = pl.BlockSpec(memory_space=pl.ANY)


def swap_with(value, axis, step):
    count = lax.axis_size(axis)
    return lax.ppermute(value, axis, [(i, i ^ step) for i in range(count)])


def exchange(value, axis):
    count = lax.axis_size(axis)
    got = {k: swap_with(value, axis, k) for k in reversed(range(1, count))}
    return [value] + [got[k] for k in range(1, count)]


def scatter_slots(pieces, cross):
    count = lax.axis_size("tensor")
    width = lax.axis_size("inner")
    got = [pieces[0]]
    for k in range(1, count):
        pairs = [
            (t * width + i, (t ^ k) * width + (i ^ cross))
            for t in range(count)
            for i in range(width)
        ]
        got.append(lax.ppermute(pieces[k], ("tensor", "inner"), pairs))
    return got


def steps_up(count):
    return [1 << n for n in range(count.bit_length() - 1)]


def params(mib):
    return pltpu.CompilerParams(vmem_limit_bytes=mib * MIB)


def resident(weight):
    return pltpu.with_memory_space_constraint(weight, pltpu.VMEM)


def in_hbm(weight):
    return pltpu.with_memory_space_constraint(weight, pltpu.HBM)


def product_cost(depth, columns):
    return pl.CostEstimate(
        flops=16 * depth * columns, bytes_accessed=2 * depth * columns, transcendentals=0
    )


def tile_of(columns):
    for tile in (1792, 1024, 896, 512, 256, 128):
        if columns % tile == 0:
            return tile
    return columns


def product_tiles(left, weight_ref, store, first=0, columns=None):
    columns = columns or weight_ref.shape[1]
    tile = tile_of(columns)

    @pl.loop(0, columns // tile)
    def _(step):
        start = pl.multiple_of(step * tile, tile)
        span = pl.ds(pl.multiple_of(first + start, math.gcd(first, tile)), tile)
        store(
            start,
            tile,
            jnp.dot(left, weight_ref[:, span], preferred_element_type=jnp.float32),
        )


def three_parts(value):
    high = value.astype(jnp.bfloat16).astype(jnp.float32)
    rest = value - high
    middle = rest.astype(jnp.bfloat16).astype(jnp.float32)
    return high, middle, rest - middle


def spread(parts, lanes, first):
    out = 0.0
    for n, part in enumerate(parts):
        out = out + jnp.where(lanes == first + n, part, 0.0)
    return out


def squares_block(total):
    lanes = lax.broadcasted_iota(jnp.int32, (total.shape[0], LANES), 1)
    return spread(three_parts(total), lanes, lax.axis_index("inner") * 4)


def copies_of(source, start, target, sems):
    size = target.shape[0]
    cuts = COPIES if len(target.shape) > 1 and size % (16 * COPIES) == 0 else 1
    each = size // cuts
    return [
        pltpu.make_async_copy(
            source.at[pl.ds(start + m * each, each)], target.at[pl.ds(m * each, each)], sems.at[m]
        )
        for m in range(cuts)
    ]


def load_kernel(spans, *refs):
    count = len(spans)
    outs = refs[count + 1 : 2 * count + 1]
    sems = refs[-1]
    copies = []
    for n, (start, _) in enumerate(spans):
        copies += copies_of(refs[n], start, outs[n], sems.at[n])
    for copy in copies:
        copy.start()
    for copy in copies:
        copy.wait()


def load(*arrays, after, spans=None):
    spans = spans or [(0, a.shape[0]) for a in arrays]
    shapes = [(size,) + a.shape[1:] for a, (_, size) in zip(arrays, spans)]
    return pl.pallas_call(
        functools.partial(load_kernel, spans),
        out_shape=tuple(pltpu.VMEM(shape, a.dtype) for shape, a in zip(shapes, arrays)),
        in_specs=[in_place] * (len(arrays) + 1),
        out_specs=tuple(in_vmem for _ in arrays),
        cost_estimate=pl.CostEstimate(
            flops=0, bytes_accessed=2 * sum(math.prod(shape) for shape in shapes), transcendentals=0
        ),
        scratch_shapes=[pltpu.SemaphoreType.DMA((len(arrays), COPIES))],
        compiler_params=params(1),
        name="load",
    )(*[in_hbm(a) for a in arrays], after)


def join_rows(refs, target):
    rows = refs[0].shape[0]
    for n, ref in enumerate(refs):
        target[n * rows : (n + 1) * rows, :] = ref[...].astype(jnp.float32)
    return target[...]


def part_rows(source, refs):
    rows = refs[0].shape[0]
    for n, ref in enumerate(refs):
        ref[...] = source[n * rows : (n + 1) * rows, :].astype(ref.dtype)


def qkv_kernel(slots, gain_ref, wq_ref, wkv_ref, *refs):
    rows_ref = refs[slots]
    out_s, rows_s = refs[-2:]
    wide = join_rows(refs[:slots][::-1], rows_s)
    rows_ref[...] = wide
    total = jnp.sum(wide * wide, axis=1, keepdims=True)
    gain = gain_ref[...].astype(jnp.float32)[None, :]
    scaled = (wide * gain).astype(jnp.bfloat16)
    query_cols = wq_ref.shape[1]
    kv_cols = wkv_ref.shape[1]

    def store_query(start, size, value):
        out_s[:, pl.ds(start, size)] = value

    product_tiles(scaled, wq_ref, store_query)
    out_s[:, query_cols : query_cols + kv_cols] = jnp.dot(
        scaled, wkv_ref[...], preferred_element_type=jnp.float32
    )
    out_s[:, query_cols + kv_cols :] = squares_block(total)
    part_rows(out_s, refs[slots + 1 : 2 * slots + 1])


def project_qkv(rows, gain, w_query, w_kv):
    slots = len(rows)
    own_rows, depth = rows[0].shape
    columns = w_query.shape[1] + w_kv.shape[1] + LANES
    return pl.pallas_call(
        functools.partial(qkv_kernel, slots),
        out_shape=(
            jax.ShapeDtypeStruct((own_rows * slots, depth), jnp.float32),
            *[jax.ShapeDtypeStruct((own_rows, columns), jnp.bfloat16)] * slots,
        ),
        in_specs=[in_vmem] * (3 + slots),
        out_specs=(in_vmem,) * (1 + slots),
        scratch_shapes=[
            pltpu.VMEM((own_rows * slots, columns), jnp.float32),
            pltpu.VMEM((own_rows * slots, depth), jnp.float32),
        ],
        compiler_params=params(2),
        name="project_qkv",
    )(gain, resident(w_query), resident(w_kv), *rows[::-1])


def stack_kernel(*refs):
    refs[-2][...] = join_rows(refs[:-2][::-1], refs[-1]).astype(refs[-2].dtype)


def stack(pieces):
    shape = (len(pieces) * pieces[0].shape[0], pieces[0].shape[1])
    return pl.pallas_call(
        stack_kernel,
        out_shape=jax.ShapeDtypeStruct(shape, pieces[0].dtype),
        in_specs=[in_vmem] * len(pieces),
        out_specs=in_vmem,
        scratch_shapes=[pltpu.VMEM(shape, jnp.float32)],
        compiler_params=params(1),
        name="stack",
    )(*pieces[::-1])


def attend_kernel(
    slots,
    shards,
    lengths_ref,
    cosine_ref,
    sine_ref,
    key_ref,
    value_ref,
    *refs,
):
    parts = refs[:shards]
    out_ref, query_s, kv_s, kv_wide_s, mixed_s, stats_s = refs[-6:]
    all_rows = parts[0].shape[0]
    own_rows = all_rows // slots
    here = HEADS // slots
    query_cols = here * HEAD_DIM
    kv_cols = 2 * KV_HEADS * HEAD_DIM // slots
    columns = query_cols + kv_cols
    tensor_index = lax.axis_index("tensor")
    inner_index = lax.axis_index("inner")
    positions = key_ref.shape[1] // KV_HEADS

    joined = functools.reduce(jnp.add, [ref[...].astype(jnp.float32) for ref in parts])
    squares = jnp.sum(joined[:, columns:], axis=1, keepdims=True)
    joined = joined[:, :columns] * lax.rsqrt(squares / D + epsilon)
    cosine = cosine_ref[...]
    sine = sine_ref[...]

    def rotate(block):
        count = block.shape[0]
        even = lax.broadcasted_iota(jnp.int32, block.shape, 1) % 2 == 0
        other = jnp.where(
            even, pltpu.roll(block, HEAD_DIM - 1, axis=1), pltpu.roll(block, 1, axis=1)
        )
        return block * cosine[:count] + other * sine[:count]

    for j in range(here):
        block = rotate(joined[:, j * HEAD_DIM : (j + 1) * HEAD_DIM])
        query_s[j * all_rows : (j + 1) * all_rows, :] = block
    for s in range(slots):
        kv_s[s] = joined[s * own_rows : (s + 1) * own_rows, query_cols:]
    for d in range(slots):
        kv_wide_s[:, d * kv_cols : (d + 1) * kv_cols] = kv_s[d ^ tensor_index]
    new_keys = []
    new_values = []
    for g in range(KV_HEADS):
        block = kv_wide_s[:, g * HEAD_DIM : (g + 1) * HEAD_DIM]
        new_keys.append(rotate(block).astype(jnp.bfloat16).astype(jnp.float32))
        block = kv_wide_s[:, (KV_HEADS + g) * HEAD_DIM : (KV_HEADS + g + 1) * HEAD_DIM]
        new_values.append(block.astype(jnp.bfloat16).astype(jnp.float32))

    score_scale = HEAD_DIM ** (-0.5)
    row = lax.broadcasted_iota(jnp.int32, (HEADS, 1), 0)
    head = ((row % slots) ^ tensor_index) * here + row // slots
    kv_head = head // GROUP
    column = lax.broadcasted_iota(jnp.int32, (1, positions * KV_HEADS), 1)
    place = column // KV_HEADS + inner_index * positions
    column_head = column % KV_HEADS
    lanes = lax.broadcasted_iota(jnp.int32, (HEADS, LANES), 1)
    for r in range(own_rows):
        queries = query_s[pl.ds(r, HEADS, stride=own_rows), :].astype(jnp.bfloat16)
        scores = (
            lax.dot_general(
                queries,
                key_ref[r],
                (((1,), (1,)), ((), ())),
                preferred_element_type=jnp.float32,
            )
            * score_scale
        )
        used = jnp.where(place < lengths_ref[r : r + 1, 0:1], column_head, -1)
        masked = jnp.where(used == kv_head, scores, -1e30)
        key_rows = 0.0
        value_rows = 0.0
        for g in range(KV_HEADS):
            key_rows = key_rows + jnp.where(kv_head == g, new_keys[g][r : r + 1], 0.0)
            value_rows = value_rows + jnp.where(kv_head == g, new_values[g][r : r + 1], 0.0)
        new_score = (
            jnp.sum(queries.astype(jnp.float32) * key_rows, axis=1, keepdims=True) * score_scale
        )
        new_score = jnp.where(inner_index == 0, new_score, -1e30)
        peak = jnp.maximum(jnp.max(masked, axis=1, keepdims=True), new_score)
        weights = jnp.exp(masked - peak)
        new_weight = jnp.exp(new_score - peak)
        totals = jnp.sum(weights, axis=1, keepdims=True) + new_weight
        mixture = jnp.dot(
            weights.astype(jnp.bfloat16), value_ref[r], preferred_element_type=jnp.float32
        )
        mixture = mixture + new_weight.astype(jnp.bfloat16).astype(jnp.float32) * value_rows
        mixed_s[pl.ds(r, HEADS, stride=own_rows), :] = mixture
        stats_s[pl.ds(r, HEADS, stride=own_rows), :] = spread(
            three_parts(peak), lanes, 0
        ) + spread(three_parts(totals), lanes, 4)
    out_ref[:, :HEAD_DIM] = mixed_s[...].astype(jnp.bfloat16)
    out_ref[:, HEAD_DIM:] = stats_s[...].astype(jnp.bfloat16)


def attend(lengths, cosine, sine, parts, keys, values, later, slots):
    own_rows = parts[0].shape[0] // slots
    kv_cols = 2 * KV_HEADS * HEAD_DIM // slots
    return pl.pallas_call(
        functools.partial(attend_kernel, slots, len(parts)),
        out_shape=jax.ShapeDtypeStruct((own_rows * HEADS, HEAD_DIM + LANES), jnp.bfloat16),
        in_specs=[in_vmem] * (5 + len(parts)) + [in_place] * len(later),
        out_specs=in_vmem,
        scratch_shapes=[
            pltpu.VMEM((own_rows * HEADS, HEAD_DIM), jnp.float32),
            pltpu.VMEM((slots, own_rows, kv_cols), jnp.float32),
            pltpu.VMEM((own_rows, slots * kv_cols), jnp.float32),
            pltpu.VMEM((own_rows * HEADS, HEAD_DIM), jnp.float32),
            pltpu.VMEM((own_rows * HEADS, LANES), jnp.float32),
        ],
        compiler_params=params(6),
        name="attend",
    )(lengths, cosine, sine, resident(keys), resident(values), *parts[::-1], *[resident(w) for w in later])


def combine_kernel(shards, slots, *refs):
    ins = refs[:shards]
    out_s = refs[-1]
    all_rows = out_s.shape[0]
    peaks = []
    totals = []
    for ref in ins:
        stats = ref[:, HEAD_DIM:].astype(jnp.float32)
        peaks.append(stats[:, 0:1] + stats[:, 1:2] + stats[:, 2:3])
        totals.append(stats[:, 4:5] + stats[:, 5:6] + stats[:, 6:7])
    top = functools.reduce(jnp.maximum, peaks)
    mixed = 0.0
    denominator = 0.0
    for ref, peak, total in zip(ins, peaks, totals):
        factor = jnp.exp(peak - top)
        mixed = mixed + factor * ref[:, :HEAD_DIM].astype(jnp.float32)
        denominator = denominator + factor * total
    attended = mixed / denominator
    for j in range(attended.shape[0] // all_rows):
        block = attended[j * all_rows : (j + 1) * all_rows]
        out_s[:, j * HEAD_DIM : (j + 1) * HEAD_DIM] = block
    part_rows(out_s, refs[-1 - slots : -1])


def combine(parts, later, all_rows, slots):
    count = len(parts)
    columns = parts[0].shape[0] // all_rows * HEAD_DIM
    return pl.pallas_call(
        functools.partial(combine_kernel, count, slots),
        out_shape=(jax.ShapeDtypeStruct((all_rows // slots, columns), jnp.bfloat16),) * slots,
        in_specs=[in_vmem] * count + [in_place] * len(later),
        out_specs=(in_vmem,) * slots,
        scratch_shapes=[pltpu.VMEM((all_rows, columns), jnp.float32)],
        compiler_params=params(2),
        name="combine",
    )(*parts[::-1], *[resident(w) for w in later])


def turned(block, step, own_rows):
    count = block.shape[0]
    span = step * own_rows
    row = lax.broadcasted_iota(jnp.int32, (count, 1), 0)
    return jnp.where(
        (row // span) % 2 == 0,
        pltpu.roll(block, count - span, axis=0),
        pltpu.roll(block, span, axis=0),
    )


def out_kernel(slots, later, weight_ref, *refs):
    pieces = refs[:slots][::-1]
    outs = refs[slots + later : 2 * slots + later]
    left_s = refs[-1]
    own_rows = pieces[0].shape[0]
    rows = left_s.shape[0]
    lefts = [join_rows(pieces, left_s)]
    for k in range(1, slots):
        low = k & -k
        lefts.append(turned(lefts[k ^ low], low, own_rows))
    left = jnp.concatenate(lefts, axis=0).astype(jnp.bfloat16)

    def store(start, size, value):
        for k, ref in enumerate(outs):
            ref[:, pl.ds(start, size)] = value[k * rows : (k + 1) * rows].astype(jnp.bfloat16)

    product_tiles(left, weight_ref, store)


def project_out(pieces, weight, later):
    slots = len(pieces)
    own_rows, depth = pieces[0].shape
    shape = jax.ShapeDtypeStruct((own_rows * slots, weight.shape[1]), jnp.bfloat16)
    return pl.pallas_call(
        functools.partial(out_kernel, slots, len(later)),
        out_shape=(shape,) * slots,
        in_specs=[in_vmem] * (1 + slots) + [in_place] * len(later),
        out_specs=(in_vmem,) * slots,
        scratch_shapes=[pltpu.VMEM((own_rows * slots, depth), jnp.float32)],
        compiler_params=params(3),
        name="project_out",
    )(resident(weight), *pieces[::-1], *[resident(w) for w in later])


def pair_kernel(first_ref, second_ref, out_ref):
    total = first_ref[...].astype(jnp.float32) + second_ref[...].astype(jnp.float32)
    out_ref[...] = total.astype(jnp.bfloat16)


def pair_sum(first, second):
    return pl.pallas_call(
        pair_kernel,
        out_shape=jax.ShapeDtypeStruct(first.shape, first.dtype),
        in_specs=[in_vmem] * 2,
        out_specs=in_vmem,
        compiler_params=params(2),
        name="pair_sum",
    )(first, second)


def gate_up_tiles(scaled, gate_ref, up_ref, out_ref, first, count):
    def store(offset):
        def place(start, size, value):
            start = pl.multiple_of(offset + start, math.gcd(offset, size))
            out_ref[:, pl.ds(start, size)] = value.astype(jnp.bfloat16)

        return place

    product_tiles(scaled, gate_ref, store(0), first, count)
    product_tiles(scaled, up_ref, store(count), first, count)


def first_gate_up_kernel(slots, count, rows_ref, gain_ref, gate_ref, up_ref, *refs):
    parts = refs[:slots]
    out_ref, updated_ref, scaled_ref = refs[-3:]
    own_rows = updated_ref.shape[0]
    total = functools.reduce(jnp.add, [ref[...].astype(jnp.float32) for ref in parts])
    updated = (rows_ref[...] + total).astype(jnp.bfloat16)
    wide = updated.astype(jnp.float32)
    updated_ref[...] = wide[:own_rows]
    squares = jnp.sum(wide * wide, axis=1, keepdims=True)
    out_ref[:, 2 * count :] = squares_block(squares).astype(jnp.bfloat16)
    scaled = (wide * gain_ref[...].astype(jnp.float32)[None, :]).astype(jnp.bfloat16)
    scaled_ref[...] = scaled
    gate_up_tiles(scaled, gate_ref, up_ref, out_ref, 0, count)


def first_gate_up(rows, gain, parts, w_gate, w_up, later, count, own_rows):
    slots = len(parts)
    return pl.pallas_call(
        functools.partial(first_gate_up_kernel, slots, count),
        out_shape=(
            jax.ShapeDtypeStruct((rows.shape[0], 2 * count + LANES), jnp.bfloat16),
            jax.ShapeDtypeStruct((own_rows, rows.shape[1]), jnp.float32),
            jax.ShapeDtypeStruct(rows.shape, jnp.bfloat16),
        ),
        in_specs=[in_vmem] * (4 + slots) + [in_place] * len(later),
        out_specs=(in_vmem,) * 3,
        compiler_params=params(3),
        cost_estimate=product_cost(w_gate.shape[0], 2 * count),
        name="first_gate_up",
    )(rows, gain, resident(w_gate), resident(w_up), *parts[::-1], *[resident(w) for w in later])


def second_gate_up_kernel(first, count, scaled_ref, gate_ref, up_ref, *refs):
    out_ref = refs[-1]
    gate_up_tiles(scaled_ref[...], gate_ref, up_ref, out_ref, first, count)


def second_gate_up(scaled, w_gate, w_up, later, first):
    count = w_gate.shape[1] - first
    return pl.pallas_call(
        functools.partial(second_gate_up_kernel, first, count),
        out_shape=jax.ShapeDtypeStruct((scaled.shape[0], 2 * count), jnp.bfloat16),
        in_specs=[in_vmem] * 3 + [in_place] * len(later),
        out_specs=in_vmem,
        compiler_params=params(3),
        cost_estimate=product_cost(w_gate.shape[0], 2 * count),
        name="second_gate_up",
    )(scaled, resident(w_gate), resident(w_up), *[resident(w) for w in later])


def hidden_of(near_ref, far_ref, scale, count):
    def total(start):
        span = slice(start, start + count)
        return (near_ref[:, span].astype(jnp.float32) + far_ref[:, span].astype(jnp.float32)) * scale

    gate = total(0)
    return (gate / (1.0 + jnp.exp(-gate)) * total(count)).astype(jnp.bfloat16)


def first_down_kernel(count, near_ref, far_ref, weight_ref, out_ref, scale_ref):
    squares = jnp.sum(
        near_ref[:, 2 * count :].astype(jnp.float32) + far_ref[:, 2 * count :].astype(jnp.float32),
        axis=1,
        keepdims=True,
    )
    scale = lax.rsqrt(squares / D + epsilon)
    scale_ref[...] = jnp.broadcast_to(scale, scale_ref.shape)

    def store(start, size, value):
        out_ref[:, pl.ds(start, size)] = value

    product_tiles(hidden_of(near_ref, far_ref, scale, count), weight_ref.at[:count], store)


def first_down(near, far, weight, count):
    rows = near.shape[0]
    return pl.pallas_call(
        functools.partial(first_down_kernel, count),
        out_shape=(
            jax.ShapeDtypeStruct((rows, weight.shape[1]), jnp.float32),
            jax.ShapeDtypeStruct((rows, LANES), jnp.float32),
        ),
        in_specs=[in_vmem] * 3,
        out_specs=(in_vmem,) * 2,
        compiler_params=params(3),
        cost_estimate=product_cost(count, weight.shape[1]),
        name="first_down",
    )(near, far, resident(weight))


def second_down_kernel(count, near_ref, far_ref, weight_ref, part_ref, scale_ref, *refs):
    out_s = refs[-1]
    first = weight_ref.shape[0] - count

    def store(start, size, value):
        span = pl.ds(start, size)
        out_s[:, span] = part_ref[:, span] + value

    hidden = hidden_of(near_ref, far_ref, scale_ref[:, 0:1], count)
    product_tiles(hidden, weight_ref.at[first:], store)
    part_rows(out_s, refs[:-1])


def second_down(near, far, weight, part, scale, slots):
    rows, columns = part.shape
    count = near.shape[1] // 2
    return pl.pallas_call(
        functools.partial(second_down_kernel, count),
        out_shape=(jax.ShapeDtypeStruct((rows // slots, columns), jnp.bfloat16),) * slots,
        in_specs=[in_vmem] * 5,
        out_specs=(in_vmem,) * slots,
        scratch_shapes=[pltpu.VMEM(part.shape, jnp.float32)],
        compiler_params=params(3),
        name="second_down",
    )(near, far, resident(weight), part, scale)


def finish_kernel(updated_ref, *refs):
    total = functools.reduce(jnp.add, [ref[...].astype(jnp.float32) for ref in refs[:-1]])
    refs[-1][...] = (updated_ref[...] + total).astype(jnp.bfloat16)


def finish(updated, parts):
    return pl.pallas_call(
        finish_kernel,
        out_shape=jax.ShapeDtypeStruct(updated.shape, jnp.bfloat16),
        in_specs=[in_vmem] * (1 + len(parts)),
        out_specs=in_vmem,
        compiler_params=params(1),
        name="finish",
    )(updated, *parts[::-1])


def rotation_tables(positions, repeats):
    inverse = jnp.exp(
        (jnp.arange(HEAD_DIM) // 2).astype(jnp.float32) * (-2.0 / HEAD_DIM) * math.log(rope_base)
    )
    angles = positions[:, None] * inverse[None, :]
    sign = jnp.where(jnp.arange(HEAD_DIM) % 2 == 0, -1.0, 1.0)
    return (
        jnp.tile(jnp.cos(angles), (repeats, 1)),
        jnp.tile(jnp.sin(angles) * sign[None, :], (repeats, 1)),
    )


def local(
    states,
    attn_gain,
    ffn_gain,
    w_query,
    w_kv,
    w_out,
    w_gate,
    w_up,
    w_down,
    key_cache,
    value_cache,
    lengths,
):
    tensor_index = lax.axis_index("tensor")
    slots = lax.axis_size("tensor")
    own_rows = states.shape[0]
    all_rows = own_rows * slots

    got = exchange(states, "tensor")
    own, attn_gain, ffn_gain, w_kv, w_query = load(
        states, attn_gain, ffn_gain, w_kv, w_query, after=states
    )
    rows, *pieces = project_qkv([own] + got[1:], attn_gain, w_query, w_kv)

    rows, lengths = lax.optimization_barrier((rows, lengths))
    my_lengths = lax.dynamic_slice_in_dim(lengths, tensor_index * own_rows, own_rows, 0)
    cosine, sine = rotation_tables(my_lengths.astype(jnp.float32), slots)
    my_lengths = jnp.broadcast_to(my_lengths[:, None], (own_rows, LANES))
    flat = (own_rows, key_cache.shape[1] * KV_HEADS, HEAD_DIM)
    keys, values = load(key_cache.reshape(flat), value_cache.reshape(flat), after=rows)
    joined = stack(scatter_slots(pieces, 1))
    joined, keys, values = lax.optimization_barrier((joined, keys, values))
    (w_out,) = load(w_out, after=joined)
    parts, w_out = lax.optimization_barrier((exchange(joined, "inner")[::-1], w_out))
    shard = attend(my_lengths, cosine, sine, parts, keys, values, [w_gate], slots)

    pieces = combine(exchange(shard, "inner"), [w_up], all_rows, slots)
    parts = scatter_slots(project_out(scatter_slots(pieces, 1), w_out, [w_down]), 0)

    tiles = w_gate.shape[1] // LANES
    first = (tiles + 1) // 2 * LANES
    one, updated, scaled = first_gate_up(
        rows, ffn_gain, parts, w_gate, w_up, [], first, own_rows
    )
    two = second_gate_up(scaled, w_gate, w_up, [], first)
    steps = steps_up(lax.axis_size("inner"))
    for step in steps[:-1]:
        one = pair_sum(one, swap_with(one, "inner", step))
        two = pair_sum(two, swap_with(two, "inner", step))
    part, scale = first_down(one, swap_with(one, "inner", steps[-1]), w_down, first)
    pieces = second_down(two, swap_with(two, "inner", steps[-1]), w_down, part, scale, slots)
    parts = scatter_slots(pieces, 0)
    return finish(updated, parts)


def solution(mesh):
    in_specs = (
        P(("groups", "tensor"), "inner"),
        P("inner"),
        P("inner"),
        P("inner", "tensor"),
        P("inner", "tensor"),
        P("tensor", "inner"),
        P("inner", "tensor"),
        P("inner", "tensor"),
        P("tensor", "inner"),
        P(("groups", "tensor"), "inner", None, None),
        P(("groups", "tensor"), "inner", None, None),
        P("groups"),
    )
    out_specs = P(("groups", "tensor"), "inner")
    return jax.shard_map(local, mesh=mesh, in_specs=in_specs, out_specs=out_specs, check_vma=False)
```

```python
import functools
import math

import jax
import jax.numpy as jnp
from jax import lax
from jax.experimental import pallas as pl
from jax.experimental.pallas import tpu as pltpu
from jax.sharding import PartitionSpec as P

D = 8192
HEADS = 32
KV_HEADS = 4
HEAD_DIM = 128
GROUP = HEADS // KV_HEADS
LANES = 128
MIB = 2**20
COPIES = 4

epsilon = 1e-05
rope_base = 500000.0

in_vmem = pl.BlockSpec(memory_space=pltpu.VMEM)
in_smem = pl.BlockSpec(memory_space=pltpu.SMEM)
in_place = pl.BlockSpec(memory_space=pl.ANY)


def swap_with(value, axis, step):
    count = lax.axis_size(axis)
    return lax.ppermute(value, axis, [(i, i ^ step) for i in range(count)])


def exchange(value, axis):
    count = lax.axis_size(axis)
    got = {k: swap_with(value, axis, k) for k in reversed(range(1, count))}
    return [value] + [got[k] for k in range(1, count)]


def scatter_slots(pieces, cross):
    count = lax.axis_size("tensor")
    width = lax.axis_size("inner")
    got = [pieces[0]]
    for k in range(1, count):
        pairs = [
            (t * width + i, (t ^ k) * width + (i ^ cross))
            for t in range(count)
            for i in range(width)
        ]
        got.append(lax.ppermute(pieces[k], ("tensor", "inner"), pairs))
    return got


def steps_up(count):
    return [1 << n for n in range(count.bit_length() - 1)]


def params(mib):
    return pltpu.CompilerParams(vmem_limit_bytes=mib * MIB)


def resident(weight):
    return pltpu.with_memory_space_constraint(weight, pltpu.VMEM)


def in_hbm(weight):
    return pltpu.with_memory_space_constraint(weight, pltpu.HBM)


def product_cost(depth, columns):
    return pl.CostEstimate(
        flops=16 * depth * columns, bytes_accessed=2 * depth * columns, transcendentals=0
    )


def tile_of(columns):
    for tile in (1792, 1024, 896, 512, 256, 128):
        if columns % tile == 0:
            return tile
    return columns


def product_tiles(left, weight_ref, store, first=0, columns=None):
    columns = columns or weight_ref.shape[1]
    tile = tile_of(columns)

    @pl.loop(0, columns // tile)
    def _(step):
        start = pl.multiple_of(step * tile, tile)
        span = pl.ds(pl.multiple_of(first + start, math.gcd(first, tile)), tile)
        store(
            start,
            tile,
            jnp.dot(left, weight_ref[:, span], preferred_element_type=jnp.float32),
        )


def three_parts(value):
    high = value.astype(jnp.bfloat16).astype(jnp.float32)
    rest = value - high
    middle = rest.astype(jnp.bfloat16).astype(jnp.float32)
    return high, middle, rest - middle


def spread(parts, lanes, first):
    out = 0.0
    for n, part in enumerate(parts):
        out = out + jnp.where(lanes == first + n, part, 0.0)
    return out


def squares_block(total):
    lanes = lax.broadcasted_iota(jnp.int32, (total.shape[0], LANES), 1)
    return spread(three_parts(total), lanes, lax.axis_index("inner") * 4)


def copies_of(source, start, target, sems):
    size = target.shape[0]
    cuts = COPIES if len(target.shape) > 1 and size % (16 * COPIES) == 0 else 1
    each = size // cuts
    return [
        pltpu.make_async_copy(
            source.at[pl.ds(start + m * each, each)], target.at[pl.ds(m * each, each)], sems.at[m]
        )
        for m in range(cuts)
    ]


def load_kernel(spans, *refs):
    count = len(spans)
    outs = refs[count + 1 : 2 * count + 1]
    sems = refs[-1]
    copies = []
    for n, (start, _) in enumerate(spans):
        copies += copies_of(refs[n], start, outs[n], sems.at[n])
    for copy in copies:
        copy.start()
    for copy in copies:
        copy.wait()


def load(*arrays, after, spans=None):
    spans = spans or [(0, a.shape[0]) for a in arrays]
    shapes = [(size,) + a.shape[1:] for a, (_, size) in zip(arrays, spans)]
    return pl.pallas_call(
        functools.partial(load_kernel, spans),
        out_shape=tuple(pltpu.VMEM(shape, a.dtype) for shape, a in zip(shapes, arrays)),
        in_specs=[in_place] * (len(arrays) + 1),
        out_specs=tuple(in_vmem for _ in arrays),
        cost_estimate=pl.CostEstimate(
            flops=0, bytes_accessed=2 * sum(math.prod(shape) for shape in shapes), transcendentals=0
        ),
        scratch_shapes=[pltpu.SemaphoreType.DMA((len(arrays), COPIES))],
        compiler_params=params(1),
        name="load",
    )(*[in_hbm(a) for a in arrays], after)


def join_rows(refs, target):
    rows = refs[0].shape[0]
    for n, ref in enumerate(refs):
        target[n * rows : (n + 1) * rows, :] = ref[...].astype(jnp.float32)
    return target[...]


def part_rows(source, refs):
    rows = refs[0].shape[0]
    for n, ref in enumerate(refs):
        ref[...] = source[n * rows : (n + 1) * rows, :].astype(ref.dtype)


def qkv_kernel(slots, gain_ref, wq_ref, wkv_ref, *refs):
    rows_ref = refs[slots]
    out_s, rows_s = refs[-2:]
    wide = join_rows(refs[:slots][::-1], rows_s)
    rows_ref[...] = wide
    total = jnp.sum(wide * wide, axis=1, keepdims=True)
    gain = gain_ref[...].astype(jnp.float32)[None, :]
    scaled = (wide * gain).astype(jnp.bfloat16)
    query_cols = wq_ref.shape[1]
    kv_cols = wkv_ref.shape[1]

    def store_query(start, size, value):
        out_s[:, pl.ds(start, size)] = value

    product_tiles(scaled, wq_ref, store_query)
    out_s[:, query_cols : query_cols + kv_cols] = jnp.dot(
        scaled, wkv_ref[...], preferred_element_type=jnp.float32
    )
    out_s[:, query_cols + kv_cols :] = squares_block(total)
    part_rows(out_s, refs[slots + 1 : 2 * slots + 1])


def project_qkv(rows, gain, w_query, w_kv):
    slots = len(rows)
    own_rows, depth = rows[0].shape
    columns = w_query.shape[1] + w_kv.shape[1] + LANES
    return pl.pallas_call(
        functools.partial(qkv_kernel, slots),
        out_shape=(
            jax.ShapeDtypeStruct((own_rows * slots, depth), jnp.float32),
            *[jax.ShapeDtypeStruct((own_rows, columns), jnp.bfloat16)] * slots,
        ),
        in_specs=[in_vmem] * (3 + slots),
        out_specs=(in_vmem,) * (1 + slots),
        scratch_shapes=[
            pltpu.VMEM((own_rows * slots, columns), jnp.float32),
            pltpu.VMEM((own_rows * slots, depth), jnp.float32),
        ],
        compiler_params=params(2),
        name="project_qkv",
    )(gain, resident(w_query), resident(w_kv), *rows[::-1])


def stack_kernel(*refs):
    refs[-2][...] = join_rows(refs[:-2][::-1], refs[-1]).astype(refs[-2].dtype)


def stack(pieces):
    shape = (len(pieces) * pieces[0].shape[0], pieces[0].shape[1])
    return pl.pallas_call(
        stack_kernel,
        out_shape=jax.ShapeDtypeStruct(shape, pieces[0].dtype),
        in_specs=[in_vmem] * len(pieces),
        out_specs=in_vmem,
        scratch_shapes=[pltpu.VMEM(shape, jnp.float32)],
        compiler_params=params(1),
        name="stack",
    )(*pieces[::-1])


def attend_kernel(
    slots,
    shards,
    lengths_ref,
    cosine_ref,
    sine_ref,
    key_ref,
    value_ref,
    *refs,
):
    parts = refs[:shards]
    out_ref, query_s, kv_s, kv_wide_s, mixed_s, stats_s = refs[-6:]
    all_rows = parts[0].shape[0]
    own_rows = all_rows // slots
    here = HEADS // slots
    query_cols = here * HEAD_DIM
    kv_cols = 2 * KV_HEADS * HEAD_DIM // slots
    columns = query_cols + kv_cols
    tensor_index = lax.axis_index("tensor")
    inner_index = lax.axis_index("inner")
    positions = key_ref.shape[1] // KV_HEADS

    joined = functools.reduce(jnp.add, [ref[...].astype(jnp.float32) for ref in parts])
    squares = jnp.sum(joined[:, columns:], axis=1, keepdims=True)
    joined = joined[:, :columns] * lax.rsqrt(squares / D + epsilon)
    cosine = cosine_ref[...]
    sine = sine_ref[...]

    def rotate(block):
        count = block.shape[0]
        even = lax.broadcasted_iota(jnp.int32, block.shape, 1) % 2 == 0
        other = jnp.where(
            even, pltpu.roll(block, HEAD_DIM - 1, axis=1), pltpu.roll(block, 1, axis=1)
        )
        return block * cosine[:count] + other * sine[:count]

    for j in range(here):
        block = rotate(joined[:, j * HEAD_DIM : (j + 1) * HEAD_DIM])
        query_s[j * all_rows : (j + 1) * all_rows, :] = block
    for s in range(slots):
        kv_s[s] = joined[s * own_rows : (s + 1) * own_rows, query_cols:]
    for d in range(slots):
        kv_wide_s[:, d * kv_cols : (d + 1) * kv_cols] = kv_s[d ^ tensor_index]
    new_keys = []
    new_values = []
    for g in range(KV_HEADS):
        block = kv_wide_s[:, g * HEAD_DIM : (g + 1) * HEAD_DIM]
        new_keys.append(rotate(block).astype(jnp.bfloat16).astype(jnp.float32))
        block = kv_wide_s[:, (KV_HEADS + g) * HEAD_DIM : (KV_HEADS + g + 1) * HEAD_DIM]
        new_values.append(block.astype(jnp.bfloat16).astype(jnp.float32))

    score_scale = HEAD_DIM ** (-0.5)
    row = lax.broadcasted_iota(jnp.int32, (HEADS, 1), 0)
    head = ((row % slots) ^ tensor_index) * here + row // slots
    kv_head = head // GROUP
    column = lax.broadcasted_iota(jnp.int32, (1, positions * KV_HEADS), 1)
    place = column // KV_HEADS + inner_index * positions
    column_head = column % KV_HEADS
    lanes = lax.broadcasted_iota(jnp.int32, (HEADS, LANES), 1)
    for r in range(own_rows):
        queries = query_s[pl.ds(r, HEADS, stride=own_rows), :].astype(jnp.bfloat16)
        scores = (
            lax.dot_general(
                queries,
                key_ref[r],
                (((1,), (1,)), ((), ())),
                preferred_element_type=jnp.float32,
            )
            * score_scale
        )
        used = jnp.where(place < lengths_ref[r : r + 1, 0:1], column_head, -1)
        masked = jnp.where(used == kv_head, scores, -1e30)
        key_rows = 0.0
        value_rows = 0.0
        for g in range(KV_HEADS):
            key_rows = key_rows + jnp.where(kv_head == g, new_keys[g][r : r + 1], 0.0)
            value_rows = value_rows + jnp.where(kv_head == g, new_values[g][r : r + 1], 0.0)
        new_score = (
            jnp.sum(queries.astype(jnp.float32) * key_rows, axis=1, keepdims=True) * score_scale
        )
        new_score = jnp.where(inner_index == 0, new_score, -1e30)
        peak = jnp.maximum(jnp.max(masked, axis=1, keepdims=True), new_score)
        weights = jnp.exp(masked - peak)
        new_weight = jnp.exp(new_score - peak)
        totals = jnp.sum(weights, axis=1, keepdims=True) + new_weight
        mixture = jnp.dot(
            weights.astype(jnp.bfloat16), value_ref[r], preferred_element_type=jnp.float32
        )
        mixture = mixture + new_weight.astype(jnp.bfloat16).astype(jnp.float32) * value_rows
        mixed_s[pl.ds(r, HEADS, stride=own_rows), :] = mixture
        stats_s[pl.ds(r, HEADS, stride=own_rows), :] = spread(
            three_parts(peak), lanes, 0
        ) + spread(three_parts(totals), lanes, 4)
    out_ref[:, :HEAD_DIM] = mixed_s[...].astype(jnp.bfloat16)
    out_ref[:, HEAD_DIM:] = stats_s[...].astype(jnp.bfloat16)


def attend(lengths, cosine, sine, parts, keys, values, later, slots):
    own_rows = parts[0].shape[0] // slots
    kv_cols = 2 * KV_HEADS * HEAD_DIM // slots
    return pl.pallas_call(
        functools.partial(attend_kernel, slots, len(parts)),
        out_shape=jax.ShapeDtypeStruct((own_rows * HEADS, HEAD_DIM + LANES), jnp.bfloat16),
        in_specs=[in_vmem] * (5 + len(parts)) + [in_place] * len(later),
        out_specs=in_vmem,
        scratch_shapes=[
            pltpu.VMEM((own_rows * HEADS, HEAD_DIM), jnp.float32),
            pltpu.VMEM((slots, own_rows, kv_cols), jnp.float32),
            pltpu.VMEM((own_rows, slots * kv_cols), jnp.float32),
            pltpu.VMEM((own_rows * HEADS, HEAD_DIM), jnp.float32),
            pltpu.VMEM((own_rows * HEADS, LANES), jnp.float32),
        ],
        compiler_params=params(6),
        name="attend",
    )(lengths, cosine, sine, resident(keys), resident(values), *parts[::-1], *[resident(w) for w in later])


def combine_kernel(shards, slots, *refs):
    ins = refs[:shards]
    out_s = refs[-1]
    all_rows = out_s.shape[0]
    peaks = []
    totals = []
    for ref in ins:
        stats = ref[:, HEAD_DIM:].astype(jnp.float32)
        peaks.append(stats[:, 0:1] + stats[:, 1:2] + stats[:, 2:3])
        totals.append(stats[:, 4:5] + stats[:, 5:6] + stats[:, 6:7])
    top = functools.reduce(jnp.maximum, peaks)
    mixed = 0.0
    denominator = 0.0
    for ref, peak, total in zip(ins, peaks, totals):
        factor = jnp.exp(peak - top)
        mixed = mixed + factor * ref[:, :HEAD_DIM].astype(jnp.float32)
        denominator = denominator + factor * total
    attended = mixed / denominator
    for j in range(attended.shape[0] // all_rows):
        block = attended[j * all_rows : (j + 1) * all_rows]
        out_s[:, j * HEAD_DIM : (j + 1) * HEAD_DIM] = block
    part_rows(out_s, refs[-1 - slots : -1])


def combine(parts, later, all_rows, slots):
    count = len(parts)
    columns = parts[0].shape[0] // all_rows * HEAD_DIM
    return pl.pallas_call(
        functools.partial(combine_kernel, count, slots),
        out_shape=(jax.ShapeDtypeStruct((all_rows // slots, columns), jnp.bfloat16),) * slots,
        in_specs=[in_vmem] * count + [in_place] * len(later),
        out_specs=(in_vmem,) * slots,
        scratch_shapes=[pltpu.VMEM((all_rows, columns), jnp.float32)],
        compiler_params=params(2),
        name="combine",
    )(*parts[::-1], *[resident(w) for w in later])


def turned(block, step, own_rows):
    count = block.shape[0]
    span = step * own_rows
    row = lax.broadcasted_iota(jnp.int32, (count, 1), 0)
    return jnp.where(
        (row // span) % 2 == 0,
        pltpu.roll(block, count - span, axis=0),
        pltpu.roll(block, span, axis=0),
    )


def out_kernel(slots, later, weight_ref, *refs):
    pieces = refs[:slots][::-1]
    outs = refs[slots + later : 2 * slots + later]
    left_s = refs[-1]
    own_rows = pieces[0].shape[0]
    rows = left_s.shape[0]
    lefts = [join_rows(pieces, left_s)]
    for k in range(1, slots):
        low = k & -k
        lefts.append(turned(lefts[k ^ low], low, own_rows))
    left = jnp.concatenate(lefts, axis=0).astype(jnp.bfloat16)

    def store(start, size, value):
        for k, ref in enumerate(outs):
            ref[:, pl.ds(start, size)] = value[k * rows : (k + 1) * rows].astype(jnp.bfloat16)

    product_tiles(left, weight_ref, store)


def project_out(pieces, weight, later):
    slots = len(pieces)
    own_rows, depth = pieces[0].shape
    shape = jax.ShapeDtypeStruct((own_rows * slots, weight.shape[1]), jnp.bfloat16)
    return pl.pallas_call(
        functools.partial(out_kernel, slots, len(later)),
        out_shape=(shape,) * slots,
        in_specs=[in_vmem] * (1 + slots) + [in_place] * len(later),
        out_specs=(in_vmem,) * slots,
        scratch_shapes=[pltpu.VMEM((own_rows * slots, depth), jnp.float32)],
        compiler_params=params(3),
        name="project_out",
    )(resident(weight), *pieces[::-1], *[resident(w) for w in later])


def pair_kernel(first_ref, second_ref, out_ref):
    total = first_ref[...].astype(jnp.float32) + second_ref[...].astype(jnp.float32)
    out_ref[...] = total.astype(jnp.bfloat16)


def pair_sum(first, second):
    return pl.pallas_call(
        pair_kernel,
        out_shape=jax.ShapeDtypeStruct(first.shape, first.dtype),
        in_specs=[in_vmem] * 2,
        out_specs=in_vmem,
        compiler_params=params(2),
        name="pair_sum",
    )(first, second)


def gate_up_tiles(scaled, gate_ref, up_ref, out_ref, first, count):
    def store(offset):
        def place(start, size, value):
            start = pl.multiple_of(offset + start, math.gcd(offset, size))
            out_ref[:, pl.ds(start, size)] = value.astype(jnp.bfloat16)

        return place

    product_tiles(scaled, gate_ref, store(0), first, count)
    product_tiles(scaled, up_ref, store(count), first, count)


def first_gate_up_kernel(slots, count, rows_ref, gain_ref, gate_ref, up_ref, *refs):
    parts = refs[:slots]
    out_ref, updated_ref, scaled_ref = refs[-3:]
    own_rows = updated_ref.shape[0]
    total = functools.reduce(jnp.add, [ref[...].astype(jnp.float32) for ref in parts])
    updated = (rows_ref[...] + total).astype(jnp.bfloat16)
    wide = updated.astype(jnp.float32)
    updated_ref[...] = wide[:own_rows]
    squares = jnp.sum(wide * wide, axis=1, keepdims=True)
    out_ref[:, 2 * count :] = squares_block(squares).astype(jnp.bfloat16)
    scaled = (wide * gain_ref[...].astype(jnp.float32)[None, :]).astype(jnp.bfloat16)
    scaled_ref[...] = scaled
    gate_up_tiles(scaled, gate_ref, up_ref, out_ref, 0, count)


def first_gate_up(rows, gain, parts, w_gate, w_up, later, count, own_rows):
    slots = len(parts)
    return pl.pallas_call(
        functools.partial(first_gate_up_kernel, slots, count),
        out_shape=(
            jax.ShapeDtypeStruct((rows.shape[0], 2 * count + LANES), jnp.bfloat16),
            jax.ShapeDtypeStruct((own_rows, rows.shape[1]), jnp.float32),
            jax.ShapeDtypeStruct(rows.shape, jnp.bfloat16),
        ),
        in_specs=[in_vmem] * (4 + slots) + [in_place] * len(later),
        out_specs=(in_vmem,) * 3,
        compiler_params=params(3),
        cost_estimate=product_cost(w_gate.shape[0], 2 * count),
        name="first_gate_up",
    )(rows, gain, resident(w_gate), resident(w_up), *parts[::-1], *[resident(w) for w in later])


def second_gate_up_kernel(first, count, scaled_ref, gate_ref, up_ref, *refs):
    out_ref = refs[-1]
    gate_up_tiles(scaled_ref[...], gate_ref, up_ref, out_ref, first, count)


def second_gate_up(scaled, w_gate, w_up, later, first):
    count = w_gate.shape[1] - first
    return pl.pallas_call(
        functools.partial(second_gate_up_kernel, first, count),
        out_shape=jax.ShapeDtypeStruct((scaled.shape[0], 2 * count), jnp.bfloat16),
        in_specs=[in_vmem] * 3 + [in_place] * len(later),
        out_specs=in_vmem,
        compiler_params=params(3),
        cost_estimate=product_cost(w_gate.shape[0], 2 * count),
        name="second_gate_up",
    )(scaled, resident(w_gate), resident(w_up), *[resident(w) for w in later])


def hidden_of(near_ref, far_ref, scale, count):
    def total(start):
        span = slice(start, start + count)
        return (near_ref[:, span].astype(jnp.float32) + far_ref[:, span].astype(jnp.float32)) * scale

    gate = total(0)
    return (gate / (1.0 + jnp.exp(-gate)) * total(count)).astype(jnp.bfloat16)


def down_kernel(one_near, one_far, two_near, two_far, weight_ref, *refs):
    hidden_s, out_s = refs[-2:]
    first = (one_near.shape[1] - LANES) // 2
    second = two_near.shape[1] // 2
    squares = jnp.sum(
        one_near[:, 2 * first :].astype(jnp.float32) + one_far[:, 2 * first :].astype(jnp.float32),
        axis=1,
        keepdims=True,
    )
    scale = lax.rsqrt(squares / D + epsilon)
    hidden_s[:, :first] = hidden_of(one_near, one_far, scale, first)
    hidden_s[:, first:] = hidden_of(two_near, two_far, scale, second)

    def store(start, size, value):
        out_s[:, pl.ds(start, size)] = value

    product_tiles(hidden_s[...], weight_ref, store)
    part_rows(out_s, refs[:-2])


def project_down(one, two, weight, slots):
    rows = one[0].shape[0]
    depth, columns = weight.shape
    return pl.pallas_call(
        down_kernel,
        out_shape=(jax.ShapeDtypeStruct((rows // slots, columns), jnp.bfloat16),) * slots,
        in_specs=[in_vmem] * 5,
        out_specs=(in_vmem,) * slots,
        scratch_shapes=[
            pltpu.VMEM((rows, depth), jnp.bfloat16),
            pltpu.VMEM((rows, columns), jnp.float32),
        ],
        compiler_params=params(3),
        name="project_down",
    )(*one, *two, resident(weight))


def finish_kernel(updated_ref, *refs):
    total = functools.reduce(jnp.add, [ref[...].astype(jnp.float32) for ref in refs[:-1]])
    refs[-1][...] = (updated_ref[...] + total).astype(jnp.bfloat16)


def finish(updated, parts):
    return pl.pallas_call(
        finish_kernel,
        out_shape=jax.ShapeDtypeStruct(updated.shape, jnp.bfloat16),
        in_specs=[in_vmem] * (1 + len(parts)),
        out_specs=in_vmem,
        compiler_params=params(1),
        name="finish",
    )(updated, *parts[::-1])


def rotation_tables(positions, repeats):
    inverse = jnp.exp(
        (jnp.arange(HEAD_DIM) // 2).astype(jnp.float32) * (-2.0 / HEAD_DIM) * math.log(rope_base)
    )
    angles = positions[:, None] * inverse[None, :]
    sign = jnp.where(jnp.arange(HEAD_DIM) % 2 == 0, -1.0, 1.0)
    return (
        jnp.tile(jnp.cos(angles), (repeats, 1)),
        jnp.tile(jnp.sin(angles) * sign[None, :], (repeats, 1)),
    )


def local(
    states,
    attn_gain,
    ffn_gain,
    w_query,
    w_kv,
    w_out,
    w_gate,
    w_up,
    w_down,
    key_cache,
    value_cache,
    lengths,
):
    tensor_index = lax.axis_index("tensor")
    slots = lax.axis_size("tensor")
    own_rows = states.shape[0]
    all_rows = own_rows * slots

    got = exchange(states, "tensor")
    own, attn_gain, ffn_gain, w_kv, w_query = load(
        states, attn_gain, ffn_gain, w_kv, w_query, after=states
    )
    rows, *pieces = project_qkv([own] + got[1:], attn_gain, w_query, w_kv)

    rows, lengths = lax.optimization_barrier((rows, lengths))
    my_lengths = lax.dynamic_slice_in_dim(lengths, tensor_index * own_rows, own_rows, 0)
    cosine, sine = rotation_tables(my_lengths.astype(jnp.float32), slots)
    my_lengths = jnp.broadcast_to(my_lengths[:, None], (own_rows, LANES))
    flat = (own_rows, key_cache.shape[1] * KV_HEADS, HEAD_DIM)
    keys, values = load(key_cache.reshape(flat), value_cache.reshape(flat), after=rows)
    joined = stack(scatter_slots(pieces, 1))
    joined, keys, values = lax.optimization_barrier((joined, keys, values))
    (w_out,) = load(w_out, after=joined)
    parts, w_out = lax.optimization_barrier((exchange(joined, "inner")[::-1], w_out))
    shard = attend(my_lengths, cosine, sine, parts, keys, values, [], slots)

    pieces = combine(exchange(shard, "inner"), [w_gate], all_rows, slots)
    parts = scatter_slots(project_out(scatter_slots(pieces, 1), w_out, [w_up]), 0)

    tiles = w_gate.shape[1] // LANES
    first = (tiles + 1) // 2 * LANES
    one, updated, scaled = first_gate_up(
        rows, ffn_gain, parts, w_gate, w_up, [], first, own_rows
    )
    two = second_gate_up(scaled, w_gate, w_up, [], first)
    steps = steps_up(lax.axis_size("inner"))
    for step in steps[:-1]:
        one = pair_sum(one, swap_with(one, "inner", step))
        two = pair_sum(two, swap_with(two, "inner", step))
    one = (one, swap_with(one, "inner", steps[-1]))
    two = (two, swap_with(two, "inner", steps[-1]))
    pieces = project_down(one, two, w_down, slots)
    parts = scatter_slots(pieces, 0)
    return finish(updated, parts)


def solution(mesh):
    in_specs = (
        P(("groups", "tensor"), "inner"),
        P("inner"),
        P("inner"),
        P("inner", "tensor"),
        P("inner", "tensor"),
        P("tensor", "inner"),
        P("inner", "tensor"),
        P("inner", "tensor"),
        P("tensor", "inner"),
        P(("groups", "tensor"), "inner", None, None),
        P(("groups", "tensor"), "inner", None, None),
        P("groups"),
    )
    out_specs = P(("groups", "tensor"), "inner")
    return jax.shard_map(local, mesh=mesh, in_specs=in_specs, out_specs=out_specs, check_vma=False)
```

```python
import functools
import math

import jax
import jax.numpy as jnp
from jax import lax
from jax.experimental import pallas as pl
from jax.experimental.pallas import tpu as pltpu
from jax.sharding import PartitionSpec as P

D = 8192
HEADS = 32
KV_HEADS = 4
HEAD_DIM = 128
GROUP = HEADS // KV_HEADS
LANES = 128
MIB = 2**20
COPIES = 4
STATS = 8

epsilon = 1e-05
rope_base = 500000.0

in_vmem = pl.BlockSpec(memory_space=pltpu.VMEM)
in_smem = pl.BlockSpec(memory_space=pltpu.SMEM)
in_place = pl.BlockSpec(memory_space=pl.ANY)


def swap_with(value, axis, step):
    count = lax.axis_size(axis)
    return lax.ppermute(value, axis, [(i, i ^ step) for i in range(count)])


def exchange(value, axis):
    count = lax.axis_size(axis)
    got = {k: swap_with(value, axis, k) for k in reversed(range(1, count))}
    return [value] + [got[k] for k in range(1, count)]


def scatter_slots(pieces, cross):
    count = lax.axis_size("tensor")
    width = lax.axis_size("inner")
    got = [pieces[0]]
    for k in range(1, count):
        pairs = [
            (t * width + i, (t ^ k) * width + (i ^ cross))
            for t in range(count)
            for i in range(width)
        ]
        got.append(lax.ppermute(pieces[k], ("tensor", "inner"), pairs))
    return got


def steps_up(count):
    return [1 << n for n in range(count.bit_length() - 1)]


def params(mib):
    return pltpu.CompilerParams(vmem_limit_bytes=mib * MIB)


def resident(weight):
    return pltpu.with_memory_space_constraint(weight, pltpu.VMEM)


def in_hbm(weight):
    return pltpu.with_memory_space_constraint(weight, pltpu.HBM)


def product_cost(depth, columns):
    return pl.CostEstimate(
        flops=16 * depth * columns, bytes_accessed=2 * depth * columns, transcendentals=0
    )


def tile_of(columns):
    for tile in (1792, 1024, 896, 512, 256, 128):
        if columns % tile == 0:
            return tile
    return columns


def product_tiles(left, weight_ref, store, first=0, columns=None):
    columns = columns or weight_ref.shape[1]
    tile = tile_of(columns)

    @pl.loop(0, columns // tile)
    def _(step):
        start = pl.multiple_of(step * tile, tile)
        span = pl.ds(pl.multiple_of(first + start, math.gcd(first, tile)), tile)
        store(
            start,
            tile,
            jnp.dot(left, weight_ref[:, span], preferred_element_type=jnp.float32),
        )


def three_parts(value):
    high = value.astype(jnp.bfloat16).astype(jnp.float32)
    rest = value - high
    middle = rest.astype(jnp.bfloat16).astype(jnp.float32)
    return high, middle, rest - middle


def spread(parts, lanes, first):
    out = 0.0
    for n, part in enumerate(parts):
        out = out + jnp.where(lanes == first + n, part, 0.0)
    return out


def squares_block(total):
    lanes = lax.broadcasted_iota(jnp.int32, (total.shape[0], LANES), 1)
    return spread(three_parts(total), lanes, lax.axis_index("inner") * 4)


def copies_of(source, start, target, sems):
    size = target.shape[0]
    cuts = COPIES if len(target.shape) > 1 and size % (16 * COPIES) == 0 else 1
    each = size // cuts
    return [
        pltpu.make_async_copy(
            source.at[pl.ds(start + m * each, each)], target.at[pl.ds(m * each, each)], sems.at[m]
        )
        for m in range(cuts)
    ]


def load_kernel(spans, *refs):
    count = len(spans)
    outs = refs[count + 1 : 2 * count + 1]
    sems = refs[-1]
    copies = []
    for n, (start, _) in enumerate(spans):
        copies += copies_of(refs[n], start, outs[n], sems.at[n])
    for copy in copies:
        copy.start()
    for copy in copies:
        copy.wait()


def load(*arrays, after, spans=None):
    spans = spans or [(0, a.shape[0]) for a in arrays]
    shapes = [(size,) + a.shape[1:] for a, (_, size) in zip(arrays, spans)]
    return pl.pallas_call(
        functools.partial(load_kernel, spans),
        out_shape=tuple(pltpu.VMEM(shape, a.dtype) for shape, a in zip(shapes, arrays)),
        in_specs=[in_place] * (len(arrays) + 1),
        out_specs=tuple(in_vmem for _ in arrays),
        cost_estimate=pl.CostEstimate(
            flops=0, bytes_accessed=2 * sum(math.prod(shape) for shape in shapes), transcendentals=0
        ),
        scratch_shapes=[pltpu.SemaphoreType.DMA((len(arrays), COPIES))],
        compiler_params=params(1),
        name="load",
    )(*[in_hbm(a) for a in arrays], after)


def join_rows(refs, target):
    rows = refs[0].shape[0]
    for n, ref in enumerate(refs):
        target[n * rows : (n + 1) * rows, :] = ref[...].astype(jnp.float32)
    return target[...]


def part_rows(source, refs):
    rows = refs[0].shape[0]
    for n, ref in enumerate(refs):
        ref[...] = source[n * rows : (n + 1) * rows, :].astype(ref.dtype)


def qkv_kernel(slots, gain_ref, wq_ref, wkv_ref, *refs):
    rows_ref = refs[slots]
    out_s, rows_s = refs[-2:]
    wide = join_rows(refs[:slots][::-1], rows_s)
    rows_ref[...] = wide
    total = jnp.sum(wide * wide, axis=1, keepdims=True)
    gain = gain_ref[...].astype(jnp.float32)[None, :]
    scaled = (wide * gain).astype(jnp.bfloat16)
    query_cols = wq_ref.shape[1]
    kv_cols = wkv_ref.shape[1]

    def store_query(start, size, value):
        out_s[:, pl.ds(start, size)] = value

    product_tiles(scaled, wq_ref, store_query)
    out_s[:, query_cols : query_cols + kv_cols] = jnp.dot(
        scaled, wkv_ref[...], preferred_element_type=jnp.float32
    )
    out_s[:, query_cols + kv_cols :] = squares_block(total)
    part_rows(out_s, refs[slots + 1 : 2 * slots + 1])


def project_qkv(rows, gain, w_query, w_kv):
    slots = len(rows)
    own_rows, depth = rows[0].shape
    columns = w_query.shape[1] + w_kv.shape[1] + LANES
    return pl.pallas_call(
        functools.partial(qkv_kernel, slots),
        out_shape=(
            jax.ShapeDtypeStruct((own_rows * slots, depth), jnp.float32),
            *[jax.ShapeDtypeStruct((own_rows, columns), jnp.bfloat16)] * slots,
        ),
        in_specs=[in_vmem] * (3 + slots),
        out_specs=(in_vmem,) * (1 + slots),
        scratch_shapes=[
            pltpu.VMEM((own_rows * slots, columns), jnp.float32),
            pltpu.VMEM((own_rows * slots, depth), jnp.float32),
        ],
        compiler_params=params(2),
        name="project_qkv",
    )(gain, resident(w_query), resident(w_kv), *rows[::-1])


def stack_kernel(*refs):
    refs[-2][...] = join_rows(refs[:-2][::-1], refs[-1]).astype(refs[-2].dtype)


def stack(pieces):
    shape = (len(pieces) * pieces[0].shape[0], pieces[0].shape[1])
    return pl.pallas_call(
        stack_kernel,
        out_shape=jax.ShapeDtypeStruct(shape, pieces[0].dtype),
        in_specs=[in_vmem] * len(pieces),
        out_specs=in_vmem,
        scratch_shapes=[pltpu.VMEM(shape, jnp.float32)],
        compiler_params=params(1),
        name="stack",
    )(*pieces[::-1])


def attend_kernel(
    slots,
    shards,
    lengths_ref,
    cosine_ref,
    sine_ref,
    key_ref,
    value_ref,
    *refs,
):
    parts = refs[:shards]
    out_ref, query_s, kv_s, kv_wide_s, mixed_s, stats_s = refs[-6:]
    all_rows = parts[0].shape[0]
    own_rows = all_rows // slots
    here = HEADS // slots
    query_cols = here * HEAD_DIM
    kv_cols = 2 * KV_HEADS * HEAD_DIM // slots
    columns = query_cols + kv_cols
    tensor_index = lax.axis_index("tensor")
    inner_index = lax.axis_index("inner")
    positions = key_ref.shape[1] // KV_HEADS

    joined = functools.reduce(jnp.add, [ref[...].astype(jnp.float32) for ref in parts])
    squares = jnp.sum(joined[:, columns:], axis=1, keepdims=True)
    joined = joined[:, :columns] * lax.rsqrt(squares / D + epsilon)
    cosine = cosine_ref[...]
    sine = sine_ref[...]

    def rotate(block):
        count = block.shape[0]
        even = lax.broadcasted_iota(jnp.int32, block.shape, 1) % 2 == 0
        other = jnp.where(
            even, pltpu.roll(block, HEAD_DIM - 1, axis=1), pltpu.roll(block, 1, axis=1)
        )
        return block * cosine[:count] + other * sine[:count]

    for j in range(here):
        block = rotate(joined[:, j * HEAD_DIM : (j + 1) * HEAD_DIM])
        query_s[j * all_rows : (j + 1) * all_rows, :] = block
    for s in range(slots):
        kv_s[s] = joined[s * own_rows : (s + 1) * own_rows, query_cols:]
    for d in range(slots):
        kv_wide_s[:, d * kv_cols : (d + 1) * kv_cols] = kv_s[d ^ tensor_index]
    new_keys = []
    new_values = []
    for g in range(KV_HEADS):
        block = kv_wide_s[:, g * HEAD_DIM : (g + 1) * HEAD_DIM]
        new_keys.append(rotate(block).astype(jnp.bfloat16).astype(jnp.float32))
        block = kv_wide_s[:, (KV_HEADS + g) * HEAD_DIM : (KV_HEADS + g + 1) * HEAD_DIM]
        new_values.append(block.astype(jnp.bfloat16).astype(jnp.float32))

    score_scale = HEAD_DIM ** (-0.5)
    row = lax.broadcasted_iota(jnp.int32, (HEADS, 1), 0)
    head = ((row % slots) ^ tensor_index) * here + row // slots
    kv_head = head // GROUP
    column = lax.broadcasted_iota(jnp.int32, (1, positions * KV_HEADS), 1)
    place = column // KV_HEADS + inner_index * positions
    column_head = column % KV_HEADS
    lanes = lax.broadcasted_iota(jnp.int32, (HEADS, LANES), 1)
    for r in range(own_rows):
        queries = query_s[pl.ds(r, HEADS, stride=own_rows), :].astype(jnp.bfloat16)
        scores = (
            lax.dot_general(
                queries,
                key_ref[r],
                (((1,), (1,)), ((), ())),
                preferred_element_type=jnp.float32,
            )
            * score_scale
        )
        used = jnp.where(place < lengths_ref[r : r + 1, 0:1], column_head, -1)
        masked = jnp.where(used == kv_head, scores, -1e30)
        key_rows = 0.0
        value_rows = 0.0
        for g in range(KV_HEADS):
            key_rows = key_rows + jnp.where(kv_head == g, new_keys[g][r : r + 1], 0.0)
            value_rows = value_rows + jnp.where(kv_head == g, new_values[g][r : r + 1], 0.0)
        new_score = (
            jnp.sum(queries.astype(jnp.float32) * key_rows, axis=1, keepdims=True) * score_scale
        )
        new_score = jnp.where(inner_index == 0, new_score, -1e30)
        peak = jnp.maximum(jnp.max(masked, axis=1, keepdims=True), new_score)
        weights = jnp.exp(masked - peak)
        new_weight = jnp.exp(new_score - peak)
        totals = jnp.sum(weights, axis=1, keepdims=True) + new_weight
        mixture = jnp.dot(
            weights.astype(jnp.bfloat16), value_ref[r], preferred_element_type=jnp.float32
        )
        mixture = mixture + new_weight.astype(jnp.bfloat16).astype(jnp.float32) * value_rows
        mixed_s[pl.ds(r, HEADS, stride=own_rows), :] = mixture
        stats_s[pl.ds(r, HEADS, stride=own_rows), :] = spread(
            three_parts(peak), lanes, 0
        ) + spread(three_parts(totals), lanes, 4)
    heads = own_rows * HEADS
    out_ref[:heads, :] = mixed_s[...].astype(jnp.bfloat16)
    packed = stats_s[:all_rows, :]
    for j in range(1, here):
        block = stats_s[j * all_rows : (j + 1) * all_rows, :]
        packed = packed + pltpu.roll(block, j * STATS, axis=1)
    spare = out_ref.shape[0] - heads - all_rows
    if spare:
        packed = jnp.concatenate([packed, jnp.zeros((spare, LANES), jnp.float32)], axis=0)
    out_ref[heads:, :] = packed.astype(jnp.bfloat16)


def attend(lengths, cosine, sine, parts, keys, values, later, slots):
    own_rows = parts[0].shape[0] // slots
    kv_cols = 2 * KV_HEADS * HEAD_DIM // slots
    return pl.pallas_call(
        functools.partial(attend_kernel, slots, len(parts)),
        out_shape=jax.ShapeDtypeStruct(
            (own_rows * HEADS + max(16, own_rows * slots), HEAD_DIM), jnp.bfloat16
        ),
        in_specs=[in_vmem] * (5 + len(parts)) + [in_place] * len(later),
        out_specs=in_vmem,
        scratch_shapes=[
            pltpu.VMEM((own_rows * HEADS, HEAD_DIM), jnp.float32),
            pltpu.VMEM((slots, own_rows, kv_cols), jnp.float32),
            pltpu.VMEM((own_rows, slots * kv_cols), jnp.float32),
            pltpu.VMEM((own_rows * HEADS, HEAD_DIM), jnp.float32),
            pltpu.VMEM((own_rows * HEADS, LANES), jnp.float32),
        ],
        compiler_params=params(6),
        name="attend",
    )(lengths, cosine, sine, resident(keys), resident(values), *parts[::-1], *[resident(w) for w in later])


def combine_kernel(shards, slots, *refs):
    out_s = refs[-1]
    all_rows, columns = out_s.shape
    here = columns // HEAD_DIM
    heads = here * all_rows
    mixtures = [ref[:heads, :].astype(jnp.float32) for ref in refs[:shards]]
    stats = [ref[heads:, :].astype(jnp.float32)[:all_rows] for ref in refs[:shards]]
    for j in range(here):

        def whole(block, first):
            lane = j * STATS + first
            return block[:, lane : lane + 1] + block[:, lane + 1 : lane + 2] + block[:, lane + 2 : lane + 3]

        peaks = [whole(block, 0) for block in stats]
        top = functools.reduce(jnp.maximum, peaks)
        mixed = 0.0
        denominator = 0.0
        for mixture, block, peak in zip(mixtures, stats, peaks):
            factor = jnp.exp(peak - top)
            mixed = mixed + factor * mixture[j * all_rows : (j + 1) * all_rows]
            denominator = denominator + factor * whole(block, 4)
        out_s[:, j * HEAD_DIM : (j + 1) * HEAD_DIM] = mixed / denominator
    part_rows(out_s, refs[-1 - slots : -1])


def combine(parts, later, all_rows, slots):
    count = len(parts)
    columns = HEADS // slots * HEAD_DIM
    return pl.pallas_call(
        functools.partial(combine_kernel, count, slots),
        out_shape=(jax.ShapeDtypeStruct((all_rows // slots, columns), jnp.bfloat16),) * slots,
        in_specs=[in_vmem] * count + [in_place] * len(later),
        out_specs=(in_vmem,) * slots,
        scratch_shapes=[pltpu.VMEM((all_rows, columns), jnp.float32)],
        compiler_params=params(2),
        name="combine",
    )(*parts[::-1], *[resident(w) for w in later])


def turned(block, step, own_rows):
    count = block.shape[0]
    span = step * own_rows
    row = lax.broadcasted_iota(jnp.int32, (count, 1), 0)
    return jnp.where(
        (row // span) % 2 == 0,
        pltpu.roll(block, count - span, axis=0),
        pltpu.roll(block, span, axis=0),
    )


def out_kernel(slots, later, weight_ref, *refs):
    pieces = refs[:slots][::-1]
    outs = refs[slots + later : 2 * slots + later]
    left_s = refs[-1]
    own_rows = pieces[0].shape[0]
    rows = left_s.shape[0]
    lefts = [join_rows(pieces, left_s)]
    for k in range(1, slots):
        low = k & -k
        lefts.append(turned(lefts[k ^ low], low, own_rows))
    left = jnp.concatenate(lefts, axis=0).astype(jnp.bfloat16)

    def store(start, size, value):
        for k, ref in enumerate(outs):
            ref[:, pl.ds(start, size)] = value[k * rows : (k + 1) * rows].astype(jnp.bfloat16)

    product_tiles(left, weight_ref, store)


def project_out(pieces, weight, later):
    slots = len(pieces)
    own_rows, depth = pieces[0].shape
    shape = jax.ShapeDtypeStruct((own_rows * slots, weight.shape[1]), jnp.bfloat16)
    return pl.pallas_call(
        functools.partial(out_kernel, slots, len(later)),
        out_shape=(shape,) * slots,
        in_specs=[in_vmem] * (1 + slots) + [in_place] * len(later),
        out_specs=(in_vmem,) * slots,
        scratch_shapes=[pltpu.VMEM((own_rows * slots, depth), jnp.float32)],
        compiler_params=params(3),
        name="project_out",
    )(resident(weight), *pieces[::-1], *[resident(w) for w in later])


def pair_kernel(first_ref, second_ref, out_ref):
    total = first_ref[...].astype(jnp.float32) + second_ref[...].astype(jnp.float32)
    out_ref[...] = total.astype(jnp.bfloat16)


def pair_sum(first, second):
    return pl.pallas_call(
        pair_kernel,
        out_shape=jax.ShapeDtypeStruct(first.shape, first.dtype),
        in_specs=[in_vmem] * 2,
        out_specs=in_vmem,
        compiler_params=params(2),
        name="pair_sum",
    )(first, second)


def gate_up_tiles(scaled, gate_ref, up_ref, out_ref, first, count):
    def store(offset):
        def place(start, size, value):
            start = pl.multiple_of(offset + start, math.gcd(offset, size))
            out_ref[:, pl.ds(start, size)] = value.astype(jnp.bfloat16)

        return place

    product_tiles(scaled, gate_ref, store(0), first, count)
    product_tiles(scaled, up_ref, store(count), first, count)


def first_gate_up_kernel(slots, count, rows_ref, gain_ref, gate_ref, up_ref, *refs):
    parts = refs[:slots]
    out_ref, updated_ref, scaled_ref = refs[-3:]
    own_rows = updated_ref.shape[0]
    total = functools.reduce(jnp.add, [ref[...].astype(jnp.float32) for ref in parts])
    updated = (rows_ref[...] + total).astype(jnp.bfloat16)
    wide = updated.astype(jnp.float32)
    updated_ref[...] = wide[:own_rows]
    squares = jnp.sum(wide * wide, axis=1, keepdims=True)
    out_ref[:, 2 * count :] = squares_block(squares).astype(jnp.bfloat16)
    scaled = (wide * gain_ref[...].astype(jnp.float32)[None, :]).astype(jnp.bfloat16)
    scaled_ref[...] = scaled
    gate_up_tiles(scaled, gate_ref, up_ref, out_ref, 0, count)


def first_gate_up(rows, gain, parts, w_gate, w_up, later, count, own_rows):
    slots = len(parts)
    return pl.pallas_call(
        functools.partial(first_gate_up_kernel, slots, count),
        out_shape=(
            jax.ShapeDtypeStruct((rows.shape[0], 2 * count + LANES), jnp.bfloat16),
            jax.ShapeDtypeStruct((own_rows, rows.shape[1]), jnp.float32),
            jax.ShapeDtypeStruct(rows.shape, jnp.bfloat16),
        ),
        in_specs=[in_vmem] * (4 + slots) + [in_place] * len(later),
        out_specs=(in_vmem,) * 3,
        compiler_params=params(3),
        cost_estimate=product_cost(w_gate.shape[0], 2 * count),
        name="first_gate_up",
    )(rows, gain, resident(w_gate), resident(w_up), *parts[::-1], *[resident(w) for w in later])


def second_gate_up_kernel(first, count, scaled_ref, gate_ref, up_ref, *refs):
    out_ref = refs[-1]
    gate_up_tiles(scaled_ref[...], gate_ref, up_ref, out_ref, first, count)


def second_gate_up(scaled, w_gate, w_up, later, first):
    count = w_gate.shape[1] - first
    return pl.pallas_call(
        functools.partial(second_gate_up_kernel, first, count),
        out_shape=jax.ShapeDtypeStruct((scaled.shape[0], 2 * count), jnp.bfloat16),
        in_specs=[in_vmem] * 3 + [in_place] * len(later),
        out_specs=in_vmem,
        compiler_params=params(3),
        cost_estimate=product_cost(w_gate.shape[0], 2 * count),
        name="second_gate_up",
    )(scaled, resident(w_gate), resident(w_up), *[resident(w) for w in later])


def hidden_of(near_ref, far_ref, scale, count):
    def total(start):
        span = slice(start, start + count)
        return (near_ref[:, span].astype(jnp.float32) + far_ref[:, span].astype(jnp.float32)) * scale

    gate = total(0)
    return (gate / (1.0 + jnp.exp(-gate)) * total(count)).astype(jnp.bfloat16)


def down_kernel(one_near, one_far, two_near, two_far, weight_ref, *refs):
    hidden_s, out_s = refs[-2:]
    first = (one_near.shape[1] - LANES) // 2
    second = two_near.shape[1] // 2
    squares = jnp.sum(
        one_near[:, 2 * first :].astype(jnp.float32) + one_far[:, 2 * first :].astype(jnp.float32),
        axis=1,
        keepdims=True,
    )
    scale = lax.rsqrt(squares / D + epsilon)
    hidden_s[:, :first] = hidden_of(one_near, one_far, scale, first)
    hidden_s[:, first:] = hidden_of(two_near, two_far, scale, second)

    def store(start, size, value):
        out_s[:, pl.ds(start, size)] = value

    product_tiles(hidden_s[...], weight_ref, store)
    part_rows(out_s, refs[:-2])


def project_down(one, two, weight, slots):
    rows = one[0].shape[0]
    depth, columns = weight.shape
    return pl.pallas_call(
        down_kernel,
        out_shape=(jax.ShapeDtypeStruct((rows // slots, columns), jnp.bfloat16),) * slots,
        in_specs=[in_vmem] * 5,
        out_specs=(in_vmem,) * slots,
        scratch_shapes=[
            pltpu.VMEM((rows, depth), jnp.bfloat16),
            pltpu.VMEM((rows, columns), jnp.float32),
        ],
        compiler_params=params(3),
        name="project_down",
    )(*one, *two, resident(weight))


def finish_kernel(updated_ref, *refs):
    total = functools.reduce(jnp.add, [ref[...].astype(jnp.float32) for ref in refs[:-1]])
    refs[-1][...] = (updated_ref[...] + total).astype(jnp.bfloat16)


def finish(updated, parts):
    return pl.pallas_call(
        finish_kernel,
        out_shape=jax.ShapeDtypeStruct(updated.shape, jnp.bfloat16),
        in_specs=[in_vmem] * (1 + len(parts)),
        out_specs=in_vmem,
        compiler_params=params(1),
        name="finish",
    )(updated, *parts[::-1])


def rotation_tables(positions, repeats):
    inverse = jnp.exp(
        (jnp.arange(HEAD_DIM) // 2).astype(jnp.float32) * (-2.0 / HEAD_DIM) * math.log(rope_base)
    )
    angles = positions[:, None] * inverse[None, :]
    sign = jnp.where(jnp.arange(HEAD_DIM) % 2 == 0, -1.0, 1.0)
    return (
        jnp.tile(jnp.cos(angles), (repeats, 1)),
        jnp.tile(jnp.sin(angles) * sign[None, :], (repeats, 1)),
    )


def local(
    states,
    attn_gain,
    ffn_gain,
    w_query,
    w_kv,
    w_out,
    w_gate,
    w_up,
    w_down,
    key_cache,
    value_cache,
    lengths,
):
    tensor_index = lax.axis_index("tensor")
    slots = lax.axis_size("tensor")
    own_rows = states.shape[0]
    all_rows = own_rows * slots

    got = exchange(states, "tensor")
    own, attn_gain, ffn_gain, w_kv, w_query = load(
        states, attn_gain, ffn_gain, w_kv, w_query, after=states
    )
    rows, *pieces = project_qkv([own] + got[1:], attn_gain, w_query, w_kv)

    rows, lengths = lax.optimization_barrier((rows, lengths))
    my_lengths = lax.dynamic_slice_in_dim(lengths, tensor_index * own_rows, own_rows, 0)
    cosine, sine = rotation_tables(my_lengths.astype(jnp.float32), slots)
    my_lengths = jnp.broadcast_to(my_lengths[:, None], (own_rows, LANES))
    flat = (own_rows, key_cache.shape[1] * KV_HEADS, HEAD_DIM)
    (keys,) = load(key_cache.reshape(flat), after=rows)
    joined = stack(scatter_slots(pieces, 1))
    joined, keys = lax.optimization_barrier((joined, keys))
    (values,) = load(value_cache.reshape(flat), after=joined)
    parts, values = lax.optimization_barrier((exchange(joined, "inner")[::-1], values))
    shard = attend(my_lengths, cosine, sine, parts, keys, values, [], slots)

    (w_out,) = load(w_out, after=shard)
    shards, w_out = lax.optimization_barrier((exchange(shard, "inner")[::-1], w_out))
    pieces = combine(shards[::-1], [w_gate], all_rows, slots)
    parts = scatter_slots(project_out(scatter_slots(pieces, 1), w_out, [w_up]), 0)

    tiles = w_gate.shape[1] // LANES
    first = (tiles + 1) // 2 * LANES
    one, updated, scaled = first_gate_up(
        rows, ffn_gain, parts, w_gate, w_up, [], first, own_rows
    )
    two = second_gate_up(scaled, w_gate, w_up, [], first)
    steps = steps_up(lax.axis_size("inner"))
    for step in steps[:-1]:
        one = pair_sum(one, swap_with(one, "inner", step))
        two = pair_sum(two, swap_with(two, "inner", step))
    one = (one, swap_with(one, "inner", steps[-1]))
    two = (two, swap_with(two, "inner", steps[-1]))
    pieces = project_down(one, two, w_down, slots)
    parts = scatter_slots(pieces, 0)
    return finish(updated, parts)


def solution(mesh):
    in_specs = (
        P(("groups", "tensor"), "inner"),
        P("inner"),
        P("inner"),
        P("inner", "tensor"),
        P("inner", "tensor"),
        P("tensor", "inner"),
        P("inner", "tensor"),
        P("inner", "tensor"),
        P("tensor", "inner"),
        P(("groups", "tensor"), "inner", None, None),
        P(("groups", "tensor"), "inner", None, None),
        P("groups"),
    )
    out_specs = P(("groups", "tensor"), "inner")
    return jax.shard_map(local, mesh=mesh, in_specs=in_specs, out_specs=out_specs, check_vma=False)
```

```python
import functools
import math

import jax
import jax.numpy as jnp
from jax import lax
from jax.experimental import pallas as pl
from jax.experimental.pallas import tpu as pltpu
from jax.sharding import PartitionSpec as P

D = 8192
HEADS = 32
KV_HEADS = 4
HEAD_DIM = 128
GROUP = HEADS // KV_HEADS
LANES = 128
MIB = 2**20
COPIES = 8
STATS = 8

epsilon = 1e-05
rope_base = 500000.0

in_vmem = pl.BlockSpec(memory_space=pltpu.VMEM)
in_smem = pl.BlockSpec(memory_space=pltpu.SMEM)
in_place = pl.BlockSpec(memory_space=pl.ANY)


def swap_with(value, axis, step):
    count = lax.axis_size(axis)
    return lax.ppermute(value, axis, [(i, i ^ step) for i in range(count)])


def exchange(value, axis):
    count = lax.axis_size(axis)
    got = {k: swap_with(value, axis, k) for k in reversed(range(1, count))}
    return [value] + [got[k] for k in range(1, count)]


def scatter_slots(pieces, cross):
    count = lax.axis_size("tensor")
    width = lax.axis_size("inner")
    got = [pieces[0]]
    for k in range(1, count):
        pairs = [
            (t * width + i, (t ^ k) * width + (i ^ cross))
            for t in range(count)
            for i in range(width)
        ]
        got.append(lax.ppermute(pieces[k], ("tensor", "inner"), pairs))
    return got


def joint_permute(value, route):
    width = lax.axis_size("inner")
    pairs = []
    for t in range(lax.axis_size("tensor")):
        for i in range(width):
            to_t, to_i = route(t, i)
            pairs.append((t * width + i, to_t * width + to_i))
    return lax.ppermute(value, ("tensor", "inner"), pairs)


def shared_slots(pieces, swap):
    count = len(pieces)
    pairs = [(k, count - k) for k in range(1, (count + 1) // 2)]
    first = [
        joint_permute(
            operand, lambda t, i, low=low, high=high: (t ^ (high if i % 2 else low), i ^ 1)
        )
        for (low, high), operand in zip(pairs, swap)
    ]
    direct = [joint_permute(pieces[count // 2], lambda t, i: (t ^ (count // 2), i ^ 1))]
    second = [swap_with(value, "inner", 1) for value in first]
    return direct, first, second


def steps_up(count):
    return [1 << n for n in range(count.bit_length() - 1)]


def params(mib):
    return pltpu.CompilerParams(vmem_limit_bytes=mib * MIB)


def resident(weight):
    return pltpu.with_memory_space_constraint(weight, pltpu.VMEM)


def in_hbm(weight):
    return pltpu.with_memory_space_constraint(weight, pltpu.HBM)


def product_cost(depth, columns):
    return pl.CostEstimate(
        flops=16 * depth * columns, bytes_accessed=2 * depth * columns, transcendentals=0
    )


def tile_of(columns):
    for tile in (1792, 1024, 896, 512, 256, 128):
        if columns % tile == 0:
            return tile
    return columns


def product_tiles(left, weight_ref, store, first=0, columns=None):
    columns = columns or weight_ref.shape[1]
    tile = tile_of(columns)

    @pl.loop(0, columns // tile)
    def _(step):
        start = pl.multiple_of(step * tile, tile)
        span = pl.ds(pl.multiple_of(first + start, math.gcd(first, tile)), tile)
        store(
            start,
            tile,
            jnp.dot(left, weight_ref[:, span], preferred_element_type=jnp.float32),
        )


def three_parts(value):
    high = value.astype(jnp.bfloat16).astype(jnp.float32)
    rest = value - high
    middle = rest.astype(jnp.bfloat16).astype(jnp.float32)
    return high, middle, rest - middle


def spread(parts, lanes, first):
    out = 0.0
    for n, part in enumerate(parts):
        out = out + jnp.where(lanes == first + n, part, 0.0)
    return out


def squares_block(total):
    lanes = lax.broadcasted_iota(jnp.int32, (total.shape[0], LANES), 1)
    return spread(three_parts(total), lanes, lax.axis_index("inner") * 4)


def copies_of(source, start, target, sems):
    size = target.shape[0]
    cuts = COPIES if len(target.shape) > 1 and size % (16 * COPIES) == 0 else 1
    each = size // cuts
    return [
        pltpu.make_async_copy(
            source.at[pl.ds(start + m * each, each)], target.at[pl.ds(m * each, each)], sems.at[m]
        )
        for m in range(cuts)
    ]


def load_kernel(spans, *refs):
    count = len(spans)
    outs = refs[count + 1 : 2 * count + 1]
    sems = refs[-1]
    copies = []
    for n, (start, _) in enumerate(spans):
        copies += copies_of(refs[n], start, outs[n], sems.at[n])
    for copy in copies:
        copy.start()
    for copy in copies:
        copy.wait()


def load(*arrays, after, spans=None):
    spans = spans or [(0, a.shape[0]) for a in arrays]
    shapes = [(size,) + a.shape[1:] for a, (_, size) in zip(arrays, spans)]
    return pl.pallas_call(
        functools.partial(load_kernel, spans),
        out_shape=tuple(pltpu.VMEM(shape, a.dtype) for shape, a in zip(shapes, arrays)),
        in_specs=[in_place] * (len(arrays) + 1),
        out_specs=tuple(in_vmem for _ in arrays),
        cost_estimate=pl.CostEstimate(
            flops=0, bytes_accessed=2 * sum(math.prod(shape) for shape in shapes), transcendentals=0
        ),
        scratch_shapes=[pltpu.SemaphoreType.DMA((len(arrays), COPIES))],
        compiler_params=params(1),
        name="load",
    )(*[in_hbm(a) for a in arrays], after)


def join_rows(refs, target):
    rows = refs[0].shape[0]
    for n, ref in enumerate(refs):
        target[n * rows : (n + 1) * rows, :] = ref[...].astype(jnp.float32)
    return target[...]


def part_rows(source, refs):
    rows = refs[0].shape[0]
    for n, ref in enumerate(refs):
        ref[...] = source[n * rows : (n + 1) * rows, :].astype(ref.dtype)


def qkv_kernel(slots, gain_ref, wq_ref, wkv_ref, *refs):
    rows_ref = refs[slots]
    out_s, rows_s = refs[-2:]
    wide = join_rows(refs[:slots][::-1], rows_s)
    rows_ref[...] = wide
    total = jnp.sum(wide * wide, axis=1, keepdims=True)
    gain = gain_ref[...].astype(jnp.float32)[None, :]
    scaled = (wide * gain).astype(jnp.bfloat16)
    query_cols = wq_ref.shape[1]
    kv_cols = wkv_ref.shape[1]

    def store_query(start, size, value):
        out_s[:, pl.ds(start, size)] = value

    product_tiles(scaled, wq_ref, store_query)
    out_s[:, query_cols : query_cols + kv_cols] = jnp.dot(
        scaled, wkv_ref[...], preferred_element_type=jnp.float32
    )
    out_s[:, query_cols + kv_cols :] = squares_block(total)
    part_rows(out_s, refs[slots + 1 : 2 * slots + 1])


def project_qkv(rows, gain, w_query, w_kv):
    slots = len(rows)
    own_rows, depth = rows[0].shape
    columns = w_query.shape[1] + w_kv.shape[1] + LANES
    return pl.pallas_call(
        functools.partial(qkv_kernel, slots),
        out_shape=(
            jax.ShapeDtypeStruct((own_rows * slots, depth), jnp.float32),
            *[jax.ShapeDtypeStruct((own_rows, columns), jnp.bfloat16)] * slots,
        ),
        in_specs=[in_vmem] * (3 + slots),
        out_specs=(in_vmem,) * (1 + slots),
        scratch_shapes=[
            pltpu.VMEM((own_rows * slots, columns), jnp.float32),
            pltpu.VMEM((own_rows * slots, depth), jnp.float32),
        ],
        compiler_params=params(2),
        name="project_qkv",
    )(gain, resident(w_query), resident(w_kv), *rows[::-1])


def stack_kernel(*refs):
    refs[-2][...] = join_rows(refs[:-2][::-1], refs[-1]).astype(refs[-2].dtype)


def stack(pieces):
    shape = (len(pieces) * pieces[0].shape[0], pieces[0].shape[1])
    return pl.pallas_call(
        stack_kernel,
        out_shape=jax.ShapeDtypeStruct(shape, pieces[0].dtype),
        in_specs=[in_vmem] * len(pieces),
        out_specs=in_vmem,
        scratch_shapes=[pltpu.VMEM(shape, jnp.float32)],
        compiler_params=params(1),
        name="stack",
    )(*pieces[::-1])


def attend_kernel(
    slots,
    shards,
    lengths_ref,
    cosine_ref,
    sine_ref,
    key_ref,
    value_ref,
    *refs,
):
    parts = refs[:shards]
    out_ref, query_s, kv_s, kv_wide_s, mixed_s, stats_s = refs[-6:]
    all_rows = parts[0].shape[0]
    own_rows = all_rows // slots
    here = HEADS // slots
    query_cols = here * HEAD_DIM
    kv_cols = 2 * KV_HEADS * HEAD_DIM // slots
    columns = query_cols + kv_cols
    tensor_index = lax.axis_index("tensor")
    inner_index = lax.axis_index("inner")
    positions = key_ref.shape[1] // KV_HEADS

    joined = functools.reduce(jnp.add, [ref[...].astype(jnp.float32) for ref in parts])
    squares = jnp.sum(joined[:, columns:], axis=1, keepdims=True)
    joined = joined[:, :columns] * lax.rsqrt(squares / D + epsilon)
    cosine = cosine_ref[...]
    sine = sine_ref[...]

    def rotate(block):
        count = block.shape[0]
        even = lax.broadcasted_iota(jnp.int32, block.shape, 1) % 2 == 0
        other = jnp.where(
            even, pltpu.roll(block, HEAD_DIM - 1, axis=1), pltpu.roll(block, 1, axis=1)
        )
        return block * cosine[:count] + other * sine[:count]

    for j in range(here):
        block = rotate(joined[:, j * HEAD_DIM : (j + 1) * HEAD_DIM])
        query_s[j * all_rows : (j + 1) * all_rows, :] = block
    for s in range(slots):
        kv_s[s] = joined[s * own_rows : (s + 1) * own_rows, query_cols:]
    for d in range(slots):
        kv_wide_s[:, d * kv_cols : (d + 1) * kv_cols] = kv_s[d ^ tensor_index]
    new_keys = []
    new_values = []
    for g in range(KV_HEADS):
        block = kv_wide_s[:, g * HEAD_DIM : (g + 1) * HEAD_DIM]
        new_keys.append(rotate(block).astype(jnp.bfloat16).astype(jnp.float32))
        block = kv_wide_s[:, (KV_HEADS + g) * HEAD_DIM : (KV_HEADS + g + 1) * HEAD_DIM]
        new_values.append(block.astype(jnp.bfloat16).astype(jnp.float32))

    score_scale = HEAD_DIM ** (-0.5)
    row = lax.broadcasted_iota(jnp.int32, (HEADS, 1), 0)
    head = ((row % slots) ^ tensor_index) * here + row // slots
    kv_head = head // GROUP
    column = lax.broadcasted_iota(jnp.int32, (1, positions * KV_HEADS), 1)
    place = column // KV_HEADS + inner_index * positions
    column_head = column % KV_HEADS
    lanes = lax.broadcasted_iota(jnp.int32, (HEADS, LANES), 1)
    for r in range(own_rows):
        queries = query_s[pl.ds(r, HEADS, stride=own_rows), :].astype(jnp.bfloat16)
        scores = (
            lax.dot_general(
                queries,
                key_ref[r],
                (((1,), (1,)), ((), ())),
                preferred_element_type=jnp.float32,
            )
            * score_scale
        )
        used = jnp.where(place < lengths_ref[r : r + 1, 0:1], column_head, -1)
        masked = jnp.where(used == kv_head, scores, -1e30)
        key_rows = 0.0
        value_rows = 0.0
        for g in range(KV_HEADS):
            key_rows = key_rows + jnp.where(kv_head == g, new_keys[g][r : r + 1], 0.0)
            value_rows = value_rows + jnp.where(kv_head == g, new_values[g][r : r + 1], 0.0)
        new_score = (
            jnp.sum(queries.astype(jnp.float32) * key_rows, axis=1, keepdims=True) * score_scale
        )
        new_score = jnp.where(inner_index == 0, new_score, -1e30)
        peak = jnp.maximum(jnp.max(masked, axis=1, keepdims=True), new_score)
        weights = jnp.exp(masked - peak)
        new_weight = jnp.exp(new_score - peak)
        totals = jnp.sum(weights, axis=1, keepdims=True) + new_weight
        mixture = jnp.dot(
            weights.astype(jnp.bfloat16), value_ref[r], preferred_element_type=jnp.float32
        )
        mixture = mixture + new_weight.astype(jnp.bfloat16).astype(jnp.float32) * value_rows
        mixed_s[pl.ds(r, HEADS, stride=own_rows), :] = mixture
        stats_s[pl.ds(r, HEADS, stride=own_rows), :] = spread(
            three_parts(peak), lanes, 0
        ) + spread(three_parts(totals), lanes, 4)
    heads = own_rows * HEADS
    out_ref[:heads, :] = mixed_s[...].astype(jnp.bfloat16)
    packed = stats_s[:all_rows, :]
    for j in range(1, here):
        block = stats_s[j * all_rows : (j + 1) * all_rows, :]
        packed = packed + pltpu.roll(block, j * STATS, axis=1)
    spare = out_ref.shape[0] - heads - all_rows
    if spare:
        packed = jnp.concatenate([packed, jnp.zeros((spare, LANES), jnp.float32)], axis=0)
    out_ref[heads:, :] = packed.astype(jnp.bfloat16)


def attend(lengths, cosine, sine, parts, keys, values, later, slots):
    own_rows = parts[0].shape[0] // slots
    kv_cols = 2 * KV_HEADS * HEAD_DIM // slots
    return pl.pallas_call(
        functools.partial(attend_kernel, slots, len(parts)),
        out_shape=jax.ShapeDtypeStruct(
            (own_rows * HEADS + max(16, own_rows * slots), HEAD_DIM), jnp.bfloat16
        ),
        in_specs=[in_vmem] * (5 + len(parts)) + [in_place] * len(later),
        out_specs=in_vmem,
        scratch_shapes=[
            pltpu.VMEM((own_rows * HEADS, HEAD_DIM), jnp.float32),
            pltpu.VMEM((slots, own_rows, kv_cols), jnp.float32),
            pltpu.VMEM((own_rows, slots * kv_cols), jnp.float32),
            pltpu.VMEM((own_rows * HEADS, HEAD_DIM), jnp.float32),
            pltpu.VMEM((own_rows * HEADS, LANES), jnp.float32),
        ],
        compiler_params=params(6),
        name="attend",
    )(lengths, cosine, sine, resident(keys), resident(values), *parts[::-1], *[resident(w) for w in later])


def combine_kernel(shards, slots, *refs):
    out_s = refs[-1]
    all_rows, columns = out_s.shape
    here = columns // HEAD_DIM
    heads = here * all_rows
    mixtures = [ref[:heads, :].astype(jnp.float32) for ref in refs[:shards]]
    stats = [ref[heads:, :].astype(jnp.float32)[:all_rows] for ref in refs[:shards]]
    for j in range(here):

        def whole(block, first):
            lane = j * STATS + first
            return block[:, lane : lane + 1] + block[:, lane + 1 : lane + 2] + block[:, lane + 2 : lane + 3]

        peaks = [whole(block, 0) for block in stats]
        top = functools.reduce(jnp.maximum, peaks)
        mixed = 0.0
        denominator = 0.0
        for mixture, block, peak in zip(mixtures, stats, peaks):
            factor = jnp.exp(peak - top)
            mixed = mixed + factor * mixture[j * all_rows : (j + 1) * all_rows]
            denominator = denominator + factor * whole(block, 4)
        out_s[:, j * HEAD_DIM : (j + 1) * HEAD_DIM] = mixed / denominator
    pairs = (slots - 1) // 2
    part_rows(out_s, refs[-1 - slots - pairs : -1 - pairs])
    rows = all_rows // slots
    odd = lax.axis_index("inner") % 2 == 1
    for n in range(pairs):
        low, high = n + 1, slots - n - 1
        sent = jnp.where(
            odd,
            out_s[high * rows : (high + 1) * rows, :],
            out_s[low * rows : (low + 1) * rows, :],
        )
        refs[-1 - pairs + n][...] = sent.astype(jnp.bfloat16)


def combine(parts, later, all_rows, slots):
    count = len(parts)
    columns = HEADS // slots * HEAD_DIM
    outs = slots + (slots - 1) // 2
    return pl.pallas_call(
        functools.partial(combine_kernel, count, slots),
        out_shape=(jax.ShapeDtypeStruct((all_rows // slots, columns), jnp.bfloat16),) * outs,
        in_specs=[in_vmem] * count + [in_place] * len(later),
        out_specs=(in_vmem,) * outs,
        scratch_shapes=[pltpu.VMEM((all_rows, columns), jnp.float32)],
        compiler_params=params(2),
        name="combine",
    )(*parts[::-1], *[resident(w) for w in later])


def turned(block, step, own_rows):
    count = block.shape[0]
    span = step * own_rows
    row = lax.broadcasted_iota(jnp.int32, (count, 1), 0)
    return jnp.where(
        (row // span) % 2 == 0,
        pltpu.roll(block, count - span, axis=0),
        pltpu.roll(block, span, axis=0),
    )


def out_kernel(slots, later, weight_ref, own_ref, *refs):
    pairs = (slots - 1) // 2
    direct_ref = refs[0]
    first = refs[1 : 1 + pairs]
    second = refs[1 + pairs : 1 + 2 * pairs]
    outs = refs[1 + 2 * pairs + later : 1 + 2 * pairs + later + slots]
    left_s = refs[-1]
    own_rows = own_ref.shape[0]
    rows = left_s.shape[0]

    def put(slot, value):
        left_s[slot * own_rows : (slot + 1) * own_rows, :] = value

    put(0, own_ref[...].astype(jnp.float32))
    put(slots // 2, direct_ref[...].astype(jnp.float32))
    odd = lax.axis_index("inner") % 2 == 1
    for n in range(pairs):
        one = first[n][...].astype(jnp.float32)
        two = second[n][...].astype(jnp.float32)
        put(n + 1, jnp.where(odd, one, two))
        put(slots - n - 1, jnp.where(odd, two, one))
    lefts = [left_s[...]]
    for k in range(1, slots):
        low = k & -k
        lefts.append(turned(lefts[k ^ low], low, own_rows))
    left = jnp.concatenate(lefts, axis=0).astype(jnp.bfloat16)

    def store(start, size, value):
        for k, ref in enumerate(outs):
            ref[:, pl.ds(start, size)] = value[k * rows : (k + 1) * rows].astype(jnp.bfloat16)

    product_tiles(left, weight_ref, store)


def project_out(own, direct, first, second, weight, later, slots):
    own_rows, depth = own.shape
    shape = jax.ShapeDtypeStruct((own_rows * slots, weight.shape[1]), jnp.bfloat16)
    ins = 3 + len(first) + len(second)
    return pl.pallas_call(
        functools.partial(out_kernel, slots, len(later)),
        out_shape=(shape,) * slots,
        in_specs=[in_vmem] * ins + [in_place] * len(later),
        out_specs=(in_vmem,) * slots,
        scratch_shapes=[pltpu.VMEM((own_rows * slots, depth), jnp.float32)],
        compiler_params=params(3),
        name="project_out",
    )(resident(weight), own, direct, *first, *second, *[resident(w) for w in later])


def pair_kernel(first_ref, second_ref, out_ref):
    total = first_ref[...].astype(jnp.float32) + second_ref[...].astype(jnp.float32)
    out_ref[...] = total.astype(jnp.bfloat16)


def pair_sum(first, second):
    return pl.pallas_call(
        pair_kernel,
        out_shape=jax.ShapeDtypeStruct(first.shape, first.dtype),
        in_specs=[in_vmem] * 2,
        out_specs=in_vmem,
        compiler_params=params(2),
        name="pair_sum",
    )(first, second)


def gate_up_tiles(scaled, gate_ref, up_ref, out_ref, first, count):
    def store(offset):
        def place(start, size, value):
            start = pl.multiple_of(offset + start, math.gcd(offset, size))
            out_ref[:, pl.ds(start, size)] = value.astype(jnp.bfloat16)

        return place

    product_tiles(scaled, gate_ref, store(0), first, count)
    product_tiles(scaled, up_ref, store(count), first, count)


def first_gate_up_kernel(slots, count, rows_ref, gain_ref, gate_ref, up_ref, *refs):
    parts = refs[:slots]
    out_ref, updated_ref, scaled_ref = refs[-3:]
    own_rows = updated_ref.shape[0]
    total = functools.reduce(jnp.add, [ref[...].astype(jnp.float32) for ref in parts])
    updated = (rows_ref[...] + total).astype(jnp.bfloat16)
    wide = updated.astype(jnp.float32)
    updated_ref[...] = wide[:own_rows]
    squares = jnp.sum(wide * wide, axis=1, keepdims=True)
    out_ref[:, 2 * count :] = squares_block(squares).astype(jnp.bfloat16)
    scaled = (wide * gain_ref[...].astype(jnp.float32)[None, :]).astype(jnp.bfloat16)
    scaled_ref[...] = scaled
    gate_up_tiles(scaled, gate_ref, up_ref, out_ref, 0, count)


def first_gate_up(rows, gain, parts, w_gate, w_up, later, count, own_rows):
    slots = len(parts)
    return pl.pallas_call(
        functools.partial(first_gate_up_kernel, slots, count),
        out_shape=(
            jax.ShapeDtypeStruct((rows.shape[0], 2 * count + LANES), jnp.bfloat16),
            jax.ShapeDtypeStruct((own_rows, rows.shape[1]), jnp.float32),
            jax.ShapeDtypeStruct(rows.shape, jnp.bfloat16),
        ),
        in_specs=[in_vmem] * (4 + slots) + [in_place] * len(later),
        out_specs=(in_vmem,) * 3,
        compiler_params=params(3),
        cost_estimate=product_cost(w_gate.shape[0], 2 * count),
        name="first_gate_up",
    )(rows, gain, resident(w_gate), resident(w_up), *parts[::-1], *[resident(w) for w in later])


def second_gate_up_kernel(first, count, scaled_ref, gate_ref, up_ref, *refs):
    out_ref = refs[-1]
    gate_up_tiles(scaled_ref[...], gate_ref, up_ref, out_ref, first, count)


def second_gate_up(scaled, w_gate, w_up, later, first):
    count = w_gate.shape[1] - first
    return pl.pallas_call(
        functools.partial(second_gate_up_kernel, first, count),
        out_shape=jax.ShapeDtypeStruct((scaled.shape[0], 2 * count), jnp.bfloat16),
        in_specs=[in_vmem] * 3 + [in_place] * len(later),
        out_specs=in_vmem,
        compiler_params=params(3),
        cost_estimate=product_cost(w_gate.shape[0], 2 * count),
        name="second_gate_up",
    )(scaled, resident(w_gate), resident(w_up), *[resident(w) for w in later])


def hidden_of(near_ref, far_ref, scale, count):
    def total(start):
        span = slice(start, start + count)
        return (near_ref[:, span].astype(jnp.float32) + far_ref[:, span].astype(jnp.float32)) * scale

    gate = total(0)
    return (gate / (1.0 + jnp.exp(-gate)) * total(count)).astype(jnp.bfloat16)


def down_kernel(one_near, one_far, two_near, two_far, weight_ref, *refs):
    hidden_s, out_s = refs[-2:]
    first = (one_near.shape[1] - LANES) // 2
    second = two_near.shape[1] // 2
    squares = jnp.sum(
        one_near[:, 2 * first :].astype(jnp.float32) + one_far[:, 2 * first :].astype(jnp.float32),
        axis=1,
        keepdims=True,
    )
    scale = lax.rsqrt(squares / D + epsilon)
    hidden_s[:, :first] = hidden_of(one_near, one_far, scale, first)
    hidden_s[:, first:] = hidden_of(two_near, two_far, scale, second)

    def store(start, size, value):
        out_s[:, pl.ds(start, size)] = value

    product_tiles(hidden_s[...], weight_ref, store)
    part_rows(out_s, refs[:-2])


def project_down(one, two, weight, slots):
    rows = one[0].shape[0]
    depth, columns = weight.shape
    return pl.pallas_call(
        down_kernel,
        out_shape=(jax.ShapeDtypeStruct((rows // slots, columns), jnp.bfloat16),) * slots,
        in_specs=[in_vmem] * 5,
        out_specs=(in_vmem,) * slots,
        scratch_shapes=[
            pltpu.VMEM((rows, depth), jnp.bfloat16),
            pltpu.VMEM((rows, columns), jnp.float32),
        ],
        compiler_params=params(3),
        name="project_down",
    )(*one, *two, resident(weight))


def finish_kernel(updated_ref, *refs):
    total = functools.reduce(jnp.add, [ref[...].astype(jnp.float32) for ref in refs[:-1]])
    refs[-1][...] = (updated_ref[...] + total).astype(jnp.bfloat16)


def finish(updated, parts):
    return pl.pallas_call(
        finish_kernel,
        out_shape=jax.ShapeDtypeStruct(updated.shape, jnp.bfloat16),
        in_specs=[in_vmem] * (1 + len(parts)),
        out_specs=in_vmem,
        compiler_params=params(1),
        name="finish",
    )(updated, *parts[::-1])


def rotation_tables(positions, repeats):
    inverse = jnp.exp(
        (jnp.arange(HEAD_DIM) // 2).astype(jnp.float32) * (-2.0 / HEAD_DIM) * math.log(rope_base)
    )
    angles = positions[:, None] * inverse[None, :]
    sign = jnp.where(jnp.arange(HEAD_DIM) % 2 == 0, -1.0, 1.0)
    return (
        jnp.tile(jnp.cos(angles), (repeats, 1)),
        jnp.tile(jnp.sin(angles) * sign[None, :], (repeats, 1)),
    )


def local(
    states,
    attn_gain,
    ffn_gain,
    w_query,
    w_kv,
    w_out,
    w_gate,
    w_up,
    w_down,
    key_cache,
    value_cache,
    lengths,
):
    tensor_index = lax.axis_index("tensor")
    slots = lax.axis_size("tensor")
    own_rows = states.shape[0]
    all_rows = own_rows * slots

    got = exchange(states, "tensor")
    own, attn_gain, ffn_gain, w_kv, w_query = load(
        states, attn_gain, ffn_gain, w_kv, w_query, after=states
    )
    rows, *pieces = project_qkv([own] + got[1:], attn_gain, w_query, w_kv)

    rows, lengths = lax.optimization_barrier((rows, lengths))
    my_lengths = lax.dynamic_slice_in_dim(lengths, tensor_index * own_rows, own_rows, 0)
    cosine, sine = rotation_tables(my_lengths.astype(jnp.float32), slots)
    my_lengths = jnp.broadcast_to(my_lengths[:, None], (own_rows, LANES))
    flat = (own_rows, key_cache.shape[1] * KV_HEADS, HEAD_DIM)
    (keys,) = load(key_cache.reshape(flat), after=rows)
    joined = stack(scatter_slots(pieces, 1))
    joined, keys = lax.optimization_barrier((joined, keys))
    (values,) = load(value_cache.reshape(flat), after=joined)
    parts, values = lax.optimization_barrier((exchange(joined, "inner")[::-1], values))
    shard = attend(my_lengths, cosine, sine, parts, keys, values, [], slots)

    (w_out,) = load(w_out, after=shard)
    shards, w_out = lax.optimization_barrier((exchange(shard, "inner")[::-1], w_out))
    pieces = combine(shards[::-1], [w_gate], all_rows, slots)
    (direct,), first, second = shared_slots(pieces[:slots], pieces[slots:])
    parts = project_out(pieces[0], direct, first, second, w_out, [w_up], slots)
    parts = scatter_slots(parts, 0)

    tiles = w_gate.shape[1] // LANES
    first = (tiles + 1) // 2 * LANES
    one, updated, scaled = first_gate_up(
        rows, ffn_gain, parts, w_gate, w_up, [], first, own_rows
    )
    two = second_gate_up(scaled, w_gate, w_up, [], first)
    steps = steps_up(lax.axis_size("inner"))
    for step in steps[:-1]:
        one = pair_sum(one, swap_with(one, "inner", step))
        two = pair_sum(two, swap_with(two, "inner", step))
    one = (one, swap_with(one, "inner", steps[-1]))
    two = (two, swap_with(two, "inner", steps[-1]))
    pieces = project_down(one, two, w_down, slots)
    parts = scatter_slots(pieces, 0)
    return finish(updated, parts)


def solution(mesh):
    in_specs = (
        P(("groups", "tensor"), "inner"),
        P("inner"),
        P("inner"),
        P("inner", "tensor"),
        P("inner", "tensor"),
        P("tensor", "inner"),
        P("inner", "tensor"),
        P("inner", "tensor"),
        P("tensor", "inner"),
        P(("groups", "tensor"), "inner", None, None),
        P(("groups", "tensor"), "inner", None, None),
        P("groups"),
    )
    out_specs = P(("groups", "tensor"), "inner")
    return jax.shard_map(local, mesh=mesh, in_specs=in_specs, out_specs=out_specs, check_vma=False)
```

```python
import functools
import math

import jax
import jax.numpy as jnp
from jax import lax
from jax.experimental import pallas as pl
from jax.experimental.pallas import tpu as pltpu
from jax.sharding import PartitionSpec as P

D = 8192
HEADS = 32
KV_HEADS = 4
HEAD_DIM = 128
GROUP = HEADS // KV_HEADS
LANES = 128
MIB = 2**20
COPIES = 1
STATS = 8

epsilon = 1e-05
rope_base = 500000.0

in_vmem = pl.BlockSpec(memory_space=pltpu.VMEM)
in_smem = pl.BlockSpec(memory_space=pltpu.SMEM)
in_place = pl.BlockSpec(memory_space=pl.ANY)


def swap_with(value, axis, step):
    count = lax.axis_size(axis)
    return lax.ppermute(value, axis, [(i, i ^ step) for i in range(count)])


def exchange(value, axis):
    count = lax.axis_size(axis)
    got = {k: swap_with(value, axis, k) for k in reversed(range(1, count))}
    return [value] + [got[k] for k in range(1, count)]


def scatter_slots(pieces, cross):
    count = lax.axis_size("tensor")
    width = lax.axis_size("inner")
    got = [pieces[0]]
    for k in range(1, count):
        pairs = [
            (t * width + i, (t ^ k) * width + (i ^ cross))
            for t in range(count)
            for i in range(width)
        ]
        got.append(lax.ppermute(pieces[k], ("tensor", "inner"), pairs))
    return got


def steps_up(count):
    return [1 << n for n in range(count.bit_length() - 1)]


def params(mib):
    return pltpu.CompilerParams(vmem_limit_bytes=mib * MIB)


def resident(weight):
    return pltpu.with_memory_space_constraint(weight, pltpu.VMEM)


def in_hbm(weight):
    return pltpu.with_memory_space_constraint(weight, pltpu.HBM)


def product_cost(depth, columns):
    return pl.CostEstimate(
        flops=16 * depth * columns, bytes_accessed=2 * depth * columns, transcendentals=0
    )


def tile_of(columns):
    for tile in (1792, 1024, 896, 512, 256, 128):
        if columns % tile == 0:
            return tile
    return columns


def product_tiles(left, weight_ref, store, first=0, columns=None):
    columns = columns or weight_ref.shape[1]
    tile = tile_of(columns)

    @pl.loop(0, columns // tile)
    def _(step):
        start = pl.multiple_of(step * tile, tile)
        span = pl.ds(pl.multiple_of(first + start, math.gcd(first, tile)), tile)
        store(
            start,
            tile,
            jnp.dot(left, weight_ref[:, span], preferred_element_type=jnp.float32),
        )


def three_parts(value):
    high = value.astype(jnp.bfloat16).astype(jnp.float32)
    rest = value - high
    middle = rest.astype(jnp.bfloat16).astype(jnp.float32)
    return high, middle, rest - middle


def spread(parts, lanes, first):
    out = 0.0
    for n, part in enumerate(parts):
        out = out + jnp.where(lanes == first + n, part, 0.0)
    return out


def squares_block(total, lanes):
    return spread(three_parts(total), lanes, 0)


def copies_of(source, start, target, sems):
    size = target.shape[0]
    cuts = COPIES if len(target.shape) > 1 and size % (16 * COPIES) == 0 else 1
    each = size // cuts
    return [
        pltpu.make_async_copy(
            source.at[pl.ds(start + m * each, each)], target.at[pl.ds(m * each, each)], sems.at[m]
        )
        for m in range(cuts)
    ]


def load_kernel(spans, *refs):
    count = len(spans)
    outs = refs[count + 1 : 2 * count + 1]
    sems = refs[-1]
    copies = []
    for n, (start, _) in enumerate(spans):
        copies += copies_of(refs[n], start, outs[n], sems.at[n])
    for copy in copies:
        copy.start()
    for copy in copies:
        copy.wait()


def load(*arrays, after, spans=None):
    spans = spans or [(0, a.shape[0]) for a in arrays]
    shapes = [(size,) + a.shape[1:] for a, (_, size) in zip(arrays, spans)]
    return pl.pallas_call(
        functools.partial(load_kernel, spans),
        out_shape=tuple(pltpu.VMEM(shape, a.dtype) for shape, a in zip(shapes, arrays)),
        in_specs=[in_place] * (len(arrays) + 1),
        out_specs=tuple(in_vmem for _ in arrays),
        cost_estimate=pl.CostEstimate(
            flops=0, bytes_accessed=2 * sum(math.prod(shape) for shape in shapes), transcendentals=0
        ),
        scratch_shapes=[pltpu.SemaphoreType.DMA((len(arrays), COPIES))],
        compiler_params=params(1),
        name="load",
    )(*[in_hbm(a) for a in arrays], after)


def join_rows(refs, target):
    rows = refs[0].shape[0]
    for n, ref in enumerate(refs):
        target[n * rows : (n + 1) * rows, :] = ref[...].astype(jnp.float32)
    return target[...]


def part_rows(source, refs):
    rows = refs[0].shape[0]
    for n, ref in enumerate(refs):
        ref[...] = source[n * rows : (n + 1) * rows, :].astype(ref.dtype)


def qkv_kernel(slots, lanes_ref, gain_ref, wq_ref, wkv_ref, *refs):
    rows_ref = refs[slots]
    out_s, rows_s = refs[-2:]
    wide = join_rows(refs[:slots][::-1], rows_s)
    rows_ref[...] = wide
    total = jnp.sum(wide * wide, axis=1, keepdims=True)
    gain = gain_ref[...].astype(jnp.float32)[None, :]
    scaled = (wide * gain).astype(jnp.bfloat16)
    query_cols = wq_ref.shape[1]
    kv_cols = wkv_ref.shape[1]

    def store_query(start, size, value):
        out_s[:, pl.ds(start, size)] = value

    product_tiles(scaled, wq_ref, store_query)
    out_s[:, query_cols : query_cols + kv_cols] = jnp.dot(
        scaled, wkv_ref[...], preferred_element_type=jnp.float32
    )
    out_s[:, query_cols + kv_cols :] = squares_block(total, lanes_ref[...])
    part_rows(out_s, refs[slots + 1 : 2 * slots + 1])


def project_qkv(lanes, rows, gain, w_query, w_kv):
    slots = len(rows)
    own_rows, depth = rows[0].shape
    columns = w_query.shape[1] + w_kv.shape[1] + LANES
    return pl.pallas_call(
        functools.partial(qkv_kernel, slots),
        out_shape=(
            jax.ShapeDtypeStruct((own_rows * slots, depth), jnp.float32),
            *[jax.ShapeDtypeStruct((own_rows, columns), jnp.bfloat16)] * slots,
        ),
        in_specs=[in_vmem] * (4 + slots),
        out_specs=(in_vmem,) * (1 + slots),
        scratch_shapes=[
            pltpu.VMEM((own_rows * slots, columns), jnp.float32),
            pltpu.VMEM((own_rows * slots, depth), jnp.float32),
        ],
        compiler_params=params(2),
        name="project_qkv",
    )(lanes, gain, resident(w_query), resident(w_kv), *rows[::-1])


def stack_kernel(*refs):
    refs[-2][...] = join_rows(refs[:-2][::-1], refs[-1]).astype(refs[-2].dtype)


def stack(pieces):
    shape = (len(pieces) * pieces[0].shape[0], pieces[0].shape[1])
    return pl.pallas_call(
        stack_kernel,
        out_shape=jax.ShapeDtypeStruct(shape, pieces[0].dtype),
        in_specs=[in_vmem] * len(pieces),
        out_specs=in_vmem,
        scratch_shapes=[pltpu.VMEM(shape, jnp.float32)],
        compiler_params=params(1),
        name="stack",
    )(*pieces[::-1])


def attend_kernel(
    slots,
    shards,
    marks_ref,
    kv_head_ref,
    cosine_ref,
    sine_ref,
    key_ref,
    value_ref,
    *refs,
):
    parts = refs[:shards]
    out_ref, query_s, kv_s, kv_wide_s, mixed_s, stats_s = refs[-6:]
    all_rows = parts[0].shape[0]
    own_rows = all_rows // slots
    here = HEADS // slots
    query_cols = here * HEAD_DIM
    kv_cols = 2 * KV_HEADS * HEAD_DIM // slots
    columns = query_cols + kv_cols
    positions = key_ref.shape[1] // KV_HEADS

    joined = functools.reduce(jnp.add, [ref[...].astype(jnp.float32) for ref in parts])
    squares = jnp.sum(joined[:, columns:], axis=1, keepdims=True)
    joined = joined[:, :columns] * lax.rsqrt(squares / D + epsilon)
    cosine = cosine_ref[...]
    sine = sine_ref[...]

    def rotate(block):
        count = block.shape[0]
        even = lax.broadcasted_iota(jnp.int32, block.shape, 1) % 2 == 0
        other = jnp.where(
            even, pltpu.roll(block, HEAD_DIM - 1, axis=1), pltpu.roll(block, 1, axis=1)
        )
        return block * cosine[:count] + other * sine[:count]

    for j in range(here):
        block = rotate(joined[:, j * HEAD_DIM : (j + 1) * HEAD_DIM])
        query_s[j * all_rows : (j + 1) * all_rows, :] = block
    block = joined[:, query_cols:]
    for n in range(slots.bit_length() - 1):
        bit = marks_ref[own_rows + 1 + n : own_rows + 2 + n, 0:1]
        block = jnp.where(bit != 0, turned(block, 1 << n, own_rows), block)
    kv_s[...] = block
    for d in range(slots):
        rows = kv_s[d * own_rows : (d + 1) * own_rows, :]
        kv_wide_s[:, d * kv_cols : (d + 1) * kv_cols] = rows
    new_keys = []
    new_values = []
    for g in range(KV_HEADS):
        block = kv_wide_s[:, g * HEAD_DIM : (g + 1) * HEAD_DIM]
        new_keys.append(rotate(block).astype(jnp.bfloat16).astype(jnp.float32))
        block = kv_wide_s[:, (KV_HEADS + g) * HEAD_DIM : (KV_HEADS + g + 1) * HEAD_DIM]
        new_values.append(block.astype(jnp.bfloat16).astype(jnp.float32))

    score_scale = HEAD_DIM ** (-0.5)
    kv_head = kv_head_ref[:, 0:1]
    column = lax.broadcasted_iota(jnp.int32, (1, positions * KV_HEADS), 1)
    place = column // KV_HEADS
    column_head = column % KV_HEADS
    lanes = lax.broadcasted_iota(jnp.int32, (HEADS, LANES), 1)
    for r in range(own_rows):
        queries = query_s[pl.ds(r, HEADS, stride=own_rows), :].astype(jnp.bfloat16)
        scores = (
            lax.dot_general(
                queries,
                key_ref[r],
                (((1,), (1,)), ((), ())),
                preferred_element_type=jnp.float32,
            )
            * score_scale
        )
        used = jnp.where(place < marks_ref[r : r + 1, 0:1], column_head, -1)
        masked = jnp.where(used == kv_head, scores, -1e30)
        key_rows = 0.0
        value_rows = 0.0
        for g in range(KV_HEADS):
            key_rows = key_rows + jnp.where(kv_head == g, new_keys[g][r : r + 1], 0.0)
            value_rows = value_rows + jnp.where(kv_head == g, new_values[g][r : r + 1], 0.0)
        new_score = (
            jnp.sum(queries.astype(jnp.float32) * key_rows, axis=1, keepdims=True) * score_scale
        )
        new_score = jnp.where(marks_ref[own_rows : own_rows + 1, 0:1] != 0, new_score, -1e30)
        peak = jnp.maximum(jnp.max(masked, axis=1, keepdims=True), new_score)
        weights = jnp.exp(masked - peak)
        new_weight = jnp.exp(new_score - peak)
        totals = jnp.sum(weights, axis=1, keepdims=True) + new_weight
        mixture = jnp.dot(
            weights.astype(jnp.bfloat16), value_ref[r], preferred_element_type=jnp.float32
        )
        mixture = mixture + new_weight.astype(jnp.bfloat16).astype(jnp.float32) * value_rows
        mixed_s[pl.ds(r, HEADS, stride=own_rows), :] = mixture
        stats_s[pl.ds(r, HEADS, stride=own_rows), :] = spread(
            three_parts(peak), lanes, 0
        ) + spread(three_parts(totals), lanes, 4)
    heads = own_rows * HEADS
    out_ref[:heads, :] = mixed_s[...].astype(jnp.bfloat16)
    packed = stats_s[:all_rows, :]
    for j in range(1, here):
        block = stats_s[j * all_rows : (j + 1) * all_rows, :]
        packed = packed + pltpu.roll(block, j * STATS, axis=1)
    spare = out_ref.shape[0] - heads - all_rows
    if spare:
        packed = jnp.concatenate([packed, jnp.zeros((spare, LANES), jnp.float32)], axis=0)
    out_ref[heads:, :] = packed.astype(jnp.bfloat16)


def attend(marks, kv_head, cosine, sine, parts, keys, values, later, slots):
    own_rows = parts[0].shape[0] // slots
    kv_cols = 2 * KV_HEADS * HEAD_DIM // slots
    return pl.pallas_call(
        functools.partial(attend_kernel, slots, len(parts)),
        out_shape=jax.ShapeDtypeStruct(
            (own_rows * HEADS + max(16, own_rows * slots), HEAD_DIM), jnp.bfloat16
        ),
        in_specs=[in_vmem] * (6 + len(parts)) + [in_place] * len(later),
        out_specs=in_vmem,
        scratch_shapes=[
            pltpu.VMEM((own_rows * HEADS, HEAD_DIM), jnp.float32),
            pltpu.VMEM((slots * own_rows, kv_cols), jnp.float32),
            pltpu.VMEM((own_rows, slots * kv_cols), jnp.float32),
            pltpu.VMEM((own_rows * HEADS, HEAD_DIM), jnp.float32),
            pltpu.VMEM((own_rows * HEADS, LANES), jnp.float32),
        ],
        compiler_params=params(6),
        name="attend",
    )(marks, kv_head, cosine, sine, resident(keys), resident(values), *parts[::-1], *[resident(w) for w in later])


def combine_kernel(shards, slots, *refs):
    out_s = refs[-1]
    all_rows, columns = out_s.shape
    here = columns // HEAD_DIM
    heads = here * all_rows
    mixtures = [ref[:heads, :].astype(jnp.float32) for ref in refs[:shards]]
    stats = [ref[heads:, :].astype(jnp.float32)[:all_rows] for ref in refs[:shards]]
    for j in range(here):

        def whole(block, first):
            lane = j * STATS + first
            return block[:, lane : lane + 1] + block[:, lane + 1 : lane + 2] + block[:, lane + 2 : lane + 3]

        peaks = [whole(block, 0) for block in stats]
        top = functools.reduce(jnp.maximum, peaks)
        mixed = 0.0
        denominator = 0.0
        for mixture, block, peak in zip(mixtures, stats, peaks):
            factor = jnp.exp(peak - top)
            mixed = mixed + factor * mixture[j * all_rows : (j + 1) * all_rows]
            denominator = denominator + factor * whole(block, 4)
        out_s[:, j * HEAD_DIM : (j + 1) * HEAD_DIM] = mixed / denominator
    part_rows(out_s, refs[-1 - slots : -1])


def combine(parts, later, all_rows, slots):
    count = len(parts)
    columns = HEADS // slots * HEAD_DIM
    return pl.pallas_call(
        functools.partial(combine_kernel, count, slots),
        out_shape=(jax.ShapeDtypeStruct((all_rows // slots, columns), jnp.bfloat16),) * slots,
        in_specs=[in_vmem] * count + [in_place] * len(later),
        out_specs=(in_vmem,) * slots,
        scratch_shapes=[pltpu.VMEM((all_rows, columns), jnp.float32)],
        compiler_params=params(2),
        name="combine",
    )(*parts[::-1], *[resident(w) for w in later])


def turned(block, step, own_rows):
    count = block.shape[0]
    span = step * own_rows
    row = lax.broadcasted_iota(jnp.int32, (count, 1), 0)
    return jnp.where(
        (row // span) % 2 == 0,
        pltpu.roll(block, count - span, axis=0),
        pltpu.roll(block, span, axis=0),
    )


def out_kernel(slots, later, weight_ref, *refs):
    pieces = refs[:slots][::-1]
    outs = refs[slots + later : 2 * slots + later]
    left_s = refs[-1]
    own_rows = pieces[0].shape[0]
    rows = left_s.shape[0]
    lefts = [join_rows(pieces, left_s)]
    for k in range(1, slots):
        low = k & -k
        lefts.append(turned(lefts[k ^ low], low, own_rows))
    left = jnp.concatenate(lefts, axis=0).astype(jnp.bfloat16)

    def store(start, size, value):
        for k, ref in enumerate(outs):
            ref[:, pl.ds(start, size)] = value[k * rows : (k + 1) * rows].astype(jnp.bfloat16)

    product_tiles(left, weight_ref, store)


def project_out(pieces, weight, later):
    slots = len(pieces)
    own_rows, depth = pieces[0].shape
    shape = jax.ShapeDtypeStruct((own_rows * slots, weight.shape[1]), jnp.bfloat16)
    return pl.pallas_call(
        functools.partial(out_kernel, slots, len(later)),
        out_shape=(shape,) * slots,
        in_specs=[in_vmem] * (1 + slots) + [in_place] * len(later),
        out_specs=(in_vmem,) * slots,
        scratch_shapes=[pltpu.VMEM((own_rows * slots, depth), jnp.float32)],
        compiler_params=params(3),
        name="project_out",
    )(resident(weight), *pieces[::-1], *[resident(w) for w in later])


def pair_kernel(first_ref, second_ref, out_ref):
    total = first_ref[...].astype(jnp.float32) + second_ref[...].astype(jnp.float32)
    out_ref[...] = total.astype(jnp.bfloat16)


def pair_sum(first, second):
    return pl.pallas_call(
        pair_kernel,
        out_shape=jax.ShapeDtypeStruct(first.shape, first.dtype),
        in_specs=[in_vmem] * 2,
        out_specs=in_vmem,
        compiler_params=params(2),
        name="pair_sum",
    )(first, second)


def gate_up_tiles(scaled, gate_ref, up_ref, out_ref, first, count):
    def store(offset):
        def place(start, size, value):
            start = pl.multiple_of(offset + start, math.gcd(offset, size))
            out_ref[:, pl.ds(start, size)] = value.astype(jnp.bfloat16)

        return place

    product_tiles(scaled, gate_ref, store(0), first, count)
    product_tiles(scaled, up_ref, store(count), first, count)


def first_gate_up_kernel(slots, count, lanes_ref, rows_ref, gain_ref, gate_ref, up_ref, *refs):
    parts = refs[:slots]
    out_ref, updated_ref, scaled_ref = refs[-3:]
    own_rows = updated_ref.shape[0]
    total = functools.reduce(jnp.add, [ref[...].astype(jnp.float32) for ref in parts])
    updated = (rows_ref[...] + total).astype(jnp.bfloat16)
    wide = updated.astype(jnp.float32)
    updated_ref[...] = wide[:own_rows]
    squares = jnp.sum(wide * wide, axis=1, keepdims=True)
    out_ref[:, 2 * count :] = squares_block(squares, lanes_ref[...]).astype(jnp.bfloat16)
    scaled = (wide * gain_ref[...].astype(jnp.float32)[None, :]).astype(jnp.bfloat16)
    scaled_ref[...] = scaled
    gate_up_tiles(scaled, gate_ref, up_ref, out_ref, 0, count)


def first_gate_up(lanes, rows, gain, parts, w_gate, w_up, later, count, own_rows):
    slots = len(parts)
    return pl.pallas_call(
        functools.partial(first_gate_up_kernel, slots, count),
        out_shape=(
            jax.ShapeDtypeStruct((rows.shape[0], 2 * count + LANES), jnp.bfloat16),
            jax.ShapeDtypeStruct((own_rows, rows.shape[1]), jnp.float32),
            jax.ShapeDtypeStruct(rows.shape, jnp.bfloat16),
        ),
        in_specs=[in_vmem] * (5 + slots) + [in_place] * len(later),
        out_specs=(in_vmem,) * 3,
        compiler_params=params(3),
        cost_estimate=product_cost(w_gate.shape[0], 2 * count),
        name="first_gate_up",
    )(lanes, rows, gain, resident(w_gate), resident(w_up), *parts[::-1], *[resident(w) for w in later])


def second_gate_up_kernel(first, count, scaled_ref, gate_ref, up_ref, *refs):
    out_ref = refs[-1]
    gate_up_tiles(scaled_ref[...], gate_ref, up_ref, out_ref, first, count)


def second_gate_up(scaled, w_gate, w_up, later, first):
    count = w_gate.shape[1] - first
    return pl.pallas_call(
        functools.partial(second_gate_up_kernel, first, count),
        out_shape=jax.ShapeDtypeStruct((scaled.shape[0], 2 * count), jnp.bfloat16),
        in_specs=[in_vmem] * 3 + [in_place] * len(later),
        out_specs=in_vmem,
        compiler_params=params(3),
        cost_estimate=product_cost(w_gate.shape[0], 2 * count),
        name="second_gate_up",
    )(scaled, resident(w_gate), resident(w_up), *[resident(w) for w in later])


def hidden_of(near_ref, far_ref, scale, count):
    def total(start):
        span = slice(start, start + count)
        return (near_ref[:, span].astype(jnp.float32) + far_ref[:, span].astype(jnp.float32)) * scale

    gate = total(0)
    return (gate / (1.0 + jnp.exp(-gate)) * total(count)).astype(jnp.bfloat16)


def down_kernel(one_near, one_far, two_near, two_far, weight_ref, *refs):
    hidden_s, out_s = refs[-2:]
    first = (one_near.shape[1] - LANES) // 2
    second = two_near.shape[1] // 2
    squares = jnp.sum(
        one_near[:, 2 * first :].astype(jnp.float32) + one_far[:, 2 * first :].astype(jnp.float32),
        axis=1,
        keepdims=True,
    )
    scale = lax.rsqrt(squares / D + epsilon)
    hidden_s[:, :first] = hidden_of(one_near, one_far, scale, first)
    hidden_s[:, first:] = hidden_of(two_near, two_far, scale, second)

    def store(start, size, value):
        out_s[:, pl.ds(start, size)] = value

    product_tiles(hidden_s[...], weight_ref, store)
    part_rows(out_s, refs[:-2])


def project_down(one, two, weight, slots):
    rows = one[0].shape[0]
    depth, columns = weight.shape
    return pl.pallas_call(
        down_kernel,
        out_shape=(jax.ShapeDtypeStruct((rows // slots, columns), jnp.bfloat16),) * slots,
        in_specs=[in_vmem] * 5,
        out_specs=(in_vmem,) * slots,
        scratch_shapes=[
            pltpu.VMEM((rows, depth), jnp.bfloat16),
            pltpu.VMEM((rows, columns), jnp.float32),
        ],
        compiler_params=params(3),
        name="project_down",
    )(*one, *two, resident(weight))


def finish_kernel(updated_ref, *refs):
    total = functools.reduce(jnp.add, [ref[...].astype(jnp.float32) for ref in refs[:-1]])
    refs[-1][...] = (updated_ref[...] + total).astype(jnp.bfloat16)


def finish(updated, parts):
    return pl.pallas_call(
        finish_kernel,
        out_shape=jax.ShapeDtypeStruct(updated.shape, jnp.bfloat16),
        in_specs=[in_vmem] * (1 + len(parts)),
        out_specs=in_vmem,
        compiler_params=params(1),
        name="finish",
    )(updated, *parts[::-1])


def attend_tables(lengths, tensor_index, inner_index, slots, positions):
    bits = [(tensor_index >> n) & 1 for n in range(slots.bit_length() - 1)]
    marks = jnp.concatenate(
        [lengths - inner_index * positions, jnp.stack([(inner_index == 0).astype(jnp.int32), *bits])]
    )
    row = jnp.arange(HEADS)
    head = ((row % slots) ^ tensor_index) * (HEADS // slots) + row // slots
    wide = lambda column: jnp.broadcast_to(column[:, None], (column.shape[0], LANES))
    return wide(marks.astype(jnp.int32)), wide((head // GROUP).astype(jnp.int32))


def rotation_tables(positions, repeats):
    inverse = jnp.exp(
        (jnp.arange(HEAD_DIM) // 2).astype(jnp.float32) * (-2.0 / HEAD_DIM) * math.log(rope_base)
    )
    angles = positions[:, None] * inverse[None, :]
    sign = jnp.where(jnp.arange(HEAD_DIM) % 2 == 0, -1.0, 1.0)
    return (
        jnp.tile(jnp.cos(angles), (repeats, 1)),
        jnp.tile(jnp.sin(angles) * sign[None, :], (repeats, 1)),
    )


def local(
    states,
    attn_gain,
    ffn_gain,
    w_query,
    w_kv,
    w_out,
    w_gate,
    w_up,
    w_down,
    key_cache,
    value_cache,
    lengths,
):
    tensor_index = lax.axis_index("tensor")
    slots = lax.axis_size("tensor")
    inner_index = lax.axis_index("inner")
    own_rows = states.shape[0]
    all_rows = own_rows * slots

    got = exchange(states, "tensor")
    own, w_kv, w_query = load(states, w_kv, w_query, after=states)
    lanes = lax.broadcasted_iota(jnp.int32, (all_rows, LANES), 1) - 4 * inner_index
    rows, *pieces = project_qkv(lanes, [own] + got[1:], attn_gain, w_query, w_kv)

    rows, lengths = lax.optimization_barrier((rows, lengths))
    my_lengths = lax.dynamic_slice_in_dim(lengths, tensor_index * own_rows, own_rows, 0)
    cosine, sine = rotation_tables(my_lengths.astype(jnp.float32), slots)
    marks, kv_head = attend_tables(
        my_lengths, tensor_index, inner_index, slots, key_cache.shape[1]
    )
    flat = (own_rows, key_cache.shape[1] * KV_HEADS, HEAD_DIM)
    (keys,) = load(key_cache.reshape(flat), after=rows)
    joined = stack(scatter_slots(pieces, 1))
    joined, keys = lax.optimization_barrier((joined, keys))
    (values,) = load(value_cache.reshape(flat), after=joined)
    parts, values = lax.optimization_barrier((exchange(joined, "inner")[::-1], values))
    shard = attend(marks, kv_head, cosine, sine, parts, keys, values, [], slots)

    (w_out,) = load(w_out, after=shard)
    shards, w_out = lax.optimization_barrier((exchange(shard, "inner")[::-1], w_out))
    pieces = combine(shards[::-1], [w_gate], all_rows, slots)
    parts = scatter_slots(project_out(scatter_slots(pieces, 1), w_out, [w_up]), 0)

    tiles = w_gate.shape[1] // LANES
    first = (tiles + 1) // 2 * LANES
    one, updated, scaled = first_gate_up(
        lanes, rows, ffn_gain, parts, w_gate, w_up, [], first, own_rows
    )
    two = second_gate_up(scaled, w_gate, w_up, [], first)
    steps = steps_up(lax.axis_size("inner"))
    for step in steps[:-1]:
        one = pair_sum(one, swap_with(one, "inner", step))
        two = pair_sum(two, swap_with(two, "inner", step))
    one = (one, swap_with(one, "inner", steps[-1]))
    two = (two, swap_with(two, "inner", steps[-1]))
    pieces = project_down(one, two, w_down, slots)
    parts = scatter_slots(pieces, 0)
    return finish(updated, parts)


def solution(mesh):
    in_specs = (
        P(("groups", "tensor"), "inner"),
        P("inner"),
        P("inner"),
        P("inner", "tensor"),
        P("inner", "tensor"),
        P("tensor", "inner"),
        P("inner", "tensor"),
        P("inner", "tensor"),
        P("tensor", "inner"),
        P(("groups", "tensor"), "inner", None, None),
        P(("groups", "tensor"), "inner", None, None),
        P("groups"),
    )
    out_specs = P(("groups", "tensor"), "inner")
    return jax.shard_map(local, mesh=mesh, in_specs=in_specs, out_specs=out_specs, check_vma=False)
```

```python
import functools
import math

import jax
import jax.numpy as jnp
from jax import lax
from jax.experimental import pallas as pl
from jax.experimental.pallas import tpu as pltpu
from jax.sharding import PartitionSpec as P

D = 8192
HEADS = 32
KV_HEADS = 4
HEAD_DIM = 128
GROUP = HEADS // KV_HEADS
LANES = 128
MIB = 2**20
COPIES = 4
STATS = 8

epsilon = 1e-05
rope_base = 500000.0

in_vmem = pl.BlockSpec(memory_space=pltpu.VMEM)
in_smem = pl.BlockSpec(memory_space=pltpu.SMEM)
in_place = pl.BlockSpec(memory_space=pl.ANY)


def swap_with(value, axis, step):
    count = lax.axis_size(axis)
    return lax.ppermute(value, axis, [(i, i ^ step) for i in range(count)])


def exchange(value, axis):
    count = lax.axis_size(axis)
    got = {k: swap_with(value, axis, k) for k in reversed(range(1, count))}
    return [value] + [got[k] for k in range(1, count)]


def scatter_slots(pieces, cross):
    count = lax.axis_size("tensor")
    width = lax.axis_size("inner")
    got = [pieces[0]]
    for k in range(1, count):
        pairs = [
            (t * width + i, (t ^ k) * width + (i ^ cross))
            for t in range(count)
            for i in range(width)
        ]
        got.append(lax.ppermute(pieces[k], ("tensor", "inner"), pairs))
    return got


def steps_up(count):
    return [1 << n for n in range(count.bit_length() - 1)]


def params(mib):
    return pltpu.CompilerParams(vmem_limit_bytes=mib * MIB)


def resident(weight):
    return pltpu.with_memory_space_constraint(weight, pltpu.VMEM)


def in_hbm(weight):
    return pltpu.with_memory_space_constraint(weight, pltpu.HBM)


def product_cost(depth, columns):
    return pl.CostEstimate(
        flops=16 * depth * columns, bytes_accessed=2 * depth * columns, transcendentals=0
    )


def tile_of(columns):
    for tile in (1792, 1024, 896, 512, 256, 128):
        if columns % tile == 0:
            return tile
    return columns


def product_tiles(left, weight_ref, store, first=0, columns=None):
    columns = columns or weight_ref.shape[1]
    tile = tile_of(columns)

    @pl.loop(0, columns // tile)
    def _(step):
        start = pl.multiple_of(step * tile, tile)
        span = pl.ds(pl.multiple_of(first + start, math.gcd(first, tile)), tile)
        store(
            start,
            tile,
            jnp.dot(left, weight_ref[:, span], preferred_element_type=jnp.float32),
        )


def three_parts(value):
    high = value.astype(jnp.bfloat16).astype(jnp.float32)
    rest = value - high
    middle = rest.astype(jnp.bfloat16).astype(jnp.float32)
    return high, middle, rest - middle


def spread(parts, lanes, first):
    out = 0.0
    for n, part in enumerate(parts):
        out = out + jnp.where(lanes == first + n, part, 0.0)
    return out


def squares_block(total):
    lanes = lax.broadcasted_iota(jnp.int32, (total.shape[0], LANES), 1)
    return spread(three_parts(total), lanes, lax.axis_index("inner") * 4)


def copies_of(source, start, target, sems):
    size = target.shape[0]
    cuts = COPIES if len(target.shape) > 1 and size % (16 * COPIES) == 0 else 1
    each = size // cuts
    return [
        pltpu.make_async_copy(
            source.at[pl.ds(start + m * each, each)], target.at[pl.ds(m * each, each)], sems.at[m]
        )
        for m in range(cuts)
    ]


def load_kernel(spans, *refs):
    count = len(spans)
    outs = refs[count + 1 : 2 * count + 1]
    sems = refs[-1]
    copies = []
    for n, (start, _) in enumerate(spans):
        copies += copies_of(refs[n], start, outs[n], sems.at[n])
    for copy in copies:
        copy.start()
    for copy in copies:
        copy.wait()


def load(*arrays, after, spans=None):
    spans = spans or [(0, a.shape[0]) for a in arrays]
    shapes = [(size,) + a.shape[1:] for a, (_, size) in zip(arrays, spans)]
    return pl.pallas_call(
        functools.partial(load_kernel, spans),
        out_shape=tuple(pltpu.VMEM(shape, a.dtype) for shape, a in zip(shapes, arrays)),
        in_specs=[in_place] * (len(arrays) + 1),
        out_specs=tuple(in_vmem for _ in arrays),
        cost_estimate=pl.CostEstimate(
            flops=0, bytes_accessed=2 * sum(math.prod(shape) for shape in shapes), transcendentals=0
        ),
        scratch_shapes=[pltpu.SemaphoreType.DMA((len(arrays), COPIES))],
        compiler_params=params(1),
        name="load",
    )(*[in_hbm(a) for a in arrays], after)


def join_rows(refs, target):
    rows = refs[0].shape[0]
    for n, ref in enumerate(refs):
        target[n * rows : (n + 1) * rows, :] = ref[...].astype(jnp.float32)
    return target[...]


def part_rows(source, refs):
    rows = refs[0].shape[0]
    for n, ref in enumerate(refs):
        ref[...] = source[n * rows : (n + 1) * rows, :].astype(ref.dtype)


def qkv_kernel(slots, gain_ref, wq_ref, wkv_ref, *refs):
    rows_ref = refs[slots]
    out_s, rows_s = refs[-2:]
    wide = join_rows(refs[:slots][::-1], rows_s)
    rows_ref[...] = wide
    total = jnp.sum(wide * wide, axis=1, keepdims=True)
    gain = gain_ref[...].astype(jnp.float32)[None, :]
    scaled = (wide * gain).astype(jnp.bfloat16)
    query_cols = wq_ref.shape[1]
    kv_cols = wkv_ref.shape[1]

    def store_query(start, size, value):
        out_s[:, pl.ds(start, size)] = value

    product_tiles(scaled, wq_ref, store_query)
    out_s[:, query_cols : query_cols + kv_cols] = jnp.dot(
        scaled, wkv_ref[...], preferred_element_type=jnp.float32
    )
    out_s[:, query_cols + kv_cols :] = squares_block(total)
    part_rows(out_s, refs[slots + 1 : 2 * slots + 1])


def project_qkv(rows, gain, w_query, w_kv):
    slots = len(rows)
    own_rows, depth = rows[0].shape
    columns = w_query.shape[1] + w_kv.shape[1] + LANES
    return pl.pallas_call(
        functools.partial(qkv_kernel, slots),
        out_shape=(
            jax.ShapeDtypeStruct((own_rows * slots, depth), jnp.float32),
            *[jax.ShapeDtypeStruct((own_rows, columns), jnp.bfloat16)] * slots,
        ),
        in_specs=[in_vmem] * (3 + slots),
        out_specs=(in_vmem,) * (1 + slots),
        scratch_shapes=[
            pltpu.VMEM((own_rows * slots, columns), jnp.float32),
            pltpu.VMEM((own_rows * slots, depth), jnp.float32),
        ],
        compiler_params=params(2),
        name="project_qkv",
    )(gain, resident(w_query), resident(w_kv), *rows[::-1])


def stack_kernel(*refs):
    refs[-2][...] = join_rows(refs[:-2][::-1], refs[-1]).astype(refs[-2].dtype)


def stack(pieces):
    shape = (len(pieces) * pieces[0].shape[0], pieces[0].shape[1])
    return pl.pallas_call(
        stack_kernel,
        out_shape=jax.ShapeDtypeStruct(shape, pieces[0].dtype),
        in_specs=[in_vmem] * len(pieces),
        out_specs=in_vmem,
        scratch_shapes=[pltpu.VMEM(shape, jnp.float32)],
        compiler_params=params(1),
        name="stack",
    )(*pieces[::-1])


def attend_kernel(
    slots,
    shards,
    lengths_ref,
    cosine_ref,
    sine_ref,
    key_ref,
    value_ref,
    *refs,
):
    parts = refs[:shards]
    out_ref, query_s, kv_s, kv_wide_s, mixed_s, stats_s = refs[-6:]
    all_rows = parts[0].shape[0]
    own_rows = all_rows // slots
    here = HEADS // slots
    query_cols = here * HEAD_DIM
    kv_cols = 2 * KV_HEADS * HEAD_DIM // slots
    columns = query_cols + kv_cols
    tensor_index = lax.axis_index("tensor")
    inner_index = lax.axis_index("inner")
    positions = key_ref.shape[1] // KV_HEADS

    joined = functools.reduce(jnp.add, [ref[...].astype(jnp.float32) for ref in parts])
    squares = jnp.sum(joined[:, columns:], axis=1, keepdims=True)
    joined = joined[:, :columns] * lax.rsqrt(squares / D + epsilon)
    cosine = cosine_ref[...]
    sine = sine_ref[...]

    def rotate(block):
        count = block.shape[0]
        even = lax.broadcasted_iota(jnp.int32, block.shape, 1) % 2 == 0
        other = jnp.where(
            even, pltpu.roll(block, HEAD_DIM - 1, axis=1), pltpu.roll(block, 1, axis=1)
        )
        return block * cosine[:count] + other * sine[:count]

    for j in range(here):
        block = rotate(joined[:, j * HEAD_DIM : (j + 1) * HEAD_DIM])
        query_s[j * all_rows : (j + 1) * all_rows, :] = block
    for s in range(slots):
        kv_s[s] = joined[s * own_rows : (s + 1) * own_rows, query_cols:]
    for d in range(slots):
        kv_wide_s[:, d * kv_cols : (d + 1) * kv_cols] = kv_s[d ^ tensor_index]
    new_keys = []
    new_values = []
    for g in range(KV_HEADS):
        block = kv_wide_s[:, g * HEAD_DIM : (g + 1) * HEAD_DIM]
        new_keys.append(rotate(block).astype(jnp.bfloat16).astype(jnp.float32))
        block = kv_wide_s[:, (KV_HEADS + g) * HEAD_DIM : (KV_HEADS + g + 1) * HEAD_DIM]
        new_values.append(block.astype(jnp.bfloat16).astype(jnp.float32))

    score_scale = HEAD_DIM ** (-0.5)
    row = lax.broadcasted_iota(jnp.int32, (HEADS, 1), 0)
    head = ((row % slots) ^ tensor_index) * here + row // slots
    kv_head = head // GROUP
    column = lax.broadcasted_iota(jnp.int32, (1, positions * KV_HEADS), 1)
    place = column // KV_HEADS + inner_index * positions
    column_head = column % KV_HEADS
    lanes = lax.broadcasted_iota(jnp.int32, (HEADS, LANES), 1)
    for r in range(own_rows):
        queries = query_s[pl.ds(r, HEADS, stride=own_rows), :].astype(jnp.bfloat16)
        scores = (
            lax.dot_general(
                queries,
                key_ref[r],
                (((1,), (1,)), ((), ())),
                preferred_element_type=jnp.float32,
            )
            * score_scale
        )
        used = jnp.where(place < lengths_ref[r : r + 1, 0:1], column_head, -1)
        masked = jnp.where(used == kv_head, scores, -1e30)
        key_rows = 0.0
        value_rows = 0.0
        for g in range(KV_HEADS):
            key_rows = key_rows + jnp.where(kv_head == g, new_keys[g][r : r + 1], 0.0)
            value_rows = value_rows + jnp.where(kv_head == g, new_values[g][r : r + 1], 0.0)
        new_score = (
            jnp.sum(queries.astype(jnp.float32) * key_rows, axis=1, keepdims=True) * score_scale
        )
        new_score = jnp.where(inner_index == 0, new_score, -1e30)
        peak = jnp.maximum(jnp.max(masked, axis=1, keepdims=True), new_score)
        weights = jnp.exp(masked - peak)
        new_weight = jnp.exp(new_score - peak)
        totals = jnp.sum(weights, axis=1, keepdims=True) + new_weight
        mixture = jnp.dot(
            weights.astype(jnp.bfloat16), value_ref[r], preferred_element_type=jnp.float32
        )
        mixture = mixture + new_weight.astype(jnp.bfloat16).astype(jnp.float32) * value_rows
        mixed_s[pl.ds(r, HEADS, stride=own_rows), :] = mixture
        stats_s[pl.ds(r, HEADS, stride=own_rows), :] = spread(
            three_parts(peak), lanes, 0
        ) + spread(three_parts(totals), lanes, 4)
    heads = own_rows * HEADS
    out_ref[:heads, :] = mixed_s[...].astype(jnp.bfloat16)
    packed = stats_s[:all_rows, :]
    for j in range(1, here):
        block = stats_s[j * all_rows : (j + 1) * all_rows, :]
        packed = packed + pltpu.roll(block, j * STATS, axis=1)
    spare = out_ref.shape[0] - heads - all_rows
    if spare:
        packed = jnp.concatenate([packed, jnp.zeros((spare, LANES), jnp.float32)], axis=0)
    out_ref[heads:, :] = packed.astype(jnp.bfloat16)


def attend(lengths, cosine, sine, parts, keys, values, later, slots):
    own_rows = parts[0].shape[0] // slots
    kv_cols = 2 * KV_HEADS * HEAD_DIM // slots
    return pl.pallas_call(
        functools.partial(attend_kernel, slots, len(parts)),
        out_shape=jax.ShapeDtypeStruct(
            (own_rows * HEADS + max(16, own_rows * slots), HEAD_DIM), jnp.bfloat16
        ),
        in_specs=[in_vmem] * (5 + len(parts)) + [in_place] * len(later),
        out_specs=in_vmem,
        scratch_shapes=[
            pltpu.VMEM((own_rows * HEADS, HEAD_DIM), jnp.float32),
            pltpu.VMEM((slots, own_rows, kv_cols), jnp.float32),
            pltpu.VMEM((own_rows, slots * kv_cols), jnp.float32),
            pltpu.VMEM((own_rows * HEADS, HEAD_DIM), jnp.float32),
            pltpu.VMEM((own_rows * HEADS, LANES), jnp.float32),
        ],
        compiler_params=params(6),
        name="attend",
    )(lengths, cosine, sine, resident(keys), resident(values), *parts[::-1], *[resident(w) for w in later])


def combine_kernel(shards, slots, *refs):
    out_s = refs[-1]
    all_rows, columns = out_s.shape
    here = columns // HEAD_DIM
    heads = here * all_rows
    mixtures = [ref[:heads, :].astype(jnp.float32) for ref in refs[:shards]]
    stats = [ref[heads:, :].astype(jnp.float32)[:all_rows] for ref in refs[:shards]]
    for j in range(here):

        def whole(block, first):
            lane = j * STATS + first
            return block[:, lane : lane + 1] + block[:, lane + 1 : lane + 2] + block[:, lane + 2 : lane + 3]

        peaks = [whole(block, 0) for block in stats]
        top = functools.reduce(jnp.maximum, peaks)
        mixed = 0.0
        denominator = 0.0
        for mixture, block, peak in zip(mixtures, stats, peaks):
            factor = jnp.exp(peak - top)
            mixed = mixed + factor * mixture[j * all_rows : (j + 1) * all_rows]
            denominator = denominator + factor * whole(block, 4)
        out_s[:, j * HEAD_DIM : (j + 1) * HEAD_DIM] = mixed / denominator
    part_rows(out_s, refs[-1 - slots : -1])


def combine(parts, later, all_rows, slots):
    count = len(parts)
    columns = HEADS // slots * HEAD_DIM
    return pl.pallas_call(
        functools.partial(combine_kernel, count, slots),
        out_shape=(jax.ShapeDtypeStruct((all_rows // slots, columns), jnp.bfloat16),) * slots,
        in_specs=[in_vmem] * count + [in_place] * len(later),
        out_specs=(in_vmem,) * slots,
        scratch_shapes=[pltpu.VMEM((all_rows, columns), jnp.float32)],
        compiler_params=params(2),
        name="combine",
    )(*parts[::-1], *[resident(w) for w in later])


def turned(block, step, own_rows):
    count = block.shape[0]
    span = step * own_rows
    row = lax.broadcasted_iota(jnp.int32, (count, 1), 0)
    return jnp.where(
        (row // span) % 2 == 0,
        pltpu.roll(block, count - span, axis=0),
        pltpu.roll(block, span, axis=0),
    )


def out_kernel(slots, later, upper_ref, lower_ref, *refs):
    pieces = refs[:slots][::-1]
    outs = refs[slots + later : 2 * slots + later]
    left_s = refs[-1]
    own_rows = pieces[0].shape[0]
    rows = left_s.shape[0]
    cut = upper_ref.shape[0]
    lefts = [join_rows(pieces, left_s)]
    for k in range(1, slots):
        low = k & -k
        lefts.append(turned(lefts[k ^ low], low, own_rows))
    left = jnp.concatenate(lefts, axis=0).astype(jnp.bfloat16)

    def store(start, size, value):
        span = pl.ds(start, size)
        value = value + jnp.dot(
            left[:, cut:], lower_ref[:, span], preferred_element_type=jnp.float32
        )
        for k, ref in enumerate(outs):
            ref[:, span] = value[k * rows : (k + 1) * rows].astype(jnp.bfloat16)

    product_tiles(left[:, :cut], upper_ref, store)


def project_out(pieces, upper, lower, later):
    slots = len(pieces)
    own_rows, depth = pieces[0].shape
    shape = jax.ShapeDtypeStruct((own_rows * slots, upper.shape[1]), jnp.bfloat16)
    return pl.pallas_call(
        functools.partial(out_kernel, slots, len(later)),
        out_shape=(shape,) * slots,
        in_specs=[in_vmem] * (2 + slots) + [in_place] * len(later),
        out_specs=(in_vmem,) * slots,
        scratch_shapes=[pltpu.VMEM((own_rows * slots, depth), jnp.float32)],
        compiler_params=params(3),
        name="project_out",
    )(resident(upper), resident(lower), *pieces[::-1], *[resident(w) for w in later])


def pair_kernel(first_ref, second_ref, out_ref):
    total = first_ref[...].astype(jnp.float32) + second_ref[...].astype(jnp.float32)
    out_ref[...] = total.astype(jnp.bfloat16)


def pair_sum(first, second):
    return pl.pallas_call(
        pair_kernel,
        out_shape=jax.ShapeDtypeStruct(first.shape, first.dtype),
        in_specs=[in_vmem] * 2,
        out_specs=in_vmem,
        compiler_params=params(2),
        name="pair_sum",
    )(first, second)


def gate_up_tiles(scaled, gate_ref, up_ref, out_ref, first, count):
    def store(offset):
        def place(start, size, value):
            start = pl.multiple_of(offset + start, math.gcd(offset, size))
            out_ref[:, pl.ds(start, size)] = value.astype(jnp.bfloat16)

        return place

    product_tiles(scaled, gate_ref, store(0), first, count)
    product_tiles(scaled, up_ref, store(count), first, count)


def first_gate_up_kernel(slots, count, rows_ref, gain_ref, gate_ref, up_ref, *refs):
    parts = refs[:slots]
    out_ref, updated_ref, scaled_ref = refs[-3:]
    own_rows = updated_ref.shape[0]
    total = functools.reduce(jnp.add, [ref[...].astype(jnp.float32) for ref in parts])
    updated = (rows_ref[...] + total).astype(jnp.bfloat16)
    wide = updated.astype(jnp.float32)
    updated_ref[...] = wide[:own_rows]
    squares = jnp.sum(wide * wide, axis=1, keepdims=True)
    out_ref[:, 2 * count :] = squares_block(squares).astype(jnp.bfloat16)
    scaled = (wide * gain_ref[...].astype(jnp.float32)[None, :]).astype(jnp.bfloat16)
    scaled_ref[...] = scaled
    gate_up_tiles(scaled, gate_ref, up_ref, out_ref, 0, count)


def first_gate_up(rows, gain, parts, w_gate, w_up, later, count, own_rows):
    slots = len(parts)
    return pl.pallas_call(
        functools.partial(first_gate_up_kernel, slots, count),
        out_shape=(
            jax.ShapeDtypeStruct((rows.shape[0], 2 * count + LANES), jnp.bfloat16),
            jax.ShapeDtypeStruct((own_rows, rows.shape[1]), jnp.float32),
            jax.ShapeDtypeStruct(rows.shape, jnp.bfloat16),
        ),
        in_specs=[in_vmem] * (4 + slots) + [in_place] * len(later),
        out_specs=(in_vmem,) * 3,
        compiler_params=params(3),
        cost_estimate=product_cost(w_gate.shape[0], 2 * count),
        name="first_gate_up",
    )(rows, gain, resident(w_gate), resident(w_up), *parts[::-1], *[resident(w) for w in later])


def second_gate_up_kernel(first, count, scaled_ref, gate_ref, up_ref, *refs):
    out_ref = refs[-1]
    gate_up_tiles(scaled_ref[...], gate_ref, up_ref, out_ref, first, count)


def second_gate_up(scaled, w_gate, w_up, later, first):
    count = w_gate.shape[1] - first
    return pl.pallas_call(
        functools.partial(second_gate_up_kernel, first, count),
        out_shape=jax.ShapeDtypeStruct((scaled.shape[0], 2 * count), jnp.bfloat16),
        in_specs=[in_vmem] * 3 + [in_place] * len(later),
        out_specs=in_vmem,
        compiler_params=params(3),
        cost_estimate=product_cost(w_gate.shape[0], 2 * count),
        name="second_gate_up",
    )(scaled, resident(w_gate), resident(w_up), *[resident(w) for w in later])


def hidden_of(near_ref, far_ref, scale, count):
    def total(start):
        span = slice(start, start + count)
        return (near_ref[:, span].astype(jnp.float32) + far_ref[:, span].astype(jnp.float32)) * scale

    gate = total(0)
    return (gate / (1.0 + jnp.exp(-gate)) * total(count)).astype(jnp.bfloat16)


def down_kernel(one_near, one_far, two_near, two_far, weight_ref, *refs):
    hidden_s, out_s = refs[-2:]
    first = (one_near.shape[1] - LANES) // 2
    second = two_near.shape[1] // 2
    squares = jnp.sum(
        one_near[:, 2 * first :].astype(jnp.float32) + one_far[:, 2 * first :].astype(jnp.float32),
        axis=1,
        keepdims=True,
    )
    scale = lax.rsqrt(squares / D + epsilon)
    hidden_s[:, :first] = hidden_of(one_near, one_far, scale, first)
    hidden_s[:, first:] = hidden_of(two_near, two_far, scale, second)

    def store(start, size, value):
        out_s[:, pl.ds(start, size)] = value

    product_tiles(hidden_s[...], weight_ref, store)
    part_rows(out_s, refs[:-2])


def project_down(one, two, weight, slots):
    rows = one[0].shape[0]
    depth, columns = weight.shape
    return pl.pallas_call(
        down_kernel,
        out_shape=(jax.ShapeDtypeStruct((rows // slots, columns), jnp.bfloat16),) * slots,
        in_specs=[in_vmem] * 5,
        out_specs=(in_vmem,) * slots,
        scratch_shapes=[
            pltpu.VMEM((rows, depth), jnp.bfloat16),
            pltpu.VMEM((rows, columns), jnp.float32),
        ],
        compiler_params=params(3),
        name="project_down",
    )(*one, *two, resident(weight))


def finish_kernel(updated_ref, *refs):
    total = functools.reduce(jnp.add, [ref[...].astype(jnp.float32) for ref in refs[:-1]])
    refs[-1][...] = (updated_ref[...] + total).astype(jnp.bfloat16)


def finish(updated, parts):
    return pl.pallas_call(
        finish_kernel,
        out_shape=jax.ShapeDtypeStruct(updated.shape, jnp.bfloat16),
        in_specs=[in_vmem] * (1 + len(parts)),
        out_specs=in_vmem,
        compiler_params=params(1),
        name="finish",
    )(updated, *parts[::-1])


def rotation_tables(positions, repeats):
    inverse = jnp.exp(
        (jnp.arange(HEAD_DIM) // 2).astype(jnp.float32) * (-2.0 / HEAD_DIM) * math.log(rope_base)
    )
    angles = positions[:, None] * inverse[None, :]
    sign = jnp.where(jnp.arange(HEAD_DIM) % 2 == 0, -1.0, 1.0)
    return (
        jnp.tile(jnp.cos(angles), (repeats, 1)),
        jnp.tile(jnp.sin(angles) * sign[None, :], (repeats, 1)),
    )


def local(
    states,
    attn_gain,
    ffn_gain,
    w_query,
    w_kv,
    w_out,
    w_gate,
    w_up,
    w_down,
    key_cache,
    value_cache,
    lengths,
):
    tensor_index = lax.axis_index("tensor")
    slots = lax.axis_size("tensor")
    own_rows = states.shape[0]
    all_rows = own_rows * slots

    got = exchange(states, "tensor")
    own, attn_gain, ffn_gain, w_kv, w_query = load(
        states, attn_gain, ffn_gain, w_kv, w_query, after=states
    )
    rows, *pieces = project_qkv([own] + got[1:], attn_gain, w_query, w_kv)

    rows, lengths = lax.optimization_barrier((rows, lengths))
    my_lengths = lax.dynamic_slice_in_dim(lengths, tensor_index * own_rows, own_rows, 0)
    cosine, sine = rotation_tables(my_lengths.astype(jnp.float32), slots)
    my_lengths = jnp.broadcast_to(my_lengths[:, None], (own_rows, LANES))
    flat = (own_rows, key_cache.shape[1] * KV_HEADS, HEAD_DIM)
    (keys,) = load(key_cache.reshape(flat), after=rows)
    joined = stack(scatter_slots(pieces, 1))
    joined, keys = lax.optimization_barrier((joined, keys))
    (values,) = load(value_cache.reshape(flat), after=joined)
    parts, values = lax.optimization_barrier((exchange(joined, "inner")[::-1], values))
    shard = attend(my_lengths, cosine, sine, parts, keys, values, [], slots)

    cut = w_out.shape[0] // 2
    (out_upper,) = load(w_out, after=shard, spans=[(0, cut)])
    shards, out_upper = lax.optimization_barrier((exchange(shard, "inner")[::-1], out_upper))
    pieces = combine(shards[::-1], [w_gate], all_rows, slots)
    (out_lower,) = load(w_out, after=pieces[0], spans=[(cut, w_out.shape[0] - cut)])
    pieces, out_lower = lax.optimization_barrier((scatter_slots(pieces, 1)[::-1], out_lower))
    parts = scatter_slots(project_out(pieces[::-1], out_upper, out_lower, [w_up]), 0)

    tiles = w_gate.shape[1] // LANES
    first = (tiles + 1) // 2 * LANES
    one, updated, scaled = first_gate_up(
        rows, ffn_gain, parts, w_gate, w_up, [], first, own_rows
    )
    two = second_gate_up(scaled, w_gate, w_up, [], first)
    steps = steps_up(lax.axis_size("inner"))
    for step in steps[:-1]:
        one = pair_sum(one, swap_with(one, "inner", step))
        two = pair_sum(two, swap_with(two, "inner", step))
    one = (one, swap_with(one, "inner", steps[-1]))
    two = (two, swap_with(two, "inner", steps[-1]))
    pieces = project_down(one, two, w_down, slots)
    parts = scatter_slots(pieces, 0)
    return finish(updated, parts)


def solution(mesh):
    in_specs = (
        P(("groups", "tensor"), "inner"),
        P("inner"),
        P("inner"),
        P("inner", "tensor"),
        P("inner", "tensor"),
        P("tensor", "inner"),
        P("inner", "tensor"),
        P("inner", "tensor"),
        P("tensor", "inner"),
        P(("groups", "tensor"), "inner", None, None),
        P(("groups", "tensor"), "inner", None, None),
        P("groups"),
    )
    out_specs = P(("groups", "tensor"), "inner")
    return jax.shard_map(local, mesh=mesh, in_specs=in_specs, out_specs=out_specs, check_vma=False)
```

```python
import functools
import math

import jax
import jax.numpy as jnp
from jax import lax
from jax.experimental import pallas as pl
from jax.experimental.pallas import tpu as pltpu
from jax.sharding import PartitionSpec as P

D = 8192
HEADS = 32
KV_HEADS = 4
HEAD_DIM = 128
GROUP = HEADS // KV_HEADS
LANES = 128
MIB = 2**20
COPIES = 4
STATS = 8

epsilon = 1e-05
rope_base = 500000.0

in_vmem = pl.BlockSpec(memory_space=pltpu.VMEM)
in_smem = pl.BlockSpec(memory_space=pltpu.SMEM)
in_place = pl.BlockSpec(memory_space=pl.ANY)


def swap_with(value, axis, step):
    count = lax.axis_size(axis)
    return lax.ppermute(value, axis, [(i, i ^ step) for i in range(count)])


def exchange(value, axis):
    count = lax.axis_size(axis)
    got = {k: swap_with(value, axis, k) for k in reversed(range(1, count))}
    return [value] + [got[k] for k in range(1, count)]


def scatter_slots(pieces, cross):
    count = lax.axis_size("tensor")
    width = lax.axis_size("inner")
    got = [pieces[0]]
    for k in range(1, count):
        pairs = [
            (t * width + i, (t ^ k) * width + (i ^ cross))
            for t in range(count)
            for i in range(width)
        ]
        got.append(lax.ppermute(pieces[k], ("tensor", "inner"), pairs))
    return got


def steps_up(count):
    return [1 << n for n in range(count.bit_length() - 1)]


def params(mib):
    return pltpu.CompilerParams(vmem_limit_bytes=mib * MIB)


def resident(weight):
    return pltpu.with_memory_space_constraint(weight, pltpu.VMEM)


def in_hbm(weight):
    return pltpu.with_memory_space_constraint(weight, pltpu.HBM)


def product_cost(depth, columns):
    return pl.CostEstimate(
        flops=16 * depth * columns, bytes_accessed=2 * depth * columns, transcendentals=0
    )


def tile_of(columns):
    for tile in (1792, 1024, 896, 512, 256, 128):
        if columns % tile == 0:
            return tile
    return columns


def product_tiles(left, weight_ref, store, first=0, columns=None):
    columns = columns or weight_ref.shape[1]
    tile = tile_of(columns)

    @pl.loop(0, columns // tile)
    def _(step):
        start = pl.multiple_of(step * tile, tile)
        span = pl.ds(pl.multiple_of(first + start, math.gcd(first, tile)), tile)
        store(
            start,
            tile,
            jnp.dot(left, weight_ref[:, span], preferred_element_type=jnp.float32),
        )


def three_parts(value):
    high = value.astype(jnp.bfloat16).astype(jnp.float32)
    rest = value - high
    middle = rest.astype(jnp.bfloat16).astype(jnp.float32)
    return high, middle, rest - middle


def spread(parts, lanes, first):
    out = 0.0
    for n, part in enumerate(parts):
        out = out + jnp.where(lanes == first + n, part, 0.0)
    return out


def squares_block(total):
    lanes = lax.broadcasted_iota(jnp.int32, (total.shape[0], LANES), 1)
    return spread(three_parts(total), lanes, lax.axis_index("inner") * 4)


def copies_of(source, start, target, sems):
    size = target.shape[0]
    cuts = COPIES if len(target.shape) > 1 and size % (16 * COPIES) == 0 else 1
    each = size // cuts
    return [
        pltpu.make_async_copy(
            source.at[pl.ds(start + m * each, each)], target.at[pl.ds(m * each, each)], sems.at[m]
        )
        for m in range(cuts)
    ]


def load_kernel(spans, *refs):
    count = len(spans)
    outs = refs[count + 1 : 2 * count + 1]
    sems = refs[-1]
    copies = []
    for n, (start, _) in enumerate(spans):
        copies += copies_of(refs[n], start, outs[n], sems.at[n])
    for copy in copies:
        copy.start()
    for copy in copies:
        copy.wait()


def load(*arrays, after, spans=None):
    spans = spans or [(0, a.shape[0]) for a in arrays]
    shapes = [(size,) + a.shape[1:] for a, (_, size) in zip(arrays, spans)]
    return pl.pallas_call(
        functools.partial(load_kernel, spans),
        out_shape=tuple(pltpu.VMEM(shape, a.dtype) for shape, a in zip(shapes, arrays)),
        in_specs=[in_place] * (len(arrays) + 1),
        out_specs=tuple(in_vmem for _ in arrays),
        cost_estimate=pl.CostEstimate(
            flops=0, bytes_accessed=2 * sum(math.prod(shape) for shape in shapes), transcendentals=0
        ),
        scratch_shapes=[pltpu.SemaphoreType.DMA((len(arrays), COPIES))],
        compiler_params=params(1),
        name="load",
    )(*[in_hbm(a) for a in arrays], after)


def join_rows(refs, target):
    rows = refs[0].shape[0]
    for n, ref in enumerate(refs):
        target[n * rows : (n + 1) * rows, :] = ref[...].astype(jnp.float32)
    return target[...]


def part_rows(source, refs):
    rows = refs[0].shape[0]
    for n, ref in enumerate(refs):
        ref[...] = source[n * rows : (n + 1) * rows, :].astype(ref.dtype)


def qkv_kernel(slots, gain_ref, wq_ref, wkv_ref, *refs):
    rows_ref = refs[slots]
    out_s, rows_s = refs[-2:]
    wide = join_rows(refs[:slots][::-1], rows_s)
    rows_ref[...] = wide
    total = jnp.sum(wide * wide, axis=1, keepdims=True)
    gain = gain_ref[...].astype(jnp.float32)[None, :]
    scaled = (wide * gain).astype(jnp.bfloat16)
    query_cols = wq_ref.shape[1]
    kv_cols = wkv_ref.shape[1]

    def store_query(start, size, value):
        out_s[:, pl.ds(start, size)] = value

    product_tiles(scaled, wq_ref, store_query)
    out_s[:, query_cols : query_cols + kv_cols] = jnp.dot(
        scaled, wkv_ref[...], preferred_element_type=jnp.float32
    )
    out_s[:, query_cols + kv_cols :] = squares_block(total)
    part_rows(out_s, refs[slots + 1 : 2 * slots + 1])


def project_qkv(rows, gain, w_query, w_kv):
    slots = len(rows)
    own_rows, depth = rows[0].shape
    columns = w_query.shape[1] + w_kv.shape[1] + LANES
    return pl.pallas_call(
        functools.partial(qkv_kernel, slots),
        out_shape=(
            jax.ShapeDtypeStruct((own_rows * slots, depth), jnp.float32),
            *[jax.ShapeDtypeStruct((own_rows, columns), jnp.bfloat16)] * slots,
        ),
        in_specs=[in_vmem] * (3 + slots),
        out_specs=(in_vmem,) * (1 + slots),
        scratch_shapes=[
            pltpu.VMEM((own_rows * slots, columns), jnp.float32),
            pltpu.VMEM((own_rows * slots, depth), jnp.float32),
        ],
        compiler_params=params(2),
        name="project_qkv",
    )(gain, resident(w_query), resident(w_kv), *rows[::-1])


def stack_kernel(*refs):
    refs[-2][...] = join_rows(refs[:-2][::-1], refs[-1]).astype(refs[-2].dtype)


def stack(pieces):
    shape = (len(pieces) * pieces[0].shape[0], pieces[0].shape[1])
    return pl.pallas_call(
        stack_kernel,
        out_shape=jax.ShapeDtypeStruct(shape, pieces[0].dtype),
        in_specs=[in_vmem] * len(pieces),
        out_specs=in_vmem,
        scratch_shapes=[pltpu.VMEM(shape, jnp.float32)],
        compiler_params=params(1),
        name="stack",
    )(*pieces[::-1])


def attend_kernel(
    slots,
    shards,
    lengths_ref,
    cosine_ref,
    sine_ref,
    key_ref,
    value_ref,
    *refs,
):
    parts = refs[:shards]
    out_ref, query_s, kv_s, kv_wide_s, mixed_s, stats_s = refs[-6:]
    all_rows = parts[0].shape[0]
    own_rows = all_rows // slots
    here = HEADS // slots
    query_cols = here * HEAD_DIM
    kv_cols = 2 * KV_HEADS * HEAD_DIM // slots
    columns = query_cols + kv_cols
    tensor_index = lax.axis_index("tensor")
    inner_index = lax.axis_index("inner")
    positions = key_ref.shape[1] // KV_HEADS

    joined = functools.reduce(jnp.add, [ref[...].astype(jnp.float32) for ref in parts])
    squares = jnp.sum(joined[:, columns:], axis=1, keepdims=True)
    joined = joined[:, :columns] * lax.rsqrt(squares / D + epsilon)
    cosine = cosine_ref[...]
    sine = sine_ref[...]

    def rotate(block):
        count = block.shape[0]
        even = lax.broadcasted_iota(jnp.int32, block.shape, 1) % 2 == 0
        other = jnp.where(
            even, pltpu.roll(block, HEAD_DIM - 1, axis=1), pltpu.roll(block, 1, axis=1)
        )
        return block * cosine[:count] + other * sine[:count]

    for j in range(here):
        block = rotate(joined[:, j * HEAD_DIM : (j + 1) * HEAD_DIM])
        query_s[j * all_rows : (j + 1) * all_rows, :] = block
    for s in range(slots):
        kv_s[s] = joined[s * own_rows : (s + 1) * own_rows, query_cols:]
    for d in range(slots):
        kv_wide_s[:, d * kv_cols : (d + 1) * kv_cols] = kv_s[d ^ tensor_index]
    new_keys = []
    new_values = []
    for g in range(KV_HEADS):
        block = kv_wide_s[:, g * HEAD_DIM : (g + 1) * HEAD_DIM]
        new_keys.append(rotate(block).astype(jnp.bfloat16).astype(jnp.float32))
        block = kv_wide_s[:, (KV_HEADS + g) * HEAD_DIM : (KV_HEADS + g + 1) * HEAD_DIM]
        new_values.append(block.astype(jnp.bfloat16).astype(jnp.float32))

    score_scale = HEAD_DIM ** (-0.5)
    row = lax.broadcasted_iota(jnp.int32, (HEADS, 1), 0)
    head = ((row % slots) ^ tensor_index) * here + row // slots
    kv_head = head // GROUP
    column = lax.broadcasted_iota(jnp.int32, (1, positions * KV_HEADS), 1)
    place = column // KV_HEADS + inner_index * positions
    column_head = column % KV_HEADS
    lanes = lax.broadcasted_iota(jnp.int32, (HEADS, LANES), 1)
    for r in range(own_rows):
        queries = query_s[pl.ds(r, HEADS, stride=own_rows), :].astype(jnp.bfloat16)
        scores = (
            lax.dot_general(
                queries,
                key_ref[r],
                (((1,), (1,)), ((), ())),
                preferred_element_type=jnp.float32,
            )
            * score_scale
        )
        used = jnp.where(place < lengths_ref[r : r + 1, 0:1], column_head, -1)
        masked = jnp.where(used == kv_head, scores, -1e30)
        key_rows = 0.0
        value_rows = 0.0
        for g in range(KV_HEADS):
            key_rows = key_rows + jnp.where(kv_head == g, new_keys[g][r : r + 1], 0.0)
            value_rows = value_rows + jnp.where(kv_head == g, new_values[g][r : r + 1], 0.0)
        new_score = (
            jnp.sum(queries.astype(jnp.float32) * key_rows, axis=1, keepdims=True) * score_scale
        )
        new_score = jnp.where(inner_index == 0, new_score, -1e30)
        peak = jnp.maximum(jnp.max(masked, axis=1, keepdims=True), new_score)
        weights = jnp.exp(masked - peak)
        new_weight = jnp.exp(new_score - peak)
        totals = jnp.sum(weights, axis=1, keepdims=True) + new_weight
        mixture = jnp.dot(
            weights.astype(jnp.bfloat16), value_ref[r], preferred_element_type=jnp.float32
        )
        mixture = mixture + new_weight.astype(jnp.bfloat16).astype(jnp.float32) * value_rows
        mixed_s[pl.ds(r, HEADS, stride=own_rows), :] = mixture
        stats_s[pl.ds(r, HEADS, stride=own_rows), :] = spread(
            three_parts(peak), lanes, 0
        ) + spread(three_parts(totals), lanes, 4)
    heads = own_rows * HEADS
    out_ref[:heads, :] = mixed_s[...].astype(jnp.bfloat16)
    packed = stats_s[:all_rows, :]
    for j in range(1, here):
        block = stats_s[j * all_rows : (j + 1) * all_rows, :]
        packed = packed + pltpu.roll(block, j * STATS, axis=1)
    spare = out_ref.shape[0] - heads - all_rows
    if spare:
        packed = jnp.concatenate([packed, jnp.zeros((spare, LANES), jnp.float32)], axis=0)
    out_ref[heads:, :] = packed.astype(jnp.bfloat16)


def attend(lengths, cosine, sine, parts, keys, values, later, slots):
    own_rows = parts[0].shape[0] // slots
    kv_cols = 2 * KV_HEADS * HEAD_DIM // slots
    return pl.pallas_call(
        functools.partial(attend_kernel, slots, len(parts)),
        out_shape=jax.ShapeDtypeStruct(
            (own_rows * HEADS + max(16, own_rows * slots), HEAD_DIM), jnp.bfloat16
        ),
        in_specs=[in_vmem] * (5 + len(parts)) + [in_place] * len(later),
        out_specs=in_vmem,
        scratch_shapes=[
            pltpu.VMEM((own_rows * HEADS, HEAD_DIM), jnp.float32),
            pltpu.VMEM((slots, own_rows, kv_cols), jnp.float32),
            pltpu.VMEM((own_rows, slots * kv_cols), jnp.float32),
            pltpu.VMEM((own_rows * HEADS, HEAD_DIM), jnp.float32),
            pltpu.VMEM((own_rows * HEADS, LANES), jnp.float32),
        ],
        compiler_params=params(6),
        name="attend",
    )(lengths, cosine, sine, resident(keys), resident(values), *parts[::-1], *[resident(w) for w in later])


def combine_kernel(shards, slots, *refs):
    out_s = refs[-1]
    all_rows, columns = out_s.shape
    here = columns // HEAD_DIM
    heads = here * all_rows
    mixtures = [ref[:heads, :].astype(jnp.float32) for ref in refs[:shards]]
    stats = [ref[heads:, :].astype(jnp.float32)[:all_rows] for ref in refs[:shards]]
    for j in range(here):

        def whole(block, first):
            lane = j * STATS + first
            return block[:, lane : lane + 1] + block[:, lane + 1 : lane + 2] + block[:, lane + 2 : lane + 3]

        peaks = [whole(block, 0) for block in stats]
        top = functools.reduce(jnp.maximum, peaks)
        mixed = 0.0
        denominator = 0.0
        for mixture, block, peak in zip(mixtures, stats, peaks):
            factor = jnp.exp(peak - top)
            mixed = mixed + factor * mixture[j * all_rows : (j + 1) * all_rows]
            denominator = denominator + factor * whole(block, 4)
        out_s[:, j * HEAD_DIM : (j + 1) * HEAD_DIM] = mixed / denominator
    part_rows(out_s, refs[-1 - slots : -1])


def combine(parts, later, all_rows, slots):
    count = len(parts)
    columns = HEADS // slots * HEAD_DIM
    return pl.pallas_call(
        functools.partial(combine_kernel, count, slots),
        out_shape=(jax.ShapeDtypeStruct((all_rows // slots, columns), jnp.bfloat16),) * slots,
        in_specs=[in_vmem] * count + [in_place] * len(later),
        out_specs=(in_vmem,) * slots,
        scratch_shapes=[pltpu.VMEM((all_rows, columns), jnp.float32)],
        compiler_params=params(2),
        name="combine",
    )(*parts[::-1], *[resident(w) for w in later])


def turned(block, step, own_rows):
    count = block.shape[0]
    span = step * own_rows
    row = lax.broadcasted_iota(jnp.int32, (count, 1), 0)
    return jnp.where(
        (row // span) % 2 == 0,
        pltpu.roll(block, count - span, axis=0),
        pltpu.roll(block, span, axis=0),
    )


def out_kernel(slots, later, upper_ref, lower_ref, *refs):
    pieces = refs[:slots][::-1]
    outs = refs[slots + later : 2 * slots + later]
    left_s = refs[-1]
    own_rows = pieces[0].shape[0]
    rows = left_s.shape[0]
    cut = upper_ref.shape[0]
    lefts = [join_rows(pieces, left_s)]
    for k in range(1, slots):
        low = k & -k
        lefts.append(turned(lefts[k ^ low], low, own_rows))
    left = jnp.concatenate(lefts, axis=0).astype(jnp.bfloat16)

    def store(start, size, value):
        span = pl.ds(start, size)
        value = value + jnp.dot(
            left[:, cut:], lower_ref[:, span], preferred_element_type=jnp.float32
        )
        for k, ref in enumerate(outs):
            ref[:, span] = value[k * rows : (k + 1) * rows].astype(jnp.bfloat16)

    product_tiles(left[:, :cut], upper_ref, store)


def project_out(pieces, upper, lower, later):
    slots = len(pieces)
    own_rows, depth = pieces[0].shape
    shape = jax.ShapeDtypeStruct((own_rows * slots, upper.shape[1]), jnp.bfloat16)
    return pl.pallas_call(
        functools.partial(out_kernel, slots, len(later)),
        out_shape=(shape,) * slots,
        in_specs=[in_vmem] * (2 + slots) + [in_place] * len(later),
        out_specs=(in_vmem,) * slots,
        scratch_shapes=[pltpu.VMEM((own_rows * slots, depth), jnp.float32)],
        compiler_params=params(3),
        name="project_out",
    )(resident(upper), resident(lower), *pieces[::-1], *[resident(w) for w in later])


def pair_kernel(first_ref, second_ref, out_ref):
    total = first_ref[...].astype(jnp.float32) + second_ref[...].astype(jnp.float32)
    out_ref[...] = total.astype(jnp.bfloat16)


def pair_sum(first, second):
    return pl.pallas_call(
        pair_kernel,
        out_shape=jax.ShapeDtypeStruct(first.shape, first.dtype),
        in_specs=[in_vmem] * 2,
        out_specs=in_vmem,
        compiler_params=params(2),
        name="pair_sum",
    )(first, second)


def gate_up_tiles(scaled, gate_ref, up_ref, out_ref, first, count):
    def store(offset):
        def place(start, size, value):
            start = pl.multiple_of(offset + start, math.gcd(offset, size))
            out_ref[:, pl.ds(start, size)] = value.astype(jnp.bfloat16)

        return place

    product_tiles(scaled, gate_ref, store(0), first, count)
    product_tiles(scaled, up_ref, store(count), first, count)


def first_gate_up_kernel(slots, count, rows_ref, gain_ref, gate_ref, up_ref, *refs):
    parts = refs[:slots]
    out_ref, updated_ref, scaled_ref = refs[-3:]
    own_rows = updated_ref.shape[0]
    total = functools.reduce(jnp.add, [ref[...].astype(jnp.float32) for ref in parts])
    updated = (rows_ref[...] + total).astype(jnp.bfloat16)
    wide = updated.astype(jnp.float32)
    updated_ref[...] = wide[:own_rows]
    squares = jnp.sum(wide * wide, axis=1, keepdims=True)
    out_ref[:, 2 * count :] = squares_block(squares).astype(jnp.bfloat16)
    scaled = (wide * gain_ref[...].astype(jnp.float32)[None, :]).astype(jnp.bfloat16)
    scaled_ref[...] = scaled
    gate_up_tiles(scaled, gate_ref, up_ref, out_ref, 0, count)


def first_gate_up(rows, gain, parts, w_gate, w_up, later, count, own_rows):
    slots = len(parts)
    return pl.pallas_call(
        functools.partial(first_gate_up_kernel, slots, count),
        out_shape=(
            jax.ShapeDtypeStruct((rows.shape[0], 2 * count + LANES), jnp.bfloat16),
            jax.ShapeDtypeStruct((own_rows, rows.shape[1]), jnp.float32),
            jax.ShapeDtypeStruct(rows.shape, jnp.bfloat16),
        ),
        in_specs=[in_vmem] * (4 + slots) + [in_place] * len(later),
        out_specs=(in_vmem,) * 3,
        compiler_params=params(3),
        cost_estimate=product_cost(w_gate.shape[0], 2 * count),
        name="first_gate_up",
    )(rows, gain, resident(w_gate), resident(w_up), *parts[::-1], *[resident(w) for w in later])


def second_gate_up_kernel(first, count, scaled_ref, gate_ref, up_ref, *refs):
    out_ref = refs[-1]
    gate_up_tiles(scaled_ref[...], gate_ref, up_ref, out_ref, first, count)


def second_gate_up(scaled, w_gate, w_up, later, first):
    count = w_gate.shape[1] - first
    return pl.pallas_call(
        functools.partial(second_gate_up_kernel, first, count),
        out_shape=jax.ShapeDtypeStruct((scaled.shape[0], 2 * count), jnp.bfloat16),
        in_specs=[in_vmem] * 3 + [in_place] * len(later),
        out_specs=in_vmem,
        compiler_params=params(3),
        cost_estimate=product_cost(w_gate.shape[0], 2 * count),
        name="second_gate_up",
    )(scaled, resident(w_gate), resident(w_up), *[resident(w) for w in later])


def hidden_of(near_ref, far_ref, scale, count):
    def total(start):
        span = slice(start, start + count)
        return (near_ref[:, span].astype(jnp.float32) + far_ref[:, span].astype(jnp.float32)) * scale

    gate = total(0)
    return (gate / (1.0 + jnp.exp(-gate)) * total(count)).astype(jnp.bfloat16)


def first_down_kernel(count, near_ref, far_ref, weight_ref, token_ref, out_ref, scale_ref):
    del token_ref
    squares = jnp.sum(
        near_ref[:, 2 * count :].astype(jnp.float32) + far_ref[:, 2 * count :].astype(jnp.float32),
        axis=1,
        keepdims=True,
    )
    scale = lax.rsqrt(squares / D + epsilon)
    scale_ref[...] = jnp.broadcast_to(scale, scale_ref.shape)

    def store(start, size, value):
        out_ref[:, pl.ds(start, size)] = value

    product_tiles(hidden_of(near_ref, far_ref, scale, count), weight_ref.at[:count], store)


def first_down(near, far, weight, token, count):
    rows = near.shape[0]
    return pl.pallas_call(
        functools.partial(first_down_kernel, count),
        out_shape=(
            jax.ShapeDtypeStruct((rows, weight.shape[1]), jnp.float32),
            jax.ShapeDtypeStruct((rows, LANES), jnp.float32),
        ),
        in_specs=[in_vmem] * 3 + [in_place],
        out_specs=(in_vmem,) * 2,
        compiler_params=params(3),
        cost_estimate=product_cost(count, weight.shape[1]),
        name="first_down",
    )(near, far, resident(weight), token)


def second_down_kernel(count, near_ref, far_ref, weight_ref, part_ref, scale_ref, *refs):
    out_s = refs[-1]
    first = weight_ref.shape[0] - count

    def store(start, size, value):
        span = pl.ds(start, size)
        out_s[:, span] = part_ref[:, span] + value

    hidden = hidden_of(near_ref, far_ref, scale_ref[:, 0:1], count)
    product_tiles(hidden, weight_ref.at[first:], store)
    part_rows(out_s, refs[:-1])


def second_down(near, far, weight, part, scale, slots):
    rows, columns = part.shape
    count = near.shape[1] // 2
    return pl.pallas_call(
        functools.partial(second_down_kernel, count),
        out_shape=(jax.ShapeDtypeStruct((rows // slots, columns), jnp.bfloat16),) * slots,
        in_specs=[in_vmem] * 5,
        out_specs=(in_vmem,) * slots,
        scratch_shapes=[pltpu.VMEM(part.shape, jnp.float32)],
        compiler_params=params(3),
        name="second_down",
    )(near, far, resident(weight), part, scale)


def hold_kernel(after_ref, weight_ref, out_ref):
    del after_ref, weight_ref
    out_ref[...] = jnp.zeros_like(out_ref)


def hold(after, weight):
    return pl.pallas_call(
        hold_kernel,
        out_shape=jax.ShapeDtypeStruct((8, LANES), jnp.float32),
        in_specs=[in_place, in_place],
        out_specs=in_vmem,
        compiler_params=params(1),
        name="hold",
    )(after, resident(weight))


def finish_kernel(updated_ref, *refs):
    total = functools.reduce(jnp.add, [ref[...].astype(jnp.float32) for ref in refs[:-1]])
    refs[-1][...] = (updated_ref[...] + total).astype(jnp.bfloat16)


def finish(updated, parts):
    return pl.pallas_call(
        finish_kernel,
        out_shape=jax.ShapeDtypeStruct(updated.shape, jnp.bfloat16),
        in_specs=[in_vmem] * (1 + len(parts)),
        out_specs=in_vmem,
        compiler_params=params(1),
        name="finish",
    )(updated, *parts[::-1])


def rotation_tables(positions, repeats):
    inverse = jnp.exp(
        (jnp.arange(HEAD_DIM) // 2).astype(jnp.float32) * (-2.0 / HEAD_DIM) * math.log(rope_base)
    )
    angles = positions[:, None] * inverse[None, :]
    sign = jnp.where(jnp.arange(HEAD_DIM) % 2 == 0, -1.0, 1.0)
    return (
        jnp.tile(jnp.cos(angles), (repeats, 1)),
        jnp.tile(jnp.sin(angles) * sign[None, :], (repeats, 1)),
    )


def local(
    states,
    attn_gain,
    ffn_gain,
    w_query,
    w_kv,
    w_out,
    w_gate,
    w_up,
    w_down,
    key_cache,
    value_cache,
    lengths,
):
    tensor_index = lax.axis_index("tensor")
    slots = lax.axis_size("tensor")
    own_rows = states.shape[0]
    all_rows = own_rows * slots

    got = exchange(states, "tensor")
    own, attn_gain, ffn_gain, w_kv, w_query = load(
        states, attn_gain, ffn_gain, w_kv, w_query, after=states
    )
    rows, *pieces = project_qkv([own] + got[1:], attn_gain, w_query, w_kv)

    rows, lengths = lax.optimization_barrier((rows, lengths))
    my_lengths = lax.dynamic_slice_in_dim(lengths, tensor_index * own_rows, own_rows, 0)
    cosine, sine = rotation_tables(my_lengths.astype(jnp.float32), slots)
    my_lengths = jnp.broadcast_to(my_lengths[:, None], (own_rows, LANES))
    flat = (own_rows, key_cache.shape[1] * KV_HEADS, HEAD_DIM)
    (keys,) = load(key_cache.reshape(flat), after=rows)
    joined = stack(scatter_slots(pieces, 1))
    joined, keys = lax.optimization_barrier((joined, keys))
    (values,) = load(value_cache.reshape(flat), after=joined)
    parts, values = lax.optimization_barrier((exchange(joined, "inner")[::-1], values))
    shard = attend(my_lengths, cosine, sine, parts, keys, values, [], slots)

    cut = w_out.shape[0] // 2
    (out_upper,) = load(w_out, after=shard, spans=[(0, cut)])
    shards, out_upper = lax.optimization_barrier((exchange(shard, "inner")[::-1], out_upper))
    pieces = combine(shards[::-1], [w_gate], all_rows, slots)
    (out_lower,) = load(w_out, after=pieces[0], spans=[(cut, w_out.shape[0] - cut)])
    pieces, out_lower = lax.optimization_barrier((scatter_slots(pieces, 1)[::-1], out_lower))
    parts = scatter_slots(project_out(pieces[::-1], out_upper, out_lower, [w_up]), 0)

    tiles = w_gate.shape[1] // LANES
    first = (tiles + 1) // 2 * LANES
    one, updated, scaled = first_gate_up(
        rows, ffn_gain, parts, w_gate, w_up, [], first, own_rows
    )
    two = second_gate_up(scaled, w_gate, w_up, [], first)
    steps = steps_up(lax.axis_size("inner"))
    for step in steps[:-1]:
        one = pair_sum(one, swap_with(one, "inner", step))
        two = pair_sum(two, swap_with(two, "inner", step))
    token = hold(two, w_down)
    part, scale = first_down(one, swap_with(one, "inner", steps[-1]), w_down, token, first)
    pieces = second_down(two, swap_with(two, "inner", steps[-1]), w_down, part, scale, slots)
    parts = scatter_slots(pieces, 0)
    return finish(updated, parts)


def solution(mesh):
    in_specs = (
        P(("groups", "tensor"), "inner"),
        P("inner"),
        P("inner"),
        P("inner", "tensor"),
        P("inner", "tensor"),
        P("tensor", "inner"),
        P("inner", "tensor"),
        P("inner", "tensor"),
        P("tensor", "inner"),
        P(("groups", "tensor"), "inner", None, None),
        P(("groups", "tensor"), "inner", None, None),
        P("groups"),
    )
    out_specs = P(("groups", "tensor"), "inner")
    return jax.shard_map(local, mesh=mesh, in_specs=in_specs, out_specs=out_specs, check_vma=False)
```

```python
import functools
import math

import jax
import jax.numpy as jnp
from jax import lax
from jax.experimental import pallas as pl
from jax.experimental.pallas import tpu as pltpu
from jax.sharding import PartitionSpec as P

D = 8192
HEADS = 32
KV_HEADS = 4
HEAD_DIM = 128
GROUP = HEADS // KV_HEADS
LANES = 128
MIB = 2**20
COPIES = 4
STATS = 8

epsilon = 1e-05
rope_base = 500000.0

in_vmem = pl.BlockSpec(memory_space=pltpu.VMEM)
in_smem = pl.BlockSpec(memory_space=pltpu.SMEM)
in_place = pl.BlockSpec(memory_space=pl.ANY)


def swap_with(value, axis, step):
    count = lax.axis_size(axis)
    return lax.ppermute(value, axis, [(i, i ^ step) for i in range(count)])


def exchange(value, axis):
    count = lax.axis_size(axis)
    got = {k: swap_with(value, axis, k) for k in reversed(range(1, count))}
    return [value] + [got[k] for k in range(1, count)]


def scatter_slots(pieces, cross):
    count = lax.axis_size("tensor")
    width = lax.axis_size("inner")
    got = [pieces[0]]
    for k in range(1, count):
        pairs = [
            (t * width + i, (t ^ k) * width + (i ^ cross))
            for t in range(count)
            for i in range(width)
        ]
        got.append(lax.ppermute(pieces[k], ("tensor", "inner"), pairs))
    return got


def steps_up(count):
    return [1 << n for n in range(count.bit_length() - 1)]


def params(mib):
    return pltpu.CompilerParams(vmem_limit_bytes=mib * MIB)


def resident(weight):
    return pltpu.with_memory_space_constraint(weight, pltpu.VMEM)


def in_hbm(weight):
    return pltpu.with_memory_space_constraint(weight, pltpu.HBM)


def product_cost(depth, columns):
    return pl.CostEstimate(
        flops=16 * depth * columns, bytes_accessed=2 * depth * columns, transcendentals=0
    )


def tile_of(columns):
    for tile in (1792, 1024, 896, 512, 256, 128):
        if columns % tile == 0:
            return tile
    return columns


def product_tiles(left, weight_ref, store, first=0, columns=None):
    columns = columns or weight_ref.shape[1]
    tile = tile_of(columns)

    @pl.loop(0, columns // tile)
    def _(step):
        start = pl.multiple_of(step * tile, tile)
        span = pl.ds(pl.multiple_of(first + start, math.gcd(first, tile)), tile)
        store(
            start,
            tile,
            jnp.dot(left, weight_ref[:, span], preferred_element_type=jnp.float32),
        )


def three_parts(value):
    high = value.astype(jnp.bfloat16).astype(jnp.float32)
    rest = value - high
    middle = rest.astype(jnp.bfloat16).astype(jnp.float32)
    return high, middle, rest - middle


def spread(parts, lanes, first):
    out = 0.0
    for n, part in enumerate(parts):
        out = out + jnp.where(lanes == first + n, part, 0.0)
    return out


def squares_block(total):
    lanes = lax.broadcasted_iota(jnp.int32, (total.shape[0], LANES), 1)
    return spread(three_parts(total), lanes, lax.axis_index("inner") * 4)


def copies_of(source, start, target, sems):
    size = target.shape[0]
    cuts = COPIES if len(target.shape) > 1 and size % (16 * COPIES) == 0 else 1
    each = size // cuts
    return [
        pltpu.make_async_copy(
            source.at[pl.ds(start + m * each, each)], target.at[pl.ds(m * each, each)], sems.at[m]
        )
        for m in range(cuts)
    ]


def load_kernel(spans, *refs):
    count = len(spans)
    outs = refs[count + 1 : 2 * count + 1]
    sems = refs[-1]
    copies = []
    for n, (start, _) in enumerate(spans):
        copies += copies_of(refs[n], start, outs[n], sems.at[n])
    for copy in copies:
        copy.start()
    for copy in copies:
        copy.wait()


def load(*arrays, after, spans=None):
    spans = spans or [(0, a.shape[0]) for a in arrays]
    shapes = [(size,) + a.shape[1:] for a, (_, size) in zip(arrays, spans)]
    return pl.pallas_call(
        functools.partial(load_kernel, spans),
        out_shape=tuple(pltpu.VMEM(shape, a.dtype) for shape, a in zip(shapes, arrays)),
        in_specs=[in_place] * (len(arrays) + 1),
        out_specs=tuple(in_vmem for _ in arrays),
        cost_estimate=pl.CostEstimate(
            flops=0, bytes_accessed=2 * sum(math.prod(shape) for shape in shapes), transcendentals=0
        ),
        scratch_shapes=[pltpu.SemaphoreType.DMA((len(arrays), COPIES))],
        compiler_params=params(1),
        name="load",
    )(*[in_hbm(a) for a in arrays], after)


def join_rows(refs, target):
    rows = refs[0].shape[0]
    for n, ref in enumerate(refs):
        target[n * rows : (n + 1) * rows, :] = ref[...].astype(jnp.float32)
    return target[...]


def part_rows(source, refs):
    rows = refs[0].shape[0]
    for n, ref in enumerate(refs):
        ref[...] = source[n * rows : (n + 1) * rows, :].astype(ref.dtype)


def qkv_kernel(slots, gain_ref, wq_ref, wkv_ref, *refs):
    rows_ref = refs[slots]
    out_s, rows_s = refs[-2:]
    wide = join_rows(refs[:slots][::-1], rows_s)
    rows_ref[...] = wide
    total = jnp.sum(wide * wide, axis=1, keepdims=True)
    gain = gain_ref[...].astype(jnp.float32)[None, :]
    scaled = (wide * gain).astype(jnp.bfloat16)
    query_cols = wq_ref.shape[1]
    kv_cols = wkv_ref.shape[1]

    def store_query(start, size, value):
        out_s[:, pl.ds(start, size)] = value

    product_tiles(scaled, wq_ref, store_query)
    out_s[:, query_cols : query_cols + kv_cols] = jnp.dot(
        scaled, wkv_ref[...], preferred_element_type=jnp.float32
    )
    out_s[:, query_cols + kv_cols :] = squares_block(total)
    part_rows(out_s, refs[slots + 1 : 2 * slots + 1])


def project_qkv(rows, gain, w_query, w_kv):
    slots = len(rows)
    own_rows, depth = rows[0].shape
    columns = w_query.shape[1] + w_kv.shape[1] + LANES
    return pl.pallas_call(
        functools.partial(qkv_kernel, slots),
        out_shape=(
            jax.ShapeDtypeStruct((own_rows * slots, depth), jnp.float32),
            *[jax.ShapeDtypeStruct((own_rows, columns), jnp.bfloat16)] * slots,
        ),
        in_specs=[in_vmem] * (3 + slots),
        out_specs=(in_vmem,) * (1 + slots),
        scratch_shapes=[
            pltpu.VMEM((own_rows * slots, columns), jnp.float32),
            pltpu.VMEM((own_rows * slots, depth), jnp.float32),
        ],
        compiler_params=params(2),
        name="project_qkv",
    )(gain, resident(w_query), resident(w_kv), *rows[::-1])


def stack_kernel(*refs):
    refs[-2][...] = join_rows(refs[:-2][::-1], refs[-1]).astype(refs[-2].dtype)


def stack(pieces):
    shape = (len(pieces) * pieces[0].shape[0], pieces[0].shape[1])
    return pl.pallas_call(
        stack_kernel,
        out_shape=jax.ShapeDtypeStruct(shape, pieces[0].dtype),
        in_specs=[in_vmem] * len(pieces),
        out_specs=in_vmem,
        scratch_shapes=[pltpu.VMEM(shape, jnp.float32)],
        compiler_params=params(1),
        name="stack",
    )(*pieces[::-1])


def attend_kernel(
    slots,
    shards,
    lengths_ref,
    cosine_ref,
    sine_ref,
    key_ref,
    value_ref,
    *refs,
):
    parts = refs[:shards]
    out_ref, query_s, kv_s, kv_wide_s, mixed_s, stats_s = refs[-6:]
    all_rows = parts[0].shape[0]
    own_rows = all_rows // slots
    here = HEADS // slots
    query_cols = here * HEAD_DIM
    kv_cols = 2 * KV_HEADS * HEAD_DIM // slots
    columns = query_cols + kv_cols
    tensor_index = lax.axis_index("tensor")
    inner_index = lax.axis_index("inner")
    positions = key_ref.shape[1] // KV_HEADS

    joined = functools.reduce(jnp.add, [ref[...].astype(jnp.float32) for ref in parts])
    squares = jnp.sum(joined[:, columns:], axis=1, keepdims=True)
    joined = joined[:, :columns] * lax.rsqrt(squares / D + epsilon)
    cosine = cosine_ref[...]
    sine = sine_ref[...]

    def rotate(block):
        count = block.shape[0]
        even = lax.broadcasted_iota(jnp.int32, block.shape, 1) % 2 == 0
        other = jnp.where(
            even, pltpu.roll(block, HEAD_DIM - 1, axis=1), pltpu.roll(block, 1, axis=1)
        )
        return block * cosine[:count] + other * sine[:count]

    for j in range(here):
        block = rotate(joined[:, j * HEAD_DIM : (j + 1) * HEAD_DIM])
        query_s[j * all_rows : (j + 1) * all_rows, :] = block
    for s in range(slots):
        kv_s[s] = joined[s * own_rows : (s + 1) * own_rows, query_cols:]
    for d in range(slots):
        kv_wide_s[:, d * kv_cols : (d + 1) * kv_cols] = kv_s[d ^ tensor_index]
    new_keys = []
    new_values = []
    for g in range(KV_HEADS):
        block = kv_wide_s[:, g * HEAD_DIM : (g + 1) * HEAD_DIM]
        new_keys.append(rotate(block).astype(jnp.bfloat16).astype(jnp.float32))
        block = kv_wide_s[:, (KV_HEADS + g) * HEAD_DIM : (KV_HEADS + g + 1) * HEAD_DIM]
        new_values.append(block.astype(jnp.bfloat16).astype(jnp.float32))

    score_scale = HEAD_DIM ** (-0.5)
    row = lax.broadcasted_iota(jnp.int32, (HEADS, 1), 0)
    head = ((row % slots) ^ tensor_index) * here + row // slots
    kv_head = head // GROUP
    column = lax.broadcasted_iota(jnp.int32, (1, positions * KV_HEADS), 1)
    place = column // KV_HEADS + inner_index * positions
    column_head = column % KV_HEADS
    lanes = lax.broadcasted_iota(jnp.int32, (HEADS, LANES), 1)
    queries = [
        query_s[pl.ds(r, HEADS, stride=own_rows), :].astype(jnp.bfloat16) for r in range(own_rows)
    ]
    scores = [
        lax.dot_general(
            queries[r], key_ref[r], (((1,), (1,)), ((), ())), preferred_element_type=jnp.float32
        )
        for r in range(own_rows)
    ]
    weights = []
    mixtures = []
    for r in range(own_rows):
        used = jnp.where(place < lengths_ref[r : r + 1, 0:1], column_head, -1)
        masked = jnp.where(used == kv_head, scores[r] * score_scale, -1e30)
        key_rows = 0.0
        value_rows = 0.0
        for g in range(KV_HEADS):
            key_rows = key_rows + jnp.where(kv_head == g, new_keys[g][r : r + 1], 0.0)
            value_rows = value_rows + jnp.where(kv_head == g, new_values[g][r : r + 1], 0.0)
        new_score = (
            jnp.sum(queries[r].astype(jnp.float32) * key_rows, axis=1, keepdims=True) * score_scale
        )
        new_score = jnp.where(inner_index == 0, new_score, -1e30)
        peak = jnp.maximum(jnp.max(masked, axis=1, keepdims=True), new_score)
        weight = jnp.exp(masked - peak)
        new_weight = jnp.exp(new_score - peak)
        totals = jnp.sum(weight, axis=1, keepdims=True) + new_weight
        weights.append(weight.astype(jnp.bfloat16))
        mixtures.append(new_weight.astype(jnp.bfloat16).astype(jnp.float32) * value_rows)
        stats_s[pl.ds(r, HEADS, stride=own_rows), :] = spread(
            three_parts(peak), lanes, 0
        ) + spread(three_parts(totals), lanes, 4)
    for r in range(own_rows):
        mixed_s[pl.ds(r, HEADS, stride=own_rows), :] = mixtures[r] + jnp.dot(
            weights[r], value_ref[r], preferred_element_type=jnp.float32
        )
    heads = own_rows * HEADS
    out_ref[:heads, :] = mixed_s[...].astype(jnp.bfloat16)
    packed = stats_s[:all_rows, :]
    for j in range(1, here):
        block = stats_s[j * all_rows : (j + 1) * all_rows, :]
        packed = packed + pltpu.roll(block, j * STATS, axis=1)
    spare = out_ref.shape[0] - heads - all_rows
    if spare:
        packed = jnp.concatenate([packed, jnp.zeros((spare, LANES), jnp.float32)], axis=0)
    out_ref[heads:, :] = packed.astype(jnp.bfloat16)


def attend(lengths, cosine, sine, parts, keys, values, later, slots):
    own_rows = parts[0].shape[0] // slots
    kv_cols = 2 * KV_HEADS * HEAD_DIM // slots
    return pl.pallas_call(
        functools.partial(attend_kernel, slots, len(parts)),
        out_shape=jax.ShapeDtypeStruct(
            (own_rows * HEADS + max(16, own_rows * slots), HEAD_DIM), jnp.bfloat16
        ),
        in_specs=[in_vmem] * (5 + len(parts)) + [in_place] * len(later),
        out_specs=in_vmem,
        scratch_shapes=[
            pltpu.VMEM((own_rows * HEADS, HEAD_DIM), jnp.float32),
            pltpu.VMEM((slots, own_rows, kv_cols), jnp.float32),
            pltpu.VMEM((own_rows, slots * kv_cols), jnp.float32),
            pltpu.VMEM((own_rows * HEADS, HEAD_DIM), jnp.float32),
            pltpu.VMEM((own_rows * HEADS, LANES), jnp.float32),
        ],
        compiler_params=params(6),
        name="attend",
    )(lengths, cosine, sine, resident(keys), resident(values), *parts[::-1], *[resident(w) for w in later])


def combine_kernel(shards, slots, *refs):
    out_s = refs[-1]
    all_rows, columns = out_s.shape
    here = columns // HEAD_DIM
    heads = here * all_rows
    mixtures = [ref[:heads, :].astype(jnp.float32) for ref in refs[:shards]]
    stats = [ref[heads:, :].astype(jnp.float32)[:all_rows] for ref in refs[:shards]]
    for j in range(here):

        def whole(block, first):
            lane = j * STATS + first
            return block[:, lane : lane + 1] + block[:, lane + 1 : lane + 2] + block[:, lane + 2 : lane + 3]

        peaks = [whole(block, 0) for block in stats]
        top = functools.reduce(jnp.maximum, peaks)
        mixed = 0.0
        denominator = 0.0
        for mixture, block, peak in zip(mixtures, stats, peaks):
            factor = jnp.exp(peak - top)
            mixed = mixed + factor * mixture[j * all_rows : (j + 1) * all_rows]
            denominator = denominator + factor * whole(block, 4)
        out_s[:, j * HEAD_DIM : (j + 1) * HEAD_DIM] = mixed / denominator
    part_rows(out_s, refs[-1 - slots : -1])


def combine(parts, later, all_rows, slots):
    count = len(parts)
    columns = HEADS // slots * HEAD_DIM
    return pl.pallas_call(
        functools.partial(combine_kernel, count, slots),
        out_shape=(jax.ShapeDtypeStruct((all_rows // slots, columns), jnp.bfloat16),) * slots,
        in_specs=[in_vmem] * count + [in_place] * len(later),
        out_specs=(in_vmem,) * slots,
        scratch_shapes=[pltpu.VMEM((all_rows, columns), jnp.float32)],
        compiler_params=params(2),
        name="combine",
    )(*parts[::-1], *[resident(w) for w in later])


def turned(block, step, own_rows):
    count = block.shape[0]
    span = step * own_rows
    row = lax.broadcasted_iota(jnp.int32, (count, 1), 0)
    return jnp.where(
        (row // span) % 2 == 0,
        pltpu.roll(block, count - span, axis=0),
        pltpu.roll(block, span, axis=0),
    )


def out_kernel(slots, later, upper_ref, lower_ref, *refs):
    pieces = refs[:slots][::-1]
    outs = refs[slots + later : 2 * slots + later]
    left_s = refs[-1]
    own_rows = pieces[0].shape[0]
    rows = left_s.shape[0]
    cut = upper_ref.shape[0]
    lefts = [join_rows(pieces, left_s)]
    for k in range(1, slots):
        low = k & -k
        lefts.append(turned(lefts[k ^ low], low, own_rows))
    left = jnp.concatenate(lefts, axis=0).astype(jnp.bfloat16)

    def store(start, size, value):
        span = pl.ds(start, size)
        value = value + jnp.dot(
            left[:, cut:], lower_ref[:, span], preferred_element_type=jnp.float32
        )
        for k, ref in enumerate(outs):
            ref[:, span] = value[k * rows : (k + 1) * rows].astype(jnp.bfloat16)

    product_tiles(left[:, :cut], upper_ref, store)


def project_out(pieces, upper, lower, later):
    slots = len(pieces)
    own_rows, depth = pieces[0].shape
    shape = jax.ShapeDtypeStruct((own_rows * slots, upper.shape[1]), jnp.bfloat16)
    return pl.pallas_call(
        functools.partial(out_kernel, slots, len(later)),
        out_shape=(shape,) * slots,
        in_specs=[in_vmem] * (2 + slots) + [in_place] * len(later),
        out_specs=(in_vmem,) * slots,
        scratch_shapes=[pltpu.VMEM((own_rows * slots, depth), jnp.float32)],
        compiler_params=params(3),
        name="project_out",
    )(resident(upper), resident(lower), *pieces[::-1], *[resident(w) for w in later])


def pair_kernel(first_ref, second_ref, out_ref):
    total = first_ref[...].astype(jnp.float32) + second_ref[...].astype(jnp.float32)
    out_ref[...] = total.astype(jnp.bfloat16)


def pair_sum(first, second):
    return pl.pallas_call(
        pair_kernel,
        out_shape=jax.ShapeDtypeStruct(first.shape, first.dtype),
        in_specs=[in_vmem] * 2,
        out_specs=in_vmem,
        compiler_params=params(2),
        name="pair_sum",
    )(first, second)


def gate_up_tiles(scaled, gate_ref, up_ref, out_ref, first, count):
    def store(offset):
        def place(start, size, value):
            start = pl.multiple_of(offset + start, math.gcd(offset, size))
            out_ref[:, pl.ds(start, size)] = value.astype(jnp.bfloat16)

        return place

    product_tiles(scaled, gate_ref, store(0), first, count)
    product_tiles(scaled, up_ref, store(count), first, count)


def first_gate_up_kernel(slots, count, rows_ref, gain_ref, gate_ref, up_ref, *refs):
    parts = refs[:slots]
    out_ref, updated_ref, scaled_ref = refs[-3:]
    own_rows = updated_ref.shape[0]
    total = functools.reduce(jnp.add, [ref[...].astype(jnp.float32) for ref in parts])
    updated = (rows_ref[...] + total).astype(jnp.bfloat16)
    wide = updated.astype(jnp.float32)
    updated_ref[...] = wide[:own_rows]
    squares = jnp.sum(wide * wide, axis=1, keepdims=True)
    out_ref[:, 2 * count :] = squares_block(squares).astype(jnp.bfloat16)
    scaled = (wide * gain_ref[...].astype(jnp.float32)[None, :]).astype(jnp.bfloat16)
    scaled_ref[...] = scaled
    gate_up_tiles(scaled, gate_ref, up_ref, out_ref, 0, count)


def first_gate_up(rows, gain, parts, w_gate, w_up, later, count, own_rows):
    slots = len(parts)
    return pl.pallas_call(
        functools.partial(first_gate_up_kernel, slots, count),
        out_shape=(
            jax.ShapeDtypeStruct((rows.shape[0], 2 * count + LANES), jnp.bfloat16),
            jax.ShapeDtypeStruct((own_rows, rows.shape[1]), jnp.float32),
            jax.ShapeDtypeStruct(rows.shape, jnp.bfloat16),
        ),
        in_specs=[in_vmem] * (4 + slots) + [in_place] * len(later),
        out_specs=(in_vmem,) * 3,
        compiler_params=params(3),
        cost_estimate=product_cost(w_gate.shape[0], 2 * count),
        name="first_gate_up",
    )(rows, gain, resident(w_gate), resident(w_up), *parts[::-1], *[resident(w) for w in later])


def second_gate_up_kernel(first, count, scaled_ref, gate_ref, up_ref, *refs):
    out_ref = refs[-1]
    gate_up_tiles(scaled_ref[...], gate_ref, up_ref, out_ref, first, count)


def second_gate_up(scaled, w_gate, w_up, later, first):
    count = w_gate.shape[1] - first
    return pl.pallas_call(
        functools.partial(second_gate_up_kernel, first, count),
        out_shape=jax.ShapeDtypeStruct((scaled.shape[0], 2 * count), jnp.bfloat16),
        in_specs=[in_vmem] * 3 + [in_place] * len(later),
        out_specs=in_vmem,
        compiler_params=params(3),
        cost_estimate=product_cost(w_gate.shape[0], 2 * count),
        name="second_gate_up",
    )(scaled, resident(w_gate), resident(w_up), *[resident(w) for w in later])


def hidden_of(near_ref, far_ref, scale, count):
    def total(start):
        span = slice(start, start + count)
        return (near_ref[:, span].astype(jnp.float32) + far_ref[:, span].astype(jnp.float32)) * scale

    gate = total(0)
    return (gate / (1.0 + jnp.exp(-gate)) * total(count)).astype(jnp.bfloat16)


def first_down_kernel(count, near_ref, far_ref, weight_ref, token_ref, out_ref, scale_ref):
    del token_ref
    squares = jnp.sum(
        near_ref[:, 2 * count :].astype(jnp.float32) + far_ref[:, 2 * count :].astype(jnp.float32),
        axis=1,
        keepdims=True,
    )
    scale = lax.rsqrt(squares / D + epsilon)
    scale_ref[...] = jnp.broadcast_to(scale, scale_ref.shape)

    def store(start, size, value):
        out_ref[:, pl.ds(start, size)] = value

    product_tiles(hidden_of(near_ref, far_ref, scale, count), weight_ref.at[:count], store)


def first_down(near, far, weight, token, count):
    rows = near.shape[0]
    return pl.pallas_call(
        functools.partial(first_down_kernel, count),
        out_shape=(
            jax.ShapeDtypeStruct((rows, weight.shape[1]), jnp.float32),
            jax.ShapeDtypeStruct((rows, LANES), jnp.float32),
        ),
        in_specs=[in_vmem] * 3 + [in_place],
        out_specs=(in_vmem,) * 2,
        compiler_params=params(3),
        cost_estimate=product_cost(count, weight.shape[1]),
        name="first_down",
    )(near, far, resident(weight), token)


def second_down_kernel(count, near_ref, far_ref, weight_ref, part_ref, scale_ref, *refs):
    out_s = refs[-1]
    first = weight_ref.shape[0] - count

    def store(start, size, value):
        span = pl.ds(start, size)
        out_s[:, span] = part_ref[:, span] + value

    hidden = hidden_of(near_ref, far_ref, scale_ref[:, 0:1], count)
    product_tiles(hidden, weight_ref.at[first:], store)
    part_rows(out_s, refs[:-1])


def second_down(near, far, weight, part, scale, slots):
    rows, columns = part.shape
    count = near.shape[1] // 2
    return pl.pallas_call(
        functools.partial(second_down_kernel, count),
        out_shape=(jax.ShapeDtypeStruct((rows // slots, columns), jnp.bfloat16),) * slots,
        in_specs=[in_vmem] * 5,
        out_specs=(in_vmem,) * slots,
        scratch_shapes=[pltpu.VMEM(part.shape, jnp.float32)],
        compiler_params=params(3),
        name="second_down",
    )(near, far, resident(weight), part, scale)


def hold_kernel(after_ref, weight_ref, out_ref):
    del after_ref, weight_ref
    out_ref[...] = jnp.zeros_like(out_ref)


def hold(after, weight):
    return pl.pallas_call(
        hold_kernel,
        out_shape=jax.ShapeDtypeStruct((8, LANES), jnp.float32),
        in_specs=[in_place, in_place],
        out_specs=in_vmem,
        compiler_params=params(1),
        name="hold",
    )(after, resident(weight))


def finish_kernel(updated_ref, *refs):
    total = functools.reduce(jnp.add, [ref[...].astype(jnp.float32) for ref in refs[:-1]])
    refs[-1][...] = (updated_ref[...] + total).astype(jnp.bfloat16)


def finish(updated, parts):
    return pl.pallas_call(
        finish_kernel,
        out_shape=jax.ShapeDtypeStruct(updated.shape, jnp.bfloat16),
        in_specs=[in_vmem] * (1 + len(parts)),
        out_specs=in_vmem,
        compiler_params=params(1),
        name="finish",
    )(updated, *parts[::-1])


def rotation_tables(positions, repeats):
    inverse = jnp.exp(
        (jnp.arange(HEAD_DIM) // 2).astype(jnp.float32) * (-2.0 / HEAD_DIM) * math.log(rope_base)
    )
    angles = positions[:, None] * inverse[None, :]
    sign = jnp.where(jnp.arange(HEAD_DIM) % 2 == 0, -1.0, 1.0)
    return (
        jnp.tile(jnp.cos(angles), (repeats, 1)),
        jnp.tile(jnp.sin(angles) * sign[None, :], (repeats, 1)),
    )


def local(
    states,
    attn_gain,
    ffn_gain,
    w_query,
    w_kv,
    w_out,
    w_gate,
    w_up,
    w_down,
    key_cache,
    value_cache,
    lengths,
):
    tensor_index = lax.axis_index("tensor")
    slots = lax.axis_size("tensor")
    own_rows = states.shape[0]
    all_rows = own_rows * slots

    got = exchange(states, "tensor")
    own, attn_gain, ffn_gain, w_kv, w_query = load(
        states, attn_gain, ffn_gain, w_kv, w_query, after=states
    )
    rows, *pieces = project_qkv([own] + got[1:], attn_gain, w_query, w_kv)

    rows, lengths = lax.optimization_barrier((rows, lengths))
    my_lengths = lax.dynamic_slice_in_dim(lengths, tensor_index * own_rows, own_rows, 0)
    cosine, sine = rotation_tables(my_lengths.astype(jnp.float32), slots)
    my_lengths = jnp.broadcast_to(my_lengths[:, None], (own_rows, LANES))
    flat = (own_rows, key_cache.shape[1] * KV_HEADS, HEAD_DIM)
    (keys,) = load(key_cache.reshape(flat), after=rows)
    joined = stack(scatter_slots(pieces, 1))
    joined, keys = lax.optimization_barrier((joined, keys))
    (values,) = load(value_cache.reshape(flat), after=joined)
    parts, values = lax.optimization_barrier((exchange(joined, "inner")[::-1], values))
    shard = attend(my_lengths, cosine, sine, parts, keys, values, [], slots)

    cut = w_out.shape[0] // 2
    (out_upper,) = load(w_out, after=shard, spans=[(0, cut)])
    shards, out_upper = lax.optimization_barrier((exchange(shard, "inner"), out_upper))
    pieces = combine(shards, [w_gate], all_rows, slots)
    (out_lower,) = load(w_out, after=pieces[0], spans=[(cut, w_out.shape[0] - cut)])
    pieces, out_lower = lax.optimization_barrier((scatter_slots(pieces, 1)[::-1], out_lower))
    parts = scatter_slots(project_out(pieces[::-1], out_upper, out_lower, [w_up]), 0)

    tiles = w_gate.shape[1] // LANES
    first = (tiles + 1) // 2 * LANES
    one, updated, scaled = first_gate_up(
        rows, ffn_gain, parts, w_gate, w_up, [], first, own_rows
    )
    two = second_gate_up(scaled, w_gate, w_up, [], first)
    steps = steps_up(lax.axis_size("inner"))
    for step in steps[:-1]:
        one = pair_sum(one, swap_with(one, "inner", step))
        two = pair_sum(two, swap_with(two, "inner", step))
    token = hold(two, w_down)
    part, scale = first_down(one, swap_with(one, "inner", steps[-1]), w_down, token, first)
    pieces = second_down(two, swap_with(two, "inner", steps[-1]), w_down, part, scale, slots)
    parts = scatter_slots(pieces, 0)
    return finish(updated, parts)


def solution(mesh):
    in_specs = (
        P(("groups", "tensor"), "inner"),
        P("inner"),
        P("inner"),
        P("inner", "tensor"),
        P("inner", "tensor"),
        P("tensor", "inner"),
        P("inner", "tensor"),
        P("inner", "tensor"),
        P("tensor", "inner"),
        P(("groups", "tensor"), "inner", None, None),
        P(("groups", "tensor"), "inner", None, None),
        P("groups"),
    )
    out_specs = P(("groups", "tensor"), "inner")
    return jax.shard_map(local, mesh=mesh, in_specs=in_specs, out_specs=out_specs, check_vma=False)
```

```python
import functools
import math

import jax
import jax.numpy as jnp
from jax import lax
from jax.experimental import pallas as pl
from jax.experimental.pallas import tpu as pltpu
from jax.sharding import PartitionSpec as P

D = 8192
HEADS = 32
KV_HEADS = 4
HEAD_DIM = 128
GROUP = HEADS // KV_HEADS
LANES = 128
MIB = 2**20
COPIES = 4
STATS = 8

epsilon = 1e-05
rope_base = 500000.0

in_vmem = pl.BlockSpec(memory_space=pltpu.VMEM)
in_smem = pl.BlockSpec(memory_space=pltpu.SMEM)
in_place = pl.BlockSpec(memory_space=pl.ANY)


def swap_with(value, axis, step):
    count = lax.axis_size(axis)
    return lax.ppermute(value, axis, [(i, i ^ step) for i in range(count)])


def exchange(value, axis):
    count = lax.axis_size(axis)
    got = {k: swap_with(value, axis, k) for k in reversed(range(1, count))}
    return [value] + [got[k] for k in range(1, count)]


def scatter_slots(pieces, cross):
    count = lax.axis_size("tensor")
    width = lax.axis_size("inner")
    got = [pieces[0]]
    for k in range(1, count):
        pairs = [
            (t * width + i, (t ^ k) * width + (i ^ cross))
            for t in range(count)
            for i in range(width)
        ]
        got.append(lax.ppermute(pieces[k], ("tensor", "inner"), pairs))
    return got


def start_order(count):
    half = count // 2
    return [half] + [k for k in reversed(range(1, count)) if k != half] + [0]


def in_start_order(slots):
    return [slots[k] for k in start_order(len(slots))]


def in_slot_order(refs):
    order = start_order(len(refs))
    return [refs[order.index(k)] for k in range(len(refs))]


def steps_up(count):
    return [1 << n for n in range(count.bit_length() - 1)]


def params(mib):
    return pltpu.CompilerParams(vmem_limit_bytes=mib * MIB)


def resident(weight):
    return pltpu.with_memory_space_constraint(weight, pltpu.VMEM)


def in_hbm(weight):
    return pltpu.with_memory_space_constraint(weight, pltpu.HBM)


def product_cost(depth, columns):
    return pl.CostEstimate(
        flops=16 * depth * columns, bytes_accessed=2 * depth * columns, transcendentals=0
    )


def tile_of(columns):
    for tile in (1792, 1024, 896, 512, 256, 128):
        if columns % tile == 0:
            return tile
    return columns


def product_tiles(left, weight_ref, store, first=0, columns=None):
    columns = columns or weight_ref.shape[1]
    tile = tile_of(columns)

    @pl.loop(0, columns // tile)
    def _(step):
        start = pl.multiple_of(step * tile, tile)
        span = pl.ds(pl.multiple_of(first + start, math.gcd(first, tile)), tile)
        store(
            start,
            tile,
            jnp.dot(left, weight_ref[:, span], preferred_element_type=jnp.float32),
        )


def three_parts(value):
    high = value.astype(jnp.bfloat16).astype(jnp.float32)
    rest = value - high
    middle = rest.astype(jnp.bfloat16).astype(jnp.float32)
    return high, middle, rest - middle


def spread(parts, lanes, first):
    out = 0.0
    for n, part in enumerate(parts):
        out = out + jnp.where(lanes == first + n, part, 0.0)
    return out


def squares_block(total):
    lanes = lax.broadcasted_iota(jnp.int32, (total.shape[0], LANES), 1)
    return spread(three_parts(total), lanes, lax.axis_index("inner") * 4)


def copies_of(source, start, target, sems):
    size = target.shape[0]
    cuts = COPIES if len(target.shape) > 1 and size % (16 * COPIES) == 0 else 1
    each = size // cuts
    return [
        pltpu.make_async_copy(
            source.at[pl.ds(start + m * each, each)], target.at[pl.ds(m * each, each)], sems.at[m]
        )
        for m in range(cuts)
    ]


def load_kernel(spans, *refs):
    count = len(spans)
    outs = refs[count + 1 : 2 * count + 1]
    sems = refs[-1]
    copies = []
    for n, (start, _) in enumerate(spans):
        copies += copies_of(refs[n], start, outs[n], sems.at[n])
    for copy in copies:
        copy.start()
    for copy in copies:
        copy.wait()


def load(*arrays, after, spans=None):
    spans = spans or [(0, a.shape[0]) for a in arrays]
    shapes = [(size,) + a.shape[1:] for a, (_, size) in zip(arrays, spans)]
    return pl.pallas_call(
        functools.partial(load_kernel, spans),
        out_shape=tuple(pltpu.VMEM(shape, a.dtype) for shape, a in zip(shapes, arrays)),
        in_specs=[in_place] * (len(arrays) + 1),
        out_specs=tuple(in_vmem for _ in arrays),
        cost_estimate=pl.CostEstimate(
            flops=0, bytes_accessed=2 * sum(math.prod(shape) for shape in shapes), transcendentals=0
        ),
        scratch_shapes=[pltpu.SemaphoreType.DMA((len(arrays), COPIES))],
        compiler_params=params(1),
        name="load",
    )(*[in_hbm(a) for a in arrays], after)


def join_rows(refs, target):
    rows = refs[0].shape[0]
    for n, ref in enumerate(refs):
        target[n * rows : (n + 1) * rows, :] = ref[...].astype(jnp.float32)
    return target[...]


def part_rows(source, refs):
    rows = refs[0].shape[0]
    for n, ref in enumerate(refs):
        ref[...] = source[n * rows : (n + 1) * rows, :].astype(ref.dtype)


def qkv_kernel(slots, gain_ref, wq_ref, wkv_ref, *refs):
    rows_ref = refs[slots]
    out_s, rows_s = refs[-2:]
    wide = join_rows(in_slot_order(refs[:slots]), rows_s)
    rows_ref[...] = wide
    total = jnp.sum(wide * wide, axis=1, keepdims=True)
    gain = gain_ref[...].astype(jnp.float32)[None, :]
    scaled = (wide * gain).astype(jnp.bfloat16)
    query_cols = wq_ref.shape[1]
    kv_cols = wkv_ref.shape[1]

    def store_query(start, size, value):
        out_s[:, pl.ds(start, size)] = value

    product_tiles(scaled, wq_ref, store_query)
    out_s[:, query_cols : query_cols + kv_cols] = jnp.dot(
        scaled, wkv_ref[...], preferred_element_type=jnp.float32
    )
    out_s[:, query_cols + kv_cols :] = squares_block(total)
    part_rows(out_s, refs[slots + 1 : 2 * slots + 1])


def project_qkv(rows, gain, w_query, w_kv):
    slots = len(rows)
    own_rows, depth = rows[0].shape
    columns = w_query.shape[1] + w_kv.shape[1] + LANES
    return pl.pallas_call(
        functools.partial(qkv_kernel, slots),
        out_shape=(
            jax.ShapeDtypeStruct((own_rows * slots, depth), jnp.float32),
            *[jax.ShapeDtypeStruct((own_rows, columns), jnp.bfloat16)] * slots,
        ),
        in_specs=[in_vmem] * (3 + slots),
        out_specs=(in_vmem,) * (1 + slots),
        scratch_shapes=[
            pltpu.VMEM((own_rows * slots, columns), jnp.float32),
            pltpu.VMEM((own_rows * slots, depth), jnp.float32),
        ],
        compiler_params=params(2),
        name="project_qkv",
    )(gain, resident(w_query), resident(w_kv), *in_start_order(rows))


def stack_kernel(*refs):
    refs[-2][...] = join_rows(refs[:-2][::-1], refs[-1]).astype(refs[-2].dtype)


def stack(pieces):
    shape = (len(pieces) * pieces[0].shape[0], pieces[0].shape[1])
    return pl.pallas_call(
        stack_kernel,
        out_shape=jax.ShapeDtypeStruct(shape, pieces[0].dtype),
        in_specs=[in_vmem] * len(pieces),
        out_specs=in_vmem,
        scratch_shapes=[pltpu.VMEM(shape, jnp.float32)],
        compiler_params=params(1),
        name="stack",
    )(*pieces[::-1])


def attend_kernel(
    slots,
    shards,
    lengths_ref,
    cosine_ref,
    sine_ref,
    key_ref,
    value_ref,
    *refs,
):
    parts = refs[:shards]
    out_ref, query_s, kv_s, kv_wide_s, mixed_s, stats_s = refs[-6:]
    all_rows = parts[0].shape[0]
    own_rows = all_rows // slots
    here = HEADS // slots
    query_cols = here * HEAD_DIM
    kv_cols = 2 * KV_HEADS * HEAD_DIM // slots
    columns = query_cols + kv_cols
    tensor_index = lax.axis_index("tensor")
    inner_index = lax.axis_index("inner")
    positions = key_ref.shape[1] // KV_HEADS

    joined = functools.reduce(jnp.add, [ref[...].astype(jnp.float32) for ref in parts])
    squares = jnp.sum(joined[:, columns:], axis=1, keepdims=True)
    joined = joined[:, :columns] * lax.rsqrt(squares / D + epsilon)
    cosine = cosine_ref[...]
    sine = sine_ref[...]

    def rotate(block):
        count = block.shape[0]
        even = lax.broadcasted_iota(jnp.int32, block.shape, 1) % 2 == 0
        other = jnp.where(
            even, pltpu.roll(block, HEAD_DIM - 1, axis=1), pltpu.roll(block, 1, axis=1)
        )
        return block * cosine[:count] + other * sine[:count]

    for j in range(here):
        block = rotate(joined[:, j * HEAD_DIM : (j + 1) * HEAD_DIM])
        query_s[j * all_rows : (j + 1) * all_rows, :] = block
    for s in range(slots):
        kv_s[s] = joined[s * own_rows : (s + 1) * own_rows, query_cols:]
    for d in range(slots):
        kv_wide_s[:, d * kv_cols : (d + 1) * kv_cols] = kv_s[d ^ tensor_index]
    new_keys = []
    new_values = []
    for g in range(KV_HEADS):
        block = kv_wide_s[:, g * HEAD_DIM : (g + 1) * HEAD_DIM]
        new_keys.append(rotate(block).astype(jnp.bfloat16).astype(jnp.float32))
        block = kv_wide_s[:, (KV_HEADS + g) * HEAD_DIM : (KV_HEADS + g + 1) * HEAD_DIM]
        new_values.append(block.astype(jnp.bfloat16).astype(jnp.float32))

    score_scale = HEAD_DIM ** (-0.5)
    two_scale = score_scale * math.log2(math.e)
    row = lax.broadcasted_iota(jnp.int32, (HEADS, 1), 0)
    head = ((row % slots) ^ tensor_index) * here + row // slots
    kv_head = head // GROUP
    column = lax.broadcasted_iota(jnp.int32, (1, positions * KV_HEADS), 1)
    place = column // KV_HEADS + inner_index * positions
    column_head = column % KV_HEADS
    lanes = lax.broadcasted_iota(jnp.int32, (HEADS, LANES), 1)
    queries = [
        query_s[pl.ds(r, HEADS, stride=own_rows), :].astype(jnp.bfloat16) for r in range(own_rows)
    ]
    scores = [
        lax.dot_general(
            queries[r], key_ref[r], (((1,), (1,)), ((), ())), preferred_element_type=jnp.float32
        )
        for r in range(own_rows)
    ]
    weights = []
    mixtures = []
    for r in range(own_rows):
        used = jnp.where(place < lengths_ref[r : r + 1, 0:1], column_head, -1)
        masked = jnp.where(used == kv_head, scores[r], -1e30)
        key_rows = 0.0
        value_rows = 0.0
        for g in range(KV_HEADS):
            key_rows = key_rows + jnp.where(kv_head == g, new_keys[g][r : r + 1], 0.0)
            value_rows = value_rows + jnp.where(kv_head == g, new_values[g][r : r + 1], 0.0)
        new_score = jnp.sum(queries[r].astype(jnp.float32) * key_rows, axis=1, keepdims=True)
        new_score = jnp.where(inner_index == 0, new_score, -1e30)
        peak = jnp.maximum(jnp.max(masked, axis=1, keepdims=True), new_score)
        weight = jnp.exp2((masked - peak) * two_scale)
        new_weight = jnp.exp2((new_score - peak) * two_scale)
        peak = peak * score_scale
        totals = jnp.sum(weight, axis=1, keepdims=True) + new_weight
        weights.append(weight.astype(jnp.bfloat16))
        mixtures.append(new_weight.astype(jnp.bfloat16).astype(jnp.float32) * value_rows)
        stats_s[pl.ds(r, HEADS, stride=own_rows), :] = spread(
            three_parts(peak), lanes, 0
        ) + spread(three_parts(totals), lanes, 4)
    for r in range(own_rows):
        mixed_s[pl.ds(r, HEADS, stride=own_rows), :] = mixtures[r] + jnp.dot(
            weights[r], value_ref[r], preferred_element_type=jnp.float32
        )
    heads = own_rows * HEADS
    out_ref[:heads, :] = mixed_s[...].astype(jnp.bfloat16)
    packed = stats_s[:all_rows, :]
    for j in range(1, here):
        block = stats_s[j * all_rows : (j + 1) * all_rows, :]
        packed = packed + pltpu.roll(block, j * STATS, axis=1)
    spare = out_ref.shape[0] - heads - all_rows
    if spare:
        packed = jnp.concatenate([packed, jnp.zeros((spare, LANES), jnp.float32)], axis=0)
    out_ref[heads:, :] = packed.astype(jnp.bfloat16)


def attend(lengths, cosine, sine, parts, keys, values, later, slots):
    own_rows = parts[0].shape[0] // slots
    kv_cols = 2 * KV_HEADS * HEAD_DIM // slots
    return pl.pallas_call(
        functools.partial(attend_kernel, slots, len(parts)),
        out_shape=jax.ShapeDtypeStruct(
            (own_rows * HEADS + max(16, own_rows * slots), HEAD_DIM), jnp.bfloat16
        ),
        in_specs=[in_vmem] * (5 + len(parts)) + [in_place] * len(later),
        out_specs=in_vmem,
        scratch_shapes=[
            pltpu.VMEM((own_rows * HEADS, HEAD_DIM), jnp.float32),
            pltpu.VMEM((slots, own_rows, kv_cols), jnp.float32),
            pltpu.VMEM((own_rows, slots * kv_cols), jnp.float32),
            pltpu.VMEM((own_rows * HEADS, HEAD_DIM), jnp.float32),
            pltpu.VMEM((own_rows * HEADS, LANES), jnp.float32),
        ],
        compiler_params=params(6),
        name="attend",
    )(lengths, cosine, sine, resident(keys), resident(values), *parts[::-1], *[resident(w) for w in later])


def combine_kernel(shards, slots, *refs):
    out_s = refs[-1]
    all_rows, columns = out_s.shape
    here = columns // HEAD_DIM
    heads = here * all_rows
    mixtures = [ref[:heads, :].astype(jnp.float32) for ref in refs[:shards]]
    stats = [ref[heads:, :].astype(jnp.float32)[:all_rows] for ref in refs[:shards]]
    for j in range(here):

        def whole(block, first):
            lane = j * STATS + first
            return block[:, lane : lane + 1] + block[:, lane + 1 : lane + 2] + block[:, lane + 2 : lane + 3]

        peaks = [whole(block, 0) for block in stats]
        top = functools.reduce(jnp.maximum, peaks)
        mixed = 0.0
        denominator = 0.0
        for mixture, block, peak in zip(mixtures, stats, peaks):
            factor = jnp.exp(peak - top)
            mixed = mixed + factor * mixture[j * all_rows : (j + 1) * all_rows]
            denominator = denominator + factor * whole(block, 4)
        out_s[:, j * HEAD_DIM : (j + 1) * HEAD_DIM] = mixed / denominator
    part_rows(out_s, refs[-1 - slots : -1])


def combine(parts, later, all_rows, slots):
    count = len(parts)
    columns = HEADS // slots * HEAD_DIM
    return pl.pallas_call(
        functools.partial(combine_kernel, count, slots),
        out_shape=(jax.ShapeDtypeStruct((all_rows // slots, columns), jnp.bfloat16),) * slots,
        in_specs=[in_vmem] * count + [in_place] * len(later),
        out_specs=(in_vmem,) * slots,
        scratch_shapes=[pltpu.VMEM((all_rows, columns), jnp.float32)],
        compiler_params=params(2),
        name="combine",
    )(*parts[::-1], *[resident(w) for w in later])


def turned(block, step, own_rows):
    count = block.shape[0]
    span = step * own_rows
    row = lax.broadcasted_iota(jnp.int32, (count, 1), 0)
    return jnp.where(
        (row // span) % 2 == 0,
        pltpu.roll(block, count - span, axis=0),
        pltpu.roll(block, span, axis=0),
    )


def out_kernel(slots, later, upper_ref, lower_ref, *refs):
    pieces = refs[:slots][::-1]
    outs = refs[slots + later : 2 * slots + later]
    left_s = refs[-1]
    own_rows = pieces[0].shape[0]
    rows = left_s.shape[0]
    cut = upper_ref.shape[0]
    lefts = [join_rows(pieces, left_s)]
    for k in range(1, slots):
        low = k & -k
        lefts.append(turned(lefts[k ^ low], low, own_rows))
    left = jnp.concatenate(lefts, axis=0).astype(jnp.bfloat16)

    def store(start, size, value):
        span = pl.ds(start, size)
        value = value + jnp.dot(
            left[:, cut:], lower_ref[:, span], preferred_element_type=jnp.float32
        )
        for k, ref in enumerate(outs):
            ref[:, span] = value[k * rows : (k + 1) * rows].astype(jnp.bfloat16)

    product_tiles(left[:, :cut], upper_ref, store)


def project_out(pieces, upper, lower, later):
    slots = len(pieces)
    own_rows, depth = pieces[0].shape
    shape = jax.ShapeDtypeStruct((own_rows * slots, upper.shape[1]), jnp.bfloat16)
    return pl.pallas_call(
        functools.partial(out_kernel, slots, len(later)),
        out_shape=(shape,) * slots,
        in_specs=[in_vmem] * (2 + slots) + [in_place] * len(later),
        out_specs=(in_vmem,) * slots,
        scratch_shapes=[pltpu.VMEM((own_rows * slots, depth), jnp.float32)],
        compiler_params=params(3),
        name="project_out",
    )(resident(upper), resident(lower), *pieces[::-1], *[resident(w) for w in later])


def pair_kernel(first_ref, second_ref, out_ref):
    total = first_ref[...].astype(jnp.float32) + second_ref[...].astype(jnp.float32)
    out_ref[...] = total.astype(jnp.bfloat16)


def pair_sum(first, second):
    return pl.pallas_call(
        pair_kernel,
        out_shape=jax.ShapeDtypeStruct(first.shape, first.dtype),
        in_specs=[in_vmem] * 2,
        out_specs=in_vmem,
        compiler_params=params(2),
        name="pair_sum",
    )(first, second)


def gate_up_tiles(scaled, gate_ref, up_ref, out_ref, first, count):
    def store(offset):
        def place(start, size, value):
            start = pl.multiple_of(offset + start, math.gcd(offset, size))
            out_ref[:, pl.ds(start, size)] = value.astype(jnp.bfloat16)

        return place

    product_tiles(scaled, gate_ref, store(0), first, count)
    product_tiles(scaled, up_ref, store(count), first, count)


def first_gate_up_kernel(slots, count, rows_ref, gain_ref, gate_ref, up_ref, *refs):
    parts = refs[:slots]
    out_ref, updated_ref, scaled_ref = refs[-3:]
    own_rows = updated_ref.shape[0]
    total = functools.reduce(jnp.add, [ref[...].astype(jnp.float32) for ref in parts])
    updated = (rows_ref[...] + total).astype(jnp.bfloat16)
    wide = updated.astype(jnp.float32)
    updated_ref[...] = wide[:own_rows]
    squares = jnp.sum(wide * wide, axis=1, keepdims=True)
    out_ref[:, 2 * count :] = squares_block(squares).astype(jnp.bfloat16)
    scaled = (wide * gain_ref[...].astype(jnp.float32)[None, :]).astype(jnp.bfloat16)
    scaled_ref[...] = scaled
    gate_up_tiles(scaled, gate_ref, up_ref, out_ref, 0, count)


def first_gate_up(rows, gain, parts, w_gate, w_up, later, count, own_rows):
    slots = len(parts)
    return pl.pallas_call(
        functools.partial(first_gate_up_kernel, slots, count),
        out_shape=(
            jax.ShapeDtypeStruct((rows.shape[0], 2 * count + LANES), jnp.bfloat16),
            jax.ShapeDtypeStruct((own_rows, rows.shape[1]), jnp.float32),
            jax.ShapeDtypeStruct(rows.shape, jnp.bfloat16),
        ),
        in_specs=[in_vmem] * (4 + slots) + [in_place] * len(later),
        out_specs=(in_vmem,) * 3,
        compiler_params=params(3),
        cost_estimate=product_cost(w_gate.shape[0], 2 * count),
        name="first_gate_up",
    )(
        rows,
        gain,
        resident(w_gate),
        resident(w_up),
        *in_start_order(parts),
        *[resident(w) for w in later],
    )


def second_gate_up_kernel(first, count, scaled_ref, gate_ref, up_ref, *refs):
    out_ref = refs[-1]
    gate_up_tiles(scaled_ref[...], gate_ref, up_ref, out_ref, first, count)


def second_gate_up(scaled, w_gate, w_up, later, first):
    count = w_gate.shape[1] - first
    return pl.pallas_call(
        functools.partial(second_gate_up_kernel, first, count),
        out_shape=jax.ShapeDtypeStruct((scaled.shape[0], 2 * count), jnp.bfloat16),
        in_specs=[in_vmem] * 3 + [in_place] * len(later),
        out_specs=in_vmem,
        compiler_params=params(3),
        cost_estimate=product_cost(w_gate.shape[0], 2 * count),
        name="second_gate_up",
    )(scaled, resident(w_gate), resident(w_up), *[resident(w) for w in later])


def hidden_of(near_ref, far_ref, scale, count):
    def total(start):
        span = slice(start, start + count)
        return (near_ref[:, span].astype(jnp.float32) + far_ref[:, span].astype(jnp.float32)) * scale

    gate = total(0)
    return (gate / (1.0 + jnp.exp(-gate)) * total(count)).astype(jnp.bfloat16)


def first_down_kernel(count, near_ref, far_ref, weight_ref, token_ref, out_ref, scale_ref):
    del token_ref
    squares = jnp.sum(
        near_ref[:, 2 * count :].astype(jnp.float32) + far_ref[:, 2 * count :].astype(jnp.float32),
        axis=1,
        keepdims=True,
    )
    scale = lax.rsqrt(squares / D + epsilon)
    scale_ref[...] = jnp.broadcast_to(scale, scale_ref.shape)

    def store(start, size, value):
        out_ref[:, pl.ds(start, size)] = value

    product_tiles(hidden_of(near_ref, far_ref, scale, count), weight_ref.at[:count], store)


def first_down(near, far, weight, token, count):
    rows = near.shape[0]
    return pl.pallas_call(
        functools.partial(first_down_kernel, count),
        out_shape=(
            jax.ShapeDtypeStruct((rows, weight.shape[1]), jnp.float32),
            jax.ShapeDtypeStruct((rows, LANES), jnp.float32),
        ),
        in_specs=[in_vmem] * 3 + [in_place],
        out_specs=(in_vmem,) * 2,
        compiler_params=params(3),
        cost_estimate=product_cost(count, weight.shape[1]),
        name="first_down",
    )(near, far, resident(weight), token)


def second_down_kernel(count, near_ref, far_ref, weight_ref, part_ref, scale_ref, *refs):
    out_s = refs[-1]
    first = weight_ref.shape[0] - count

    def store(start, size, value):
        span = pl.ds(start, size)
        out_s[:, span] = part_ref[:, span] + value

    hidden = hidden_of(near_ref, far_ref, scale_ref[:, 0:1], count)
    product_tiles(hidden, weight_ref.at[first:], store)
    part_rows(out_s, refs[:-1])


def second_down(near, far, weight, part, scale, slots):
    rows, columns = part.shape
    count = near.shape[1] // 2
    return pl.pallas_call(
        functools.partial(second_down_kernel, count),
        out_shape=(jax.ShapeDtypeStruct((rows // slots, columns), jnp.bfloat16),) * slots,
        in_specs=[in_vmem] * 5,
        out_specs=(in_vmem,) * slots,
        scratch_shapes=[pltpu.VMEM(part.shape, jnp.float32)],
        compiler_params=params(3),
        name="second_down",
    )(near, far, resident(weight), part, scale)


def hold_kernel(after_ref, weight_ref, out_ref):
    del after_ref, weight_ref
    out_ref[...] = jnp.zeros_like(out_ref)


def hold(after, weight):
    return pl.pallas_call(
        hold_kernel,
        out_shape=jax.ShapeDtypeStruct((8, LANES), jnp.float32),
        in_specs=[in_place, in_place],
        out_specs=in_vmem,
        compiler_params=params(1),
        name="hold",
    )(after, resident(weight))


def finish_kernel(updated_ref, *refs):
    total = functools.reduce(jnp.add, [ref[...].astype(jnp.float32) for ref in refs[:-1]])
    refs[-1][...] = (updated_ref[...] + total).astype(jnp.bfloat16)


def finish(updated, parts):
    return pl.pallas_call(
        finish_kernel,
        out_shape=jax.ShapeDtypeStruct(updated.shape, jnp.bfloat16),
        in_specs=[in_vmem] * (1 + len(parts)),
        out_specs=in_vmem,
        compiler_params=params(1),
        name="finish",
    )(updated, *in_start_order(parts))


def rotation_tables(positions, repeats):
    inverse = jnp.exp(
        (jnp.arange(HEAD_DIM) // 2).astype(jnp.float32) * (-2.0 / HEAD_DIM) * math.log(rope_base)
    )
    angles = positions[:, None] * inverse[None, :]
    sign = jnp.where(jnp.arange(HEAD_DIM) % 2 == 0, -1.0, 1.0)
    return (
        jnp.tile(jnp.cos(angles), (repeats, 1)),
        jnp.tile(jnp.sin(angles) * sign[None, :], (repeats, 1)),
    )


def local(
    states,
    attn_gain,
    ffn_gain,
    w_query,
    w_kv,
    w_out,
    w_gate,
    w_up,
    w_down,
    key_cache,
    value_cache,
    lengths,
):
    tensor_index = lax.axis_index("tensor")
    slots = lax.axis_size("tensor")
    own_rows = states.shape[0]
    all_rows = own_rows * slots

    got = exchange(states, "tensor")
    own, attn_gain, ffn_gain, w_kv, w_query = load(
        states, attn_gain, ffn_gain, w_kv, w_query, after=states
    )
    rows, *pieces = project_qkv([own] + got[1:], attn_gain, w_query, w_kv)

    rows, lengths = lax.optimization_barrier((rows, lengths))
    my_lengths = lax.dynamic_slice_in_dim(lengths, tensor_index * own_rows, own_rows, 0)
    cosine, sine = rotation_tables(my_lengths.astype(jnp.float32), slots)
    my_lengths = jnp.broadcast_to(my_lengths[:, None], (own_rows, LANES))
    flat = (own_rows, key_cache.shape[1] * KV_HEADS, HEAD_DIM)
    (keys,) = load(key_cache.reshape(flat), after=rows)
    joined = stack(scatter_slots(pieces, 1))
    joined, keys = lax.optimization_barrier((joined, keys))
    (values,) = load(value_cache.reshape(flat), after=joined)
    parts, values = lax.optimization_barrier((exchange(joined, "inner")[::-1], values))
    shard = attend(my_lengths, cosine, sine, parts, keys, values, [], slots)

    cut = w_out.shape[0] // 2
    (out_upper,) = load(w_out, after=shard, spans=[(0, cut)])
    shards, out_upper = lax.optimization_barrier((exchange(shard, "inner"), out_upper))
    pieces = combine(shards, [w_gate], all_rows, slots)
    (out_lower,) = load(w_out, after=pieces[0], spans=[(cut, w_out.shape[0] - cut)])
    pieces, out_lower = lax.optimization_barrier((scatter_slots(pieces, 1)[::-1], out_lower))
    parts = scatter_slots(project_out(pieces[::-1], out_upper, out_lower, [w_up]), 0)

    tiles = w_gate.shape[1] // LANES
    first = (tiles + 1) // 2 * LANES
    one, updated, scaled = first_gate_up(
        rows, ffn_gain, parts, w_gate, w_up, [], first, own_rows
    )
    two = second_gate_up(scaled, w_gate, w_up, [], first)
    steps = steps_up(lax.axis_size("inner"))
    for step in steps[:-1]:
        one = pair_sum(one, swap_with(one, "inner", step))
        two = pair_sum(two, swap_with(two, "inner", step))
    token = hold(two, w_down)
    part, scale = first_down(one, swap_with(one, "inner", steps[-1]), w_down, token, first)
    pieces = second_down(two, swap_with(two, "inner", steps[-1]), w_down, part, scale, slots)
    parts = scatter_slots(pieces, 0)
    return finish(updated, parts)


def solution(mesh):
    in_specs = (
        P(("groups", "tensor"), "inner"),
        P("inner"),
        P("inner"),
        P("inner", "tensor"),
        P("inner", "tensor"),
        P("tensor", "inner"),
        P("inner", "tensor"),
        P("inner", "tensor"),
        P("tensor", "inner"),
        P(("groups", "tensor"), "inner", None, None),
        P(("groups", "tensor"), "inner", None, None),
        P("groups"),
    )
    out_specs = P(("groups", "tensor"), "inner")
    return jax.shard_map(local, mesh=mesh, in_specs=in_specs, out_specs=out_specs, check_vma=False)
```

```python
import functools
import math

import jax
import jax.numpy as jnp
from jax import lax
from jax.experimental import pallas as pl
from jax.experimental.pallas import tpu as pltpu
from jax.sharding import PartitionSpec as P

D = 8192
HEADS = 32
KV_HEADS = 4
HEAD_DIM = 128
GROUP = HEADS // KV_HEADS
LANES = 128
MIB = 2**20
COPIES = 4
STATS = 8

epsilon = 1e-05
rope_base = 500000.0

in_vmem = pl.BlockSpec(memory_space=pltpu.VMEM)
in_smem = pl.BlockSpec(memory_space=pltpu.SMEM)
in_place = pl.BlockSpec(memory_space=pl.ANY)


def swap_with(value, axis, step):
    count = lax.axis_size(axis)
    return lax.ppermute(value, axis, [(i, i ^ step) for i in range(count)])


def exchange(value, axis):
    count = lax.axis_size(axis)
    got = {k: swap_with(value, axis, k) for k in reversed(range(1, count))}
    return [value] + [got[k] for k in range(1, count)]


def scatter_slots(pieces, cross):
    count = lax.axis_size("tensor")
    width = lax.axis_size("inner")
    got = [pieces[0]]
    for k in range(1, count):
        pairs = [
            (t * width + i, (t ^ k) * width + (i ^ cross))
            for t in range(count)
            for i in range(width)
        ]
        got.append(lax.ppermute(pieces[k], ("tensor", "inner"), pairs))
    return got


def start_order(count):
    half = count // 2
    return [half] + [k for k in reversed(range(1, count)) if k != half] + [0]


def in_start_order(slots):
    return [slots[k] for k in start_order(len(slots))]


def in_slot_order(refs):
    order = start_order(len(refs))
    return [refs[order.index(k)] for k in range(len(refs))]


def steps_up(count):
    return [1 << n for n in range(count.bit_length() - 1)]


def params(mib):
    return pltpu.CompilerParams(vmem_limit_bytes=mib * MIB)


def resident(weight):
    return pltpu.with_memory_space_constraint(weight, pltpu.VMEM)


def in_hbm(weight):
    return pltpu.with_memory_space_constraint(weight, pltpu.HBM)


def product_cost(depth, columns):
    return pl.CostEstimate(
        flops=16 * depth * columns, bytes_accessed=2 * depth * columns, transcendentals=0
    )


def tile_of(columns):
    for tile in (1792, 1024, 896, 512, 256, 128):
        if columns % tile == 0:
            return tile
    return columns


def product_tiles(left, weight_ref, store, first=0, columns=None):
    columns = columns or weight_ref.shape[1]
    tile = tile_of(columns)

    @pl.loop(0, columns // tile)
    def _(step):
        start = pl.multiple_of(step * tile, tile)
        span = pl.ds(pl.multiple_of(first + start, math.gcd(first, tile)), tile)
        store(
            start,
            tile,
            jnp.dot(left, weight_ref[:, span], preferred_element_type=jnp.float32),
        )


def three_parts(value):
    high = value.astype(jnp.bfloat16).astype(jnp.float32)
    rest = value - high
    middle = rest.astype(jnp.bfloat16).astype(jnp.float32)
    return high, middle, rest - middle


def spread(parts, lanes, first):
    out = 0.0
    for n, part in enumerate(parts):
        out = out + jnp.where(lanes == first + n, part, 0.0)
    return out


def squares_block(total):
    lanes = lax.broadcasted_iota(jnp.int32, (total.shape[0], LANES), 1)
    return spread(three_parts(total), lanes, lax.axis_index("inner") * 4)


def copies_of(source, start, target, sems):
    size = target.shape[0]
    cuts = COPIES if len(target.shape) > 1 and size % (16 * COPIES) == 0 else 1
    each = size // cuts
    return [
        pltpu.make_async_copy(
            source.at[pl.ds(start + m * each, each)], target.at[pl.ds(m * each, each)], sems.at[m]
        )
        for m in range(cuts)
    ]


def load_kernel(spans, *refs):
    count = len(spans)
    outs = refs[count + 1 : 2 * count + 1]
    sems = refs[-1]
    copies = []
    for n, (start, _) in enumerate(spans):
        copies += copies_of(refs[n], start, outs[n], sems.at[n])
    for copy in copies:
        copy.start()
    for copy in copies:
        copy.wait()


def load(*arrays, after, spans=None):
    spans = spans or [(0, a.shape[0]) for a in arrays]
    shapes = [(size,) + a.shape[1:] for a, (_, size) in zip(arrays, spans)]
    return pl.pallas_call(
        functools.partial(load_kernel, spans),
        out_shape=tuple(pltpu.VMEM(shape, a.dtype) for shape, a in zip(shapes, arrays)),
        in_specs=[in_place] * (len(arrays) + 1),
        out_specs=tuple(in_vmem for _ in arrays),
        cost_estimate=pl.CostEstimate(
            flops=0, bytes_accessed=2 * sum(math.prod(shape) for shape in shapes), transcendentals=0
        ),
        scratch_shapes=[pltpu.SemaphoreType.DMA((len(arrays), COPIES))],
        compiler_params=params(1),
        name="load",
    )(*[in_hbm(a) for a in arrays], after)


def join_rows(refs, target):
    rows = refs[0].shape[0]
    for n, ref in enumerate(refs):
        target[n * rows : (n + 1) * rows, :] = ref[...].astype(jnp.float32)
    return target[...]


def part_rows(source, refs):
    rows = refs[0].shape[0]
    for n, ref in enumerate(refs):
        ref[...] = source[n * rows : (n + 1) * rows, :].astype(ref.dtype)


def qkv_kernel(slots, gain_ref, wq_ref, wkv_ref, *refs):
    rows_ref = refs[slots]
    out_s, rows_s = refs[-2:]
    wide = join_rows(in_slot_order(refs[:slots]), rows_s)
    rows_ref[...] = wide
    total = jnp.sum(wide * wide, axis=1, keepdims=True)
    gain = gain_ref[...].astype(jnp.float32)[None, :]
    scaled = (wide * gain).astype(jnp.bfloat16)
    query_cols = wq_ref.shape[1]
    kv_cols = wkv_ref.shape[1]

    def store_query(start, size, value):
        out_s[:, pl.ds(start, size)] = value

    product_tiles(scaled, wq_ref, store_query)
    out_s[:, query_cols : query_cols + kv_cols] = jnp.dot(
        scaled, wkv_ref[...], preferred_element_type=jnp.float32
    )
    out_s[:, query_cols + kv_cols :] = squares_block(total)
    part_rows(out_s, refs[slots + 1 : 2 * slots + 1])


def project_qkv(rows, gain, w_query, w_kv):
    slots = len(rows)
    own_rows, depth = rows[0].shape
    columns = w_query.shape[1] + w_kv.shape[1] + LANES
    return pl.pallas_call(
        functools.partial(qkv_kernel, slots),
        out_shape=(
            jax.ShapeDtypeStruct((own_rows * slots, depth), jnp.float32),
            *[jax.ShapeDtypeStruct((own_rows, columns), jnp.bfloat16)] * slots,
        ),
        in_specs=[in_vmem] * (3 + slots),
        out_specs=(in_vmem,) * (1 + slots),
        scratch_shapes=[
            pltpu.VMEM((own_rows * slots, columns), jnp.float32),
            pltpu.VMEM((own_rows * slots, depth), jnp.float32),
        ],
        compiler_params=params(2),
        name="project_qkv",
    )(gain, resident(w_query), resident(w_kv), *in_start_order(rows))


def stack_kernel(*refs):
    refs[-2][...] = join_rows(refs[:-2][::-1], refs[-1]).astype(refs[-2].dtype)


def stack(pieces):
    shape = (len(pieces) * pieces[0].shape[0], pieces[0].shape[1])
    return pl.pallas_call(
        stack_kernel,
        out_shape=jax.ShapeDtypeStruct(shape, pieces[0].dtype),
        in_specs=[in_vmem] * len(pieces),
        out_specs=in_vmem,
        scratch_shapes=[pltpu.VMEM(shape, jnp.float32)],
        compiler_params=params(1),
        name="stack",
    )(*pieces[::-1])


def attend_kernel(
    slots,
    shards,
    lengths_ref,
    cosine_ref,
    sine_ref,
    key_ref,
    value_ref,
    *refs,
):
    parts = refs[:shards]
    out_ref, query_s, kv_s, kv_wide_s, mixed_s, stats_s = refs[-6:]
    all_rows = parts[0].shape[0]
    own_rows = all_rows // slots
    here = HEADS // slots
    query_cols = here * HEAD_DIM
    kv_cols = 2 * KV_HEADS * HEAD_DIM // slots
    columns = query_cols + kv_cols
    tensor_index = lax.axis_index("tensor")
    inner_index = lax.axis_index("inner")
    positions = key_ref.shape[1] // KV_HEADS

    joined = functools.reduce(jnp.add, [ref[...].astype(jnp.float32) for ref in parts])
    squares = jnp.sum(joined[:, columns:], axis=1, keepdims=True)
    joined = joined[:, :columns] * lax.rsqrt(squares / D + epsilon)
    cosine = cosine_ref[...]
    sine = sine_ref[...]

    def rotate(block):
        count = block.shape[0]
        even = lax.broadcasted_iota(jnp.int32, block.shape, 1) % 2 == 0
        other = jnp.where(
            even, pltpu.roll(block, HEAD_DIM - 1, axis=1), pltpu.roll(block, 1, axis=1)
        )
        return block * cosine[:count] + other * sine[:count]

    for j in range(here):
        block = rotate(joined[:, j * HEAD_DIM : (j + 1) * HEAD_DIM])
        query_s[j * all_rows : (j + 1) * all_rows, :] = block
    for s in range(slots):
        kv_s[s] = joined[s * own_rows : (s + 1) * own_rows, query_cols:]
    for d in range(slots):
        kv_wide_s[:, d * kv_cols : (d + 1) * kv_cols] = kv_s[d ^ tensor_index]
    new_keys = []
    new_values = []
    for g in range(KV_HEADS):
        block = kv_wide_s[:, g * HEAD_DIM : (g + 1) * HEAD_DIM]
        new_keys.append(rotate(block).astype(jnp.bfloat16).astype(jnp.float32))
        block = kv_wide_s[:, (KV_HEADS + g) * HEAD_DIM : (KV_HEADS + g + 1) * HEAD_DIM]
        new_values.append(block.astype(jnp.bfloat16).astype(jnp.float32))

    score_scale = HEAD_DIM ** (-0.5)
    two_scale = score_scale * math.log2(math.e)
    row = lax.broadcasted_iota(jnp.int32, (HEADS, 1), 0)
    head = ((row % slots) ^ tensor_index) * here + row // slots
    kv_head = head // GROUP
    column = lax.broadcasted_iota(jnp.int32, (1, positions * KV_HEADS), 1)
    place = column // KV_HEADS + inner_index * positions
    column_head = column % KV_HEADS
    lanes = lax.broadcasted_iota(jnp.int32, (HEADS, LANES), 1)
    queries = [
        query_s[pl.ds(r, HEADS, stride=own_rows), :].astype(jnp.bfloat16) for r in range(own_rows)
    ]
    scores = [
        lax.dot_general(
            queries[r], key_ref[r], (((1,), (1,)), ((), ())), preferred_element_type=jnp.float32
        )
        for r in range(own_rows)
    ]
    weights = []
    mixtures = []
    for r in range(own_rows):
        used = jnp.where(place < lengths_ref[r : r + 1, 0:1], column_head, -1)
        masked = jnp.where(used == kv_head, scores[r], -1e30)
        key_rows = 0.0
        value_rows = 0.0
        for g in range(KV_HEADS):
            key_rows = key_rows + jnp.where(kv_head == g, new_keys[g][r : r + 1], 0.0)
            value_rows = value_rows + jnp.where(kv_head == g, new_values[g][r : r + 1], 0.0)
        new_score = jnp.sum(queries[r].astype(jnp.float32) * key_rows, axis=1, keepdims=True)
        new_score = jnp.where(inner_index == 0, new_score, -1e30)
        peak = jnp.maximum(jnp.max(masked, axis=1, keepdims=True), new_score)
        weight = jnp.exp2((masked - peak) * two_scale)
        new_weight = jnp.exp2((new_score - peak) * two_scale)
        peak = peak * score_scale
        totals = jnp.sum(weight, axis=1, keepdims=True) + new_weight
        weights.append(weight.astype(jnp.bfloat16))
        mixtures.append(new_weight.astype(jnp.bfloat16).astype(jnp.float32) * value_rows)
        stats_s[pl.ds(r, HEADS, stride=own_rows), :] = spread(
            three_parts(peak), lanes, 0
        ) + spread(three_parts(totals), lanes, 4)
    for r in range(own_rows):
        mixed_s[pl.ds(r, HEADS, stride=own_rows), :] = mixtures[r] + jnp.dot(
            weights[r], value_ref[r], preferred_element_type=jnp.float32
        )
    heads = own_rows * HEADS
    out_ref[:heads, :] = mixed_s[...].astype(jnp.bfloat16)
    packed = stats_s[:all_rows, :]
    for j in range(1, here):
        block = stats_s[j * all_rows : (j + 1) * all_rows, :]
        packed = packed + pltpu.roll(block, j * STATS, axis=1)
    spare = out_ref.shape[0] - heads - all_rows
    if spare:
        packed = jnp.concatenate([packed, jnp.zeros((spare, LANES), jnp.float32)], axis=0)
    out_ref[heads:, :] = packed.astype(jnp.bfloat16)


def attend(lengths, cosine, sine, parts, keys, values, later, slots):
    own_rows = parts[0].shape[0] // slots
    kv_cols = 2 * KV_HEADS * HEAD_DIM // slots
    return pl.pallas_call(
        functools.partial(attend_kernel, slots, len(parts)),
        out_shape=jax.ShapeDtypeStruct(
            (own_rows * HEADS + max(16, own_rows * slots), HEAD_DIM), jnp.bfloat16
        ),
        in_specs=[in_vmem] * (5 + len(parts)) + [in_place] * len(later),
        out_specs=in_vmem,
        scratch_shapes=[
            pltpu.VMEM((own_rows * HEADS, HEAD_DIM), jnp.float32),
            pltpu.VMEM((slots, own_rows, kv_cols), jnp.float32),
            pltpu.VMEM((own_rows, slots * kv_cols), jnp.float32),
            pltpu.VMEM((own_rows * HEADS, HEAD_DIM), jnp.float32),
            pltpu.VMEM((own_rows * HEADS, LANES), jnp.float32),
        ],
        compiler_params=params(6),
        name="attend",
    )(lengths, cosine, sine, resident(keys), resident(values), *parts[::-1], *[resident(w) for w in later])


def combine_kernel(shards, slots, *refs):
    out_s = refs[-1]
    all_rows, columns = out_s.shape
    here = columns // HEAD_DIM
    heads = here * all_rows
    mixtures = [ref[:heads, :].astype(jnp.float32) for ref in refs[:shards]]
    stats = [ref[heads:, :].astype(jnp.float32)[:all_rows] for ref in refs[:shards]]
    for j in range(here):

        def whole(block, first):
            lane = j * STATS + first
            return block[:, lane : lane + 1] + block[:, lane + 1 : lane + 2] + block[:, lane + 2 : lane + 3]

        peaks = [whole(block, 0) for block in stats]
        top = functools.reduce(jnp.maximum, peaks)
        mixed = 0.0
        denominator = 0.0
        for mixture, block, peak in zip(mixtures, stats, peaks):
            factor = jnp.exp(peak - top)
            mixed = mixed + factor * mixture[j * all_rows : (j + 1) * all_rows]
            denominator = denominator + factor * whole(block, 4)
        out_s[:, j * HEAD_DIM : (j + 1) * HEAD_DIM] = mixed / denominator
    part_rows(out_s, refs[-1 - slots : -1])


def combine(parts, later, all_rows, slots):
    count = len(parts)
    columns = HEADS // slots * HEAD_DIM
    return pl.pallas_call(
        functools.partial(combine_kernel, count, slots),
        out_shape=(jax.ShapeDtypeStruct((all_rows // slots, columns), jnp.bfloat16),) * slots,
        in_specs=[in_vmem] * count + [in_place] * len(later),
        out_specs=(in_vmem,) * slots,
        scratch_shapes=[pltpu.VMEM((all_rows, columns), jnp.float32)],
        compiler_params=params(2),
        name="combine",
    )(*parts[::-1], *[resident(w) for w in later])


def turned(block, step, own_rows):
    count = block.shape[0]
    span = step * own_rows
    row = lax.broadcasted_iota(jnp.int32, (count, 1), 0)
    return jnp.where(
        (row // span) % 2 == 0,
        pltpu.roll(block, count - span, axis=0),
        pltpu.roll(block, span, axis=0),
    )


def out_kernel(slots, later, upper_ref, lower_ref, *refs):
    pieces = refs[:slots][::-1]
    outs = refs[slots + later : 2 * slots + later]
    left_s = refs[-1]
    own_rows = pieces[0].shape[0]
    rows = left_s.shape[0]
    cut = upper_ref.shape[0]
    lefts = [join_rows(pieces, left_s)]
    for k in range(1, slots):
        low = k & -k
        lefts.append(turned(lefts[k ^ low], low, own_rows))
    left = jnp.concatenate(lefts, axis=0).astype(jnp.bfloat16)

    def store(start, size, value):
        span = pl.ds(start, size)
        value = value + jnp.dot(
            left[:, cut:], lower_ref[:, span], preferred_element_type=jnp.float32
        )
        for k, ref in enumerate(outs):
            ref[:, span] = value[k * rows : (k + 1) * rows].astype(jnp.bfloat16)

    product_tiles(left[:, :cut], upper_ref, store)


def project_out(pieces, upper, lower, later):
    slots = len(pieces)
    own_rows, depth = pieces[0].shape
    shape = jax.ShapeDtypeStruct((own_rows * slots, upper.shape[1]), jnp.bfloat16)
    return pl.pallas_call(
        functools.partial(out_kernel, slots, len(later)),
        out_shape=(shape,) * slots,
        in_specs=[in_vmem] * (2 + slots) + [in_place] * len(later),
        out_specs=(in_vmem,) * slots,
        scratch_shapes=[pltpu.VMEM((own_rows * slots, depth), jnp.float32)],
        compiler_params=params(3),
        name="project_out",
    )(resident(upper), resident(lower), *pieces[::-1], *[resident(w) for w in later])


def pair_kernel(first_ref, second_ref, out_ref):
    total = first_ref[...].astype(jnp.float32) + second_ref[...].astype(jnp.float32)
    out_ref[...] = total.astype(jnp.bfloat16)


def pair_sum(first, second):
    return pl.pallas_call(
        pair_kernel,
        out_shape=jax.ShapeDtypeStruct(first.shape, first.dtype),
        in_specs=[in_vmem] * 2,
        out_specs=in_vmem,
        compiler_params=params(2),
        name="pair_sum",
    )(first, second)


def gate_up_tiles(scaled, gate_ref, up_ref, out_ref, first, count):
    def store(offset):
        def place(start, size, value):
            start = pl.multiple_of(offset + start, math.gcd(offset, size))
            out_ref[:, pl.ds(start, size)] = value.astype(jnp.bfloat16)

        return place

    product_tiles(scaled, gate_ref, store(0), first, count)
    product_tiles(scaled, up_ref, store(count), first, count)


def first_gate_up_kernel(slots, count, rows_ref, gain_ref, gate_ref, up_ref, *refs):
    parts = refs[:slots]
    out_ref, updated_ref, scaled_ref = refs[-3:]
    own_rows = updated_ref.shape[0]
    total = functools.reduce(jnp.add, [ref[...].astype(jnp.float32) for ref in parts])
    updated = (rows_ref[...] + total).astype(jnp.bfloat16)
    wide = updated.astype(jnp.float32)
    updated_ref[...] = wide[:own_rows]
    squares = jnp.sum(wide * wide, axis=1, keepdims=True)
    out_ref[:, 2 * count :] = squares_block(squares).astype(jnp.bfloat16)
    scaled = (wide * gain_ref[...].astype(jnp.float32)[None, :]).astype(jnp.bfloat16)
    scaled_ref[...] = scaled
    gate_up_tiles(scaled, gate_ref, up_ref, out_ref, 0, count)


def first_gate_up(rows, gain, parts, w_gate, w_up, later, count, own_rows):
    slots = len(parts)
    return pl.pallas_call(
        functools.partial(first_gate_up_kernel, slots, count),
        out_shape=(
            jax.ShapeDtypeStruct((rows.shape[0], 2 * count + LANES), jnp.bfloat16),
            jax.ShapeDtypeStruct((own_rows, rows.shape[1]), jnp.float32),
            jax.ShapeDtypeStruct(rows.shape, jnp.bfloat16),
        ),
        in_specs=[in_vmem] * (4 + slots) + [in_place] * len(later),
        out_specs=(in_vmem,) * 3,
        compiler_params=params(3),
        cost_estimate=product_cost(w_gate.shape[0], 2 * count),
        name="first_gate_up",
    )(
        rows,
        gain,
        resident(w_gate),
        resident(w_up),
        *parts[::-1],
        *[resident(w) for w in later],
    )


def second_gate_up_kernel(first, count, scaled_ref, gate_ref, up_ref, *refs):
    out_ref = refs[-1]
    gate_up_tiles(scaled_ref[...], gate_ref, up_ref, out_ref, first, count)


def second_gate_up(scaled, w_gate, w_up, later, first):
    count = w_gate.shape[1] - first
    return pl.pallas_call(
        functools.partial(second_gate_up_kernel, first, count),
        out_shape=jax.ShapeDtypeStruct((scaled.shape[0], 2 * count), jnp.bfloat16),
        in_specs=[in_vmem] * 3 + [in_place] * len(later),
        out_specs=in_vmem,
        compiler_params=params(3),
        cost_estimate=product_cost(w_gate.shape[0], 2 * count),
        name="second_gate_up",
    )(scaled, resident(w_gate), resident(w_up), *[resident(w) for w in later])


def hidden_of(near_ref, far_ref, scale, count):
    def total(start):
        span = slice(start, start + count)
        return (near_ref[:, span].astype(jnp.float32) + far_ref[:, span].astype(jnp.float32)) * scale

    gate = total(0)
    return (gate / (1.0 + jnp.exp(-gate)) * total(count)).astype(jnp.bfloat16)


def first_down_kernel(count, near_ref, far_ref, weight_ref, token_ref, out_ref, scale_ref):
    del token_ref
    squares = jnp.sum(
        near_ref[:, 2 * count :].astype(jnp.float32) + far_ref[:, 2 * count :].astype(jnp.float32),
        axis=1,
        keepdims=True,
    )
    scale = lax.rsqrt(squares / D + epsilon)
    scale_ref[...] = jnp.broadcast_to(scale, scale_ref.shape)

    def store(start, size, value):
        out_ref[:, pl.ds(start, size)] = value

    product_tiles(hidden_of(near_ref, far_ref, scale, count), weight_ref.at[:count], store)


def first_down(near, far, weight, token, count):
    rows = near.shape[0]
    return pl.pallas_call(
        functools.partial(first_down_kernel, count),
        out_shape=(
            jax.ShapeDtypeStruct((rows, weight.shape[1]), jnp.float32),
            jax.ShapeDtypeStruct((rows, LANES), jnp.float32),
        ),
        in_specs=[in_vmem] * 3 + [in_place],
        out_specs=(in_vmem,) * 2,
        compiler_params=params(3),
        cost_estimate=product_cost(count, weight.shape[1]),
        name="first_down",
    )(near, far, resident(weight), token)


def second_down_kernel(count, near_ref, far_ref, weight_ref, part_ref, scale_ref, *refs):
    out_s = refs[-1]
    first = weight_ref.shape[0] - count

    def store(start, size, value):
        span = pl.ds(start, size)
        out_s[:, span] = part_ref[:, span] + value

    hidden = hidden_of(near_ref, far_ref, scale_ref[:, 0:1], count)
    product_tiles(hidden, weight_ref.at[first:], store)
    part_rows(out_s, refs[:-1])


def second_down(near, far, weight, part, scale, slots):
    rows, columns = part.shape
    count = near.shape[1] // 2
    return pl.pallas_call(
        functools.partial(second_down_kernel, count),
        out_shape=(jax.ShapeDtypeStruct((rows // slots, columns), jnp.bfloat16),) * slots,
        in_specs=[in_vmem] * 5,
        out_specs=(in_vmem,) * slots,
        scratch_shapes=[pltpu.VMEM(part.shape, jnp.float32)],
        compiler_params=params(3),
        name="second_down",
    )(near, far, resident(weight), part, scale)


def hold_kernel(after_ref, weight_ref, out_ref):
    del after_ref, weight_ref
    out_ref[...] = jnp.zeros_like(out_ref)


def hold(after, weight):
    return pl.pallas_call(
        hold_kernel,
        out_shape=jax.ShapeDtypeStruct((8, LANES), jnp.float32),
        in_specs=[in_place, in_place],
        out_specs=in_vmem,
        compiler_params=params(1),
        name="hold",
    )(after, resident(weight))


def finish_kernel(updated_ref, *refs):
    total = functools.reduce(jnp.add, [ref[...].astype(jnp.float32) for ref in refs[:-1]])
    refs[-1][...] = (updated_ref[...] + total).astype(jnp.bfloat16)


def finish(updated, parts):
    return pl.pallas_call(
        finish_kernel,
        out_shape=jax.ShapeDtypeStruct(updated.shape, jnp.bfloat16),
        in_specs=[in_vmem] * (1 + len(parts)),
        out_specs=in_vmem,
        compiler_params=params(1),
        name="finish",
    )(updated, *in_start_order(parts))


def rotation_tables(positions, repeats):
    inverse = jnp.exp(
        (jnp.arange(HEAD_DIM) // 2).astype(jnp.float32) * (-2.0 / HEAD_DIM) * math.log(rope_base)
    )
    angles = positions[:, None] * inverse[None, :]
    sign = jnp.where(jnp.arange(HEAD_DIM) % 2 == 0, -1.0, 1.0)
    return (
        jnp.tile(jnp.cos(angles), (repeats, 1)),
        jnp.tile(jnp.sin(angles) * sign[None, :], (repeats, 1)),
    )


def local(
    states,
    attn_gain,
    ffn_gain,
    w_query,
    w_kv,
    w_out,
    w_gate,
    w_up,
    w_down,
    key_cache,
    value_cache,
    lengths,
):
    tensor_index = lax.axis_index("tensor")
    slots = lax.axis_size("tensor")
    own_rows = states.shape[0]
    all_rows = own_rows * slots

    got = exchange(states, "tensor")
    own, attn_gain, ffn_gain, w_kv, w_query = load(
        states, attn_gain, ffn_gain, w_kv, w_query, after=states
    )
    rows, *pieces = project_qkv([own] + got[1:], attn_gain, w_query, w_kv)

    rows, lengths = lax.optimization_barrier((rows, lengths))
    my_lengths = lax.dynamic_slice_in_dim(lengths, tensor_index * own_rows, own_rows, 0)
    cosine, sine = rotation_tables(my_lengths.astype(jnp.float32), slots)
    my_lengths = jnp.broadcast_to(my_lengths[:, None], (own_rows, LANES))
    flat = (own_rows, key_cache.shape[1] * KV_HEADS, HEAD_DIM)
    (keys,) = load(key_cache.reshape(flat), after=rows)
    joined = stack(scatter_slots(pieces, 1))
    joined, keys = lax.optimization_barrier((joined, keys))
    (values,) = load(value_cache.reshape(flat), after=joined)
    parts, values = lax.optimization_barrier((exchange(joined, "inner")[::-1], values))
    shard = attend(my_lengths, cosine, sine, parts, keys, values, [], slots)

    cut = w_out.shape[0] // 2
    (out_upper,) = load(w_out, after=shard, spans=[(0, cut)])
    shards, out_upper = lax.optimization_barrier((exchange(shard, "inner"), out_upper))
    pieces = combine(shards, [w_gate], all_rows, slots)
    (out_lower,) = load(w_out, after=pieces[0], spans=[(cut, w_out.shape[0] - cut)])
    pieces, out_lower = lax.optimization_barrier((scatter_slots(pieces, 1)[::-1], out_lower))
    parts = scatter_slots(project_out(pieces[::-1], out_upper, out_lower, [w_up]), 0)

    tiles = w_gate.shape[1] // LANES
    first = (tiles + 1) // 2 * LANES
    one, updated, scaled = first_gate_up(
        rows, ffn_gain, parts, w_gate, w_up, [], first, own_rows
    )
    two = second_gate_up(scaled, w_gate, w_up, [], first)
    steps = steps_up(lax.axis_size("inner"))
    for step in steps[:-1]:
        one = pair_sum(one, swap_with(one, "inner", step))
        two = pair_sum(two, swap_with(two, "inner", step))
    token = hold(two, w_down)
    part, scale = first_down(one, swap_with(one, "inner", steps[-1]), w_down, token, first)
    pieces = second_down(two, swap_with(two, "inner", steps[-1]), w_down, part, scale, slots)
    parts = scatter_slots(pieces, 0)
    return finish(updated, parts)


def solution(mesh):
    in_specs = (
        P(("groups", "tensor"), "inner"),
        P("inner"),
        P("inner"),
        P("inner", "tensor"),
        P("inner", "tensor"),
        P("tensor", "inner"),
        P("inner", "tensor"),
        P("inner", "tensor"),
        P("tensor", "inner"),
        P(("groups", "tensor"), "inner", None, None),
        P(("groups", "tensor"), "inner", None, None),
        P("groups"),
    )
    out_specs = P(("groups", "tensor"), "inner")
    return jax.shard_map(local, mesh=mesh, in_specs=in_specs, out_specs=out_specs, check_vma=False)
```

```python
import functools
import math

import jax
import jax.numpy as jnp
from jax import lax
from jax.experimental import pallas as pl
from jax.experimental.pallas import tpu as pltpu
from jax.sharding import PartitionSpec as P

D = 8192
HEADS = 32
KV_HEADS = 4
HEAD_DIM = 128
GROUP = HEADS // KV_HEADS
LANES = 128
MIB = 2**20
COPIES = 4
STATS = 8

epsilon = 1e-05
rope_base = 500000.0

in_vmem = pl.BlockSpec(memory_space=pltpu.VMEM)
in_smem = pl.BlockSpec(memory_space=pltpu.SMEM)
in_place = pl.BlockSpec(memory_space=pl.ANY)


def swap_with(value, axis, step):
    count = lax.axis_size(axis)
    return lax.ppermute(value, axis, [(i, i ^ step) for i in range(count)])


def exchange(value, axis):
    count = lax.axis_size(axis)
    got = {k: swap_with(value, axis, k) for k in reversed(range(1, count))}
    return [value] + [got[k] for k in range(1, count)]


def scatter_slots(pieces, cross):
    count = lax.axis_size("tensor")
    width = lax.axis_size("inner")
    got = [pieces[0]]
    for k in range(1, count):
        pairs = [
            (t * width + i, (t ^ k) * width + (i ^ cross))
            for t in range(count)
            for i in range(width)
        ]
        got.append(lax.ppermute(pieces[k], ("tensor", "inner"), pairs))
    return got


def start_order(count):
    half = count // 2
    return [half] + [k for k in reversed(range(1, count)) if k != half] + [0]


def in_start_order(slots):
    return [slots[k] for k in start_order(len(slots))]


def in_slot_order(refs):
    order = start_order(len(refs))
    return [refs[order.index(k)] for k in range(len(refs))]


def steps_up(count):
    return [1 << n for n in range(count.bit_length() - 1)]


def params(mib):
    return pltpu.CompilerParams(vmem_limit_bytes=mib * MIB)


def resident(weight):
    return pltpu.with_memory_space_constraint(weight, pltpu.VMEM)


def in_hbm(weight):
    return pltpu.with_memory_space_constraint(weight, pltpu.HBM)


def product_cost(depth, columns):
    return pl.CostEstimate(
        flops=16 * depth * columns, bytes_accessed=2 * depth * columns, transcendentals=0
    )


def tile_of(columns):
    for tile in (1792, 1024, 896, 512, 256, 128):
        if columns % tile == 0:
            return tile
    return columns


def product_tiles(left, weight_ref, store, first=0, columns=None):
    columns = columns or weight_ref.shape[1]
    tile = tile_of(columns)

    @pl.loop(0, columns // tile)
    def _(step):
        start = pl.multiple_of(step * tile, tile)
        span = pl.ds(pl.multiple_of(first + start, math.gcd(first, tile)), tile)
        store(
            start,
            tile,
            jnp.dot(left, weight_ref[:, span], preferred_element_type=jnp.float32),
        )


def three_parts(value):
    high = value.astype(jnp.bfloat16).astype(jnp.float32)
    rest = value - high
    middle = rest.astype(jnp.bfloat16).astype(jnp.float32)
    return high, middle, rest - middle


def spread(parts, lanes, first):
    out = 0.0
    for n, part in enumerate(parts):
        out = out + jnp.where(lanes == first + n, part, 0.0)
    return out


def squares_block(total):
    lanes = lax.broadcasted_iota(jnp.int32, (total.shape[0], LANES), 1)
    return spread(three_parts(total), lanes, lax.axis_index("inner") * 4)


def copies_of(source, start, target, sems):
    size = target.shape[0]
    cuts = COPIES if len(target.shape) > 1 and size % (16 * COPIES) == 0 else 1
    each = size // cuts
    return [
        pltpu.make_async_copy(
            source.at[pl.ds(start + m * each, each)], target.at[pl.ds(m * each, each)], sems.at[m]
        )
        for m in range(cuts)
    ]


def load_kernel(spans, *refs):
    count = len(spans)
    outs = refs[count + 1 : 2 * count + 1]
    sems = refs[-1]
    copies = []
    for n, (start, _) in enumerate(spans):
        copies += copies_of(refs[n], start, outs[n], sems.at[n])
    for copy in copies:
        copy.start()
    for copy in copies:
        copy.wait()


def load(*arrays, after, spans=None):
    spans = spans or [(0, a.shape[0]) for a in arrays]
    shapes = [(size,) + a.shape[1:] for a, (_, size) in zip(arrays, spans)]
    return pl.pallas_call(
        functools.partial(load_kernel, spans),
        out_shape=tuple(pltpu.VMEM(shape, a.dtype) for shape, a in zip(shapes, arrays)),
        in_specs=[in_place] * (len(arrays) + 1),
        out_specs=tuple(in_vmem for _ in arrays),
        cost_estimate=pl.CostEstimate(
            flops=0, bytes_accessed=2 * sum(math.prod(shape) for shape in shapes), transcendentals=0
        ),
        scratch_shapes=[pltpu.SemaphoreType.DMA((len(arrays), COPIES))],
        compiler_params=params(1),
        name="load",
    )(*[in_hbm(a) for a in arrays], after)


def join_rows(refs, target):
    rows = refs[0].shape[0]
    for n, ref in enumerate(refs):
        target[n * rows : (n + 1) * rows, :] = ref[...].astype(jnp.float32)
    return target[...]


def part_rows(source, refs):
    rows = refs[0].shape[0]
    for n, ref in enumerate(refs):
        ref[...] = source[n * rows : (n + 1) * rows, :].astype(ref.dtype)


def qkv_kernel(slots, gain_ref, wq_ref, wkv_ref, *refs):
    rows_ref = refs[slots]
    out_s, rows_s = refs[-2:]
    wide = join_rows(in_slot_order(refs[:slots]), rows_s)
    rows_ref[...] = wide
    total = jnp.sum(wide * wide, axis=1, keepdims=True)
    gain = gain_ref[...].astype(jnp.float32)[None, :]
    scaled = (wide * gain).astype(jnp.bfloat16)
    query_cols = wq_ref.shape[1]
    kv_cols = wkv_ref.shape[1]

    def store_query(start, size, value):
        out_s[:, pl.ds(start, size)] = value

    product_tiles(scaled, wq_ref, store_query)
    out_s[:, query_cols : query_cols + kv_cols] = jnp.dot(
        scaled, wkv_ref[...], preferred_element_type=jnp.float32
    )
    out_s[:, query_cols + kv_cols :] = squares_block(total)
    part_rows(out_s, refs[slots + 1 : 2 * slots + 1])


def project_qkv(rows, gain, w_query, w_kv):
    slots = len(rows)
    own_rows, depth = rows[0].shape
    columns = w_query.shape[1] + w_kv.shape[1] + LANES
    return pl.pallas_call(
        functools.partial(qkv_kernel, slots),
        out_shape=(
            jax.ShapeDtypeStruct((own_rows * slots, depth), jnp.float32),
            *[jax.ShapeDtypeStruct((own_rows, columns), jnp.bfloat16)] * slots,
        ),
        in_specs=[in_vmem] * (3 + slots),
        out_specs=(in_vmem,) * (1 + slots),
        scratch_shapes=[
            pltpu.VMEM((own_rows * slots, columns), jnp.float32),
            pltpu.VMEM((own_rows * slots, depth), jnp.float32),
        ],
        compiler_params=params(2),
        name="project_qkv",
    )(gain, resident(w_query), resident(w_kv), *in_start_order(rows))


def stack_kernel(*refs):
    refs[-2][...] = join_rows(in_slot_order(refs[:-2]), refs[-1]).astype(refs[-2].dtype)


def stack(pieces):
    shape = (len(pieces) * pieces[0].shape[0], pieces[0].shape[1])
    return pl.pallas_call(
        stack_kernel,
        out_shape=jax.ShapeDtypeStruct(shape, pieces[0].dtype),
        in_specs=[in_vmem] * len(pieces),
        out_specs=in_vmem,
        scratch_shapes=[pltpu.VMEM(shape, jnp.float32)],
        compiler_params=params(1),
        name="stack",
    )(*in_start_order(pieces))


def attend_kernel(
    slots,
    shards,
    lengths_ref,
    cosine_ref,
    sine_ref,
    key_ref,
    value_ref,
    *refs,
):
    parts = refs[:shards]
    out_ref, query_s, kv_s, kv_wide_s, mixed_s, stats_s = refs[-6:]
    all_rows = parts[0].shape[0]
    own_rows = all_rows // slots
    here = HEADS // slots
    query_cols = here * HEAD_DIM
    kv_cols = 2 * KV_HEADS * HEAD_DIM // slots
    columns = query_cols + kv_cols
    tensor_index = lax.axis_index("tensor")
    inner_index = lax.axis_index("inner")
    positions = key_ref.shape[1] // KV_HEADS

    joined = functools.reduce(jnp.add, [ref[...].astype(jnp.float32) for ref in parts])
    squares = jnp.sum(joined[:, columns:], axis=1, keepdims=True)
    joined = joined[:, :columns] * lax.rsqrt(squares / D + epsilon)
    cosine = cosine_ref[...]
    sine = sine_ref[...]

    def rotate(block):
        count = block.shape[0]
        even = lax.broadcasted_iota(jnp.int32, block.shape, 1) % 2 == 0
        other = jnp.where(
            even, pltpu.roll(block, HEAD_DIM - 1, axis=1), pltpu.roll(block, 1, axis=1)
        )
        return block * cosine[:count] + other * sine[:count]

    for j in range(here):
        block = rotate(joined[:, j * HEAD_DIM : (j + 1) * HEAD_DIM])
        query_s[j * all_rows : (j + 1) * all_rows, :] = block
    for s in range(slots):
        kv_s[s] = joined[s * own_rows : (s + 1) * own_rows, query_cols:]
    for d in range(slots):
        kv_wide_s[:, d * kv_cols : (d + 1) * kv_cols] = kv_s[d ^ tensor_index]
    new_keys = []
    new_values = []
    for g in range(KV_HEADS):
        block = kv_wide_s[:, g * HEAD_DIM : (g + 1) * HEAD_DIM]
        new_keys.append(rotate(block).astype(jnp.bfloat16).astype(jnp.float32))
        block = kv_wide_s[:, (KV_HEADS + g) * HEAD_DIM : (KV_HEADS + g + 1) * HEAD_DIM]
        new_values.append(block.astype(jnp.bfloat16).astype(jnp.float32))

    score_scale = HEAD_DIM ** (-0.5)
    two_scale = score_scale * math.log2(math.e)
    row = lax.broadcasted_iota(jnp.int32, (HEADS, 1), 0)
    head = ((row % slots) ^ tensor_index) * here + row // slots
    kv_head = head // GROUP
    column = lax.broadcasted_iota(jnp.int32, (1, positions * KV_HEADS), 1)
    place = column // KV_HEADS + inner_index * positions
    column_head = column % KV_HEADS
    lanes = lax.broadcasted_iota(jnp.int32, (HEADS, LANES), 1)
    queries = [
        query_s[pl.ds(r, HEADS, stride=own_rows), :].astype(jnp.bfloat16) for r in range(own_rows)
    ]
    scores = [
        lax.dot_general(
            queries[r], key_ref[r], (((1,), (1,)), ((), ())), preferred_element_type=jnp.float32
        )
        for r in range(own_rows)
    ]
    weights = []
    mixtures = []
    for r in range(own_rows):
        used = jnp.where(place < lengths_ref[r : r + 1, 0:1], column_head, -1)
        masked = jnp.where(used == kv_head, scores[r], -1e30)
        key_rows = 0.0
        value_rows = 0.0
        for g in range(KV_HEADS):
            key_rows = key_rows + jnp.where(kv_head == g, new_keys[g][r : r + 1], 0.0)
            value_rows = value_rows + jnp.where(kv_head == g, new_values[g][r : r + 1], 0.0)
        new_score = jnp.sum(queries[r].astype(jnp.float32) * key_rows, axis=1, keepdims=True)
        new_score = jnp.where(inner_index == 0, new_score, -1e30)
        peak = jnp.maximum(jnp.max(masked, axis=1, keepdims=True), new_score)
        weight = jnp.exp2((masked - peak) * two_scale)
        new_weight = jnp.exp2((new_score - peak) * two_scale)
        peak = peak * score_scale
        totals = jnp.sum(weight, axis=1, keepdims=True) + new_weight
        weights.append(weight.astype(jnp.bfloat16))
        mixtures.append(new_weight.astype(jnp.bfloat16).astype(jnp.float32) * value_rows)
        stats_s[pl.ds(r, HEADS, stride=own_rows), :] = spread(
            three_parts(peak), lanes, 0
        ) + spread(three_parts(totals), lanes, 4)
    for r in range(own_rows):
        mixed_s[pl.ds(r, HEADS, stride=own_rows), :] = mixtures[r] + jnp.dot(
            weights[r], value_ref[r], preferred_element_type=jnp.float32
        )
    heads = own_rows * HEADS
    out_ref[:heads, :] = mixed_s[...].astype(jnp.bfloat16)
    packed = stats_s[:all_rows, :]
    for j in range(1, here):
        block = stats_s[j * all_rows : (j + 1) * all_rows, :]
        packed = packed + pltpu.roll(block, j * STATS, axis=1)
    spare = out_ref.shape[0] - heads - all_rows
    if spare:
        packed = jnp.concatenate([packed, jnp.zeros((spare, LANES), jnp.float32)], axis=0)
    out_ref[heads:, :] = packed.astype(jnp.bfloat16)


def attend(lengths, cosine, sine, parts, keys, values, later, slots):
    own_rows = parts[0].shape[0] // slots
    kv_cols = 2 * KV_HEADS * HEAD_DIM // slots
    return pl.pallas_call(
        functools.partial(attend_kernel, slots, len(parts)),
        out_shape=jax.ShapeDtypeStruct(
            (own_rows * HEADS + max(16, own_rows * slots), HEAD_DIM), jnp.bfloat16
        ),
        in_specs=[in_vmem] * (5 + len(parts)) + [in_place] * len(later),
        out_specs=in_vmem,
        scratch_shapes=[
            pltpu.VMEM((own_rows * HEADS, HEAD_DIM), jnp.float32),
            pltpu.VMEM((slots, own_rows, kv_cols), jnp.float32),
            pltpu.VMEM((own_rows, slots * kv_cols), jnp.float32),
            pltpu.VMEM((own_rows * HEADS, HEAD_DIM), jnp.float32),
            pltpu.VMEM((own_rows * HEADS, LANES), jnp.float32),
        ],
        compiler_params=params(6),
        name="attend",
    )(lengths, cosine, sine, resident(keys), resident(values), *parts[::-1], *[resident(w) for w in later])


def combine_kernel(shards, slots, *refs):
    out_s = refs[-1]
    all_rows, columns = out_s.shape
    here = columns // HEAD_DIM
    heads = here * all_rows
    mixtures = [ref[:heads, :].astype(jnp.float32) for ref in refs[:shards]]
    stats = [ref[heads:, :].astype(jnp.float32)[:all_rows] for ref in refs[:shards]]
    for j in range(here):

        def whole(block, first):
            lane = j * STATS + first
            return block[:, lane : lane + 1] + block[:, lane + 1 : lane + 2] + block[:, lane + 2 : lane + 3]

        peaks = [whole(block, 0) for block in stats]
        top = functools.reduce(jnp.maximum, peaks)
        mixed = 0.0
        denominator = 0.0
        for mixture, block, peak in zip(mixtures, stats, peaks):
            factor = jnp.exp(peak - top)
            mixed = mixed + factor * mixture[j * all_rows : (j + 1) * all_rows]
            denominator = denominator + factor * whole(block, 4)
        out_s[:, j * HEAD_DIM : (j + 1) * HEAD_DIM] = mixed / denominator
    part_rows(out_s, refs[-1 - slots : -1])


def combine(parts, later, all_rows, slots):
    count = len(parts)
    columns = HEADS // slots * HEAD_DIM
    return pl.pallas_call(
        functools.partial(combine_kernel, count, slots),
        out_shape=(jax.ShapeDtypeStruct((all_rows // slots, columns), jnp.bfloat16),) * slots,
        in_specs=[in_vmem] * count + [in_place] * len(later),
        out_specs=(in_vmem,) * slots,
        scratch_shapes=[pltpu.VMEM((all_rows, columns), jnp.float32)],
        compiler_params=params(2),
        name="combine",
    )(*parts[::-1], *[resident(w) for w in later])


def turned(block, step, own_rows):
    count = block.shape[0]
    span = step * own_rows
    row = lax.broadcasted_iota(jnp.int32, (count, 1), 0)
    return jnp.where(
        (row // span) % 2 == 0,
        pltpu.roll(block, count - span, axis=0),
        pltpu.roll(block, span, axis=0),
    )


def out_kernel(slots, later, upper_ref, lower_ref, *refs):
    pieces = refs[:slots][::-1]
    outs = refs[slots + later : 2 * slots + later]
    left_s = refs[-1]
    own_rows = pieces[0].shape[0]
    rows = left_s.shape[0]
    cut = upper_ref.shape[0]
    lefts = [join_rows(pieces, left_s)]
    for k in range(1, slots):
        low = k & -k
        lefts.append(turned(lefts[k ^ low], low, own_rows))
    left = jnp.concatenate(lefts, axis=0).astype(jnp.bfloat16)

    def store(start, size, value):
        span = pl.ds(start, size)
        value = value + jnp.dot(
            left[:, cut:], lower_ref[:, span], preferred_element_type=jnp.float32
        )
        for k, ref in enumerate(outs):
            ref[:, span] = value[k * rows : (k + 1) * rows].astype(jnp.bfloat16)

    product_tiles(left[:, :cut], upper_ref, store)


def project_out(pieces, upper, lower, later):
    slots = len(pieces)
    own_rows, depth = pieces[0].shape
    shape = jax.ShapeDtypeStruct((own_rows * slots, upper.shape[1]), jnp.bfloat16)
    return pl.pallas_call(
        functools.partial(out_kernel, slots, len(later)),
        out_shape=(shape,) * slots,
        in_specs=[in_vmem] * (2 + slots) + [in_place] * len(later),
        out_specs=(in_vmem,) * slots,
        scratch_shapes=[pltpu.VMEM((own_rows * slots, depth), jnp.float32)],
        compiler_params=params(3),
        name="project_out",
    )(resident(upper), resident(lower), *pieces[::-1], *[resident(w) for w in later])


def pair_kernel(first_ref, second_ref, out_ref):
    total = first_ref[...].astype(jnp.float32) + second_ref[...].astype(jnp.float32)
    out_ref[...] = total.astype(jnp.bfloat16)


def pair_sum(first, second):
    return pl.pallas_call(
        pair_kernel,
        out_shape=jax.ShapeDtypeStruct(first.shape, first.dtype),
        in_specs=[in_vmem] * 2,
        out_specs=in_vmem,
        compiler_params=params(2),
        name="pair_sum",
    )(first, second)


def gate_up_tiles(scaled, gate_ref, up_ref, out_ref, first, count):
    def store(offset):
        def place(start, size, value):
            start = pl.multiple_of(offset + start, math.gcd(offset, size))
            out_ref[:, pl.ds(start, size)] = value.astype(jnp.bfloat16)

        return place

    product_tiles(scaled, gate_ref, store(0), first, count)
    product_tiles(scaled, up_ref, store(count), first, count)


def first_gate_up_kernel(slots, count, rows_ref, gain_ref, gate_ref, up_ref, *refs):
    parts = refs[:slots]
    out_ref, updated_ref, scaled_ref = refs[-3:]
    own_rows = updated_ref.shape[0]
    total = functools.reduce(jnp.add, [ref[...].astype(jnp.float32) for ref in parts])
    updated = (rows_ref[...] + total).astype(jnp.bfloat16)
    wide = updated.astype(jnp.float32)
    updated_ref[...] = wide[:own_rows]
    squares = jnp.sum(wide * wide, axis=1, keepdims=True)
    out_ref[:, 2 * count :] = squares_block(squares).astype(jnp.bfloat16)
    scaled = (wide * gain_ref[...].astype(jnp.float32)[None, :]).astype(jnp.bfloat16)
    scaled_ref[...] = scaled
    gate_up_tiles(scaled, gate_ref, up_ref, out_ref, 0, count)


def first_gate_up(rows, gain, parts, w_gate, w_up, later, count, own_rows):
    slots = len(parts)
    return pl.pallas_call(
        functools.partial(first_gate_up_kernel, slots, count),
        out_shape=(
            jax.ShapeDtypeStruct((rows.shape[0], 2 * count + LANES), jnp.bfloat16),
            jax.ShapeDtypeStruct((own_rows, rows.shape[1]), jnp.float32),
            jax.ShapeDtypeStruct(rows.shape, jnp.bfloat16),
        ),
        in_specs=[in_vmem] * (4 + slots) + [in_place] * len(later),
        out_specs=(in_vmem,) * 3,
        compiler_params=params(3),
        cost_estimate=product_cost(w_gate.shape[0], 2 * count),
        name="first_gate_up",
    )(
        rows,
        gain,
        resident(w_gate),
        resident(w_up),
        *parts[::-1],
        *[resident(w) for w in later],
    )


def second_gate_up_kernel(first, count, scaled_ref, gate_ref, up_ref, *refs):
    out_ref = refs[-1]
    gate_up_tiles(scaled_ref[...], gate_ref, up_ref, out_ref, first, count)


def second_gate_up(scaled, w_gate, w_up, later, first):
    count = w_gate.shape[1] - first
    return pl.pallas_call(
        functools.partial(second_gate_up_kernel, first, count),
        out_shape=jax.ShapeDtypeStruct((scaled.shape[0], 2 * count), jnp.bfloat16),
        in_specs=[in_vmem] * 3 + [in_place] * len(later),
        out_specs=in_vmem,
        compiler_params=params(3),
        cost_estimate=product_cost(w_gate.shape[0], 2 * count),
        name="second_gate_up",
    )(scaled, resident(w_gate), resident(w_up), *[resident(w) for w in later])


def hidden_of(near_ref, far_ref, scale, count):
    def total(start):
        span = slice(start, start + count)
        return (near_ref[:, span].astype(jnp.float32) + far_ref[:, span].astype(jnp.float32)) * scale

    gate = total(0)
    return (gate / (1.0 + jnp.exp(-gate)) * total(count)).astype(jnp.bfloat16)


def first_down_kernel(count, near_ref, far_ref, weight_ref, token_ref, out_ref, scale_ref):
    del token_ref
    squares = jnp.sum(
        near_ref[:, 2 * count :].astype(jnp.float32) + far_ref[:, 2 * count :].astype(jnp.float32),
        axis=1,
        keepdims=True,
    )
    scale = lax.rsqrt(squares / D + epsilon)
    scale_ref[...] = jnp.broadcast_to(scale, scale_ref.shape)

    def store(start, size, value):
        out_ref[:, pl.ds(start, size)] = value

    product_tiles(hidden_of(near_ref, far_ref, scale, count), weight_ref.at[:count], store)


def first_down(near, far, weight, token, count):
    rows = near.shape[0]
    return pl.pallas_call(
        functools.partial(first_down_kernel, count),
        out_shape=(
            jax.ShapeDtypeStruct((rows, weight.shape[1]), jnp.float32),
            jax.ShapeDtypeStruct((rows, LANES), jnp.float32),
        ),
        in_specs=[in_vmem] * 3 + [in_place],
        out_specs=(in_vmem,) * 2,
        compiler_params=params(3),
        cost_estimate=product_cost(count, weight.shape[1]),
        name="first_down",
    )(near, far, resident(weight), token)


def second_down_kernel(count, near_ref, far_ref, weight_ref, part_ref, scale_ref, *refs):
    out_s = refs[-1]
    first = weight_ref.shape[0] - count

    def store(start, size, value):
        span = pl.ds(start, size)
        out_s[:, span] = part_ref[:, span] + value

    hidden = hidden_of(near_ref, far_ref, scale_ref[:, 0:1], count)
    product_tiles(hidden, weight_ref.at[first:], store)
    part_rows(out_s, refs[:-1])


def second_down(near, far, weight, part, scale, slots):
    rows, columns = part.shape
    count = near.shape[1] // 2
    return pl.pallas_call(
        functools.partial(second_down_kernel, count),
        out_shape=(jax.ShapeDtypeStruct((rows // slots, columns), jnp.bfloat16),) * slots,
        in_specs=[in_vmem] * 5,
        out_specs=(in_vmem,) * slots,
        scratch_shapes=[pltpu.VMEM(part.shape, jnp.float32)],
        compiler_params=params(3),
        name="second_down",
    )(near, far, resident(weight), part, scale)


def hold_kernel(after_ref, weight_ref, out_ref):
    del after_ref, weight_ref
    out_ref[...] = jnp.zeros_like(out_ref)


def hold(after, weight):
    return pl.pallas_call(
        hold_kernel,
        out_shape=jax.ShapeDtypeStruct((8, LANES), jnp.float32),
        in_specs=[in_place, in_place],
        out_specs=in_vmem,
        compiler_params=params(1),
        name="hold",
    )(after, resident(weight))


def finish_kernel(updated_ref, *refs):
    total = functools.reduce(jnp.add, [ref[...].astype(jnp.float32) for ref in refs[:-1]])
    refs[-1][...] = (updated_ref[...] + total).astype(jnp.bfloat16)


def finish(updated, parts):
    return pl.pallas_call(
        finish_kernel,
        out_shape=jax.ShapeDtypeStruct(updated.shape, jnp.bfloat16),
        in_specs=[in_vmem] * (1 + len(parts)),
        out_specs=in_vmem,
        compiler_params=params(1),
        name="finish",
    )(updated, *parts[::-1])


def rotation_tables(positions, repeats):
    inverse = jnp.exp(
        (jnp.arange(HEAD_DIM) // 2).astype(jnp.float32) * (-2.0 / HEAD_DIM) * math.log(rope_base)
    )
    angles = positions[:, None] * inverse[None, :]
    sign = jnp.where(jnp.arange(HEAD_DIM) % 2 == 0, -1.0, 1.0)
    return (
        jnp.tile(jnp.cos(angles), (repeats, 1)),
        jnp.tile(jnp.sin(angles) * sign[None, :], (repeats, 1)),
    )


def local(
    states,
    attn_gain,
    ffn_gain,
    w_query,
    w_kv,
    w_out,
    w_gate,
    w_up,
    w_down,
    key_cache,
    value_cache,
    lengths,
):
    tensor_index = lax.axis_index("tensor")
    slots = lax.axis_size("tensor")
    own_rows = states.shape[0]
    all_rows = own_rows * slots

    got = exchange(states, "tensor")
    own, attn_gain, ffn_gain, w_kv, w_query = load(
        states, attn_gain, ffn_gain, w_kv, w_query, after=states
    )
    rows, *pieces = project_qkv([own] + got[1:], attn_gain, w_query, w_kv)

    rows, lengths = lax.optimization_barrier((rows, lengths))
    my_lengths = lax.dynamic_slice_in_dim(lengths, tensor_index * own_rows, own_rows, 0)
    cosine, sine = rotation_tables(my_lengths.astype(jnp.float32), slots)
    my_lengths = jnp.broadcast_to(my_lengths[:, None], (own_rows, LANES))
    flat = (own_rows, key_cache.shape[1] * KV_HEADS, HEAD_DIM)
    (keys,) = load(key_cache.reshape(flat), after=rows)
    joined = stack(scatter_slots(pieces, 1))
    joined, keys = lax.optimization_barrier((joined, keys))
    (values,) = load(value_cache.reshape(flat), after=joined)
    parts, values = lax.optimization_barrier((exchange(joined, "inner")[::-1], values))
    shard = attend(my_lengths, cosine, sine, parts, keys, values, [], slots)

    cut = w_out.shape[0] // 2
    (out_upper,) = load(w_out, after=shard, spans=[(0, cut)])
    shards, out_upper = lax.optimization_barrier((exchange(shard, "inner"), out_upper))
    pieces = combine(shards, [w_gate], all_rows, slots)
    (out_lower,) = load(w_out, after=pieces[0], spans=[(cut, w_out.shape[0] - cut)])
    pieces, out_lower = lax.optimization_barrier((scatter_slots(pieces, 1)[::-1], out_lower))
    parts = scatter_slots(project_out(pieces[::-1], out_upper, out_lower, [w_up]), 0)

    tiles = w_gate.shape[1] // LANES
    first = (tiles + 1) // 2 * LANES
    one, updated, scaled = first_gate_up(
        rows, ffn_gain, parts, w_gate, w_up, [], first, own_rows
    )
    two = second_gate_up(scaled, w_gate, w_up, [], first)
    steps = steps_up(lax.axis_size("inner"))
    for step in steps[:-1]:
        one = pair_sum(one, swap_with(one, "inner", step))
        two = pair_sum(two, swap_with(two, "inner", step))
    token = hold(two, w_down)
    part, scale = first_down(one, swap_with(one, "inner", steps[-1]), w_down, token, first)
    pieces = second_down(two, swap_with(two, "inner", steps[-1]), w_down, part, scale, slots)
    parts = scatter_slots(pieces, 0)
    return finish(updated, parts)


def solution(mesh):
    in_specs = (
        P(("groups", "tensor"), "inner"),
        P("inner"),
        P("inner"),
        P("inner", "tensor"),
        P("inner", "tensor"),
        P("tensor", "inner"),
        P("inner", "tensor"),
        P("inner", "tensor"),
        P("tensor", "inner"),
        P(("groups", "tensor"), "inner", None, None),
        P(("groups", "tensor"), "inner", None, None),
        P("groups"),
    )
    out_specs = P(("groups", "tensor"), "inner")
    return jax.shard_map(local, mesh=mesh, in_specs=in_specs, out_specs=out_specs, check_vma=False)
```

```python
import functools
import math

import jax
import jax.numpy as jnp
from jax import lax
from jax.experimental import pallas as pl
from jax.experimental.pallas import tpu as pltpu
from jax.sharding import PartitionSpec as P

D = 8192
HEADS = 32
KV_HEADS = 4
HEAD_DIM = 128
GROUP = HEADS // KV_HEADS
LANES = 128
MIB = 2**20
COPIES = 4
STATS = 8

epsilon = 1e-05
rope_base = 500000.0

in_vmem = pl.BlockSpec(memory_space=pltpu.VMEM)
in_smem = pl.BlockSpec(memory_space=pltpu.SMEM)
in_place = pl.BlockSpec(memory_space=pl.ANY)


def swap_with(value, axis, step):
    count = lax.axis_size(axis)
    return lax.ppermute(value, axis, [(i, i ^ step) for i in range(count)])


def exchange(value, axis):
    count = lax.axis_size(axis)
    got = {k: swap_with(value, axis, k) for k in reversed(range(1, count))}
    return [value] + [got[k] for k in range(1, count)]


def scatter_slots(pieces, cross):
    count = lax.axis_size("tensor")
    width = lax.axis_size("inner")
    got = [pieces[0]]
    for k in range(1, count):
        pairs = [
            (t * width + i, (t ^ k) * width + (i ^ cross))
            for t in range(count)
            for i in range(width)
        ]
        got.append(lax.ppermute(pieces[k], ("tensor", "inner"), pairs))
    return got


def start_order(count):
    half = count // 2
    return [half] + [k for k in reversed(range(1, count)) if k != half] + [0]


def in_start_order(slots):
    return [slots[k] for k in start_order(len(slots))]


def in_slot_order(refs):
    order = start_order(len(refs))
    return [refs[order.index(k)] for k in range(len(refs))]


def steps_up(count):
    return [1 << n for n in range(count.bit_length() - 1)]


def params(mib):
    return pltpu.CompilerParams(vmem_limit_bytes=mib * MIB)


def resident(weight):
    return pltpu.with_memory_space_constraint(weight, pltpu.VMEM)


def in_hbm(weight):
    return pltpu.with_memory_space_constraint(weight, pltpu.HBM)


def product_cost(depth, columns):
    return pl.CostEstimate(
        flops=16 * depth * columns, bytes_accessed=2 * depth * columns, transcendentals=0
    )


def tile_of(columns):
    for tile in (1792, 1024, 896, 512, 256, 128):
        if columns % tile == 0:
            return tile
    return columns


def product_tiles(left, weight_ref, store, first=0, columns=None):
    columns = columns or weight_ref.shape[1]
    tile = tile_of(columns)

    @pl.loop(0, columns // tile)
    def _(step):
        start = pl.multiple_of(step * tile, tile)
        span = pl.ds(pl.multiple_of(first + start, math.gcd(first, tile)), tile)
        store(
            start,
            tile,
            jnp.dot(left, weight_ref[:, span], preferred_element_type=jnp.float32),
        )


def three_parts(value):
    high = value.astype(jnp.bfloat16).astype(jnp.float32)
    rest = value - high
    middle = rest.astype(jnp.bfloat16).astype(jnp.float32)
    return high, middle, rest - middle


def spread(parts, lanes, first):
    out = 0.0
    for n, part in enumerate(parts):
        out = out + jnp.where(lanes == first + n, part, 0.0)
    return out


def squares_block(total):
    lanes = lax.broadcasted_iota(jnp.int32, (total.shape[0], LANES), 1)
    return spread(three_parts(total), lanes, lax.axis_index("inner") * 4)


def copies_of(source, start, target, sems):
    size = target.shape[0]
    cuts = COPIES if len(target.shape) > 1 and size % (16 * COPIES) == 0 else 1
    each = size // cuts
    return [
        pltpu.make_async_copy(
            source.at[pl.ds(start + m * each, each)], target.at[pl.ds(m * each, each)], sems.at[m]
        )
        for m in range(cuts)
    ]


def load_kernel(spans, *refs):
    count = len(spans)
    outs = refs[count + 1 : 2 * count + 1]
    sems = refs[-1]
    copies = []
    for n, (start, _) in enumerate(spans):
        copies += copies_of(refs[n], start, outs[n], sems.at[n])
    for copy in copies:
        copy.start()
    for copy in copies:
        copy.wait()


def load(*arrays, after, spans=None):
    spans = spans or [(0, a.shape[0]) for a in arrays]
    shapes = [(size,) + a.shape[1:] for a, (_, size) in zip(arrays, spans)]
    return pl.pallas_call(
        functools.partial(load_kernel, spans),
        out_shape=tuple(pltpu.VMEM(shape, a.dtype) for shape, a in zip(shapes, arrays)),
        in_specs=[in_place] * (len(arrays) + 1),
        out_specs=tuple(in_vmem for _ in arrays),
        cost_estimate=pl.CostEstimate(
            flops=0, bytes_accessed=2 * sum(math.prod(shape) for shape in shapes), transcendentals=0
        ),
        scratch_shapes=[pltpu.SemaphoreType.DMA((len(arrays), COPIES))],
        compiler_params=params(1),
        name="load",
    )(*[in_hbm(a) for a in arrays], after)


def join_rows(refs, target):
    rows = refs[0].shape[0]
    for n, ref in enumerate(refs):
        target[n * rows : (n + 1) * rows, :] = ref[...].astype(jnp.float32)
    return target[...]


def part_rows(source, refs):
    rows = refs[0].shape[0]
    for n, ref in enumerate(refs):
        ref[...] = source[n * rows : (n + 1) * rows, :].astype(ref.dtype)


def qkv_kernel(slots, gain_ref, wq_ref, wkv_ref, *refs):
    rows_ref = refs[slots]
    out_s, rows_s = refs[-2:]
    wide = join_rows(in_slot_order(refs[:slots]), rows_s)
    rows_ref[...] = wide
    total = jnp.sum(wide * wide, axis=1, keepdims=True)
    gain = gain_ref[...].astype(jnp.float32)[None, :]
    scaled = (wide * gain).astype(jnp.bfloat16)
    query_cols = wq_ref.shape[1]
    kv_cols = wkv_ref.shape[1]

    def store_query(start, size, value):
        out_s[:, pl.ds(start, size)] = value

    product_tiles(scaled, wq_ref, store_query)
    out_s[:, query_cols : query_cols + kv_cols] = jnp.dot(
        scaled, wkv_ref[...], preferred_element_type=jnp.float32
    )
    out_s[:, query_cols + kv_cols :] = squares_block(total)
    part_rows(out_s, refs[slots + 1 : 2 * slots + 1])


def project_qkv(rows, gain, w_query, w_kv):
    slots = len(rows)
    own_rows, depth = rows[0].shape
    columns = w_query.shape[1] + w_kv.shape[1] + LANES
    return pl.pallas_call(
        functools.partial(qkv_kernel, slots),
        out_shape=(
            jax.ShapeDtypeStruct((own_rows * slots, depth), jnp.float32),
            *[jax.ShapeDtypeStruct((own_rows, columns), jnp.bfloat16)] * slots,
        ),
        in_specs=[in_vmem] * (3 + slots),
        out_specs=(in_vmem,) * (1 + slots),
        scratch_shapes=[
            pltpu.VMEM((own_rows * slots, columns), jnp.float32),
            pltpu.VMEM((own_rows * slots, depth), jnp.float32),
        ],
        compiler_params=params(2),
        name="project_qkv",
    )(gain, resident(w_query), resident(w_kv), *in_start_order(rows))


def stack_kernel(*refs):
    refs[-2][...] = join_rows(refs[:-2][::-1], refs[-1]).astype(refs[-2].dtype)


def stack(pieces):
    shape = (len(pieces) * pieces[0].shape[0], pieces[0].shape[1])
    return pl.pallas_call(
        stack_kernel,
        out_shape=jax.ShapeDtypeStruct(shape, pieces[0].dtype),
        in_specs=[in_vmem] * len(pieces),
        out_specs=in_vmem,
        scratch_shapes=[pltpu.VMEM(shape, jnp.float32)],
        compiler_params=params(1),
        name="stack",
    )(*pieces[::-1])


def attend_kernel(
    slots,
    shards,
    lengths_ref,
    cosine_ref,
    sine_ref,
    key_ref,
    value_ref,
    *refs,
):
    parts = refs[:shards]
    out_ref, query_s, kv_s, kv_wide_s, mixed_s, stats_s = refs[-6:]
    all_rows = parts[0].shape[0]
    own_rows = all_rows // slots
    here = HEADS // slots
    query_cols = here * HEAD_DIM
    kv_cols = 2 * KV_HEADS * HEAD_DIM // slots
    columns = query_cols + kv_cols
    tensor_index = lax.axis_index("tensor")
    inner_index = lax.axis_index("inner")
    positions = key_ref.shape[1] // KV_HEADS

    joined = functools.reduce(jnp.add, [ref[...].astype(jnp.float32) for ref in parts])
    squares = jnp.sum(joined[:, columns:], axis=1, keepdims=True)
    joined = joined[:, :columns] * lax.rsqrt(squares / D + epsilon)
    cosine = cosine_ref[...]
    sine = sine_ref[...]

    def rotate(block):
        count = block.shape[0]
        even = lax.broadcasted_iota(jnp.int32, block.shape, 1) % 2 == 0
        other = jnp.where(
            even, pltpu.roll(block, HEAD_DIM - 1, axis=1), pltpu.roll(block, 1, axis=1)
        )
        return block * cosine[:count] + other * sine[:count]

    for j in range(here):
        block = rotate(joined[:, j * HEAD_DIM : (j + 1) * HEAD_DIM])
        query_s[j * all_rows : (j + 1) * all_rows, :] = block
    for s in range(slots):
        kv_s[s] = joined[s * own_rows : (s + 1) * own_rows, query_cols:]
    for d in range(slots):
        kv_wide_s[:, d * kv_cols : (d + 1) * kv_cols] = kv_s[d ^ tensor_index]
    new_keys = []
    new_values = []
    for g in range(KV_HEADS):
        block = kv_wide_s[:, g * HEAD_DIM : (g + 1) * HEAD_DIM]
        new_keys.append(rotate(block).astype(jnp.bfloat16).astype(jnp.float32))
        block = kv_wide_s[:, (KV_HEADS + g) * HEAD_DIM : (KV_HEADS + g + 1) * HEAD_DIM]
        new_values.append(block.astype(jnp.bfloat16).astype(jnp.float32))

    score_scale = HEAD_DIM ** (-0.5)
    two_scale = score_scale * math.log2(math.e)
    row = lax.broadcasted_iota(jnp.int32, (HEADS, 1), 0)
    head = ((row % slots) ^ tensor_index) * here + row // slots
    kv_head = head // GROUP
    column = lax.broadcasted_iota(jnp.int32, (1, positions * KV_HEADS), 1)
    place = column // KV_HEADS + inner_index * positions
    column_head = column % KV_HEADS
    lanes = lax.broadcasted_iota(jnp.int32, (HEADS, LANES), 1)
    queries = [
        query_s[pl.ds(r, HEADS, stride=own_rows), :].astype(jnp.bfloat16) for r in range(own_rows)
    ]
    scores = [
        lax.dot_general(
            queries[r], key_ref[r], (((1,), (1,)), ((), ())), preferred_element_type=jnp.float32
        )
        for r in range(own_rows)
    ]
    weights = []
    mixtures = []
    for r in range(own_rows):
        used = jnp.where(place < lengths_ref[r : r + 1, 0:1], column_head, -1)
        masked = jnp.where(used == kv_head, scores[r], -1e30)
        key_rows = 0.0
        value_rows = 0.0
        for g in range(KV_HEADS):
            key_rows = key_rows + jnp.where(kv_head == g, new_keys[g][r : r + 1], 0.0)
            value_rows = value_rows + jnp.where(kv_head == g, new_values[g][r : r + 1], 0.0)
        new_score = jnp.sum(queries[r].astype(jnp.float32) * key_rows, axis=1, keepdims=True)
        new_score = jnp.where(inner_index == 0, new_score, -1e30)
        peak = jnp.maximum(jnp.max(masked, axis=1, keepdims=True), new_score)
        weight = jnp.exp2((masked - peak) * two_scale)
        new_weight = jnp.exp2((new_score - peak) * two_scale)
        peak = peak * score_scale
        totals = jnp.sum(weight, axis=1, keepdims=True) + new_weight
        weights.append(weight.astype(jnp.bfloat16))
        mixtures.append(new_weight.astype(jnp.bfloat16).astype(jnp.float32) * value_rows)
        stats_s[pl.ds(r, HEADS, stride=own_rows), :] = spread(
            three_parts(peak), lanes, 0
        ) + spread(three_parts(totals), lanes, 4)
    for r in range(own_rows):
        mixed_s[pl.ds(r, HEADS, stride=own_rows), :] = mixtures[r] + jnp.dot(
            weights[r], value_ref[r], preferred_element_type=jnp.float32
        )
    heads = own_rows * HEADS
    out_ref[:heads, :] = mixed_s[...].astype(jnp.bfloat16)
    packed = stats_s[:all_rows, :]
    for j in range(1, here):
        block = stats_s[j * all_rows : (j + 1) * all_rows, :]
        packed = packed + pltpu.roll(block, j * STATS, axis=1)
    spare = out_ref.shape[0] - heads - all_rows
    if spare:
        packed = jnp.concatenate([packed, jnp.zeros((spare, LANES), jnp.float32)], axis=0)
    out_ref[heads:, :] = packed.astype(jnp.bfloat16)


def attend(lengths, cosine, sine, parts, keys, values, later, slots):
    own_rows = parts[0].shape[0] // slots
    kv_cols = 2 * KV_HEADS * HEAD_DIM // slots
    return pl.pallas_call(
        functools.partial(attend_kernel, slots, len(parts)),
        out_shape=jax.ShapeDtypeStruct(
            (own_rows * HEADS + max(16, own_rows * slots), HEAD_DIM), jnp.bfloat16
        ),
        in_specs=[in_vmem] * (5 + len(parts)) + [in_place] * len(later),
        out_specs=in_vmem,
        scratch_shapes=[
            pltpu.VMEM((own_rows * HEADS, HEAD_DIM), jnp.float32),
            pltpu.VMEM((slots, own_rows, kv_cols), jnp.float32),
            pltpu.VMEM((own_rows, slots * kv_cols), jnp.float32),
            pltpu.VMEM((own_rows * HEADS, HEAD_DIM), jnp.float32),
            pltpu.VMEM((own_rows * HEADS, LANES), jnp.float32),
        ],
        compiler_params=params(6),
        name="attend",
    )(lengths, cosine, sine, resident(keys), resident(values), *parts[::-1], *[resident(w) for w in later])


def combine_kernel(shards, slots, *refs):
    out_s = refs[-1]
    all_rows, columns = out_s.shape
    here = columns // HEAD_DIM
    heads = here * all_rows
    mixtures = [ref[:heads, :].astype(jnp.float32) for ref in refs[:shards]]
    stats = [ref[heads:, :].astype(jnp.float32)[:all_rows] for ref in refs[:shards]]
    for j in range(here):

        def whole(block, first):
            lane = j * STATS + first
            return block[:, lane : lane + 1] + block[:, lane + 1 : lane + 2] + block[:, lane + 2 : lane + 3]

        peaks = [whole(block, 0) for block in stats]
        top = functools.reduce(jnp.maximum, peaks)
        mixed = 0.0
        denominator = 0.0
        for mixture, block, peak in zip(mixtures, stats, peaks):
            factor = jnp.exp(peak - top)
            mixed = mixed + factor * mixture[j * all_rows : (j + 1) * all_rows]
            denominator = denominator + factor * whole(block, 4)
        out_s[:, j * HEAD_DIM : (j + 1) * HEAD_DIM] = mixed / denominator
    part_rows(out_s, refs[-1 - slots : -1])


def combine(parts, later, all_rows, slots):
    count = len(parts)
    columns = HEADS // slots * HEAD_DIM
    return pl.pallas_call(
        functools.partial(combine_kernel, count, slots),
        out_shape=(jax.ShapeDtypeStruct((all_rows // slots, columns), jnp.bfloat16),) * slots,
        in_specs=[in_vmem] * count + [in_place] * len(later),
        out_specs=(in_vmem,) * slots,
        scratch_shapes=[pltpu.VMEM((all_rows, columns), jnp.float32)],
        compiler_params=params(2),
        name="combine",
    )(*parts[::-1], *[resident(w) for w in later])


def turned(block, step, own_rows):
    count = block.shape[0]
    span = step * own_rows
    row = lax.broadcasted_iota(jnp.int32, (count, 1), 0)
    return jnp.where(
        (row // span) % 2 == 0,
        pltpu.roll(block, count - span, axis=0),
        pltpu.roll(block, span, axis=0),
    )


def out_kernel(slots, later, upper_ref, lower_ref, *refs):
    pieces = refs[:slots][::-1]
    outs = refs[slots + later : 2 * slots + later]
    left_s = refs[-1]
    own_rows = pieces[0].shape[0]
    rows = left_s.shape[0]
    cut = upper_ref.shape[0]
    lefts = [join_rows(pieces, left_s)]
    for k in range(1, slots):
        low = k & -k
        lefts.append(turned(lefts[k ^ low], low, own_rows))
    left = jnp.concatenate(lefts, axis=0).astype(jnp.bfloat16)

    def store(start, size, value):
        span = pl.ds(start, size)
        value = value + jnp.dot(
            left[:, cut:], lower_ref[:, span], preferred_element_type=jnp.float32
        )
        for k, ref in enumerate(outs):
            ref[:, span] = value[k * rows : (k + 1) * rows].astype(jnp.bfloat16)

    product_tiles(left[:, :cut], upper_ref, store)


def project_out(pieces, upper, lower, later):
    slots = len(pieces)
    own_rows, depth = pieces[0].shape
    shape = jax.ShapeDtypeStruct((own_rows * slots, upper.shape[1]), jnp.bfloat16)
    return pl.pallas_call(
        functools.partial(out_kernel, slots, len(later)),
        out_shape=(shape,) * slots,
        in_specs=[in_vmem] * (2 + slots) + [in_place] * len(later),
        out_specs=(in_vmem,) * slots,
        scratch_shapes=[pltpu.VMEM((own_rows * slots, depth), jnp.float32)],
        compiler_params=params(3),
        name="project_out",
    )(resident(upper), resident(lower), *pieces[::-1], *[resident(w) for w in later])


def pair_kernel(first_ref, second_ref, out_ref):
    total = first_ref[...].astype(jnp.float32) + second_ref[...].astype(jnp.float32)
    out_ref[...] = total.astype(jnp.bfloat16)


def pair_sum(first, second):
    return pl.pallas_call(
        pair_kernel,
        out_shape=jax.ShapeDtypeStruct(first.shape, first.dtype),
        in_specs=[in_vmem] * 2,
        out_specs=in_vmem,
        compiler_params=params(2),
        name="pair_sum",
    )(first, second)


def gate_up_tiles(scaled, gate_ref, up_ref, out_ref, first, count):
    def store(offset):
        def place(start, size, value):
            start = pl.multiple_of(offset + start, math.gcd(offset, size))
            out_ref[:, pl.ds(start, size)] = value.astype(jnp.bfloat16)

        return place

    product_tiles(scaled, gate_ref, store(0), first, count)
    product_tiles(scaled, up_ref, store(count), first, count)


def first_gate_up_kernel(slots, count, rows_ref, gain_ref, gate_ref, up_ref, *refs):
    parts = refs[:slots]
    out_ref, updated_ref, scaled_ref = refs[-3:]
    own_rows = updated_ref.shape[0]
    total = functools.reduce(jnp.add, [ref[...].astype(jnp.float32) for ref in parts])
    updated = (rows_ref[...] + total).astype(jnp.bfloat16)
    wide = updated.astype(jnp.float32)
    updated_ref[...] = wide[:own_rows]
    squares = jnp.sum(wide * wide, axis=1, keepdims=True)
    out_ref[:, 2 * count :] = squares_block(squares).astype(jnp.bfloat16)
    scaled = (wide * gain_ref[...].astype(jnp.float32)[None, :]).astype(jnp.bfloat16)
    scaled_ref[...] = scaled
    gate_up_tiles(scaled, gate_ref, up_ref, out_ref, 0, count)


def first_gate_up(rows, gain, parts, w_gate, w_up, later, count, own_rows):
    slots = len(parts)
    return pl.pallas_call(
        functools.partial(first_gate_up_kernel, slots, count),
        out_shape=(
            jax.ShapeDtypeStruct((rows.shape[0], 2 * count + LANES), jnp.bfloat16),
            jax.ShapeDtypeStruct((own_rows, rows.shape[1]), jnp.float32),
            jax.ShapeDtypeStruct(rows.shape, jnp.bfloat16),
        ),
        in_specs=[in_vmem] * (4 + slots) + [in_place] * len(later),
        out_specs=(in_vmem,) * 3,
        compiler_params=params(3),
        cost_estimate=product_cost(w_gate.shape[0], 2 * count),
        name="first_gate_up",
    )(
        rows,
        gain,
        resident(w_gate),
        resident(w_up),
        *parts[::-1],
        *[resident(w) for w in later],
    )


def second_gate_up_kernel(first, count, scaled_ref, gate_ref, up_ref, *refs):
    out_ref = refs[-1]
    gate_up_tiles(scaled_ref[...], gate_ref, up_ref, out_ref, first, count)


def second_gate_up(scaled, w_gate, w_up, later, first):
    count = w_gate.shape[1] - first
    return pl.pallas_call(
        functools.partial(second_gate_up_kernel, first, count),
        out_shape=jax.ShapeDtypeStruct((scaled.shape[0], 2 * count), jnp.bfloat16),
        in_specs=[in_vmem] * 3 + [in_place] * len(later),
        out_specs=in_vmem,
        compiler_params=params(3),
        cost_estimate=product_cost(w_gate.shape[0], 2 * count),
        name="second_gate_up",
    )(scaled, resident(w_gate), resident(w_up), *[resident(w) for w in later])


def hidden_of(near_ref, far_ref, scale, count):
    def total(start):
        span = slice(start, start + count)
        return (near_ref[:, span].astype(jnp.float32) + far_ref[:, span].astype(jnp.float32)) * scale

    gate = total(0)
    return (gate / (1.0 + jnp.exp(-gate)) * total(count)).astype(jnp.bfloat16)


def first_down_kernel(count, near_ref, far_ref, weight_ref, token_ref, out_ref, scale_ref):
    del token_ref
    squares = jnp.sum(
        near_ref[:, 2 * count :].astype(jnp.float32) + far_ref[:, 2 * count :].astype(jnp.float32),
        axis=1,
        keepdims=True,
    )
    scale = lax.rsqrt(squares / D + epsilon)
    scale_ref[...] = jnp.broadcast_to(scale, scale_ref.shape)

    def store(start, size, value):
        out_ref[:, pl.ds(start, size)] = value

    product_tiles(hidden_of(near_ref, far_ref, scale, count), weight_ref.at[:count], store)


def first_down(near, far, weight, token, count):
    rows = near.shape[0]
    return pl.pallas_call(
        functools.partial(first_down_kernel, count),
        out_shape=(
            jax.ShapeDtypeStruct((rows, weight.shape[1]), jnp.float32),
            jax.ShapeDtypeStruct((rows, LANES), jnp.float32),
        ),
        in_specs=[in_vmem] * 3 + [in_place],
        out_specs=(in_vmem,) * 2,
        compiler_params=params(3),
        cost_estimate=product_cost(count, weight.shape[1]),
        name="first_down",
    )(near, far, resident(weight), token)


def second_down_kernel(count, near_ref, far_ref, weight_ref, part_ref, scale_ref, *refs):
    out_s = refs[-1]
    first = weight_ref.shape[0] - count

    def store(start, size, value):
        span = pl.ds(start, size)
        out_s[:, span] = part_ref[:, span] + value

    hidden = hidden_of(near_ref, far_ref, scale_ref[:, 0:1], count)
    product_tiles(hidden, weight_ref.at[first:], store)
    part_rows(out_s, refs[:-1])


def second_down(near, far, weight, part, scale, slots):
    rows, columns = part.shape
    count = near.shape[1] // 2
    return pl.pallas_call(
        functools.partial(second_down_kernel, count),
        out_shape=(jax.ShapeDtypeStruct((rows // slots, columns), jnp.bfloat16),) * slots,
        in_specs=[in_vmem] * 5,
        out_specs=(in_vmem,) * slots,
        scratch_shapes=[pltpu.VMEM(part.shape, jnp.float32)],
        compiler_params=params(3),
        name="second_down",
    )(near, far, resident(weight), part, scale)


def hold_kernel(after_ref, weight_ref, out_ref):
    del after_ref, weight_ref
    out_ref[...] = jnp.zeros_like(out_ref)


def hold(after, weight):
    return pl.pallas_call(
        hold_kernel,
        out_shape=jax.ShapeDtypeStruct((8, LANES), jnp.float32),
        in_specs=[in_place, in_place],
        out_specs=in_vmem,
        compiler_params=params(1),
        name="hold",
    )(after, resident(weight))


def finish_kernel(updated_ref, *refs):
    total = functools.reduce(jnp.add, [ref[...].astype(jnp.float32) for ref in refs[:-1]])
    refs[-1][...] = (updated_ref[...] + total).astype(jnp.bfloat16)


def finish(updated, parts):
    return pl.pallas_call(
        finish_kernel,
        out_shape=jax.ShapeDtypeStruct(updated.shape, jnp.bfloat16),
        in_specs=[in_vmem] * (1 + len(parts)),
        out_specs=in_vmem,
        compiler_params=params(1),
        name="finish",
    )(updated, *parts[::-1])


def rotation_tables(positions, repeats):
    inverse = jnp.exp(
        (jnp.arange(HEAD_DIM) // 2).astype(jnp.float32) * (-2.0 / HEAD_DIM) * math.log(rope_base)
    )
    angles = positions[:, None] * inverse[None, :]
    sign = jnp.where(jnp.arange(HEAD_DIM) % 2 == 0, -1.0, 1.0)
    return (
        jnp.tile(jnp.cos(angles), (repeats, 1)),
        jnp.tile(jnp.sin(angles) * sign[None, :], (repeats, 1)),
    )


def local(
    states,
    attn_gain,
    ffn_gain,
    w_query,
    w_kv,
    w_out,
    w_gate,
    w_up,
    w_down,
    key_cache,
    value_cache,
    lengths,
):
    tensor_index = lax.axis_index("tensor")
    slots = lax.axis_size("tensor")
    own_rows = states.shape[0]
    all_rows = own_rows * slots

    got = exchange(states, "tensor")
    own, attn_gain, ffn_gain, w_kv, w_query = load(
        states, attn_gain, ffn_gain, w_kv, w_query, after=states
    )
    rows, *pieces = project_qkv([own] + got[1:], attn_gain, w_query, w_kv)

    rows, lengths = lax.optimization_barrier((rows, lengths))
    my_lengths = lax.dynamic_slice_in_dim(lengths, tensor_index * own_rows, own_rows, 0)
    cosine, sine = rotation_tables(my_lengths.astype(jnp.float32), slots)
    my_lengths = jnp.broadcast_to(my_lengths[:, None], (own_rows, LANES))
    flat = (own_rows, key_cache.shape[1] * KV_HEADS, HEAD_DIM)
    (keys,) = load(key_cache.reshape(flat), after=rows)
    joined = stack(scatter_slots(pieces, 1))
    joined, keys = lax.optimization_barrier((joined, keys))
    (values,) = load(value_cache.reshape(flat), after=joined)
    parts, values = lax.optimization_barrier((exchange(joined, "inner")[::-1], values))
    shard = attend(my_lengths, cosine, sine, parts, keys, values, [], slots)

    cut = w_out.shape[0] // 2
    (out_upper,) = load(w_out, after=shard, spans=[(0, cut)])
    shards, out_upper = lax.optimization_barrier((exchange(shard, "inner"), out_upper))
    pieces = combine(shards, [w_gate], all_rows, slots)
    (out_lower,) = load(w_out, after=pieces[0], spans=[(cut, w_out.shape[0] - cut)])
    pieces, out_lower = lax.optimization_barrier((scatter_slots(pieces, 1)[::-1], out_lower))
    parts = scatter_slots(project_out(pieces[::-1], out_upper, out_lower, [w_up]), 0)

    tiles = w_gate.shape[1] // LANES
    first = (tiles + 1) // 2 * LANES
    one, updated, scaled = first_gate_up(
        rows, ffn_gain, parts, w_gate, w_up, [], first, own_rows
    )
    two = second_gate_up(scaled, w_gate, w_up, [], first)
    steps = steps_up(lax.axis_size("inner"))
    for step in steps[:-1]:
        one = pair_sum(one, swap_with(one, "inner", step))
        two = pair_sum(two, swap_with(two, "inner", step))
    token = hold(two, w_down)
    part, scale = first_down(one, swap_with(one, "inner", steps[-1]), w_down, token, first)
    pieces = second_down(two, swap_with(two, "inner", steps[-1]), w_down, part, scale, slots)
    parts = scatter_slots(pieces, 0)
    return finish(updated, parts)


def solution(mesh):
    in_specs = (
        P(("groups", "tensor"), "inner"),
        P("inner"),
        P("inner"),
        P("inner", "tensor"),
        P("inner", "tensor"),
        P("tensor", "inner"),
        P("inner", "tensor"),
        P("inner", "tensor"),
        P("tensor", "inner"),
        P(("groups", "tensor"), "inner", None, None),
        P(("groups", "tensor"), "inner", None, None),
        P("groups"),
    )
    out_specs = P(("groups", "tensor"), "inner")
    return jax.shard_map(local, mesh=mesh, in_specs=in_specs, out_specs=out_specs, check_vma=False)
```

```python
import functools
import math

import jax
import jax.numpy as jnp
from jax import lax
from jax.experimental import pallas as pl
from jax.experimental.pallas import tpu as pltpu
from jax.sharding import PartitionSpec as P

D = 8192
HEADS = 32
KV_HEADS = 4
HEAD_DIM = 128
GROUP = HEADS // KV_HEADS
LANES = 128
MIB = 2**20
COPIES = 4
STATS = 8

epsilon = 1e-05
rope_base = 500000.0

in_vmem = pl.BlockSpec(memory_space=pltpu.VMEM)
in_smem = pl.BlockSpec(memory_space=pltpu.SMEM)
in_place = pl.BlockSpec(memory_space=pl.ANY)


def swap_with(value, axis, step):
    count = lax.axis_size(axis)
    return lax.ppermute(value, axis, [(i, i ^ step) for i in range(count)])


def exchange(value, axis):
    count = lax.axis_size(axis)
    got = {k: swap_with(value, axis, k) for k in reversed(range(1, count))}
    return [value] + [got[k] for k in range(1, count)]


def scatter_slots(pieces, cross):
    count = lax.axis_size("tensor")
    width = lax.axis_size("inner")
    got = [pieces[0]]
    for k in range(1, count):
        pairs = [
            (t * width + i, (t ^ k) * width + (i ^ cross))
            for t in range(count)
            for i in range(width)
        ]
        got.append(lax.ppermute(pieces[k], ("tensor", "inner"), pairs))
    return got


def start_order(count):
    half = count // 2
    return [half] + [k for k in reversed(range(1, count)) if k != half] + [0]


def in_start_order(slots):
    return [slots[k] for k in start_order(len(slots))]


def in_slot_order(refs):
    order = start_order(len(refs))
    return [refs[order.index(k)] for k in range(len(refs))]


def steps_up(count):
    return [1 << n for n in range(count.bit_length() - 1)]


def params(mib):
    return pltpu.CompilerParams(vmem_limit_bytes=mib * MIB)


def resident(weight):
    return pltpu.with_memory_space_constraint(weight, pltpu.VMEM)


def in_hbm(weight):
    return pltpu.with_memory_space_constraint(weight, pltpu.HBM)


def product_cost(depth, columns):
    return pl.CostEstimate(
        flops=16 * depth * columns, bytes_accessed=2 * depth * columns, transcendentals=0
    )


def tile_of(columns):
    for tile in (1792, 1024, 896, 512, 256, 128):
        if columns % tile == 0:
            return tile
    return columns


def product_tiles(left, weight_ref, store, first=0, columns=None):
    columns = columns or weight_ref.shape[1]
    tile = tile_of(columns)

    @pl.loop(0, columns // tile)
    def _(step):
        start = pl.multiple_of(step * tile, tile)
        span = pl.ds(pl.multiple_of(first + start, math.gcd(first, tile)), tile)
        store(
            start,
            tile,
            jnp.dot(left, weight_ref[:, span], preferred_element_type=jnp.float32),
        )


def three_parts(value):
    high = value.astype(jnp.bfloat16).astype(jnp.float32)
    rest = value - high
    middle = rest.astype(jnp.bfloat16).astype(jnp.float32)
    return high, middle, rest - middle


def spread(parts, lanes, first):
    out = 0.0
    for n, part in enumerate(parts):
        out = out + jnp.where(lanes == first + n, part, 0.0)
    return out


def squares_block(total):
    lanes = lax.broadcasted_iota(jnp.int32, (total.shape[0], LANES), 1)
    return spread(three_parts(total), lanes, lax.axis_index("inner") * 4)


def copies_of(source, start, target, sems):
    size = target.shape[0]
    cuts = COPIES if len(target.shape) > 1 and size % (16 * COPIES) == 0 else 1
    each = size // cuts
    return [
        pltpu.make_async_copy(
            source.at[pl.ds(start + m * each, each)], target.at[pl.ds(m * each, each)], sems.at[m]
        )
        for m in range(cuts)
    ]


def load_kernel(spans, *refs):
    count = len(spans)
    outs = refs[count + 1 : 2 * count + 1]
    sems = refs[-1]
    copies = []
    for n, (start, _) in enumerate(spans):
        copies += copies_of(refs[n], start, outs[n], sems.at[n])
    for copy in copies:
        copy.start()
    for copy in copies:
        copy.wait()


def load(*arrays, after, spans=None):
    spans = spans or [(0, a.shape[0]) for a in arrays]
    shapes = [(size,) + a.shape[1:] for a, (_, size) in zip(arrays, spans)]
    return pl.pallas_call(
        functools.partial(load_kernel, spans),
        out_shape=tuple(pltpu.VMEM(shape, a.dtype) for shape, a in zip(shapes, arrays)),
        in_specs=[in_place] * (len(arrays) + 1),
        out_specs=tuple(in_vmem for _ in arrays),
        cost_estimate=pl.CostEstimate(
            flops=0, bytes_accessed=2 * sum(math.prod(shape) for shape in shapes), transcendentals=0
        ),
        scratch_shapes=[pltpu.SemaphoreType.DMA((len(arrays), COPIES))],
        compiler_params=params(1),
        name="load",
    )(*[in_hbm(a) for a in arrays], after)


def join_rows(refs, target):
    rows = refs[0].shape[0]
    for n, ref in enumerate(refs):
        target[n * rows : (n + 1) * rows, :] = ref[...].astype(jnp.float32)
    return target[...]


def part_rows(source, refs):
    rows = refs[0].shape[0]
    for n, ref in enumerate(refs):
        ref[...] = source[n * rows : (n + 1) * rows, :].astype(ref.dtype)


def qkv_kernel(slots, gain_ref, wq_ref, wkv_ref, *refs):
    rows_ref = refs[slots]
    out_s, rows_s = refs[-2:]
    wide = join_rows(in_slot_order(refs[:slots]), rows_s)
    rows_ref[...] = wide
    total = jnp.sum(wide * wide, axis=1, keepdims=True)
    gain = gain_ref[...].astype(jnp.float32)[None, :]
    scaled = (wide * gain).astype(jnp.bfloat16)
    query_cols = wq_ref.shape[1]
    kv_cols = wkv_ref.shape[1]

    def store_query(start, size, value):
        out_s[:, pl.ds(start, size)] = value

    product_tiles(scaled, wq_ref, store_query)
    out_s[:, query_cols : query_cols + kv_cols] = jnp.dot(
        scaled, wkv_ref[...], preferred_element_type=jnp.float32
    )
    out_s[:, query_cols + kv_cols :] = squares_block(total)
    part_rows(out_s, refs[slots + 1 : 2 * slots + 1])


def project_qkv(rows, gain, w_query, w_kv):
    slots = len(rows)
    own_rows, depth = rows[0].shape
    columns = w_query.shape[1] + w_kv.shape[1] + LANES
    return pl.pallas_call(
        functools.partial(qkv_kernel, slots),
        out_shape=(
            jax.ShapeDtypeStruct((own_rows * slots, depth), jnp.float32),
            *[jax.ShapeDtypeStruct((own_rows, columns), jnp.bfloat16)] * slots,
        ),
        in_specs=[in_vmem] * (3 + slots),
        out_specs=(in_vmem,) * (1 + slots),
        scratch_shapes=[
            pltpu.VMEM((own_rows * slots, columns), jnp.float32),
            pltpu.VMEM((own_rows * slots, depth), jnp.float32),
        ],
        compiler_params=params(2),
        name="project_qkv",
    )(gain, resident(w_query), resident(w_kv), *in_start_order(rows))


def stack_kernel(*refs):
    refs[-2][...] = join_rows(refs[:-2][::-1], refs[-1]).astype(refs[-2].dtype)


def stack(pieces):
    shape = (len(pieces) * pieces[0].shape[0], pieces[0].shape[1])
    return pl.pallas_call(
        stack_kernel,
        out_shape=jax.ShapeDtypeStruct(shape, pieces[0].dtype),
        in_specs=[in_vmem] * len(pieces),
        out_specs=in_vmem,
        scratch_shapes=[pltpu.VMEM(shape, jnp.float32)],
        compiler_params=params(1),
        name="stack",
    )(*pieces[::-1])


def attend_kernel(
    slots,
    shards,
    lengths_ref,
    cosine_ref,
    sine_ref,
    key_ref,
    value_ref,
    *refs,
):
    parts = refs[:shards]
    out_ref, query_s, kv_s, kv_wide_s, mixed_s, stats_s = refs[-6:]
    all_rows = parts[0].shape[0]
    own_rows = all_rows // slots
    here = HEADS // slots
    query_cols = here * HEAD_DIM
    kv_cols = 2 * KV_HEADS * HEAD_DIM // slots
    columns = query_cols + kv_cols
    tensor_index = lax.axis_index("tensor")
    inner_index = lax.axis_index("inner")
    positions = key_ref.shape[1] // KV_HEADS

    joined = functools.reduce(jnp.add, [ref[...].astype(jnp.float32) for ref in parts])
    squares = jnp.sum(joined[:, columns:], axis=1, keepdims=True)
    joined = joined[:, :columns] * lax.rsqrt(squares / D + epsilon)
    cosine = cosine_ref[...]
    sine = sine_ref[...]

    def rotate(block):
        count = block.shape[0]
        even = lax.broadcasted_iota(jnp.int32, block.shape, 1) % 2 == 0
        other = jnp.where(
            even, pltpu.roll(block, HEAD_DIM - 1, axis=1), pltpu.roll(block, 1, axis=1)
        )
        return block * cosine[:count] + other * sine[:count]

    for j in range(here):
        block = rotate(joined[:, j * HEAD_DIM : (j + 1) * HEAD_DIM])
        query_s[j * all_rows : (j + 1) * all_rows, :] = block
    for s in range(slots):
        kv_s[s] = joined[s * own_rows : (s + 1) * own_rows, query_cols:]
    for d in range(slots):
        kv_wide_s[:, d * kv_cols : (d + 1) * kv_cols] = kv_s[d ^ tensor_index]
    new_keys = []
    new_values = []
    for g in range(KV_HEADS):
        block = kv_wide_s[:, g * HEAD_DIM : (g + 1) * HEAD_DIM]
        new_keys.append(rotate(block).astype(jnp.bfloat16).astype(jnp.float32))
        block = kv_wide_s[:, (KV_HEADS + g) * HEAD_DIM : (KV_HEADS + g + 1) * HEAD_DIM]
        new_values.append(block.astype(jnp.bfloat16).astype(jnp.float32))

    score_scale = HEAD_DIM ** (-0.5)
    two_scale = score_scale * math.log2(math.e)
    row = lax.broadcasted_iota(jnp.int32, (HEADS, 1), 0)
    head = ((row % slots) ^ tensor_index) * here + row // slots
    kv_head = head // GROUP
    column = lax.broadcasted_iota(jnp.int32, (1, positions * KV_HEADS), 1)
    place = column // KV_HEADS + inner_index * positions
    column_head = column % KV_HEADS
    lanes = lax.broadcasted_iota(jnp.int32, (HEADS, LANES), 1)
    queries = [
        query_s[pl.ds(r, HEADS, stride=own_rows), :].astype(jnp.bfloat16) for r in range(own_rows)
    ]
    scores = [
        lax.dot_general(
            queries[r], key_ref[r], (((1,), (1,)), ((), ())), preferred_element_type=jnp.float32
        )
        for r in range(own_rows)
    ]
    weights = []
    mixtures = []
    for r in range(own_rows):
        used = jnp.where(place < lengths_ref[r : r + 1, 0:1], column_head, -1)
        masked = jnp.where(used == kv_head, scores[r], -1e30)
        key_rows = 0.0
        value_rows = 0.0
        for g in range(KV_HEADS):
            key_rows = key_rows + jnp.where(kv_head == g, new_keys[g][r : r + 1], 0.0)
            value_rows = value_rows + jnp.where(kv_head == g, new_values[g][r : r + 1], 0.0)
        new_score = jnp.sum(queries[r].astype(jnp.float32) * key_rows, axis=1, keepdims=True)
        new_score = jnp.where(inner_index == 0, new_score, -1e30)
        peak = jnp.maximum(jnp.max(masked, axis=1, keepdims=True), new_score)
        weight = jnp.exp2((masked - peak) * two_scale)
        new_weight = jnp.exp2((new_score - peak) * two_scale)
        peak = peak * score_scale
        totals = jnp.sum(weight, axis=1, keepdims=True) + new_weight
        weights.append(weight.astype(jnp.bfloat16))
        mixtures.append(new_weight.astype(jnp.bfloat16).astype(jnp.float32) * value_rows)
        stats_s[pl.ds(r, HEADS, stride=own_rows), :] = spread(
            three_parts(peak), lanes, 0
        ) + spread(three_parts(totals), lanes, 4)
    for r in range(own_rows):
        mixed_s[pl.ds(r, HEADS, stride=own_rows), :] = mixtures[r] + jnp.dot(
            weights[r], value_ref[r], preferred_element_type=jnp.float32
        )
    heads = own_rows * HEADS
    out_ref[:heads, :] = mixed_s[...].astype(jnp.bfloat16)
    packed = stats_s[:all_rows, :]
    for j in range(1, here):
        block = stats_s[j * all_rows : (j + 1) * all_rows, :]
        packed = packed + pltpu.roll(block, j * STATS, axis=1)
    spare = out_ref.shape[0] - heads - all_rows
    if spare:
        packed = jnp.concatenate([packed, jnp.zeros((spare, LANES), jnp.float32)], axis=0)
    out_ref[heads:, :] = packed.astype(jnp.bfloat16)


def attend(lengths, cosine, sine, parts, keys, values, later, slots):
    own_rows = parts[0].shape[0] // slots
    kv_cols = 2 * KV_HEADS * HEAD_DIM // slots
    return pl.pallas_call(
        functools.partial(attend_kernel, slots, len(parts)),
        out_shape=jax.ShapeDtypeStruct(
            (own_rows * HEADS + max(16, own_rows * slots), HEAD_DIM), jnp.bfloat16
        ),
        in_specs=[in_vmem] * (5 + len(parts)) + [in_place] * len(later),
        out_specs=in_vmem,
        scratch_shapes=[
            pltpu.VMEM((own_rows * HEADS, HEAD_DIM), jnp.float32),
            pltpu.VMEM((slots, own_rows, kv_cols), jnp.float32),
            pltpu.VMEM((own_rows, slots * kv_cols), jnp.float32),
            pltpu.VMEM((own_rows * HEADS, HEAD_DIM), jnp.float32),
            pltpu.VMEM((own_rows * HEADS, LANES), jnp.float32),
        ],
        compiler_params=params(6),
        name="attend",
    )(lengths, cosine, sine, resident(keys), resident(values), *parts[::-1], *[resident(w) for w in later])


def combine_kernel(shards, slots, *refs):
    out_s = refs[-1]
    all_rows, columns = out_s.shape
    here = columns // HEAD_DIM
    heads = here * all_rows
    mixtures = [ref[:heads, :].astype(jnp.float32) for ref in refs[:shards]]
    stats = [ref[heads:, :].astype(jnp.float32)[:all_rows] for ref in refs[:shards]]
    for j in range(here):

        def whole(block, first):
            lane = j * STATS + first
            return block[:, lane : lane + 1] + block[:, lane + 1 : lane + 2] + block[:, lane + 2 : lane + 3]

        peaks = [whole(block, 0) for block in stats]
        top = functools.reduce(jnp.maximum, peaks)
        mixed = 0.0
        denominator = 0.0
        for mixture, block, peak in zip(mixtures, stats, peaks):
            factor = jnp.exp(peak - top)
            mixed = mixed + factor * mixture[j * all_rows : (j + 1) * all_rows]
            denominator = denominator + factor * whole(block, 4)
        out_s[:, j * HEAD_DIM : (j + 1) * HEAD_DIM] = mixed / denominator
    part_rows(out_s, refs[-1 - slots : -1])


def combine(parts, later, all_rows, slots):
    count = len(parts)
    columns = HEADS // slots * HEAD_DIM
    return pl.pallas_call(
        functools.partial(combine_kernel, count, slots),
        out_shape=(jax.ShapeDtypeStruct((all_rows // slots, columns), jnp.bfloat16),) * slots,
        in_specs=[in_vmem] * count + [in_place] * len(later),
        out_specs=(in_vmem,) * slots,
        scratch_shapes=[pltpu.VMEM((all_rows, columns), jnp.float32)],
        compiler_params=params(2),
        name="combine",
    )(*parts[::-1], *[resident(w) for w in later])


def turned(block, step, own_rows):
    count = block.shape[0]
    span = step * own_rows
    row = lax.broadcasted_iota(jnp.int32, (count, 1), 0)
    return jnp.where(
        (row // span) % 2 == 0,
        pltpu.roll(block, count - span, axis=0),
        pltpu.roll(block, span, axis=0),
    )


def out_kernel(slots, later, upper_ref, lower_ref, *refs):
    pieces = in_slot_order(refs[:slots])
    outs = refs[slots + later : 2 * slots + later]
    left_s = refs[-1]
    own_rows = pieces[0].shape[0]
    rows = left_s.shape[0]
    cut = upper_ref.shape[0]
    lefts = [join_rows(pieces, left_s)]
    for k in range(1, slots):
        low = k & -k
        lefts.append(turned(lefts[k ^ low], low, own_rows))
    left = jnp.concatenate(lefts, axis=0).astype(jnp.bfloat16)

    def store(start, size, value):
        span = pl.ds(start, size)
        value = value + jnp.dot(
            left[:, cut:], lower_ref[:, span], preferred_element_type=jnp.float32
        )
        for k, ref in enumerate(outs):
            ref[:, span] = value[k * rows : (k + 1) * rows].astype(jnp.bfloat16)

    product_tiles(left[:, :cut], upper_ref, store)


def project_out(pieces, upper, lower, later):
    slots = len(pieces)
    own_rows, depth = pieces[0].shape
    shape = jax.ShapeDtypeStruct((own_rows * slots, upper.shape[1]), jnp.bfloat16)
    return pl.pallas_call(
        functools.partial(out_kernel, slots, len(later)),
        out_shape=(shape,) * slots,
        in_specs=[in_vmem] * (2 + slots) + [in_place] * len(later),
        out_specs=(in_vmem,) * slots,
        scratch_shapes=[pltpu.VMEM((own_rows * slots, depth), jnp.float32)],
        compiler_params=params(3),
        name="project_out",
    )(
        resident(upper),
        resident(lower),
        *in_start_order(pieces),
        *[resident(w) for w in later],
    )


def pair_kernel(first_ref, second_ref, out_ref):
    total = first_ref[...].astype(jnp.float32) + second_ref[...].astype(jnp.float32)
    out_ref[...] = total.astype(jnp.bfloat16)


def pair_sum(first, second):
    return pl.pallas_call(
        pair_kernel,
        out_shape=jax.ShapeDtypeStruct(first.shape, first.dtype),
        in_specs=[in_vmem] * 2,
        out_specs=in_vmem,
        compiler_params=params(2),
        name="pair_sum",
    )(first, second)


def gate_up_tiles(scaled, gate_ref, up_ref, out_ref, first, count):
    def store(offset):
        def place(start, size, value):
            start = pl.multiple_of(offset + start, math.gcd(offset, size))
            out_ref[:, pl.ds(start, size)] = value.astype(jnp.bfloat16)

        return place

    product_tiles(scaled, gate_ref, store(0), first, count)
    product_tiles(scaled, up_ref, store(count), first, count)


def first_gate_up_kernel(slots, count, rows_ref, gain_ref, gate_ref, up_ref, *refs):
    parts = refs[:slots]
    out_ref, updated_ref, scaled_ref = refs[-3:]
    own_rows = updated_ref.shape[0]
    total = functools.reduce(jnp.add, [ref[...].astype(jnp.float32) for ref in parts])
    updated = (rows_ref[...] + total).astype(jnp.bfloat16)
    wide = updated.astype(jnp.float32)
    updated_ref[...] = wide[:own_rows]
    squares = jnp.sum(wide * wide, axis=1, keepdims=True)
    out_ref[:, 2 * count :] = squares_block(squares).astype(jnp.bfloat16)
    scaled = (wide * gain_ref[...].astype(jnp.float32)[None, :]).astype(jnp.bfloat16)
    scaled_ref[...] = scaled
    gate_up_tiles(scaled, gate_ref, up_ref, out_ref, 0, count)


def first_gate_up(rows, gain, parts, w_gate, w_up, later, count, own_rows):
    slots = len(parts)
    return pl.pallas_call(
        functools.partial(first_gate_up_kernel, slots, count),
        out_shape=(
            jax.ShapeDtypeStruct((rows.shape[0], 2 * count + LANES), jnp.bfloat16),
            jax.ShapeDtypeStruct((own_rows, rows.shape[1]), jnp.float32),
            jax.ShapeDtypeStruct(rows.shape, jnp.bfloat16),
        ),
        in_specs=[in_vmem] * (4 + slots) + [in_place] * len(later),
        out_specs=(in_vmem,) * 3,
        compiler_params=params(3),
        cost_estimate=product_cost(w_gate.shape[0], 2 * count),
        name="first_gate_up",
    )(
        rows,
        gain,
        resident(w_gate),
        resident(w_up),
        *parts[::-1],
        *[resident(w) for w in later],
    )


def second_gate_up_kernel(first, count, scaled_ref, gate_ref, up_ref, *refs):
    out_ref = refs[-1]
    gate_up_tiles(scaled_ref[...], gate_ref, up_ref, out_ref, first, count)


def second_gate_up(scaled, w_gate, w_up, later, first):
    count = w_gate.shape[1] - first
    return pl.pallas_call(
        functools.partial(second_gate_up_kernel, first, count),
        out_shape=jax.ShapeDtypeStruct((scaled.shape[0], 2 * count), jnp.bfloat16),
        in_specs=[in_vmem] * 3 + [in_place] * len(later),
        out_specs=in_vmem,
        compiler_params=params(3),
        cost_estimate=product_cost(w_gate.shape[0], 2 * count),
        name="second_gate_up",
    )(scaled, resident(w_gate), resident(w_up), *[resident(w) for w in later])


def hidden_of(near_ref, far_ref, scale, count):
    def total(start):
        span = slice(start, start + count)
        return (near_ref[:, span].astype(jnp.float32) + far_ref[:, span].astype(jnp.float32)) * scale

    gate = total(0)
    return (gate / (1.0 + jnp.exp(-gate)) * total(count)).astype(jnp.bfloat16)


def first_down_kernel(count, near_ref, far_ref, weight_ref, token_ref, out_ref, scale_ref):
    del token_ref
    squares = jnp.sum(
        near_ref[:, 2 * count :].astype(jnp.float32) + far_ref[:, 2 * count :].astype(jnp.float32),
        axis=1,
        keepdims=True,
    )
    scale = lax.rsqrt(squares / D + epsilon)
    scale_ref[...] = jnp.broadcast_to(scale, scale_ref.shape)

    def store(start, size, value):
        out_ref[:, pl.ds(start, size)] = value

    product_tiles(hidden_of(near_ref, far_ref, scale, count), weight_ref.at[:count], store)


def first_down(near, far, weight, token, count):
    rows = near.shape[0]
    return pl.pallas_call(
        functools.partial(first_down_kernel, count),
        out_shape=(
            jax.ShapeDtypeStruct((rows, weight.shape[1]), jnp.float32),
            jax.ShapeDtypeStruct((rows, LANES), jnp.float32),
        ),
        in_specs=[in_vmem] * 3 + [in_place],
        out_specs=(in_vmem,) * 2,
        compiler_params=params(3),
        cost_estimate=product_cost(count, weight.shape[1]),
        name="first_down",
    )(near, far, resident(weight), token)


def second_down_kernel(count, near_ref, far_ref, weight_ref, part_ref, scale_ref, *refs):
    out_s = refs[-1]
    first = weight_ref.shape[0] - count

    def store(start, size, value):
        span = pl.ds(start, size)
        out_s[:, span] = part_ref[:, span] + value

    hidden = hidden_of(near_ref, far_ref, scale_ref[:, 0:1], count)
    product_tiles(hidden, weight_ref.at[first:], store)
    part_rows(out_s, refs[:-1])


def second_down(near, far, weight, part, scale, slots):
    rows, columns = part.shape
    count = near.shape[1] // 2
    return pl.pallas_call(
        functools.partial(second_down_kernel, count),
        out_shape=(jax.ShapeDtypeStruct((rows // slots, columns), jnp.bfloat16),) * slots,
        in_specs=[in_vmem] * 5,
        out_specs=(in_vmem,) * slots,
        scratch_shapes=[pltpu.VMEM(part.shape, jnp.float32)],
        compiler_params=params(3),
        name="second_down",
    )(near, far, resident(weight), part, scale)


def hold_kernel(after_ref, weight_ref, out_ref):
    del after_ref, weight_ref
    out_ref[...] = jnp.zeros_like(out_ref)


def hold(after, weight):
    return pl.pallas_call(
        hold_kernel,
        out_shape=jax.ShapeDtypeStruct((8, LANES), jnp.float32),
        in_specs=[in_place, in_place],
        out_specs=in_vmem,
        compiler_params=params(1),
        name="hold",
    )(after, resident(weight))


def finish_kernel(updated_ref, *refs):
    total = functools.reduce(jnp.add, [ref[...].astype(jnp.float32) for ref in refs[:-1]])
    refs[-1][...] = (updated_ref[...] + total).astype(jnp.bfloat16)


def finish(updated, parts):
    return pl.pallas_call(
        finish_kernel,
        out_shape=jax.ShapeDtypeStruct(updated.shape, jnp.bfloat16),
        in_specs=[in_vmem] * (1 + len(parts)),
        out_specs=in_vmem,
        compiler_params=params(1),
        name="finish",
    )(updated, *parts[::-1])


def rotation_tables(positions, repeats):
    inverse = jnp.exp(
        (jnp.arange(HEAD_DIM) // 2).astype(jnp.float32) * (-2.0 / HEAD_DIM) * math.log(rope_base)
    )
    angles = positions[:, None] * inverse[None, :]
    sign = jnp.where(jnp.arange(HEAD_DIM) % 2 == 0, -1.0, 1.0)
    return (
        jnp.tile(jnp.cos(angles), (repeats, 1)),
        jnp.tile(jnp.sin(angles) * sign[None, :], (repeats, 1)),
    )


def local(
    states,
    attn_gain,
    ffn_gain,
    w_query,
    w_kv,
    w_out,
    w_gate,
    w_up,
    w_down,
    key_cache,
    value_cache,
    lengths,
):
    tensor_index = lax.axis_index("tensor")
    slots = lax.axis_size("tensor")
    own_rows = states.shape[0]
    all_rows = own_rows * slots

    got = exchange(states, "tensor")
    own, attn_gain, ffn_gain, w_kv, w_query = load(
        states, attn_gain, ffn_gain, w_kv, w_query, after=states
    )
    rows, *pieces = project_qkv([own] + got[1:], attn_gain, w_query, w_kv)

    rows, lengths = lax.optimization_barrier((rows, lengths))
    my_lengths = lax.dynamic_slice_in_dim(lengths, tensor_index * own_rows, own_rows, 0)
    cosine, sine = rotation_tables(my_lengths.astype(jnp.float32), slots)
    my_lengths = jnp.broadcast_to(my_lengths[:, None], (own_rows, LANES))
    flat = (own_rows, key_cache.shape[1] * KV_HEADS, HEAD_DIM)
    (keys,) = load(key_cache.reshape(flat), after=rows)
    joined = stack(scatter_slots(pieces, 1))
    joined, keys = lax.optimization_barrier((joined, keys))
    (values,) = load(value_cache.reshape(flat), after=joined)
    parts, values = lax.optimization_barrier((exchange(joined, "inner")[::-1], values))
    shard = attend(my_lengths, cosine, sine, parts, keys, values, [], slots)

    cut = w_out.shape[0] // 2
    (out_upper,) = load(w_out, after=shard, spans=[(0, cut)])
    shards, out_upper = lax.optimization_barrier((exchange(shard, "inner"), out_upper))
    pieces = combine(shards, [w_gate], all_rows, slots)
    (out_lower,) = load(w_out, after=pieces[0], spans=[(cut, w_out.shape[0] - cut)])
    pieces, out_lower = lax.optimization_barrier(
        (in_start_order(scatter_slots(pieces, 1)), out_lower)
    )
    parts = scatter_slots(
        project_out(in_slot_order(pieces), out_upper, out_lower, [w_up]), 0
    )

    tiles = w_gate.shape[1] // LANES
    first = (tiles + 1) // 2 * LANES
    one, updated, scaled = first_gate_up(
        rows, ffn_gain, parts, w_gate, w_up, [], first, own_rows
    )
    two = second_gate_up(scaled, w_gate, w_up, [], first)
    steps = steps_up(lax.axis_size("inner"))
    for step in steps[:-1]:
        one = pair_sum(one, swap_with(one, "inner", step))
        two = pair_sum(two, swap_with(two, "inner", step))
    token = hold(two, w_down)
    part, scale = first_down(one, swap_with(one, "inner", steps[-1]), w_down, token, first)
    pieces = second_down(two, swap_with(two, "inner", steps[-1]), w_down, part, scale, slots)
    parts = scatter_slots(pieces, 0)
    return finish(updated, parts)


def solution(mesh):
    in_specs = (
        P(("groups", "tensor"), "inner"),
        P("inner"),
        P("inner"),
        P("inner", "tensor"),
        P("inner", "tensor"),
        P("tensor", "inner"),
        P("inner", "tensor"),
        P("inner", "tensor"),
        P("tensor", "inner"),
        P(("groups", "tensor"), "inner", None, None),
        P(("groups", "tensor"), "inner", None, None),
        P("groups"),
    )
    out_specs = P(("groups", "tensor"), "inner")
    return jax.shard_map(local, mesh=mesh, in_specs=in_specs, out_specs=out_specs, check_vma=False)
```

```python
import functools
import math

import jax
import jax.numpy as jnp
from jax import lax
from jax.experimental import pallas as pl
from jax.experimental.pallas import tpu as pltpu
from jax.sharding import PartitionSpec as P

D = 8192
HEADS = 32
KV_HEADS = 4
HEAD_DIM = 128
GROUP = HEADS // KV_HEADS
LANES = 128
MIB = 2**20
COPIES = 4
STATS = 8

epsilon = 1e-05
rope_base = 500000.0

in_vmem = pl.BlockSpec(memory_space=pltpu.VMEM)
in_smem = pl.BlockSpec(memory_space=pltpu.SMEM)
in_place = pl.BlockSpec(memory_space=pl.ANY)


def swap_with(value, axis, step):
    count = lax.axis_size(axis)
    return lax.ppermute(value, axis, [(i, i ^ step) for i in range(count)])


def exchange(value, axis):
    count = lax.axis_size(axis)
    got = {k: swap_with(value, axis, k) for k in reversed(range(1, count))}
    return [value] + [got[k] for k in range(1, count)]


def scatter_slots(pieces, cross):
    count = lax.axis_size("tensor")
    width = lax.axis_size("inner")
    got = [pieces[0]]
    for k in range(1, count):
        pairs = [
            (t * width + i, (t ^ k) * width + (i ^ cross))
            for t in range(count)
            for i in range(width)
        ]
        got.append(lax.ppermute(pieces[k], ("tensor", "inner"), pairs))
    return got


def start_order(count):
    half = count // 2
    return [half] + [k for k in reversed(range(1, count)) if k != half] + [0]


def in_start_order(slots):
    return [slots[k] for k in start_order(len(slots))]


def in_slot_order(refs):
    order = start_order(len(refs))
    return [refs[order.index(k)] for k in range(len(refs))]


def steps_up(count):
    return [1 << n for n in range(count.bit_length() - 1)]


def params(mib):
    return pltpu.CompilerParams(vmem_limit_bytes=mib * MIB)


def resident(weight):
    return pltpu.with_memory_space_constraint(weight, pltpu.VMEM)


def in_hbm(weight):
    return pltpu.with_memory_space_constraint(weight, pltpu.HBM)


def product_cost(depth, columns):
    return pl.CostEstimate(
        flops=16 * depth * columns, bytes_accessed=2 * depth * columns, transcendentals=0
    )


def tile_of(columns):
    for tile in (2048, 1792, 1024, 896, 512, 256, 128):
        if columns % tile == 0:
            return tile
    return columns


def product_tiles(left, weight_ref, store, first=0, columns=None):
    columns = columns or weight_ref.shape[1]
    tile = tile_of(columns)

    @pl.loop(0, columns // tile)
    def _(step):
        start = pl.multiple_of(step * tile, tile)
        span = pl.ds(pl.multiple_of(first + start, math.gcd(first, tile)), tile)
        store(
            start,
            tile,
            jnp.dot(left, weight_ref[:, span], preferred_element_type=jnp.float32),
        )


def three_parts(value):
    high = value.astype(jnp.bfloat16).astype(jnp.float32)
    rest = value - high
    middle = rest.astype(jnp.bfloat16).astype(jnp.float32)
    return high, middle, rest - middle


def spread(parts, lanes, first):
    out = 0.0
    for n, part in enumerate(parts):
        out = out + jnp.where(lanes == first + n, part, 0.0)
    return out


def squares_block(total):
    lanes = lax.broadcasted_iota(jnp.int32, (total.shape[0], LANES), 1)
    return spread(three_parts(total), lanes, lax.axis_index("inner") * 4)


def copies_of(source, start, target, sems):
    size = target.shape[0]
    cuts = COPIES if len(target.shape) > 1 and size % (16 * COPIES) == 0 else 1
    each = size // cuts
    return [
        pltpu.make_async_copy(
            source.at[pl.ds(start + m * each, each)], target.at[pl.ds(m * each, each)], sems.at[m]
        )
        for m in range(cuts)
    ]


def load_kernel(spans, *refs):
    count = len(spans)
    outs = refs[count + 1 : 2 * count + 1]
    sems = refs[-1]
    copies = []
    for n, (start, _) in enumerate(spans):
        copies += copies_of(refs[n], start, outs[n], sems.at[n])
    for copy in copies:
        copy.start()
    for copy in copies:
        copy.wait()


def load(*arrays, after, spans=None):
    spans = spans or [(0, a.shape[0]) for a in arrays]
    shapes = [(size,) + a.shape[1:] for a, (_, size) in zip(arrays, spans)]
    return pl.pallas_call(
        functools.partial(load_kernel, spans),
        out_shape=tuple(pltpu.VMEM(shape, a.dtype) for shape, a in zip(shapes, arrays)),
        in_specs=[in_place] * (len(arrays) + 1),
        out_specs=tuple(in_vmem for _ in arrays),
        cost_estimate=pl.CostEstimate(
            flops=0, bytes_accessed=2 * sum(math.prod(shape) for shape in shapes), transcendentals=0
        ),
        scratch_shapes=[pltpu.SemaphoreType.DMA((len(arrays), COPIES))],
        compiler_params=params(1),
        name="load",
    )(*[in_hbm(a) for a in arrays], after)


def join_rows(refs, target):
    rows = refs[0].shape[0]
    for n, ref in enumerate(refs):
        target[n * rows : (n + 1) * rows, :] = ref[...].astype(jnp.float32)
    return target[...]


def part_rows(source, refs):
    rows = refs[0].shape[0]
    for n, ref in enumerate(refs):
        ref[...] = source[n * rows : (n + 1) * rows, :].astype(ref.dtype)


def qkv_kernel(slots, gain_ref, wq_ref, wkv_ref, *refs):
    rows_ref = refs[slots]
    out_s, rows_s = refs[-2:]
    wide = join_rows(in_slot_order(refs[:slots]), rows_s)
    rows_ref[...] = wide
    total = jnp.sum(wide * wide, axis=1, keepdims=True)
    gain = gain_ref[...].astype(jnp.float32)[None, :]
    scaled = (wide * gain).astype(jnp.bfloat16)
    query_cols = wq_ref.shape[1]
    kv_cols = wkv_ref.shape[1]

    def store_query(start, size, value):
        out_s[:, pl.ds(start, size)] = value

    product_tiles(scaled, wq_ref, store_query)
    out_s[:, query_cols : query_cols + kv_cols] = jnp.dot(
        scaled, wkv_ref[...], preferred_element_type=jnp.float32
    )
    out_s[:, query_cols + kv_cols :] = squares_block(total)
    part_rows(out_s, refs[slots + 1 : 2 * slots + 1])


def project_qkv(rows, gain, w_query, w_kv):
    slots = len(rows)
    own_rows, depth = rows[0].shape
    columns = w_query.shape[1] + w_kv.shape[1] + LANES
    return pl.pallas_call(
        functools.partial(qkv_kernel, slots),
        out_shape=(
            jax.ShapeDtypeStruct((own_rows * slots, depth), jnp.float32),
            *[jax.ShapeDtypeStruct((own_rows, columns), jnp.bfloat16)] * slots,
        ),
        in_specs=[in_vmem] * (3 + slots),
        out_specs=(in_vmem,) * (1 + slots),
        scratch_shapes=[
            pltpu.VMEM((own_rows * slots, columns), jnp.float32),
            pltpu.VMEM((own_rows * slots, depth), jnp.float32),
        ],
        compiler_params=params(2),
        name="project_qkv",
    )(gain, resident(w_query), resident(w_kv), *in_start_order(rows))


def stack_kernel(*refs):
    refs[-2][...] = join_rows(refs[:-2][::-1], refs[-1]).astype(refs[-2].dtype)


def stack(pieces):
    shape = (len(pieces) * pieces[0].shape[0], pieces[0].shape[1])
    return pl.pallas_call(
        stack_kernel,
        out_shape=jax.ShapeDtypeStruct(shape, pieces[0].dtype),
        in_specs=[in_vmem] * len(pieces),
        out_specs=in_vmem,
        scratch_shapes=[pltpu.VMEM(shape, jnp.float32)],
        compiler_params=params(1),
        name="stack",
    )(*pieces[::-1])


def attend_kernel(
    slots,
    shards,
    lengths_ref,
    cosine_ref,
    sine_ref,
    key_ref,
    value_ref,
    *refs,
):
    parts = refs[:shards]
    out_ref, query_s, kv_s, kv_wide_s, mixed_s, stats_s = refs[-6:]
    all_rows = parts[0].shape[0]
    own_rows = all_rows // slots
    here = HEADS // slots
    query_cols = here * HEAD_DIM
    kv_cols = 2 * KV_HEADS * HEAD_DIM // slots
    columns = query_cols + kv_cols
    tensor_index = lax.axis_index("tensor")
    inner_index = lax.axis_index("inner")
    positions = key_ref.shape[1] // KV_HEADS

    joined = functools.reduce(jnp.add, [ref[...].astype(jnp.float32) for ref in parts])
    squares = jnp.sum(joined[:, columns:], axis=1, keepdims=True)
    joined = joined[:, :columns] * lax.rsqrt(squares / D + epsilon)
    cosine = cosine_ref[...]
    sine = sine_ref[...]

    def rotate(block):
        count = block.shape[0]
        even = lax.broadcasted_iota(jnp.int32, block.shape, 1) % 2 == 0
        other = jnp.where(
            even, pltpu.roll(block, HEAD_DIM - 1, axis=1), pltpu.roll(block, 1, axis=1)
        )
        return block * cosine[:count] + other * sine[:count]

    for j in range(here):
        block = rotate(joined[:, j * HEAD_DIM : (j + 1) * HEAD_DIM])
        query_s[j * all_rows : (j + 1) * all_rows, :] = block
    for s in range(slots):
        kv_s[s] = joined[s * own_rows : (s + 1) * own_rows, query_cols:]
    for d in range(slots):
        kv_wide_s[:, d * kv_cols : (d + 1) * kv_cols] = kv_s[d ^ tensor_index]
    new_keys = []
    new_values = []
    for g in range(KV_HEADS):
        block = kv_wide_s[:, g * HEAD_DIM : (g + 1) * HEAD_DIM]
        new_keys.append(rotate(block).astype(jnp.bfloat16).astype(jnp.float32))
        block = kv_wide_s[:, (KV_HEADS + g) * HEAD_DIM : (KV_HEADS + g + 1) * HEAD_DIM]
        new_values.append(block.astype(jnp.bfloat16).astype(jnp.float32))

    score_scale = HEAD_DIM ** (-0.5)
    two_scale = score_scale * math.log2(math.e)
    row = lax.broadcasted_iota(jnp.int32, (HEADS, 1), 0)
    head = ((row % slots) ^ tensor_index) * here + row // slots
    kv_head = head // GROUP
    column = lax.broadcasted_iota(jnp.int32, (1, positions * KV_HEADS), 1)
    place = column // KV_HEADS + inner_index * positions
    column_head = column % KV_HEADS
    lanes = lax.broadcasted_iota(jnp.int32, (HEADS, LANES), 1)
    queries = [
        query_s[pl.ds(r, HEADS, stride=own_rows), :].astype(jnp.bfloat16) for r in range(own_rows)
    ]
    scores = [
        lax.dot_general(
            queries[r], key_ref[r], (((1,), (1,)), ((), ())), preferred_element_type=jnp.float32
        )
        for r in range(own_rows)
    ]
    weights = []
    mixtures = []
    for r in range(own_rows):
        used = jnp.where(place < lengths_ref[r : r + 1, 0:1], column_head, -1)
        masked = jnp.where(used == kv_head, scores[r], -1e30)
        key_rows = 0.0
        value_rows = 0.0
        for g in range(KV_HEADS):
            key_rows = key_rows + jnp.where(kv_head == g, new_keys[g][r : r + 1], 0.0)
            value_rows = value_rows + jnp.where(kv_head == g, new_values[g][r : r + 1], 0.0)
        new_score = jnp.sum(queries[r].astype(jnp.float32) * key_rows, axis=1, keepdims=True)
        new_score = jnp.where(inner_index == 0, new_score, -1e30)
        peak = jnp.maximum(jnp.max(masked, axis=1, keepdims=True), new_score)
        weight = jnp.exp2((masked - peak) * two_scale)
        new_weight = jnp.exp2((new_score - peak) * two_scale)
        peak = peak * score_scale
        totals = jnp.sum(weight, axis=1, keepdims=True) + new_weight
        weights.append(weight.astype(jnp.bfloat16))
        mixtures.append(new_weight.astype(jnp.bfloat16).astype(jnp.float32) * value_rows)
        stats_s[pl.ds(r, HEADS, stride=own_rows), :] = spread(
            three_parts(peak), lanes, 0
        ) + spread(three_parts(totals), lanes, 4)
    for r in range(own_rows):
        mixed_s[pl.ds(r, HEADS, stride=own_rows), :] = mixtures[r] + jnp.dot(
            weights[r], value_ref[r], preferred_element_type=jnp.float32
        )
    heads = own_rows * HEADS
    out_ref[:heads, :] = mixed_s[...].astype(jnp.bfloat16)
    packed = stats_s[:all_rows, :]
    for j in range(1, here):
        block = stats_s[j * all_rows : (j + 1) * all_rows, :]
        packed = packed + pltpu.roll(block, j * STATS, axis=1)
    spare = out_ref.shape[0] - heads - all_rows
    if spare:
        packed = jnp.concatenate([packed, jnp.zeros((spare, LANES), jnp.float32)], axis=0)
    out_ref[heads:, :] = packed.astype(jnp.bfloat16)


def attend(lengths, cosine, sine, parts, keys, values, later, slots):
    own_rows = parts[0].shape[0] // slots
    kv_cols = 2 * KV_HEADS * HEAD_DIM // slots
    return pl.pallas_call(
        functools.partial(attend_kernel, slots, len(parts)),
        out_shape=jax.ShapeDtypeStruct(
            (own_rows * HEADS + max(16, own_rows * slots), HEAD_DIM), jnp.bfloat16
        ),
        in_specs=[in_vmem] * (5 + len(parts)) + [in_place] * len(later),
        out_specs=in_vmem,
        scratch_shapes=[
            pltpu.VMEM((own_rows * HEADS, HEAD_DIM), jnp.float32),
            pltpu.VMEM((slots, own_rows, kv_cols), jnp.float32),
            pltpu.VMEM((own_rows, slots * kv_cols), jnp.float32),
            pltpu.VMEM((own_rows * HEADS, HEAD_DIM), jnp.float32),
            pltpu.VMEM((own_rows * HEADS, LANES), jnp.float32),
        ],
        compiler_params=params(6),
        name="attend",
    )(lengths, cosine, sine, resident(keys), resident(values), *parts[::-1], *[resident(w) for w in later])


def combine_kernel(shards, slots, *refs):
    out_s = refs[-1]
    all_rows, columns = out_s.shape
    here = columns // HEAD_DIM
    heads = here * all_rows
    mixtures = [ref[:heads, :].astype(jnp.float32) for ref in refs[:shards]]
    stats = [ref[heads:, :].astype(jnp.float32)[:all_rows] for ref in refs[:shards]]
    for j in range(here):

        def whole(block, first):
            lane = j * STATS + first
            return block[:, lane : lane + 1] + block[:, lane + 1 : lane + 2] + block[:, lane + 2 : lane + 3]

        peaks = [whole(block, 0) for block in stats]
        top = functools.reduce(jnp.maximum, peaks)
        mixed = 0.0
        denominator = 0.0
        for mixture, block, peak in zip(mixtures, stats, peaks):
            factor = jnp.exp(peak - top)
            mixed = mixed + factor * mixture[j * all_rows : (j + 1) * all_rows]
            denominator = denominator + factor * whole(block, 4)
        out_s[:, j * HEAD_DIM : (j + 1) * HEAD_DIM] = mixed / denominator
    part_rows(out_s, refs[-1 - slots : -1])


def combine(parts, later, all_rows, slots):
    count = len(parts)
    columns = HEADS // slots * HEAD_DIM
    return pl.pallas_call(
        functools.partial(combine_kernel, count, slots),
        out_shape=(jax.ShapeDtypeStruct((all_rows // slots, columns), jnp.bfloat16),) * slots,
        in_specs=[in_vmem] * count + [in_place] * len(later),
        out_specs=(in_vmem,) * slots,
        scratch_shapes=[pltpu.VMEM((all_rows, columns), jnp.float32)],
        compiler_params=params(2),
        name="combine",
    )(*parts[::-1], *[resident(w) for w in later])


def turned(block, step, own_rows):
    count = block.shape[0]
    span = step * own_rows
    row = lax.broadcasted_iota(jnp.int32, (count, 1), 0)
    return jnp.where(
        (row // span) % 2 == 0,
        pltpu.roll(block, count - span, axis=0),
        pltpu.roll(block, span, axis=0),
    )


def out_kernel(slots, later, upper_ref, lower_ref, *refs):
    pieces = refs[:slots][::-1]
    outs = refs[slots + later : 2 * slots + later]
    left_s = refs[-1]
    own_rows = pieces[0].shape[0]
    rows = left_s.shape[0]
    cut = upper_ref.shape[0]
    lefts = [join_rows(pieces, left_s)]
    for k in range(1, slots):
        low = k & -k
        lefts.append(turned(lefts[k ^ low], low, own_rows))
    left = jnp.concatenate(lefts, axis=0).astype(jnp.bfloat16)

    def store(start, size, value):
        span = pl.ds(start, size)
        value = value + jnp.dot(
            left[:, cut:], lower_ref[:, span], preferred_element_type=jnp.float32
        )
        for k, ref in enumerate(outs):
            ref[:, span] = value[k * rows : (k + 1) * rows].astype(jnp.bfloat16)

    product_tiles(left[:, :cut], upper_ref, store)


def project_out(pieces, upper, lower, later):
    slots = len(pieces)
    own_rows, depth = pieces[0].shape
    shape = jax.ShapeDtypeStruct((own_rows * slots, upper.shape[1]), jnp.bfloat16)
    return pl.pallas_call(
        functools.partial(out_kernel, slots, len(later)),
        out_shape=(shape,) * slots,
        in_specs=[in_vmem] * (2 + slots) + [in_place] * len(later),
        out_specs=(in_vmem,) * slots,
        scratch_shapes=[pltpu.VMEM((own_rows * slots, depth), jnp.float32)],
        compiler_params=params(3),
        name="project_out",
    )(resident(upper), resident(lower), *pieces[::-1], *[resident(w) for w in later])


def pair_kernel(first_ref, second_ref, out_ref):
    total = first_ref[...].astype(jnp.float32) + second_ref[...].astype(jnp.float32)
    out_ref[...] = total.astype(jnp.bfloat16)


def pair_sum(first, second):
    return pl.pallas_call(
        pair_kernel,
        out_shape=jax.ShapeDtypeStruct(first.shape, first.dtype),
        in_specs=[in_vmem] * 2,
        out_specs=in_vmem,
        compiler_params=params(2),
        name="pair_sum",
    )(first, second)


def gate_up_tiles(scaled, gate_ref, up_ref, out_ref, first, count):
    def store(offset):
        def place(start, size, value):
            start = pl.multiple_of(offset + start, math.gcd(offset, size))
            out_ref[:, pl.ds(start, size)] = value.astype(jnp.bfloat16)

        return place

    product_tiles(scaled, gate_ref, store(0), first, count)
    product_tiles(scaled, up_ref, store(count), first, count)


def first_gate_up_kernel(slots, count, rows_ref, gain_ref, gate_ref, up_ref, *refs):
    parts = refs[:slots]
    out_ref, updated_ref, scaled_ref = refs[-3:]
    own_rows = updated_ref.shape[0]
    total = functools.reduce(jnp.add, [ref[...].astype(jnp.float32) for ref in parts])
    updated = (rows_ref[...] + total).astype(jnp.bfloat16)
    wide = updated.astype(jnp.float32)
    updated_ref[...] = wide[:own_rows]
    squares = jnp.sum(wide * wide, axis=1, keepdims=True)
    out_ref[:, 2 * count :] = squares_block(squares).astype(jnp.bfloat16)
    scaled = (wide * gain_ref[...].astype(jnp.float32)[None, :]).astype(jnp.bfloat16)
    scaled_ref[...] = scaled
    gate_up_tiles(scaled, gate_ref, up_ref, out_ref, 0, count)


def first_gate_up(rows, gain, parts, w_gate, w_up, later, count, own_rows):
    slots = len(parts)
    return pl.pallas_call(
        functools.partial(first_gate_up_kernel, slots, count),
        out_shape=(
            jax.ShapeDtypeStruct((rows.shape[0], 2 * count + LANES), jnp.bfloat16),
            jax.ShapeDtypeStruct((own_rows, rows.shape[1]), jnp.float32),
            jax.ShapeDtypeStruct(rows.shape, jnp.bfloat16),
        ),
        in_specs=[in_vmem] * (4 + slots) + [in_place] * len(later),
        out_specs=(in_vmem,) * 3,
        compiler_params=params(3),
        cost_estimate=product_cost(w_gate.shape[0], 2 * count),
        name="first_gate_up",
    )(
        rows,
        gain,
        resident(w_gate),
        resident(w_up),
        *parts[::-1],
        *[resident(w) for w in later],
    )


def second_gate_up_kernel(first, count, scaled_ref, gate_ref, up_ref, *refs):
    out_ref = refs[-1]
    gate_up_tiles(scaled_ref[...], gate_ref, up_ref, out_ref, first, count)


def second_gate_up(scaled, w_gate, w_up, later, first):
    count = w_gate.shape[1] - first
    return pl.pallas_call(
        functools.partial(second_gate_up_kernel, first, count),
        out_shape=jax.ShapeDtypeStruct((scaled.shape[0], 2 * count), jnp.bfloat16),
        in_specs=[in_vmem] * 3 + [in_place] * len(later),
        out_specs=in_vmem,
        compiler_params=params(3),
        cost_estimate=product_cost(w_gate.shape[0], 2 * count),
        name="second_gate_up",
    )(scaled, resident(w_gate), resident(w_up), *[resident(w) for w in later])


def hidden_of(near_ref, far_ref, scale, count):
    def total(start):
        span = slice(start, start + count)
        return (near_ref[:, span].astype(jnp.float32) + far_ref[:, span].astype(jnp.float32)) * scale

    gate = total(0)
    return (gate / (1.0 + jnp.exp(-gate)) * total(count)).astype(jnp.bfloat16)


def first_down_kernel(count, near_ref, far_ref, weight_ref, token_ref, out_ref, scale_ref):
    del token_ref
    squares = jnp.sum(
        near_ref[:, 2 * count :].astype(jnp.float32) + far_ref[:, 2 * count :].astype(jnp.float32),
        axis=1,
        keepdims=True,
    )
    scale = lax.rsqrt(squares / D + epsilon)
    scale_ref[...] = jnp.broadcast_to(scale, scale_ref.shape)

    def store(start, size, value):
        out_ref[:, pl.ds(start, size)] = value

    product_tiles(hidden_of(near_ref, far_ref, scale, count), weight_ref.at[:count], store)


def first_down(near, far, weight, token, count):
    rows = near.shape[0]
    return pl.pallas_call(
        functools.partial(first_down_kernel, count),
        out_shape=(
            jax.ShapeDtypeStruct((rows, weight.shape[1]), jnp.float32),
            jax.ShapeDtypeStruct((rows, LANES), jnp.float32),
        ),
        in_specs=[in_vmem] * 3 + [in_place],
        out_specs=(in_vmem,) * 2,
        compiler_params=params(3),
        cost_estimate=product_cost(count, weight.shape[1]),
        name="first_down",
    )(near, far, resident(weight), token)


def second_down_kernel(count, near_ref, far_ref, weight_ref, part_ref, scale_ref, *refs):
    out_s = refs[-1]
    first = weight_ref.shape[0] - count

    def store(start, size, value):
        span = pl.ds(start, size)
        out_s[:, span] = part_ref[:, span] + value

    hidden = hidden_of(near_ref, far_ref, scale_ref[:, 0:1], count)
    product_tiles(hidden, weight_ref.at[first:], store)
    part_rows(out_s, refs[:-1])


def second_down(near, far, weight, part, scale, slots):
    rows, columns = part.shape
    count = near.shape[1] // 2
    return pl.pallas_call(
        functools.partial(second_down_kernel, count),
        out_shape=(jax.ShapeDtypeStruct((rows // slots, columns), jnp.bfloat16),) * slots,
        in_specs=[in_vmem] * 5,
        out_specs=(in_vmem,) * slots,
        scratch_shapes=[pltpu.VMEM(part.shape, jnp.float32)],
        compiler_params=params(3),
        name="second_down",
    )(near, far, resident(weight), part, scale)


def hold_kernel(after_ref, weight_ref, out_ref):
    del after_ref, weight_ref
    out_ref[...] = jnp.zeros_like(out_ref)


def hold(after, weight):
    return pl.pallas_call(
        hold_kernel,
        out_shape=jax.ShapeDtypeStruct((8, LANES), jnp.float32),
        in_specs=[in_place, in_place],
        out_specs=in_vmem,
        compiler_params=params(1),
        name="hold",
    )(after, resident(weight))


def finish_kernel(updated_ref, *refs):
    total = functools.reduce(jnp.add, [ref[...].astype(jnp.float32) for ref in refs[:-1]])
    refs[-1][...] = (updated_ref[...] + total).astype(jnp.bfloat16)


def finish(updated, parts):
    return pl.pallas_call(
        finish_kernel,
        out_shape=jax.ShapeDtypeStruct(updated.shape, jnp.bfloat16),
        in_specs=[in_vmem] * (1 + len(parts)),
        out_specs=in_vmem,
        compiler_params=params(1),
        name="finish",
    )(updated, *parts[::-1])


def rotation_tables(positions, repeats):
    inverse = jnp.exp(
        (jnp.arange(HEAD_DIM) // 2).astype(jnp.float32) * (-2.0 / HEAD_DIM) * math.log(rope_base)
    )
    angles = positions[:, None] * inverse[None, :]
    sign = jnp.where(jnp.arange(HEAD_DIM) % 2 == 0, -1.0, 1.0)
    return (
        jnp.tile(jnp.cos(angles), (repeats, 1)),
        jnp.tile(jnp.sin(angles) * sign[None, :], (repeats, 1)),
    )


def local(
    states,
    attn_gain,
    ffn_gain,
    w_query,
    w_kv,
    w_out,
    w_gate,
    w_up,
    w_down,
    key_cache,
    value_cache,
    lengths,
):
    tensor_index = lax.axis_index("tensor")
    slots = lax.axis_size("tensor")
    own_rows = states.shape[0]
    all_rows = own_rows * slots

    got = exchange(states, "tensor")
    own, attn_gain, ffn_gain, w_kv, w_query = load(
        states, attn_gain, ffn_gain, w_kv, w_query, after=states
    )
    rows, *pieces = project_qkv([own] + got[1:], attn_gain, w_query, w_kv)

    rows, lengths = lax.optimization_barrier((rows, lengths))
    my_lengths = lax.dynamic_slice_in_dim(lengths, tensor_index * own_rows, own_rows, 0)
    cosine, sine = rotation_tables(my_lengths.astype(jnp.float32), slots)
    my_lengths = jnp.broadcast_to(my_lengths[:, None], (own_rows, LANES))
    flat = (own_rows, key_cache.shape[1] * KV_HEADS, HEAD_DIM)
    (keys,) = load(key_cache.reshape(flat), after=rows)
    joined = stack(scatter_slots(pieces, 1))
    joined, keys = lax.optimization_barrier((joined, keys))
    (values,) = load(value_cache.reshape(flat), after=joined)
    parts, values = lax.optimization_barrier((exchange(joined, "inner")[::-1], values))
    shard = attend(my_lengths, cosine, sine, parts, keys, values, [], slots)

    cut = w_out.shape[0] // 2
    (out_upper,) = load(w_out, after=shard, spans=[(0, cut)])
    shards, out_upper = lax.optimization_barrier((exchange(shard, "inner"), out_upper))
    pieces = combine(shards, [w_gate], all_rows, slots)
    (out_lower,) = load(w_out, after=pieces[0], spans=[(cut, w_out.shape[0] - cut)])
    pieces, out_lower = lax.optimization_barrier((scatter_slots(pieces, 1)[::-1], out_lower))
    parts = scatter_slots(project_out(pieces[::-1], out_upper, out_lower, [w_up]), 0)

    tiles = w_gate.shape[1] // LANES
    first = (tiles + 1) // 2 * LANES
    one, updated, scaled = first_gate_up(
        rows, ffn_gain, parts, w_gate, w_up, [], first, own_rows
    )
    two = second_gate_up(scaled, w_gate, w_up, [], first)
    steps = steps_up(lax.axis_size("inner"))
    for step in steps[:-1]:
        one = pair_sum(one, swap_with(one, "inner", step))
        two = pair_sum(two, swap_with(two, "inner", step))
    token = hold(two, w_down)
    part, scale = first_down(one, swap_with(one, "inner", steps[-1]), w_down, token, first)
    pieces = second_down(two, swap_with(two, "inner", steps[-1]), w_down, part, scale, slots)
    parts = scatter_slots(pieces, 0)
    return finish(updated, parts)


def solution(mesh):
    in_specs = (
        P(("groups", "tensor"), "inner"),
        P("inner"),
        P("inner"),
        P("inner", "tensor"),
        P("inner", "tensor"),
        P("tensor", "inner"),
        P("inner", "tensor"),
        P("inner", "tensor"),
        P("tensor", "inner"),
        P(("groups", "tensor"), "inner", None, None),
        P(("groups", "tensor"), "inner", None, None),
        P("groups"),
    )
    out_specs = P(("groups", "tensor"), "inner")
    return jax.shard_map(local, mesh=mesh, in_specs=in_specs, out_specs=out_specs, check_vma=False)
```
